32 devices in a mesh: dp: 4 (over x, core), seq: 8 (over z, y).
Axes of the slice: x: 2, y: 2, z: 4, core: 2. Of those that a mesh axis runs over, the one named last changes fastest.
Arguments:
- tokens: bfloat16 [4, 2048, 512], P('dp', 'seq'), may hold values from -6 to 6
- segment_ids: int32 [4, 2048], P('dp'), may hold values from 0 to 2, as said below
- gain_one: float32 [512], replicated, may hold values from 0.5 to 1.5
- bias_one: float32 [512], replicated, may hold values from -3 to 3
- w_qkv: bfloat16 [512, 1536], replicated, may hold values from -0.375 to 0.375
- b_val: float32 [512], replicated, may hold values from -0.3 to 0.3
- w_out: bfloat16 [512, 512], replicated, may hold values from -4 to 4
- b_out: float32 [512], replicated, may hold values from -3 to 3
- gain_two: float32 [512], replicated, may hold values from 0.5 to 1.5
- bias_two: float32 [512], replicated, may hold values from -3 to 3
- w_up: bfloat16 [512, 2048], replicated, may hold values from -0.25 to 0.25
- b_up: float32 [2048], replicated, may hold values from -3 to 3
- w_down: bfloat16 [2048, 512], replicated, may hold values from -0.125 to 0.125
- b_down: float32 [512], replicated, may hold values from -3 to 3
- cotangent: bfloat16 [4, 2048, 512], P('dp', 'seq'), may hold values from -6 to 6
Outputs:
- output: bfloat16 [4, 2048, 512], P('dp', 'seq')
- tokens_grad: float32 [4, 2048, 512], P('dp', 'seq')
- gain_one_grad: float32 [512], replicated
- bias_one_grad: float32 [512], replicated
- w_qkv_grad: float32 [512, 1536], replicated
- b_val_grad: float32 [512], replicated
- w_out_grad: float32 [512, 512], replicated
- b_out_grad: float32 [512], replicated
- gain_two_grad: float32 [512], replicated
- bias_two_grad: float32 [512], replicated
- w_up_grad: float32 [512, 2048], replicated
- b_up_grad: float32 [2048], replicated
- w_down_grad: float32 [2048, 512], replicated
- b_down_grad: float32 [512], replicated
The draws below stay inside these ranges and needn't reach their ends.
Inputs may be any that keep to these rules, and one draw needn't show every extreme that they name: `segment_ids`: every row holds exactly three documents, numbered 0, 1, 2 in order along the row, each a run of equal ids; the first ends within the first 256 positions and the last begins within the last 256.
All inputs are finite; a program needn't handle non-finite values.
Results may differ from the reference program's by a relative error of at most 0.019.
Values may be sent and summed in bfloat16 or wider, within the bound.
A program may use at most 192 MiB of HBM per device.

```python
import math
import jax
import jax.numpy as jnp
from jax import lax

D = 512
HEADS = 8
HD = 64
FF = 2048
TOK_DEV = 256
LEN = 2048
ROWS = 4


def draw_segment_ids(key, part):
    key = jax.random.fold_in(key, 11)

    def one_row(row_key):
        start_key, end_key = jax.random.split(row_key, 2)
        first_pos = jax.random.randint(start_key, (), 1, TOK_DEV)
        finish = LEN - jax.random.randint(end_key, (), 1, TOK_DEV)
        positions = jnp.arange(LEN, dtype=jnp.int32)
        return (positions >= first_pos).astype(jnp.int32) + (positions >= finish).astype(jnp.int32)
    return jax.vmap(one_row)(jax.random.split(key, ROWS))


def levels(own_key, extent, pieces, low, largest):
    loudness = 1.0
    for position, blocks in pieces:
        heights = jax.random.uniform(jax.random.fold_in(jax.random.fold_in(own_key, 6), position), (blocks,), jnp.float32, low / len(pieces), largest / len(pieces))
        loudness = loudness * jnp.repeat(jnp.exp(heights), extent[position] // blocks).reshape((-1,) + (1,) * (len(extent) - 1 - position))
    return loudness


def normal_values(own_key, shape, deviation, most, cuts=(), kind=jnp.bfloat16):
    factor_of = levels(own_key, shape, cuts, -0.22, 0.18) if cuts else 1.0
    array = jax.random.normal(own_key, shape, jnp.float32) * deviation * factor_of
    return jnp.minimum(jnp.maximum(array, -most), most).astype(kind)


def setup_inputs(seed: int = 0) -> dict:
    seeds = jax.random.split(jax.random.key(seed), 16)
    return {
        "tokens": normal_values(seeds[0], (ROWS, LEN, D), 1.0, 6.0, ((0, 4), (1, 8))),
        "segment_ids": draw_segment_ids(jax.random.fold_in(seeds[15], 71), 0),
        "gain_one": jnp.clip(1.0 + 0.1 * jax.random.normal(seeds[2], (D,), jnp.float32), 0.5, 1.5),
        "bias_one": normal_values(seeds[3], (D,), 0.5, 3.0, (), jnp.float32),
        "w_qkv": normal_values(seeds[4], (D, 3 * D), (D // 2) ** -0.5, 0.375),
        "b_val": normal_values(seeds[5], (D,), 0.05, 0.3, (), jnp.float32),
        "w_out": normal_values(seeds[6], (D, D), (max(1, D * 8 // LEN)) ** -0.5, 4.0),
        "b_out": normal_values(seeds[7], (D,), 0.5, 3.0, (), jnp.float32),
        "gain_two": jnp.clip(1.0 + 0.1 * jax.random.normal(seeds[8], (D,), jnp.float32), 0.5, 1.5),
        "bias_two": normal_values(seeds[9], (D,), 0.5, 3.0, (), jnp.float32),
        "w_up": normal_values(seeds[10], (D, FF), D ** -0.5, 0.25),
        "b_up": normal_values(seeds[11], (FF,), 0.5, 3.0, (), jnp.float32),
        "w_down": normal_values(seeds[12], (FF, D), FF ** -0.5, 0.125),
        "b_down": normal_values(seeds[13], (D,), 0.5, 3.0, (), jnp.float32),
        "cotangent": normal_values(seeds[14], (ROWS, LEN, D), 1.0, 6.0, ((0, 4), (1, 8))),
    }


@jax.custom_vjp
def low(v):
    return lax.optimization_barrier(v.astype(jnp.bfloat16)).astype(jnp.float32)

@jax.custom_vjp
def low_back(v):
    return v

def low_keep(v):
    return (low(v), None)

def low_pass(kept, grad):
    return (grad,)

def back_keep(v):
    return (v, None)

def back_low(kept, grad):
    return (low(grad),)
low.defvjp(low_keep, low_pass)
low_back.defvjp(back_keep, back_low)
highest = lax.Precision.HIGHEST
norm_eps = 1e-05
select_weight = 4.0
neg_large = -1e+30

def layer_norm(values, norm_gain, norm_shift):
    centered = values - lax.optimization_barrier(jnp.mean(values, axis=-1, keepdims=True))
    variance = lax.optimization_barrier(jnp.mean(centered * centered, axis=-1, keepdims=True))
    return centered * lax.rsqrt(variance + norm_eps) * norm_gain + norm_shift

def row_layer(row_tokens, row_segments, weights):
    gain_one, bias_one, w_qkv, b_val, w_out, b_out, gain_two, bias_two, w_up, b_up, w_down, b_down = weights
    score_scale = 1.0 / math.sqrt(HD)
    normed_one = low(layer_norm(row_tokens, gain_one, bias_one))
    value_bias = jnp.concatenate([jnp.zeros((2 * D,), jnp.float32), b_val])
    joined_qkv = low_back(low(jnp.dot(normed_one, w_qkv, precision=highest) + value_bias))
    queries = joined_qkv[:, :D].reshape(LEN, HEADS, HD)
    keys_all = joined_qkv[:, D:2 * D].reshape(LEN, HEADS, HD)
    values_all = joined_qkv[:, 2 * D:].reshape(LEN, HEADS, HD)
    block_rows = min(512, LEN)
    block_count = LEN // block_rows
    positions = jnp.arange(LEN, dtype=jnp.int32)
    lower_mask = (jnp.arange(block_rows)[:, None] > jnp.arange(block_rows)[None, :]).astype(jnp.float32)

    def query_block(column_sums, inputs):
        block_queries, block_pos, block_segs = inputs
        scores = low_back(jnp.einsum('qhd,khd->hqk', block_queries, keys_all, precision=highest) * score_scale)
        same_doc = block_segs[:, None] == row_segments[None, :]
        attend_mask = same_doc & (positions[None, :] <= block_pos[:, None])
        select_mask = same_doc & (positions[None, :] < block_pos[:, None])
        chosen = jnp.where(select_mask, jax.nn.softplus(scores[0]), 0.0)
        forgotten = column_sums[None, :] + jnp.dot(lower_mask, chosen, precision=highest)
        logits = jnp.where(attend_mask[None], scores - select_weight / LEN * forgotten[None], neg_large)
        shifted = logits - lax.optimization_barrier(jnp.max(logits, axis=-1, keepdims=True))
        exp_terms = jnp.exp(shifted)
        prob_rows = exp_terms / lax.optimization_barrier(jnp.sum(exp_terms, axis=-1, keepdims=True))
        mixed_block = jnp.einsum('hqk,khd->qhd', low(prob_rows), values_all, precision=highest)
        return (column_sums + lax.optimization_barrier(jnp.sum(chosen, axis=0)), mixed_block)
    start_sums = jnp.zeros((LEN,), jnp.float32)
    final_sums, mixed_heads = lax.scan(jax.checkpoint(query_block), start_sums, (queries.reshape(block_count, block_rows, HEADS, HD), positions.reshape(block_count, block_rows), row_segments.reshape(block_count, block_rows)))
    mixed_rows = low_back(low(mixed_heads.reshape(LEN, D)))
    branch = low_back(jnp.dot(mixed_rows, w_out, precision=highest) + b_out)
    middle = row_tokens + branch
    normed_two = low(layer_norm(middle, gain_two, bias_two))
    hidden = low_back(jnp.dot(normed_two, w_up, precision=highest) + b_up)
    active = low(jax.nn.gelu(hidden, approximate=False))
    feed_out = low_back(jnp.dot(active, w_down, precision=highest) + b_down)
    return middle + feed_out

def reference(tokens, segment_ids, gain_one, bias_one, w_qkv, b_val, w_out, b_out, gain_two, bias_two, w_up, b_up, w_down, b_down, cotangent):
    weights = (gain_one.astype(jnp.float32), bias_one.astype(jnp.float32), w_qkv.astype(jnp.float32), b_val.astype(jnp.float32), w_out.astype(jnp.float32), b_out.astype(jnp.float32), gain_two.astype(jnp.float32), bias_two.astype(jnp.float32), w_up.astype(jnp.float32), b_up.astype(jnp.float32), w_down.astype(jnp.float32), b_down.astype(jnp.float32))

    def forward(inputs, params):

        def one_row(row_pair):
            return jax.checkpoint(row_layer)(row_pair[0], row_pair[1], params)
        return lax.map(one_row, (inputs, segment_ids))
    output, pullback = jax.vjp(forward, tokens.astype(jnp.float32), weights)
    tokens_grad, weight_grads = pullback(cotangent.astype(jnp.float32))
    return (output.astype(jnp.bfloat16), tokens_grad, weight_grads[0], weight_grads[1], weight_grads[2], weight_grads[3], weight_grads[4], weight_grads[5], weight_grads[6], weight_grads[7], weight_grads[8], weight_grads[9], weight_grads[10], weight_grads[11])
```

```python
import functools
import math

import jax
import jax.numpy as jnp
from jax import lax
from jax.experimental import pallas as pl
from jax.experimental.pallas import tpu as pltpu
from jax.sharding import PartitionSpec as P

HD = 64


norm_eps = 1e-05
select_weight = 4.0
neg_large = -1e30
highest = lax.Precision.HIGHEST
vmem_bytes = 60 * 1024 * 1024


def prefix(array, axis, combine, identity, reverse):
    length, here = (lax.axis_size(axis), lax.axis_index(axis))
    everything = lax.all_gather(array.astype(jnp.bfloat16), axis)
    start = jnp.broadcast_to(jnp.asarray(identity, array.dtype), array.shape)

    def hop(k, before):
        at = length - 1 - k if reverse else k
        reached = at > here if reverse else at < here
        new = combine(before, everything[at].astype(array.dtype))
        return jnp.where(reached, new, before)

    return lax.fori_loop(0, length, hop, start)


def layer_norm(values, norm_gain, norm_shift):
    centered = values - jnp.mean(values, axis=-1, keepdims=True)
    variance = jnp.mean(centered * centered, axis=-1, keepdims=True)
    return centered * lax.rsqrt(variance + norm_eps) * norm_gain + norm_shift


def exact_gelu(values):
    return jax.nn.gelu(values, approximate=False)


def add_arrays(earlier, later):
    return earlier + later


def keep_state(state_in):
    return state_in


def pick_block():
    return 512


def local(
    tokens,
    segment_ids,
    gain_one,
    bias_one,
    w_qkv,
    b_val,
    w_out,
    b_out,
    gain_two,
    bias_two,
    w_up,
    b_up,
    w_down,
    b_down,
    cotangent,
):
    seq_count = lax.axis_size("seq")
    seq_rank = lax.axis_index("seq")
    row_tokens = tokens[0].astype(jnp.float32)
    tok_rows = row_tokens.shape[0]
    model_width = row_tokens.shape[1]
    head_count = model_width // HD
    length = tok_rows * seq_count
    score_scale = 1.0 / math.sqrt(HD)
    select_coeff = select_weight / length
    row_segments = segment_ids[0]
    row_base = seq_rank * tok_rows
    query_pos = row_base + jnp.arange(tok_rows, dtype=jnp.int32)
    query_segs = lax.dynamic_slice_in_dim(row_segments, row_base, tok_rows)
    last_query = row_base + tok_rows - 1
    lower_mask = (jnp.arange(tok_rows)[:, None] > jnp.arange(tok_rows)[None, :]).astype(jnp.float32)
    upper_mask = lower_mask.T
    normed_one, norm_one_back = jax.vjp(layer_norm, row_tokens, gain_one, bias_one)
    normed_one_low = normed_one.astype(jnp.bfloat16)
    value_bias = jnp.concatenate([jnp.zeros((2 * model_width,), jnp.float32), b_val])
    joined_low = (
        jnp.dot(normed_one_low, w_qkv, preferred_element_type=jnp.float32) + value_bias
    ).astype(jnp.bfloat16)
    queries = joined_low[:, :model_width]
    keys_mine = joined_low[:, model_width : 2 * model_width]
    values_mine = joined_low[:, 2 * model_width :]
    query_heads = queries.reshape(tok_rows, head_count, HD)
    query_zero = queries[:, :HD]
    query_rest = query_heads[:, 1:]

    def pair_masks(key_start, key_rows):
        key_pos = key_start + jnp.arange(key_rows, dtype=jnp.int32)
        key_segs = lax.dynamic_slice_in_dim(row_segments, key_start, key_rows)
        same_doc = query_segs[:, None] == key_segs[None, :]
        attend_mask = same_doc & (key_pos[None, :] <= query_pos[:, None])
        select_mask = same_doc & (key_pos[None, :] < query_pos[:, None])
        return (attend_mask, select_mask)

    select_init = (
        jnp.zeros((tok_rows, length), jnp.float32),
        jnp.zeros((tok_rows, length), jnp.float32),
        jnp.zeros((length,), jnp.float32),
    )
    running = select_init
    key_piece = lax.all_gather(keys_mine[:, :HD], "seq", axis=0, tiled=True)
    piece_rows = key_piece.shape[0]
    block_rows = pick_block()

    def select_block(state_now, offset):
        zero_scores, local_forgot, column_sums = state_now
        key_block = lax.dynamic_slice_in_dim(key_piece, offset, block_rows)
        attend_mask, select_mask = pair_masks(offset, block_rows)
        scores = (
            jnp.einsum("qd,kd->qk", query_zero, key_block, preferred_element_type=jnp.float32)
            * score_scale
        )
        chosen = jnp.where(select_mask, jax.nn.softplus(scores), 0.0)
        forgot = jnp.dot(lower_mask, chosen, precision=highest)
        zero_scores = lax.dynamic_update_slice_in_dim(zero_scores, scores, offset, 1)
        local_forgot = lax.dynamic_update_slice_in_dim(local_forgot, forgot, offset, 1)
        column_sums = lax.dynamic_update_slice_in_dim(
            column_sums, jnp.sum(chosen, axis=0), offset, 0
        )
        return ((zero_scores, local_forgot, column_sums), None)

    offsets = jnp.arange(piece_rows // block_rows, dtype=jnp.int32) * block_rows
    running, unused = lax.scan(select_block, running, offsets)
    zero_scores, local_forgot, column_sums = running
    column_prefix = prefix(column_sums, "seq", add_arrays, jnp.zeros((length,), jnp.float32), False)
    attend_init = (
        jnp.full((head_count, tok_rows), neg_large, jnp.float32),
        jnp.zeros((head_count, tok_rows), jnp.float32),
        jnp.zeros((tok_rows, head_count, HD), jnp.float32),
    )
    running = attend_init
    attend_key_piece = lax.all_gather(keys_mine, "seq", axis=0, tiled=True)
    value_piece = lax.all_gather(values_mine, "seq", axis=0, tiled=True)
    piece_rows = attend_key_piece.shape[0]
    attend_block_rows = pick_block()

    def attend_block(state_now, offset):
        key_start = offset

        def attend_compute(state_in):
            run_max, run_total, accumulated = state_in
            key_block = lax.dynamic_slice_in_dim(
                attend_key_piece, offset, attend_block_rows
            ).reshape(attend_block_rows, head_count, HD)
            value_block = lax.dynamic_slice_in_dim(value_piece, offset, attend_block_rows).reshape(
                attend_block_rows, head_count, HD
            )
            attend_mask, select_mask = pair_masks(key_start, attend_block_rows)
            rest_scores = (
                jnp.einsum(
                    "qhd,khd->hqk", query_rest, key_block[:, 1:], preferred_element_type=jnp.float32
                )
                * score_scale
            )
            head_zero = lax.dynamic_slice_in_dim(zero_scores, key_start, attend_block_rows, 1)
            scores = jnp.concatenate([head_zero[None], rest_scores], axis=0)
            forgot = lax.dynamic_slice_in_dim(column_prefix, key_start, attend_block_rows)[
                None, :
            ] + lax.dynamic_slice_in_dim(local_forgot, key_start, attend_block_rows, 1)
            logits = jnp.where(attend_mask[None], scores - select_coeff * forgot[None], neg_large)
            new_max = jnp.maximum(run_max, jnp.max(logits, axis=-1))
            weights = jnp.where(attend_mask[None], jnp.exp(logits - new_max[:, :, None]), 0.0)
            decay_factor = jnp.exp(run_max - new_max)
            run_total = run_total * decay_factor + jnp.sum(weights, axis=-1)
            accumulated = accumulated * decay_factor.T[:, :, None] + jnp.einsum(
                "hqk,khd->qhd",
                weights.astype(jnp.bfloat16),
                value_block,
                preferred_element_type=jnp.float32,
            )
            return (new_max, run_total, accumulated)

        state_now = lax.cond(key_start <= last_query, attend_compute, keep_state, state_now)
        return (state_now, None)

    offsets = jnp.arange(piece_rows // attend_block_rows, dtype=jnp.int32) * attend_block_rows
    running, unused = lax.scan(attend_block, running, offsets)
    run_max, run_total, accumulated = running
    log_total = run_max + jnp.log(run_total)
    mixed_float = accumulated / run_total.T[:, :, None]
    mixed_low = mixed_float.reshape(tok_rows, model_width).astype(jnp.bfloat16)
    middle = row_tokens + jnp.dot(mixed_low, w_out, preferred_element_type=jnp.float32) + b_out
    normed_two, norm_two_back = jax.vjp(layer_norm, middle, gain_two, bias_two)
    normed_two_low = normed_two.astype(jnp.bfloat16)
    hidden = jnp.dot(normed_two_low, w_up, preferred_element_type=jnp.float32) + b_up
    active, gelu_back = jax.vjp(exact_gelu, hidden)
    active_low = active.astype(jnp.bfloat16)
    output = middle + jnp.dot(active_low, w_down, preferred_element_type=jnp.float32) + b_down
    grad_out = cotangent[0]
    grad_float = grad_out.astype(jnp.float32)
    w_down_grad = jnp.einsum("tf,td->fd", active_low, grad_out, preferred_element_type=jnp.float32)
    b_down_grad = jnp.sum(grad_float, axis=0)
    grad_active = jnp.einsum("td,fd->tf", grad_out, w_down, preferred_element_type=jnp.float32)
    (grad_hidden,) = gelu_back(grad_active)
    grad_hidden_low = grad_hidden.astype(jnp.bfloat16)
    w_up_grad = jnp.einsum(
        "td,tf->df", normed_two_low, grad_hidden_low, preferred_element_type=jnp.float32
    )
    b_up_grad = jnp.sum(grad_hidden_low.astype(jnp.float32), axis=0)
    grad_normed_two = jnp.einsum(
        "tf,df->td", grad_hidden_low, w_up, preferred_element_type=jnp.float32
    )
    grad_middle_norm, gain_two_grad, bias_two_grad = norm_two_back(grad_normed_two)
    grad_middle = grad_float + grad_middle_norm
    grad_branch_low = grad_middle.astype(jnp.bfloat16)
    w_out_grad = jnp.einsum(
        "td,te->de", mixed_low, grad_branch_low, preferred_element_type=jnp.float32
    )
    b_out_grad = jnp.sum(grad_branch_low.astype(jnp.float32), axis=0)
    grad_mixed_low = jnp.einsum(
        "te,de->td", grad_branch_low, w_out, preferred_element_type=jnp.float32
    ).astype(jnp.bfloat16)
    grad_mixed_heads = grad_mixed_low.reshape(tok_rows, head_count, HD)
    row_delta = jnp.sum(grad_mixed_heads.astype(jnp.float32) * mixed_float, axis=-1).T
    keys_back, values_back = (
        lax.all_gather(keys_mine, "seq", axis=0, tiled=True),
        lax.all_gather(values_mine, "seq", axis=0, tiled=True),
    )
    back_rows = pick_block()
    key_heads = keys_back.reshape(length, head_count, HD)
    value_heads = values_back.reshape(length, head_count, HD)

    def grad_block(state_now, offset):

        def grad_compute(state_in):
            query_grad, key_grad, value_grad, first_part, second_part, grad_cols = state_in
            key_block = lax.dynamic_slice_in_dim(key_heads, offset, back_rows)
            value_block = lax.dynamic_slice_in_dim(value_heads, offset, back_rows)
            attend_mask, select_mask = pair_masks(offset, back_rows)
            scores = (
                jnp.einsum(
                    "qhd,khd->hqk", query_heads, key_block, preferred_element_type=jnp.float32
                )
                * score_scale
            )
            chosen = jnp.where(select_mask, jax.nn.softplus(scores[0]), 0.0)
            forgot = lax.dynamic_slice_in_dim(column_prefix, offset, back_rows)[None, :] + jnp.dot(
                lower_mask, chosen, precision=highest
            )
            logits = scores - select_coeff * forgot[None]
            prob_block = jnp.where(attend_mask[None], jnp.exp(logits - log_total[:, :, None]), 0.0)
            grad_probs = jnp.einsum(
                "qhd,khd->hqk", grad_mixed_heads, value_block, preferred_element_type=jnp.float32
            )
            grad_logits = prob_block * (grad_probs - row_delta[:, :, None])
            value_part = jnp.einsum(
                "hqk,qhd->khd",
                prob_block.astype(jnp.bfloat16),
                grad_mixed_heads,
                preferred_element_type=jnp.float32,
            )
            rest_low = grad_logits[1:].astype(jnp.bfloat16)
            query_grad = (
                query_grad
                + jnp.einsum(
                    "hqk,khd->qhd", rest_low, key_block[:, 1:], preferred_element_type=jnp.float32
                )
                * score_scale
            )
            key_part = (
                jnp.einsum("hqk,qhd->khd", rest_low, query_rest, preferred_element_type=jnp.float32)
                * score_scale
            )
            total_grad = jnp.sum(grad_logits, axis=0)
            suffix_local = jnp.dot(upper_mask, total_grad, precision=highest)
            select_gate = jnp.where(select_mask, select_coeff * jax.nn.sigmoid(scores[0]), 0.0)
            first_part = lax.dynamic_update_slice_in_dim(
                first_part, grad_logits[0] - select_gate * suffix_local, offset, 1
            )
            second_part = lax.dynamic_update_slice_in_dim(second_part, select_gate, offset, 1)
            key_grad = lax.dynamic_update_slice_in_dim(key_grad, key_part, offset, 0)
            value_grad = lax.dynamic_update_slice_in_dim(value_grad, value_part, offset, 0)
            grad_cols = lax.dynamic_update_slice_in_dim(
                grad_cols, jnp.sum(total_grad, axis=0), offset, 0
            )
            return (query_grad, key_grad, value_grad, first_part, second_part, grad_cols)

        state_now = lax.cond(offset <= last_query, grad_compute, keep_state, state_now)
        return (state_now, None)

    grad_init = (
        jnp.zeros((tok_rows, head_count - 1, HD), jnp.float32),
        jnp.zeros((length, head_count - 1, HD), jnp.float32),
        jnp.zeros((length, head_count, HD), jnp.float32),
        jnp.zeros((tok_rows, length), jnp.float32),
        jnp.zeros((tok_rows, length), jnp.float32),
        jnp.zeros((length,), jnp.float32),
    )
    back_offsets = jnp.arange(length // back_rows, dtype=jnp.int32) * back_rows
    grad_state, unused = lax.scan(grad_block, grad_init, back_offsets)
    query_grad, key_grad, value_grad, first_part, second_part, grad_cols = grad_state
    grad_suffix = prefix(grad_cols, "seq", add_arrays, jnp.zeros((length,), jnp.float32), True)
    zero_grad_low = (first_part - second_part * grad_suffix[None, :]).astype(jnp.bfloat16)
    query_zero_grad = (
        jnp.dot(zero_grad_low, keys_back[:, :HD], preferred_element_type=jnp.float32) * score_scale
    )
    key_zero_grad = (
        jnp.einsum("ql,qd->ld", zero_grad_low, query_zero, preferred_element_type=jnp.float32)
        * score_scale
    )
    key_total = jnp.concatenate([key_zero_grad[:, None, :], key_grad], axis=1).reshape(
        length, model_width
    )
    value_total = value_grad.reshape(length, model_width)
    key_mine_grad, value_mine_grad = (
        lax.psum_scatter(
            key_total.astype(jnp.bfloat16), "seq", scatter_dimension=0, tiled=True
        ).astype(jnp.float32),
        lax.psum_scatter(
            value_total.astype(jnp.bfloat16), "seq", scatter_dimension=0, tiled=True
        ).astype(jnp.float32),
    )
    query_total = jnp.concatenate([query_zero_grad[:, None, :], query_grad], axis=1).reshape(
        tok_rows, model_width
    )
    grad_joined_low = jnp.concatenate([query_total, key_mine_grad, value_mine_grad], axis=1).astype(
        jnp.bfloat16
    )
    b_val_grad = jnp.sum(grad_joined_low[:, 2 * model_width :].astype(jnp.float32), axis=0)
    w_qkv_grad = jnp.einsum(
        "td,te->de", normed_one_low, grad_joined_low, preferred_element_type=jnp.float32
    )
    grad_normed_one = jnp.einsum(
        "te,de->td", grad_joined_low, w_qkv, preferred_element_type=jnp.float32
    )
    grad_tokens_norm, gain_one_grad, bias_one_grad = norm_one_back(grad_normed_one)
    tokens_grad = grad_middle + grad_tokens_norm
    summed = lax.psum(
        (
            gain_one_grad,
            bias_one_grad,
            w_qkv_grad,
            b_val_grad,
            w_out_grad,
            b_out_grad,
            gain_two_grad,
            bias_two_grad,
            w_up_grad,
            b_up_grad,
            w_down_grad,
            b_down_grad,
        ),
        ("dp", "seq"),
    )
    return (
        output.astype(jnp.bfloat16)[None],
        tokens_grad[None],
        summed[0],
        summed[1],
        summed[2],
        summed[3],
        summed[4],
        summed[5],
        summed[6],
        summed[7],
        summed[8],
        summed[9],
        summed[10],
        summed[11],
    )


low = jnp.bfloat16
MESH = pl.DeviceIdType.MESH


def dot_nn(left, right):
    return lax.dot_general(left, right, (((1,), (0,)), ((), ())), preferred_element_type=jnp.float32)


def dot_nt(left, right):
    return lax.dot_general(left, right, (((1,), (1,)), ((), ())), preferred_element_type=jnp.float32)


def dot_tn(left, right):
    return lax.dot_general(left, right, (((0,), (0,)), ((), ())), preferred_element_type=jnp.float32)


def swap_halves(wide):
    return pltpu.roll(wide, HD, 1)


def left_lanes(shape):
    return lax.broadcasted_iota(jnp.int32, shape, 1) < HD


def join_heads(left, right):
    return jnp.where(left_lanes(left.shape), left, right)


def fold_rows(wide):
    half = wide.shape[0] // 2
    return join_heads(wide[:half], swap_halves(wide[half:]))


def spread_rows(folded):
    return jnp.concatenate([folded, swap_halves(folded)], axis=0)


def exact_cdf(values):
    return 0.5 * (1.0 + lax.erf(values * (1.0 / math.sqrt(2.0))))


def normalise(values):
    centered = values - jnp.mean(values, axis=-1, keepdims=True)
    rstd = lax.rsqrt(jnp.mean(centered * centered, axis=-1, keepdims=True) + norm_eps)
    return centered * rstd, rstd


def normalise_back(grad, unit, rstd, gain):
    scaled = grad * gain
    mean_one = jnp.mean(scaled, axis=-1, keepdims=True)
    mean_two = jnp.mean(scaled * unit, axis=-1, keepdims=True)
    return rstd * (scaled - mean_one - unit * mean_two)


def layer_kernel(
    tokens_ref,
    seg_ref,
    gain_one_ref,
    bias_one_ref,
    w_qkv_ref,
    b_val_ref,
    w_out_hbm,
    b_out_ref,
    gain_two_ref,
    bias_two_ref,
    w_up_hbm,
    b_up_ref,
    w_down_hbm,
    b_down_ref,
    cot_ref,
    output_ref,
    tokens_grad_ref,
    vec_mid_ref,
    vec_in_ref,
    w_down_out,
    w_up_out,
    w_out_out,
    w_qkv_out,
    *scratch,
):
    (
        w_out_ref, w_up_ref, w_down_ref, load_sem, store_sem,
        send_qkv, recv_qkv, first, vals, query_t, first_t, wide_q, wide_first,
        probs, gates, logit, carry, row_top, row_acc, mixed_keep,
        send_mix, recv_mix, send_gmix, recv_gmix, grad_rows, grad_rows_t,
        dq_acc, dq0_acc, dkv_acc, dk0_acc, back_carry,
        send_back, recv_back, send_first, recv_first,
        lower, upper,
        normed_one_ref, unit_one_ref, rstd_one_ref,
        mixed_ref, unit_two_ref, rstd_two_ref, normed_two_ref, middle_ref, out_acc, gn_acc, joined_ref,
        mid_mine, mid_final, mid_core, mid_two, mid_three, mid_four,
        in_mine, in_final, in_core, in_two, in_three, in_four,
        vec_mid_mine, vec_mid_seq, vec_mid_sum, vec_mid_dp,
        vec_in_mine, vec_in_seq, vec_in_sum, vec_in_dp,
        qkv_s, qkv_r, first_s, first_r, mix_s, mix_r, gmix_s, gmix_r,
        back_s, back_r, fback_s, fback_r,
        mid_s, mid_r, in_s, in_r, mid_cs, mid_cr, vec_s, vec_r,
    ) = scratch
    dp_count, count = lax.axis_size("dp"), lax.axis_size("seq")
    dp, me = lax.axis_index("dp"), lax.axis_index("seq")
    rows, width = tokens_ref.shape[1], tokens_ref.shape[2]
    half = rows // 2
    length = rows * count
    coeff = select_weight / length
    hidden_width = w_up_hbm.shape[1]
    pairs = width // (2 * HD)

    barrier = pltpu.get_barrier_semaphore()

    def greet_seq(step, carried):
        pl.semaphore_signal(
            barrier, inc=1, device_id=(dp, lax.rem(me + step, count)), device_id_type=MESH
        )
        return carried

    def greet_dp(step, carried):
        pl.semaphore_signal(
            barrier, inc=1, device_id=(lax.rem(dp + step, dp_count), me), device_id_type=MESH
        )
        return carried

    lax.fori_loop(1, count, greet_seq, 0)
    lax.fori_loop(1, dp_count, greet_dp, 0)
    loads = [
        pltpu.make_async_copy(w_out_hbm, w_out_ref, load_sem.at[0]),
        pltpu.make_async_copy(w_up_hbm, w_up_ref, load_sem.at[1]),
        pltpu.make_async_copy(w_down_hbm, w_down_ref, load_sem.at[2]),
    ]
    for load in loads:
        load.start()

    def exchange(src, dst, send_sem, recv_sem, target):
        return pltpu.make_async_remote_copy(
            src_ref=src, dst_ref=dst, send_sem=send_sem, recv_sem=recv_sem,
            device_id=(dp, target), device_id_type=MESH,
        )

    tokens = tokens_ref[0].astype(jnp.float32)
    unit, rstd = normalise(tokens)
    unit_one_ref[...] = unit
    rstd_one_ref[...] = rstd
    normed_one_ref[...] = (unit * gain_one_ref[...] + bias_one_ref[...]).astype(low)
    score_scale = 1.0 / math.sqrt(HD)

    def project(pair, carried):
        at = pl.multiple_of(pair * 2 * HD, 2 * HD)
        normed = normed_one_ref[...]
        query = dot_nn(normed, w_qkv_ref[:, pl.ds(at, 2 * HD)]).astype(low).astype(jnp.float32) * score_scale
        key = dot_nn(normed, w_qkv_ref[:, pl.ds(width + at, 2 * HD)]).astype(low).astype(jnp.float32)
        value = dot_nn(normed, w_qkv_ref[:, pl.ds(2 * width + at, 2 * HD)]) + b_val_ref[:, pl.ds(at, 2 * HD)]
        value = value.astype(low).astype(jnp.float32)
        even, odd = 2 * pair, 2 * pair + 1
        send_qkv[even, :rows] = join_heads(key, swap_halves(query)).astype(low)
        send_qkv[odd, :rows] = join_heads(swap_halves(key), query).astype(low)
        top, bottom = value[:half], value[half:]
        send_qkv[even, rows:] = join_heads(top, swap_halves(bottom)).astype(low)
        send_qkv[odd, rows:] = join_heads(swap_halves(top), bottom).astype(low)
        return carried

    lax.fori_loop(0, pairs, project, 0)
    pl.semaphore_wait(barrier, count + dp_count - 2)

    def send_projected(step, carried):
        to = lax.rem(me + step, count)
        exchange(send_qkv.at[to], recv_qkv.at[me], qkv_s.at[to], qkv_r.at[me], to).start()
        exchange(send_qkv.at[0, pl.ds(0, rows)], first.at[me], first_s.at[to], first_r.at[me], to).start()
        return carried

    lax.fori_loop(1, count, send_projected, 0)
    recv_qkv[me] = send_qkv[me]
    first[me] = send_qkv[0, :rows]

    ids = seg_ref[...]
    start_one = jnp.sum(jnp.where(ids < 1, 1.0, 0.0), axis=1, keepdims=True)
    start_two = jnp.sum(jnp.where(ids < 2, 1.0, 0.0), axis=1, keepdims=True)
    square = (rows, rows)
    row_at = lax.broadcasted_iota(jnp.int32, square, 0)
    col_at = lax.broadcasted_iota(jnp.int32, square, 1)
    lower[...] = jnp.where(row_at > col_at, -coeff, 0.0).astype(low)
    upper[...] = jnp.where(row_at < col_at, -coeff, 0.0).astype(low)

    def masks(i, j):
        query_pos = lax.broadcasted_iota(jnp.int32, (rows, 1), 0).astype(jnp.float32) + (i * rows).astype(jnp.float32)
        key_pos = lax.broadcasted_iota(jnp.int32, square, 1).astype(jnp.float32) + (j * rows).astype(jnp.float32)
        begin = jnp.where(
            query_pos >= start_two, start_two, jnp.where(query_pos >= start_one, start_one, 0.0)
        )
        inside = key_pos >= begin
        return inside & (key_pos <= query_pos), inside & (key_pos < query_pos)

    def needs_mask(i, j):
        return (j == 0) | (j == i) | (i == count - 1)

    def pair_at(i, j):
        return i * (i + 1) // 2 + j

    carry[...] = jnp.zeros_like(carry)

    def forward_tile(i, j, masked):
        start_scores = dot_nt(wide_first[...], first[j])
        soft = jnp.maximum(start_scores, 0.0) + jnp.log(1.0 + jnp.exp(-jnp.abs(start_scores)))
        gate = jnp.exp(start_scores - soft)
        if masked:
            attend, select = masks(i, j)
            soft = jnp.where(select, soft, 0.0)
            gate = jnp.where(select, gate, 0.0)
        gates[pair_at(i, j)] = gate.astype(low)
        soft_low = soft.astype(low)
        forgot = dot_nn(lower[...], soft_low) + carry[j]
        carry[j] = forgot[rows - 1 :] - coeff * soft_low[rows - 1 :].astype(jnp.float32)
        scores = dot_nt(wide_q[...], recv_qkv[j, :rows]) + forgot
        if masked:
            scores = jnp.where(attend, scores, neg_large)
        logit[j] = scores
        top = row_top[...]
        for at in range(0, rows, 2 * HD):
            top = jnp.maximum(top, scores[:, at : at + 2 * HD])
        row_top[...] = top

    def forward_row(i, carried):
        @pl.when(i != me)
        def _():
            exchange(send_qkv.at[i], recv_qkv.at[i], qkv_s.at[i], qkv_r.at[i], i).wait_recv()
            exchange(send_qkv.at[0, pl.ds(0, rows)], first.at[i], first_s.at[i], first_r.at[i], i).wait_recv()

        lane = lax.broadcasted_iota(jnp.int32, (rows, 2 * HD), 1)
        query = swap_halves(recv_qkv[i, :rows].astype(jnp.float32))
        wide_q[...] = jnp.where(lane < HD, query, 0.0).astype(low)
        query_t[i] = query.T[:HD].astype(low)
        query = swap_halves(first[i].astype(jnp.float32))
        wide_first[...] = jnp.where(lane < HD, query, 0.0).astype(low)
        first_t[i] = query.T[:HD].astype(low)
        value = spread_rows(recv_qkv[i, rows:].astype(jnp.float32))
        vals[i] = jnp.where(lane < HD, value, jnp.where(lane < HD + 2, 1.0, 0.0)).astype(low)
        row_top[...] = jnp.full_like(row_top, neg_large)

        def tiles(j, inner):
            pl.when(needs_mask(i, j))(functools.partial(forward_tile, i, j, True))
            pl.when(jnp.logical_not(needs_mask(i, j)))(functools.partial(forward_tile, i, j, False))
            return inner

        lax.fori_loop(0, i + 1, tiles, 0)
        top = jnp.max(row_top[...], axis=1, keepdims=True)
        row_acc[...] = jnp.zeros_like(row_acc)

        def weigh(j, inner):
            prob = jnp.exp(logit[j] - top).astype(low)
            probs[pair_at(i, j)] = prob
            row_acc[...] += dot_nn(prob, vals[j])
            return inner

        lax.fori_loop(0, i + 1, weigh, 0)
        mixed = row_acc[...]
        inverse = 1.0 / mixed[:, HD : HD + 1]
        mixed = mixed * inverse
        mixed_keep[i] = jnp.where(lane < HD, mixed, inverse)
        send_mix[i] = fold_rows(mixed).astype(low)

        @pl.when(i != me)
        def _():
            exchange(send_mix.at[i], recv_mix.at[me], mix_s.at[i], mix_r.at[me], i).start()

        return carried

    lax.fori_loop(0, count, forward_row, 0)
    recv_mix[me] = send_mix[me]

    for load in loads:
        load.wait()

    def wait_mixed(step, carried):
        source = lax.rem(me + step, count)
        exchange(send_mix.at[source], recv_mix.at[source], mix_s.at[source], mix_r.at[source], source).wait_recv()
        return carried

    lax.fori_loop(1, count, wait_mixed, 0)
    for pair in range(pairs):
        even = recv_mix[2 * pair].astype(jnp.float32)
        odd = recv_mix[2 * pair + 1].astype(jnp.float32)
        columns = pl.ds(pair * 2 * HD, 2 * HD)
        mixed_ref[pl.ds(0, half), columns] = join_heads(even, swap_halves(odd)).astype(low)
        mixed_ref[pl.ds(half, half), columns] = join_heads(swap_halves(even), odd).astype(low)
    middle = tokens_ref[0].astype(jnp.float32) + dot_nn(mixed_ref[...], w_out_ref[...]) + b_out_ref[...]
    middle_ref[...] = middle
    unit, rstd = normalise(middle)
    unit_two_ref[...] = unit
    rstd_two_ref[...] = rstd
    normed_two_ref[...] = (unit * gain_two_ref[...] + bias_two_ref[...]).astype(low)
    out_acc[...] = jnp.zeros_like(out_acc)
    gn_acc[...] = jnp.zeros_like(gn_acc)
    core, x = lax.rem(dp, 2), dp // 2
    y, z = lax.rem(me, 2), me // 2
    mid_rows = mid_mine.shape[0]
    core_dp = dp + 1 - 2 * core

    def core_copy(at, size, slot):
        return pltpu.make_async_remote_copy(
            src_ref=mid_mine.at[pl.ds(pl.multiple_of((1 - core) * (mid_rows // 2) + at, 16), size)],
            dst_ref=mid_core.at[pl.ds(pl.multiple_of(at, 16), size)],
            send_sem=mid_cs.at[slot], recv_sem=mid_cr.at[slot],
            device_id=(core_dp, me), device_id_type=MESH,
        )

    chunk = width

    def dense(c, carried):
        at = pl.multiple_of(c * chunk, chunk)
        cols = pl.ds(at, chunk)
        hidden = dot_nn(normed_two_ref[...], w_up_ref[:, cols]) + b_up_ref[:, cols]
        cdf = exact_cdf(hidden)
        slope = cdf + hidden * jnp.exp(-0.5 * hidden * hidden) * (1.0 / math.sqrt(2.0 * math.pi))
        active = (hidden * cdf).astype(low)
        out_acc[...] += dot_nn(active, w_down_ref[cols, :])
        grad_hidden = (dot_nt(cot_ref[0], w_down_ref[cols, :]) * slope).astype(low)
        mid_mine[cols, :] = dot_tn(active, cot_ref[0]).astype(low)
        mid_mine[pl.ds(pl.multiple_of(mid_rows // 2 + at, 16), chunk), :] = dot_tn(
            normed_two_ref[...], grad_hidden
        ).astype(low)
        vec_mid_mine[pl.ds(c, 1), :] = jnp.sum(grad_hidden.astype(jnp.float32), axis=0, keepdims=True)
        gn_acc[...] += dot_nt(grad_hidden, w_up_ref[:, cols])
        core_copy(at, chunk, c).start()
        return carried

    chunks = hidden_width // chunk
    lax.fori_loop(0, chunks, dense, 0)
    output_ref[0] = (middle_ref[...] + out_acc[...] + b_down_ref[...]).astype(low)
    cot = cot_ref[0].astype(jnp.float32)
    grad = gn_acc[...]
    unit = unit_two_ref[...]
    vec_mid_mine[pl.ds(chunks, 1), :] = jnp.sum(cot, axis=0, keepdims=True)
    vec_mid_mine[pl.ds(chunks + 1, 1), :] = jnp.sum(grad * unit, axis=0, keepdims=True)
    vec_mid_mine[pl.ds(chunks + 2, 1), :] = jnp.sum(grad, axis=0, keepdims=True)
    middle = cot + normalise_back(grad, unit, rstd_two_ref[...], gain_two_ref[...])
    middle_ref[...] = middle
    branch = middle.astype(low)
    vec_mid_mine[pl.ds(chunks + 3, 1), :] = jnp.sum(branch.astype(jnp.float32), axis=0, keepdims=True)
    for pair in range(pairs):
        back = dot_nt(branch, w_out_ref[pl.ds(pair * 2 * HD, 2 * HD), :]).astype(low).astype(jnp.float32)
        top, bottom = back[:half], back[half:]
        send_gmix[2 * pair] = join_heads(top, swap_halves(bottom)).astype(low)
        send_gmix[2 * pair + 1] = join_heads(swap_halves(top), bottom).astype(low)

    def send_grads(step, carried):
        to = lax.rem(me + step, count)
        exchange(send_gmix.at[to], recv_gmix.at[me], gmix_s.at[to], gmix_r.at[me], to).start()
        return carried

    lax.fori_loop(1, count, send_grads, 0)
    recv_gmix[me] = send_gmix[me]
    w_out_grad = dot_tn(mixed_ref[...], branch).astype(low)
    mid_mine[pl.ds(hidden_width, width // 2), :] = w_out_grad[: width // 2]
    mid_mine[pl.ds(mid_rows // 2 + hidden_width, width // 2), :] = w_out_grad[width // 2 :]
    core_copy(hidden_width, width // 2, chunks).start()

    def other(step_two):
        along_x = (1 - core) if step_two else core
        return (dp + along_x * (2 - 4 * x), me + (1 - along_x) * (1 - 2 * y))

    two_bit = (1 - core) * x + core * y
    three_bit = (1 - core) * y + core * x
    piece_rows = 48

    def add_rows(into, at, source, source_at, size):
        def step(k, carried):
            here = pl.ds(pl.multiple_of(at + k * piece_rows, 16), piece_rows)
            there = pl.ds(pl.multiple_of(source_at + k * piece_rows, 16), piece_rows)
            into[here, :] = (into[here, :].astype(jnp.float32) + source[there, :].astype(jnp.float32)).astype(low)
            return carried

        lax.fori_loop(0, size // piece_rows, step, 0)

    def reducer(mine, final, core_got, two_got, three_got, four_got, send_sem, recv_sem):
        total = mine.shape[0]
        one = core * (total // 2)
        keep_two, give_two = one + two_bit * (total // 4), one + (1 - two_bit) * (total // 4)
        keep_three = keep_two + three_bit * (total // 8)
        give_three = keep_two + (1 - three_bit) * (total // 8)
        shard = total // 32
        depth = count // 2

        def remote(src, dst, slot, target):
            return pltpu.make_async_remote_copy(
                src_ref=src, dst_ref=dst, send_sem=send_sem.at[slot], recv_sem=recv_sem.at[slot],
                device_id=target, device_id_type=MESH,
            )

        def piece(ref, at, size):
            return ref.at[pl.ds(pl.multiple_of(at, 16), size)]

        def scatter_core():
            at = (1 - core) * (total // 2)
            return remote(piece(mine, at, total // 2), core_got, 0, (core_dp, me))

        copy_two = remote(piece(mine, give_two, total // 4), two_got, 1, other(True))
        copy_three = remote(piece(mine, give_three, total // 8), three_got, 2, other(False))

        def deep(step):
            to_z = lax.rem(z + step, depth)
            at = keep_three + to_z * shard
            return pltpu.make_async_remote_copy(
                src_ref=piece(mine, at, shard), dst_ref=four_got.at[depth - 1 - step],
                send_sem=send_sem.at[2 + step], recv_sem=recv_sem.at[2 + step],
                device_id=(dp, to_z * 2 + y), device_id_type=MESH,
            )

        def begin_two():
            add_rows(mine, give_two, core_got, give_two - one, total // 4)
            copy_two.start()
            add_rows(mine, keep_two, core_got, keep_two - one, total // 4)

        def begin_three():
            copy_two.wait_recv()
            add_rows(mine, give_three, two_got, give_three - keep_two, total // 8)
            copy_three.start()
            add_rows(mine, keep_three, two_got, keep_three - keep_two, total // 8)

        def begin_deep():
            copy_three.wait_recv()
            add_rows(mine, keep_three, three_got, 0, total // 8)
            for step in range(1, depth):
                deep(step).start()

        own = keep_three + z * shard

        def gather_deep(step):
            to_z = lax.rem(z + step, depth)
            return pltpu.make_async_remote_copy(
                src_ref=piece(final, own, shard), dst_ref=piece(final, own, shard),
                send_sem=send_sem.at[5 + step], recv_sem=recv_sem.at[5 + step],
                device_id=(dp, to_z * 2 + y), device_id_type=MESH,
            )

        def begin_gather():
            for step in range(1, depth):
                deep(step).wait_recv()

            def step(k, carried):
                at = pl.ds(pl.multiple_of(k * 16, 16), 16)
                here = pl.ds(pl.multiple_of(own + k * 16, 16), 16)
                summed = mine[here, :].astype(jnp.float32)
                for slot in range(depth - 1):
                    summed = summed + four_got[slot, at, :].astype(jnp.float32)
                final[here, :] = summed.astype(low)
                return carried

            lax.fori_loop(0, shard // 16, step, 0)
            for step in range(1, depth):
                gather_deep(step).start()

        back_three = remote(piece(final, keep_three, total // 8), piece(final, keep_three, total // 8), 9, other(False))
        back_two = remote(piece(final, keep_two, total // 4), piece(final, keep_two, total // 4), 10, other(True))
        back_core = remote(piece(final, one, total // 2), piece(final, one, total // 2), 11, (core_dp, me))

        def gather_three():
            for step in range(1, depth):
                gather_deep(step).wait_recv()
            back_three.start()

        def gather_two():
            back_three.wait_recv()
            back_two.start()

        def gather_core():
            back_two.wait_recv()
            back_core.start()

        def finish():
            back_core.wait_recv()

        def drain(own_core):
            if own_core:
                scatter_core().wait_send()
            copy_two.wait_send()
            copy_three.wait_send()
            for step in range(1, depth):
                deep(step).wait_send()
                gather_deep(step).wait_send()
            back_three.wait_send()
            back_two.wait_send()
            back_core.wait_send()

        return (scatter_core, begin_two, begin_three, begin_deep, begin_gather, gather_three, gather_two, gather_core, finish, drain)

    def vector_sum(mine, seq_got, seq_sum, dp_got, base):
        def over_seq(to, slot):
            return pltpu.make_async_remote_copy(
                src_ref=mine, dst_ref=seq_got.at[slot],
                send_sem=vec_s.at[base, to], recv_sem=vec_r.at[base, slot],
                device_id=(dp, to), device_id_type=MESH,
            )

        def over_dp(to, slot):
            return pltpu.make_async_remote_copy(
                src_ref=seq_sum, dst_ref=dp_got.at[slot],
                send_sem=vec_s.at[base + 1, to], recv_sem=vec_r.at[base + 1, slot],
                device_id=(to, me), device_id_type=MESH,
            )

        def start_seq():
            def step(k, carried):
                over_seq(lax.rem(me + k, count), me).start()
                return carried

            lax.fori_loop(1, count, step, 0)
            seq_got[me] = mine[...]

        def start_dp():
            def step(k, carried):
                source = lax.rem(me + k, count)
                over_seq(source, source).wait_recv()
                return carried

            lax.fori_loop(1, count, step, 0)
            summed = seq_got[0]
            for k in range(1, count):
                summed = summed + seq_got[k]
            seq_sum[...] = summed

            def send(k, carried):
                over_dp(lax.rem(dp + k, dp_count), dp).start()
                return carried

            lax.fori_loop(1, dp_count, send, 0)
            dp_got[dp] = seq_sum[...]

        def finish():
            def step(k, carried):
                source = lax.rem(dp + k, dp_count)
                over_dp(source, source).wait_recv()
                return carried

            lax.fori_loop(1, dp_count, step, 0)
            summed = dp_got[0]
            for k in range(1, dp_count):
                summed = summed + dp_got[k]
            return summed

        def drain():
            def step(k, carried):
                over_seq(lax.rem(me + k, count), me).wait_send()
                return carried

            def send(k, carried):
                over_dp(lax.rem(dp + k, dp_count), dp).wait_send()
                return carried

            lax.fori_loop(1, count, step, 0)
            lax.fori_loop(1, dp_count, send, 0)

        return start_seq, start_dp, finish, drain

    mid_steps = reducer(mid_mine, mid_final, mid_core, mid_two, mid_three, mid_four, mid_s, mid_r)
    in_steps = reducer(in_mine, in_final, in_core, in_two, in_three, in_four, in_s, in_r)
    mid_vec = vector_sum(vec_mid_mine, vec_mid_seq, vec_mid_sum, vec_mid_dp, 0)
    in_vec = vector_sum(vec_in_mine, vec_in_seq, vec_in_sum, vec_in_dp, 2)
    mid_vec[0]()
    for slot in range(chunks):
        core_copy(slot * chunk, chunk, slot).wait_recv()
    core_copy(hidden_width, width // 2, chunks).wait_recv()
    mid_steps[1]()

    dkv_acc[...] = jnp.zeros_like(dkv_acc)
    dk0_acc[...] = jnp.zeros_like(dk0_acc)
    back_carry[...] = jnp.zeros_like(back_carry)

    def backward_tile(i, j):
        prob = probs[pair_at(i, j)]
        grad_logits = (prob.astype(jnp.float32) * dot_nt(grad_rows[...], vals[j])).astype(low)
        dkv_acc[j, :HD] += dot_nn(grad_rows_t[...], prob)
        dkv_acc[j, HD:] += dot_nn(query_t[i], grad_logits)
        dq_acc[...] += dot_nn(grad_logits, recv_qkv[j, :rows])
        later = dot_nn(upper[...], grad_logits) + back_carry[j]
        back_carry[j] = later[:1] - coeff * grad_logits[:1].astype(jnp.float32)
        gated = (later * gates[pair_at(i, j)].astype(jnp.float32)).astype(low)
        dq0_acc[...] += dot_nn(gated, first[j])
        dk0_acc[j, HD:] += dot_nn(first_t[i], gated)

    def backward_row(step, carried):
        i = count - 1 - step

        @pl.when(i != me)
        def _():
            exchange(send_gmix.at[i], recv_gmix.at[i], gmix_s.at[i], gmix_r.at[i], i).wait_recv()

        lane = lax.broadcasted_iota(jnp.int32, (rows, 2 * HD), 1)
        grad = jnp.where(lane < HD, spread_rows(recv_gmix[i].astype(jnp.float32)), 0.0)
        kept = mixed_keep[i]
        inverse = kept[:, HD : HD + 1]
        delta = -jnp.sum(grad * kept, axis=1, keepdims=True) * inverse
        grad = grad * inverse
        grad_rows_t[...] = grad.T[:HD].astype(low)
        delta_high = delta.astype(low).astype(jnp.float32)
        grad = jnp.where(lane == HD, delta_high, jnp.where(lane == HD + 1, delta - delta_high, grad))
        grad_rows[...] = grad.astype(low)
        dq_acc[...] = jnp.zeros_like(dq_acc)
        dq0_acc[...] = jnp.zeros_like(dq0_acc)

        def tiles(j, inner):
            backward_tile(i, j)
            return inner

        lax.fori_loop(0, i + 1, tiles, 0)
        flipped = dkv_acc[i].T
        send_back[i, :rows] = join_heads(dq_acc[...] * score_scale, flipped).astype(low)
        send_back[i, rows:] = fold_rows(flipped).astype(low)
        send_first[i] = join_heads(dq0_acc[...] * score_scale, dk0_acc[i].T).astype(low)

        @pl.when(i != me)
        def _():
            exchange(send_back.at[i], recv_back.at[me], back_s.at[i], back_r.at[me], i).start()
            exchange(send_first.at[i], recv_first.at[me], fback_s.at[i], fback_r.at[me], i).start()

        return carried

    lax.fori_loop(0, count, backward_row, 0)
    recv_back[me] = send_back[me]
    recv_first[me] = send_first[me]
    mid_steps[2]()
    mid_vec[1]()

    def wait_back(step, carried):
        source = lax.rem(me + step, count)
        exchange(send_back.at[source], recv_back.at[source], back_s.at[source], back_r.at[source], source).wait_recv()
        exchange(send_first.at[source], recv_first.at[source], fback_s.at[source], fback_r.at[source], source).wait_recv()
        return carried

    lax.fori_loop(1, count, wait_back, 0)
    first_sum = recv_first[0].astype(jnp.float32)
    for source in range(1, count):
        first_sum = first_sum + recv_first[source].astype(jnp.float32)
    for pair in range(pairs):
        even = recv_back[2 * pair, :rows].astype(jnp.float32)
        odd = recv_back[2 * pair + 1, :rows].astype(jnp.float32)
        if pair == 0:
            even = even + first_sum
        columns = 2 * HD * pair
        joined_ref[:, pl.ds(columns, 2 * HD)] = join_heads(even, swap_halves(odd)).astype(low)
        joined_ref[:, pl.ds(width + columns, 2 * HD)] = join_heads(swap_halves(even), odd).astype(low)
        even = recv_back[2 * pair, rows:].astype(jnp.float32)
        odd = recv_back[2 * pair + 1, rows:].astype(jnp.float32)
        columns = pl.ds(2 * width + columns, 2 * HD)
        joined_ref[pl.ds(0, half), columns] = join_heads(even, swap_halves(odd)).astype(low)
        joined_ref[pl.ds(half, half), columns] = join_heads(swap_halves(even), odd).astype(low)

    def project_back(c, carried):
        cols = pl.ds(pl.multiple_of(c * width, width), width)
        in_mine[cols, :] = dot_tn(normed_one_ref[...], joined_ref[:, cols]).astype(low)
        return carried

    lax.fori_loop(0, 3, project_back, 0)
    in_steps[0]().start()
    grad = dot_nt(joined_ref[...], w_qkv_ref[...])
    unit = unit_one_ref[...]
    vec_in_mine[...] = jnp.zeros_like(vec_in_mine)
    vec_in_mine[pl.ds(0, 1), :] = jnp.sum(grad * unit, axis=0, keepdims=True)
    vec_in_mine[pl.ds(1, 1), :] = jnp.sum(grad, axis=0, keepdims=True)
    vec_in_mine[pl.ds(2, 1), :] = jnp.sum(joined_ref[:, pl.ds(2 * width, width)].astype(jnp.float32), axis=0, keepdims=True)
    in_vec[0]()
    tokens_grad_ref[0] = middle_ref[...] + normalise_back(grad, unit, rstd_one_ref[...], gain_one_ref[...])
    in_steps[0]().wait_recv()
    in_steps[1]()
    mid_steps[3]()
    in_steps[2]()
    in_vec[1]()
    vec_mid_ref[...] = mid_vec[2]()
    mid_steps[4]()
    in_steps[3]()
    mid_steps[5]()
    in_steps[4]()
    mid_steps[6]()
    in_steps[5]()
    mid_steps[7]()
    in_steps[6]()
    mid_steps[8]()
    stores = [
        pltpu.make_async_copy(mid_final.at[pl.ds(0, hidden_width)], w_down_out, store_sem.at[0]),
        pltpu.make_async_copy(mid_final.at[pl.ds(hidden_width, width // 2)], w_out_out.at[pl.ds(0, width // 2)], store_sem.at[1]),
        pltpu.make_async_copy(mid_final.at[pl.ds(mid_rows // 2 + hidden_width, width // 2)], w_out_out.at[pl.ds(width // 2, width // 2)], store_sem.at[2]),
    ]
    for c in range(chunks):
        stores.append(
            pltpu.make_async_copy(
                mid_final.at[pl.ds(mid_rows // 2 + c * chunk, chunk)],
                w_up_out.at[:, pl.ds(c * chunk, chunk)], store_sem.at[3 + c],
            )
        )
    for store in stores:
        store.start()
    in_steps[7]()
    vec_in_ref[...] = in_vec[2]()
    in_steps[8]()
    for c in range(3):
        store = pltpu.make_async_copy(
            in_final.at[pl.ds(c * width, width)], w_qkv_out.at[:, pl.ds(c * width, width)],
            store_sem.at[3 + chunks + c],
        )
        store.start()
        stores.append(store)

    def drain(step, carried):
        to = lax.rem(me + step, count)
        exchange(send_qkv.at[to], recv_qkv.at[me], qkv_s.at[to], qkv_r.at[me], to).wait_send()
        exchange(send_qkv.at[0, pl.ds(0, rows)], first.at[me], first_s.at[to], first_r.at[me], to).wait_send()
        exchange(send_mix.at[to], recv_mix.at[me], mix_s.at[to], mix_r.at[me], to).wait_send()
        exchange(send_gmix.at[to], recv_gmix.at[me], gmix_s.at[to], gmix_r.at[me], to).wait_send()
        exchange(send_back.at[to], recv_back.at[me], back_s.at[to], back_r.at[me], to).wait_send()
        exchange(send_first.at[to], recv_first.at[me], fback_s.at[to], fback_r.at[me], to).wait_send()
        return carried

    lax.fori_loop(1, count, drain, 0)
    for slot in range(chunks):
        core_copy(slot * chunk, chunk, slot).wait_send()
    core_copy(hidden_width, width // 2, chunks).wait_send()
    mid_steps[9](False)
    in_steps[9](True)
    mid_vec[3]()
    in_vec[3]()
    for store in stores:
        store.wait()


def exchange_heads(
    tokens, segment_ids, gain_one, bias_one, w_qkv, b_val, w_out, b_out,
    gain_two, bias_two, w_up, b_up, w_down, b_down, cotangent,
):
    count, dp_count = lax.axis_size("seq"), lax.axis_size("dp")
    rows, width = tokens.shape[1], tokens.shape[2]
    hidden = w_up.shape[1]
    half = rows // 2
    tiles = count * (count + 1) // 2
    wide = 2 * HD
    f32 = jnp.float32
    packed = rows + half
    mid, inner = 2 * hidden + width, 3 * width
    depth = count // 2

    def vmem(*shape, dtype=low):
        return pltpu.VMEM(shape, dtype)

    def sems(*shape):
        return pltpu.SemaphoreType.DMA(shape)

    scratch = [
        vmem(width, width), vmem(width, hidden), vmem(hidden, width), sems(3), sems(16),
        vmem(count, packed, wide), vmem(count, packed, wide), vmem(count, rows, wide), vmem(count, rows, wide),
        vmem(count, HD, rows), vmem(count, HD, rows), vmem(rows, wide), vmem(rows, wide),
        vmem(tiles, rows, rows), vmem(tiles, rows, rows), vmem(count, rows, rows, dtype=f32),
        vmem(count, 1, rows, dtype=f32), vmem(rows, wide, dtype=f32), vmem(rows, wide, dtype=f32), vmem(count, rows, wide, dtype=f32),
        vmem(count, half, wide), vmem(count, half, wide), vmem(count, half, wide), vmem(count, half, wide), vmem(rows, wide), vmem(HD, rows),
        vmem(rows, wide, dtype=f32), vmem(rows, wide, dtype=f32), vmem(count, wide, rows, dtype=f32), vmem(count, wide, rows, dtype=f32), vmem(count, 1, rows, dtype=f32),
        vmem(count, packed, wide), vmem(count, packed, wide), vmem(count, rows, wide), vmem(count, rows, wide),
        vmem(rows, rows), vmem(rows, rows),
        vmem(rows, width), vmem(rows, width, dtype=f32), vmem(rows, 1, dtype=f32),
        vmem(rows, width), vmem(rows, width, dtype=f32), vmem(rows, 1, dtype=f32), vmem(rows, width), vmem(rows, width, dtype=f32), vmem(rows, width, dtype=f32), vmem(rows, width, dtype=f32), vmem(rows, 3 * width),
    ]
    for total in (mid, inner):
        scratch += [vmem(total, width), vmem(total, width), vmem(total // 2, width), vmem(total // 4, width), vmem(total // 8, width), vmem(depth - 1, total // 32, width)]
    for _ in range(2):
        scratch += [vmem(8, width, dtype=f32), vmem(count, 8, width, dtype=f32), vmem(8, width, dtype=f32), vmem(dp_count, 8, width, dtype=f32)]
    scratch += [sems(count)] * 12
    scratch += [sems(12)] * 4 + [sems(5), sems(5), sems(4, count), sems(4, count)]
    in_vmem = pl.BlockSpec(memory_space=pltpu.VMEM)
    anywhere = pl.BlockSpec(memory_space=pl.ANY)
    specs = [in_vmem] * 15
    for at in (6, 10, 12):
        specs[at] = anywhere
    shape = jax.ShapeDtypeStruct
    results = pl.pallas_call(
        layer_kernel,
        out_shape=[
            shape((1, rows, width), low), shape((1, rows, width), f32), shape((8, width), f32), shape((8, width), f32),
            shape((hidden, width), low), shape((width, hidden), low), shape((width, width), low), shape((width, 3 * width), low),
        ],
        in_specs=specs,
        out_specs=[in_vmem] * 4 + [anywhere] * 4,
        scratch_shapes=scratch,
        compiler_params=pltpu.CompilerParams(
            collective_id=0, has_side_effects=True, vmem_limit_bytes=vmem_bytes
        ),
    )(
        tokens, segment_ids, gain_one[None], bias_one[None], w_qkv, b_val[None], w_out, b_out[None],
        gain_two[None], bias_two[None], w_up, b_up[None], w_down, b_down[None], cotangent,
    )
    output, tokens_grad, vec_mid, vec_in, w_down_grad, w_up_grad, w_out_grad, w_qkv_grad = results
    chunks = hidden // width
    return (
        output,
        tokens_grad,
        vec_in[0],
        vec_in[1],
        w_qkv_grad.astype(f32),
        vec_in[2],
        w_out_grad.astype(f32),
        vec_mid[chunks + 3],
        vec_mid[chunks + 1],
        vec_mid[chunks + 2],
        w_up_grad.astype(f32),
        vec_mid[:chunks].reshape(hidden),
        w_down_grad.astype(f32),
        vec_mid[chunks],
    )


def picks_heads(mesh, length, width, hidden):
    dp_count, count = mesh.shape["dp"], mesh.shape["seq"]
    power = length & (length - 1) == 0
    return dp_count == 4 and count == 8 and width == count * HD and hidden == 4 * width and power


def solution(mesh):
    placed = (
        P("dp", "seq", None),
        P("dp", None),
        P(),
        P(),
        P(),
        P(),
        P(),
        P(),
        P(),
        P(),
        P(),
        P(),
        P(),
        P(),
        P("dp", "seq", None),
    )

    def layer(tokens, *others):
        width, hidden = tokens.shape[-1], others[9].shape[-1]
        length = tokens.shape[1] * mesh.shape["seq"]
        body = exchange_heads if picks_heads(mesh, length, width, hidden) else local
        return body(tokens, *others)

    return jax.shard_map(
        layer,
        mesh=mesh,
        in_specs=placed,
        out_specs=(
            P("dp", "seq", None),
            P("dp", "seq", None),
            P(),
            P(),
            P(),
            P(),
            P(),
            P(),
            P(),
            P(),
            P(),
            P(),
            P(),
            P(),
        ),
        check_vma=False,
    )
```

```python
import functools
import math

import jax
import jax.numpy as jnp
from jax import lax
from jax.experimental import pallas as pl
from jax.experimental.pallas import tpu as pltpu
from jax.sharding import PartitionSpec as P

HD = 64


norm_eps = 1e-05
select_weight = 4.0
neg_large = -1e30
highest = lax.Precision.HIGHEST
vmem_bytes = 63 * 1024 * 1024


def prefix(array, axis, combine, identity, reverse):
    length, here = (lax.axis_size(axis), lax.axis_index(axis))
    everything = lax.all_gather(array.astype(jnp.bfloat16), axis)
    start = jnp.broadcast_to(jnp.asarray(identity, array.dtype), array.shape)

    def hop(k, before):
        at = length - 1 - k if reverse else k
        reached = at > here if reverse else at < here
        new = combine(before, everything[at].astype(array.dtype))
        return jnp.where(reached, new, before)

    return lax.fori_loop(0, length, hop, start)


def layer_norm(values, norm_gain, norm_shift):
    centered = values - jnp.mean(values, axis=-1, keepdims=True)
    variance = jnp.mean(centered * centered, axis=-1, keepdims=True)
    return centered * lax.rsqrt(variance + norm_eps) * norm_gain + norm_shift


def exact_gelu(values):
    return jax.nn.gelu(values, approximate=False)


def add_arrays(earlier, later):
    return earlier + later


def keep_state(state_in):
    return state_in


def pick_block():
    return 512


def local(
    tokens,
    segment_ids,
    gain_one,
    bias_one,
    w_qkv,
    b_val,
    w_out,
    b_out,
    gain_two,
    bias_two,
    w_up,
    b_up,
    w_down,
    b_down,
    cotangent,
):
    seq_count = lax.axis_size("seq")
    seq_rank = lax.axis_index("seq")
    row_tokens = tokens[0].astype(jnp.float32)
    tok_rows = row_tokens.shape[0]
    model_width = row_tokens.shape[1]
    head_count = model_width // HD
    length = tok_rows * seq_count
    score_scale = 1.0 / math.sqrt(HD)
    select_coeff = select_weight / length
    row_segments = segment_ids[0]
    row_base = seq_rank * tok_rows
    query_pos = row_base + jnp.arange(tok_rows, dtype=jnp.int32)
    query_segs = lax.dynamic_slice_in_dim(row_segments, row_base, tok_rows)
    last_query = row_base + tok_rows - 1
    lower_mask = (jnp.arange(tok_rows)[:, None] > jnp.arange(tok_rows)[None, :]).astype(jnp.float32)
    upper_mask = lower_mask.T
    normed_one, norm_one_back = jax.vjp(layer_norm, row_tokens, gain_one, bias_one)
    normed_one_low = normed_one.astype(jnp.bfloat16)
    value_bias = jnp.concatenate([jnp.zeros((2 * model_width,), jnp.float32), b_val])
    joined_low = (
        jnp.dot(normed_one_low, w_qkv, preferred_element_type=jnp.float32) + value_bias
    ).astype(jnp.bfloat16)
    queries = joined_low[:, :model_width]
    keys_mine = joined_low[:, model_width : 2 * model_width]
    values_mine = joined_low[:, 2 * model_width :]
    query_heads = queries.reshape(tok_rows, head_count, HD)
    query_zero = queries[:, :HD]
    query_rest = query_heads[:, 1:]

    def pair_masks(key_start, key_rows):
        key_pos = key_start + jnp.arange(key_rows, dtype=jnp.int32)
        key_segs = lax.dynamic_slice_in_dim(row_segments, key_start, key_rows)
        same_doc = query_segs[:, None] == key_segs[None, :]
        attend_mask = same_doc & (key_pos[None, :] <= query_pos[:, None])
        select_mask = same_doc & (key_pos[None, :] < query_pos[:, None])
        return (attend_mask, select_mask)

    select_init = (
        jnp.zeros((tok_rows, length), jnp.float32),
        jnp.zeros((tok_rows, length), jnp.float32),
        jnp.zeros((length,), jnp.float32),
    )
    running = select_init
    key_piece = lax.all_gather(keys_mine[:, :HD], "seq", axis=0, tiled=True)
    piece_rows = key_piece.shape[0]
    block_rows = pick_block()

    def select_block(state_now, offset):
        zero_scores, local_forgot, column_sums = state_now
        key_block = lax.dynamic_slice_in_dim(key_piece, offset, block_rows)
        attend_mask, select_mask = pair_masks(offset, block_rows)
        scores = (
            jnp.einsum("qd,kd->qk", query_zero, key_block, preferred_element_type=jnp.float32)
            * score_scale
        )
        chosen = jnp.where(select_mask, jax.nn.softplus(scores), 0.0)
        forgot = jnp.dot(lower_mask, chosen, precision=highest)
        zero_scores = lax.dynamic_update_slice_in_dim(zero_scores, scores, offset, 1)
        local_forgot = lax.dynamic_update_slice_in_dim(local_forgot, forgot, offset, 1)
        column_sums = lax.dynamic_update_slice_in_dim(
            column_sums, jnp.sum(chosen, axis=0), offset, 0
        )
        return ((zero_scores, local_forgot, column_sums), None)

    offsets = jnp.arange(piece_rows // block_rows, dtype=jnp.int32) * block_rows
    running, unused = lax.scan(select_block, running, offsets)
    zero_scores, local_forgot, column_sums = running
    column_prefix = prefix(column_sums, "seq", add_arrays, jnp.zeros((length,), jnp.float32), False)
    attend_init = (
        jnp.full((head_count, tok_rows), neg_large, jnp.float32),
        jnp.zeros((head_count, tok_rows), jnp.float32),
        jnp.zeros((tok_rows, head_count, HD), jnp.float32),
    )
    running = attend_init
    attend_key_piece = lax.all_gather(keys_mine, "seq", axis=0, tiled=True)
    value_piece = lax.all_gather(values_mine, "seq", axis=0, tiled=True)
    piece_rows = attend_key_piece.shape[0]
    attend_block_rows = pick_block()

    def attend_block(state_now, offset):
        key_start = offset

        def attend_compute(state_in):
            run_max, run_total, accumulated = state_in
            key_block = lax.dynamic_slice_in_dim(
                attend_key_piece, offset, attend_block_rows
            ).reshape(attend_block_rows, head_count, HD)
            value_block = lax.dynamic_slice_in_dim(value_piece, offset, attend_block_rows).reshape(
                attend_block_rows, head_count, HD
            )
            attend_mask, select_mask = pair_masks(key_start, attend_block_rows)
            rest_scores = (
                jnp.einsum(
                    "qhd,khd->hqk", query_rest, key_block[:, 1:], preferred_element_type=jnp.float32
                )
                * score_scale
            )
            head_zero = lax.dynamic_slice_in_dim(zero_scores, key_start, attend_block_rows, 1)
            scores = jnp.concatenate([head_zero[None], rest_scores], axis=0)
            forgot = lax.dynamic_slice_in_dim(column_prefix, key_start, attend_block_rows)[
                None, :
            ] + lax.dynamic_slice_in_dim(local_forgot, key_start, attend_block_rows, 1)
            logits = jnp.where(attend_mask[None], scores - select_coeff * forgot[None], neg_large)
            new_max = jnp.maximum(run_max, jnp.max(logits, axis=-1))
            weights = jnp.where(attend_mask[None], jnp.exp(logits - new_max[:, :, None]), 0.0)
            decay_factor = jnp.exp(run_max - new_max)
            run_total = run_total * decay_factor + jnp.sum(weights, axis=-1)
            accumulated = accumulated * decay_factor.T[:, :, None] + jnp.einsum(
                "hqk,khd->qhd",
                weights.astype(jnp.bfloat16),
                value_block,
                preferred_element_type=jnp.float32,
            )
            return (new_max, run_total, accumulated)

        state_now = lax.cond(key_start <= last_query, attend_compute, keep_state, state_now)
        return (state_now, None)

    offsets = jnp.arange(piece_rows // attend_block_rows, dtype=jnp.int32) * attend_block_rows
    running, unused = lax.scan(attend_block, running, offsets)
    run_max, run_total, accumulated = running
    log_total = run_max + jnp.log(run_total)
    mixed_float = accumulated / run_total.T[:, :, None]
    mixed_low = mixed_float.reshape(tok_rows, model_width).astype(jnp.bfloat16)
    middle = row_tokens + jnp.dot(mixed_low, w_out, preferred_element_type=jnp.float32) + b_out
    normed_two, norm_two_back = jax.vjp(layer_norm, middle, gain_two, bias_two)
    normed_two_low = normed_two.astype(jnp.bfloat16)
    hidden = jnp.dot(normed_two_low, w_up, preferred_element_type=jnp.float32) + b_up
    active, gelu_back = jax.vjp(exact_gelu, hidden)
    active_low = active.astype(jnp.bfloat16)
    output = middle + jnp.dot(active_low, w_down, preferred_element_type=jnp.float32) + b_down
    grad_out = cotangent[0]
    grad_float = grad_out.astype(jnp.float32)
    w_down_grad = jnp.einsum("tf,td->fd", active_low, grad_out, preferred_element_type=jnp.float32)
    b_down_grad = jnp.sum(grad_float, axis=0)
    grad_active = jnp.einsum("td,fd->tf", grad_out, w_down, preferred_element_type=jnp.float32)
    (grad_hidden,) = gelu_back(grad_active)
    grad_hidden_low = grad_hidden.astype(jnp.bfloat16)
    w_up_grad = jnp.einsum(
        "td,tf->df", normed_two_low, grad_hidden_low, preferred_element_type=jnp.float32
    )
    b_up_grad = jnp.sum(grad_hidden_low.astype(jnp.float32), axis=0)
    grad_normed_two = jnp.einsum(
        "tf,df->td", grad_hidden_low, w_up, preferred_element_type=jnp.float32
    )
    grad_middle_norm, gain_two_grad, bias_two_grad = norm_two_back(grad_normed_two)
    grad_middle = grad_float + grad_middle_norm
    grad_branch_low = grad_middle.astype(jnp.bfloat16)
    w_out_grad = jnp.einsum(
        "td,te->de", mixed_low, grad_branch_low, preferred_element_type=jnp.float32
    )
    b_out_grad = jnp.sum(grad_branch_low.astype(jnp.float32), axis=0)
    grad_mixed_low = jnp.einsum(
        "te,de->td", grad_branch_low, w_out, preferred_element_type=jnp.float32
    ).astype(jnp.bfloat16)
    grad_mixed_heads = grad_mixed_low.reshape(tok_rows, head_count, HD)
    row_delta = jnp.sum(grad_mixed_heads.astype(jnp.float32) * mixed_float, axis=-1).T
    keys_back, values_back = (
        lax.all_gather(keys_mine, "seq", axis=0, tiled=True),
        lax.all_gather(values_mine, "seq", axis=0, tiled=True),
    )
    back_rows = pick_block()
    key_heads = keys_back.reshape(length, head_count, HD)
    value_heads = values_back.reshape(length, head_count, HD)

    def grad_block(state_now, offset):

        def grad_compute(state_in):
            query_grad, key_grad, value_grad, first_part, second_part, grad_cols = state_in
            key_block = lax.dynamic_slice_in_dim(key_heads, offset, back_rows)
            value_block = lax.dynamic_slice_in_dim(value_heads, offset, back_rows)
            attend_mask, select_mask = pair_masks(offset, back_rows)
            scores = (
                jnp.einsum(
                    "qhd,khd->hqk", query_heads, key_block, preferred_element_type=jnp.float32
                )
                * score_scale
            )
            chosen = jnp.where(select_mask, jax.nn.softplus(scores[0]), 0.0)
            forgot = lax.dynamic_slice_in_dim(column_prefix, offset, back_rows)[None, :] + jnp.dot(
                lower_mask, chosen, precision=highest
            )
            logits = scores - select_coeff * forgot[None]
            prob_block = jnp.where(attend_mask[None], jnp.exp(logits - log_total[:, :, None]), 0.0)
            grad_probs = jnp.einsum(
                "qhd,khd->hqk", grad_mixed_heads, value_block, preferred_element_type=jnp.float32
            )
            grad_logits = prob_block * (grad_probs - row_delta[:, :, None])
            value_part = jnp.einsum(
                "hqk,qhd->khd",
                prob_block.astype(jnp.bfloat16),
                grad_mixed_heads,
                preferred_element_type=jnp.float32,
            )
            rest_low = grad_logits[1:].astype(jnp.bfloat16)
            query_grad = (
                query_grad
                + jnp.einsum(
                    "hqk,khd->qhd", rest_low, key_block[:, 1:], preferred_element_type=jnp.float32
                )
                * score_scale
            )
            key_part = (
                jnp.einsum("hqk,qhd->khd", rest_low, query_rest, preferred_element_type=jnp.float32)
                * score_scale
            )
            total_grad = jnp.sum(grad_logits, axis=0)
            suffix_local = jnp.dot(upper_mask, total_grad, precision=highest)
            select_gate = jnp.where(select_mask, select_coeff * jax.nn.sigmoid(scores[0]), 0.0)
            first_part = lax.dynamic_update_slice_in_dim(
                first_part, grad_logits[0] - select_gate * suffix_local, offset, 1
            )
            second_part = lax.dynamic_update_slice_in_dim(second_part, select_gate, offset, 1)
            key_grad = lax.dynamic_update_slice_in_dim(key_grad, key_part, offset, 0)
            value_grad = lax.dynamic_update_slice_in_dim(value_grad, value_part, offset, 0)
            grad_cols = lax.dynamic_update_slice_in_dim(
                grad_cols, jnp.sum(total_grad, axis=0), offset, 0
            )
            return (query_grad, key_grad, value_grad, first_part, second_part, grad_cols)

        state_now = lax.cond(offset <= last_query, grad_compute, keep_state, state_now)
        return (state_now, None)

    grad_init = (
        jnp.zeros((tok_rows, head_count - 1, HD), jnp.float32),
        jnp.zeros((length, head_count - 1, HD), jnp.float32),
        jnp.zeros((length, head_count, HD), jnp.float32),
        jnp.zeros((tok_rows, length), jnp.float32),
        jnp.zeros((tok_rows, length), jnp.float32),
        jnp.zeros((length,), jnp.float32),
    )
    back_offsets = jnp.arange(length // back_rows, dtype=jnp.int32) * back_rows
    grad_state, unused = lax.scan(grad_block, grad_init, back_offsets)
    query_grad, key_grad, value_grad, first_part, second_part, grad_cols = grad_state
    grad_suffix = prefix(grad_cols, "seq", add_arrays, jnp.zeros((length,), jnp.float32), True)
    zero_grad_low = (first_part - second_part * grad_suffix[None, :]).astype(jnp.bfloat16)
    query_zero_grad = (
        jnp.dot(zero_grad_low, keys_back[:, :HD], preferred_element_type=jnp.float32) * score_scale
    )
    key_zero_grad = (
        jnp.einsum("ql,qd->ld", zero_grad_low, query_zero, preferred_element_type=jnp.float32)
        * score_scale
    )
    key_total = jnp.concatenate([key_zero_grad[:, None, :], key_grad], axis=1).reshape(
        length, model_width
    )
    value_total = value_grad.reshape(length, model_width)
    key_mine_grad, value_mine_grad = (
        lax.psum_scatter(
            key_total.astype(jnp.bfloat16), "seq", scatter_dimension=0, tiled=True
        ).astype(jnp.float32),
        lax.psum_scatter(
            value_total.astype(jnp.bfloat16), "seq", scatter_dimension=0, tiled=True
        ).astype(jnp.float32),
    )
    query_total = jnp.concatenate([query_zero_grad[:, None, :], query_grad], axis=1).reshape(
        tok_rows, model_width
    )
    grad_joined_low = jnp.concatenate([query_total, key_mine_grad, value_mine_grad], axis=1).astype(
        jnp.bfloat16
    )
    b_val_grad = jnp.sum(grad_joined_low[:, 2 * model_width :].astype(jnp.float32), axis=0)
    w_qkv_grad = jnp.einsum(
        "td,te->de", normed_one_low, grad_joined_low, preferred_element_type=jnp.float32
    )
    grad_normed_one = jnp.einsum(
        "te,de->td", grad_joined_low, w_qkv, preferred_element_type=jnp.float32
    )
    grad_tokens_norm, gain_one_grad, bias_one_grad = norm_one_back(grad_normed_one)
    tokens_grad = grad_middle + grad_tokens_norm
    summed = lax.psum(
        (
            gain_one_grad,
            bias_one_grad,
            w_qkv_grad,
            b_val_grad,
            w_out_grad,
            b_out_grad,
            gain_two_grad,
            bias_two_grad,
            w_up_grad,
            b_up_grad,
            w_down_grad,
            b_down_grad,
        ),
        ("dp", "seq"),
    )
    return (
        output.astype(jnp.bfloat16)[None],
        tokens_grad[None],
        summed[0],
        summed[1],
        summed[2],
        summed[3],
        summed[4],
        summed[5],
        summed[6],
        summed[7],
        summed[8],
        summed[9],
        summed[10],
        summed[11],
    )


low = jnp.bfloat16
MESH = pl.DeviceIdType.MESH


def dot_nn(left, right):
    return lax.dot_general(left, right, (((1,), (0,)), ((), ())), preferred_element_type=jnp.float32)


def dot_nt(left, right):
    return lax.dot_general(left, right, (((1,), (1,)), ((), ())), preferred_element_type=jnp.float32)


def dot_tn(left, right):
    return lax.dot_general(left, right, (((0,), (0,)), ((), ())), preferred_element_type=jnp.float32)


def swap_halves(wide):
    return pltpu.roll(wide, HD, 1)


def left_lanes(shape):
    return lax.broadcasted_iota(jnp.int32, shape, 1) < HD


def join_heads(left, right):
    return jnp.where(left_lanes(left.shape), left, right)


def fold_rows(wide):
    half = wide.shape[0] // 2
    return join_heads(wide[:half], swap_halves(wide[half:]))


def spread_rows(folded):
    return jnp.concatenate([folded, swap_halves(folded)], axis=0)


def exact_cdf(values):
    return 0.5 * (1.0 + lax.erf(values * (1.0 / math.sqrt(2.0))))


def normalise(values):
    centered = values - jnp.mean(values, axis=-1, keepdims=True)
    rstd = lax.rsqrt(jnp.mean(centered * centered, axis=-1, keepdims=True) + norm_eps)
    return centered * rstd, rstd


def normalise_back(grad, unit, rstd, gain):
    scaled = grad * gain
    mean_one = jnp.mean(scaled, axis=-1, keepdims=True)
    mean_two = jnp.mean(scaled * unit, axis=-1, keepdims=True)
    return rstd * (scaled - mean_one - unit * mean_two)


def rows_of(ref, at, size):
    return ref.at[pl.ds(pl.multiple_of(at, 16), size)]


def add_rows(into, at, source, source_at, size, piece=16):
    def step(k, carried):
        here = pl.ds(pl.multiple_of(at + k * piece, 16), piece)
        there = pl.ds(pl.multiple_of(source_at + k * piece, 16), piece)
        summed = into[here, :].astype(jnp.float32) + source[there, :].astype(jnp.float32)
        into[here, :] = summed.astype(low)
        return carried

    lax.fori_loop(0, size // piece, step, 0)


class Places:
    def __init__(self):
        self.dp_count, self.count = lax.axis_size("dp"), lax.axis_size("seq")
        self.dp, self.me = lax.axis_index("dp"), lax.axis_index("seq")
        self.core, self.x = lax.rem(self.dp, 2), self.dp // 2
        self.y, self.z = lax.rem(self.me, 2), self.me // 2
        self.depth = self.count // 2
        self.core_peer = (self.dp + 1 - 2 * self.core, self.me)
        self.x_peer = (self.dp + 2 - 4 * self.x, self.me)
        self.y_peer = (self.dp, self.me + 1 - 2 * self.y)
        along_x = 1 - self.core
        self.two_peer = (self.dp + along_x * (2 - 4 * self.x), self.me + (1 - along_x) * (1 - 2 * self.y))
        self.three_peer = (self.dp + (1 - along_x) * (2 - 4 * self.x), self.me + along_x * (1 - 2 * self.y))
        self.two_bit = along_x * self.x + (1 - along_x) * self.y
        self.three_bit = (1 - along_x) * self.x + along_x * self.y
        self.z_low, self.z_high = lax.rem(self.z, 2), self.z // 2
        self.z_near = (self.dp, self.me + 2 * (1 - 2 * self.z_low))
        self.z_far = (self.dp, self.me + 4 * (1 - 2 * self.z_high))


def remote(src, dst, send_sem, recv_sem, target):
    return pltpu.make_async_remote_copy(
        src_ref=src, dst_ref=dst, send_sem=send_sem, recv_sem=recv_sem, device_id=target, device_id_type=MESH
    )


class StagedSum:
    def __init__(self, at, mine, final, got, send_sem, recv_sem):
        self.mine, self.final, self.got = mine, final, got
        total = mine.shape[0]
        bits = (at.core, at.two_bit, at.three_bit, at.z_low, at.z_high)
        peers = (at.core_peer, at.two_peer, at.three_peer, at.z_near, at.z_far)
        start, size = 0, total
        self.down, self.up, self.keeps = [], [], []
        for stage, (bit, peer) in enumerate(zip(bits, peers)):
            size //= 2
            keep, give = start + bit * size, start + (1 - bit) * size
            self.keeps.append((start, keep, give, size))
            self.down.append(
                remote(rows_of(mine, give, size), got[stage], send_sem.at[stage], recv_sem.at[stage], peer)
            )
            self.up.append(
                remote(
                    rows_of(final, keep, size), rows_of(final, keep, size),
                    send_sem.at[5 + stage], recv_sem.at[5 + stage], peer,
                )
            )
            start = keep

    def send(self, stage):
        if stage > 0:
            self.down[stage - 1].wait_recv()
            begin, keep_before = self.keeps[stage - 1][1], self.keeps[stage]
            _, keep, give, size = keep_before
            add_rows(self.mine, give, self.got[stage - 1], give - begin, size)
            self.down[stage].start()
            add_rows(self.mine, keep, self.got[stage - 1], keep - begin, size)
        else:
            self.down[0].start()

    def turn(self):
        self.down[4].wait_recv()
        _, keep, _, size = self.keeps[4]

        def step(k, carried):
            there = pl.ds(pl.multiple_of(k * 16, 16), 16)
            here = pl.ds(pl.multiple_of(keep + k * 16, 16), 16)
            summed = self.mine[here, :].astype(jnp.float32) + self.got[4][there, :].astype(jnp.float32)
            self.final[here, :] = summed.astype(low)
            return carried

        lax.fori_loop(0, size // 16, step, 0)
        self.up[4].start()

    def gather(self, stage):
        self.up[stage + 1].wait_recv()
        self.up[stage].start()

    def finish(self):
        self.up[0].wait_recv()

    def drain(self, first=0):
        for copy in self.down[first:] + self.up:
            copy.wait_send()


class VectorSum:
    def __init__(self, at, mine, seq_got, seq_sum, dp_got, send_sem, recv_sem, base):
        self.at, self.mine, self.seq_got, self.seq_sum, self.dp_got = at, mine, seq_got, seq_sum, dp_got
        self.send_sem, self.recv_sem, self.base = send_sem, recv_sem, base

    def over_seq(self, to, slot):
        return remote(
            self.mine, self.seq_got.at[slot], self.send_sem.at[self.base, to], self.recv_sem.at[self.base, slot],
            (self.at.dp, to),
        )

    def over_dp(self, to, slot):
        return remote(
            self.seq_sum, self.dp_got.at[slot], self.send_sem.at[self.base + 1, to],
            self.recv_sem.at[self.base + 1, slot], (to, self.at.me),
        )

    def each(self, count, mine, act):
        def step(k, carried):
            act(lax.rem(mine + k, count))
            return carried

        lax.fori_loop(1, count, step, 0)

    def start_seq(self):
        at = self.at
        self.each(at.count, at.me, lambda to: self.over_seq(to, at.me).start())
        self.seq_got[at.me] = self.mine[...]

    def start_dp(self):
        at = self.at
        self.each(at.count, at.me, lambda source: self.over_seq(source, source).wait_recv())
        summed = self.seq_got[0]
        for k in range(1, at.count):
            summed = summed + self.seq_got[k]
        self.seq_sum[...] = summed
        self.each(at.dp_count, at.dp, lambda to: self.over_dp(to, at.dp).start())
        self.dp_got[at.dp] = summed

    def finish(self):
        at = self.at
        self.each(at.dp_count, at.dp, lambda source: self.over_dp(source, source).wait_recv())
        summed = self.dp_got[0]
        for k in range(1, at.dp_count):
            summed = summed + self.dp_got[k]
        return summed

    def drain(self):
        at = self.at
        self.each(at.count, at.me, lambda to: self.over_seq(to, at.me).wait_send())
        self.each(at.dp_count, at.dp, lambda to: self.over_dp(to, at.dp).wait_send())


def layer_kernel(
    tokens_ref,
    seg_ref,
    gain_one_ref,
    bias_one_ref,
    w_qkv_ref,
    b_val_ref,
    w_out_hbm,
    b_out_ref,
    gain_two_ref,
    bias_two_ref,
    w_up_hbm,
    b_up_ref,
    w_down_hbm,
    b_down_ref,
    cot_ref,
    output_ref,
    tokens_grad_ref,
    vec_mid_ref,
    vec_in_ref,
    w_down_out,
    w_up_out,
    w_out_out,
    w_qkv_out,
    first_out,
    *scratch,
):
    (
        w_out_ref, w_up_ref, w_down_ref, load_sem, store_sem,
        normed_all, w_head, w_value, b_value, key_query, first, vals, query_t, first_t, wide_q, wide_first,
        probs, gates, logit, carry, row_top, row_acc, mixed_keep,
        send_mix, recv_mix, send_gmix, recv_gmix, grad_rows, grad_rows_t,
        dq_acc, dq0_acc, dkv_acc, dk0_acc, back_carry,
        send_back, recv_back, send_first, y_first, recv_first,
        lower, upper,
        unit_one_ref, rstd_one_ref, unit_two_ref, rstd_two_ref,
        mixed_ref, normed_two_ref, middle_ref, out_acc, gn_acc, joined_ref,
        near_mine, near_final, near_core, near_two, near_three, near_four, near_five,
        rest_mine, rest_final, rest_core, rest_two, rest_three, rest_four, rest_five,
        wkv_acc, wqq_acc, wk0_acc, in_mine, in_core, in_x, in_final,
        extra_mine, extra_seq, extra_sum, extra_dp, extra_all,
        vec_mid_mine, vec_mid_seq, vec_mid_sum, vec_mid_dp,
        vec_in_mine, vec_in_seq, vec_in_sum, vec_in_dp,
        norm_y, norm_up, norm_down, norm_r, mix_s, mix_r, gmix_s, gmix_r,
        back_s, back_r, fback_y, fback_yr, fback_s, fback_r, extra_s, extra_r, gather_s, gather_r,
        near_s, near_r, rest_s, rest_r, in_s, in_r, part_s, part_r, vec_s, vec_r, edp_s, edp_r,
    ) = scratch
    at = Places()
    dp_count, count, dp, me = at.dp_count, at.count, at.dp, at.me
    y, z, depth = at.y, at.z, at.depth
    rows, width = tokens_ref.shape[1], tokens_ref.shape[2]
    half, wide = rows // 2, 2 * HD
    coeff = select_weight / (rows * count)
    hidden_width = w_up_hbm.shape[1]
    pairs = width // wide
    score_scale = 1.0 / math.sqrt(HD)

    barrier = pltpu.get_barrier_semaphore()

    def greet_seq(step, carried):
        to = lax.rem(me + step, count)
        pl.semaphore_signal(barrier, inc=1, device_id=(dp, to), device_id_type=MESH)
        return carried

    def greet_dp(step, carried):
        to = lax.rem(dp + step, dp_count)
        pl.semaphore_signal(barrier, inc=1, device_id=(to, me), device_id_type=MESH)
        return carried

    lax.fori_loop(1, count, greet_seq, 0)
    lax.fori_loop(1, dp_count, greet_dp, 0)
    loads = [
        pltpu.make_async_copy(w_out_hbm, w_out_ref, load_sem.at[0]),
        pltpu.make_async_copy(w_up_hbm, w_up_ref, load_sem.at[1]),
        pltpu.make_async_copy(w_down_hbm, w_down_ref, load_sem.at[2]),
    ]
    for load in loads:
        load.start()

    def exchange(src, dst, send_sem, recv_sem, target):
        return remote(src, dst, send_sem, recv_sem, (dp, target))

    tokens = tokens_ref[0].astype(jnp.float32)
    unit, rstd = normalise(tokens)
    unit_one_ref[...] = unit
    rstd_one_ref[...] = rstd
    normed_all[me] = (unit * gain_one_ref[...] + bias_one_ref[...]).astype(low)
    pl.semaphore_wait(barrier, count + dp_count - 2)

    def pass_y(block):
        return exchange(normed_all.at[block], normed_all.at[block], norm_y.at[block], norm_r.at[block], z * 2 + 1 - y)

    def pass_up(block):
        return exchange(normed_all.at[block], normed_all.at[block], norm_up.at[block], norm_r.at[block], me + 2)

    def pass_down(block):
        return exchange(normed_all.at[block], normed_all.at[block], norm_down.at[block], norm_r.at[block], me - 2)

    def arrived(block):
        exchange(normed_all.at[block], normed_all.at[block], norm_y.at[block], norm_r.at[block], block).wait_recv()

    def has_up(zz):
        return zz < depth - 1

    pl.when(has_up(z))(lambda: pass_up(me).start())
    pl.when(z > 0)(lambda: pass_down(me).start())
    pass_y(me).start()

    def relay(distance):
        def from_below():
            block = me - 2 * distance
            arrived(block)
            pl.when(has_up(z))(lambda: pass_up(block).start())
            pass_y(block).start()

        def from_above():
            block = me + 2 * distance
            arrived(block)
            pl.when(z > 0)(lambda: pass_down(block).start())
            pass_y(block).start()

        pl.when(z - distance >= 0)(from_below)
        pl.when(z + distance < depth)(from_above)

    odd_head = lax.rem(me, 2) == 1
    pair_at_lane = pl.multiple_of((me // 2) * wide, wide)

    def head_columns(part, right):
        columns = w_qkv_ref[:, pl.ds(part * width + pair_at_lane, wide)].astype(jnp.float32)
        swapped = swap_halves(columns)
        return jnp.where(odd_head, columns, swapped) if right else jnp.where(odd_head, swapped, columns)

    w_head[:, :wide] = join_heads(head_columns(1, False), head_columns(0, True) * score_scale).astype(low)
    zero_query = swap_halves(w_qkv_ref[:, :wide].astype(jnp.float32)) * score_scale
    w_head[:, wide:] = join_heads(w_qkv_ref[:, width : width + wide].astype(jnp.float32), zero_query).astype(low)
    w_value[...] = head_columns(2, False).astype(low)
    bias = b_val_ref[:, pl.ds(pair_at_lane, wide)]
    b_value[...] = jnp.where(odd_head, swap_halves(bias), bias)

    ids = seg_ref[...]
    start_one = jnp.sum(jnp.where(ids < 1, 1.0, 0.0), axis=1, keepdims=True)
    start_two = jnp.sum(jnp.where(ids < 2, 1.0, 0.0), axis=1, keepdims=True)
    square = (rows, rows)
    row_at = lax.broadcasted_iota(jnp.int32, square, 0)
    col_at = lax.broadcasted_iota(jnp.int32, square, 1)
    lower[...] = jnp.where(row_at > col_at, -coeff, 0.0).astype(low)
    upper[...] = jnp.where(row_at < col_at, -coeff, 0.0).astype(low)
    lane = lax.broadcasted_iota(jnp.int32, (rows, wide), 1)

    def masks(i, j):
        query_pos = lax.broadcasted_iota(jnp.int32, (rows, 1), 0).astype(jnp.float32) + (i * rows).astype(jnp.float32)
        key_pos = lax.broadcasted_iota(jnp.int32, square, 1).astype(jnp.float32) + (j * rows).astype(jnp.float32)
        begin = jnp.where(
            query_pos >= start_two, start_two, jnp.where(query_pos >= start_one, start_one, 0.0)
        )
        inside = key_pos >= begin
        return inside & (key_pos <= query_pos), inside & (key_pos < query_pos)

    def needs_mask(i, j):
        return (j == 0) | (j == i) | (i == count - 1)

    def pair_at(i, j):
        return i * (i + 1) // 2 + j

    carry[...] = jnp.zeros_like(carry)
    row_top[...] = jnp.full_like(row_top, neg_large)

    def project(block):
        normed = normed_all[block]
        both = dot_nn(normed, w_head[...]).astype(low)
        key_query[block] = both[:, :wide]
        query = swap_halves(both[:, :wide].astype(jnp.float32))
        wide_q[block] = jnp.where(lane < HD, query, 0.0).astype(low)
        query_t[block] = query.T[:HD].astype(low)
        first[block] = both[:, wide:]
        query = swap_halves(both[:, wide:].astype(jnp.float32))
        wide_first[block] = jnp.where(lane < HD, query, 0.0).astype(low)
        first_t[block] = query.T[:HD].astype(low)
        value = dot_nn(normed, w_value[...]) + b_value[...]
        vals[block] = jnp.where(lane < HD, value, jnp.where(lane < HD + 2, 1.0, 0.0)).astype(low)

    def forward_tile(i, j, masked):
        start_scores = dot_nt(wide_first[i], first[j])
        soft = jnp.maximum(start_scores, 0.0) + jnp.log(1.0 + jnp.exp(-jnp.abs(start_scores)))
        gate = jnp.exp(start_scores - soft)
        if masked:
            attend, select = masks(i, j)
            soft = jnp.where(select, soft, 0.0)
            gate = jnp.where(select, gate, 0.0)
        gates[pair_at(i, j)] = gate.astype(low)
        soft_low = soft.astype(low)
        forgot = dot_nn(lower[...], soft_low) + carry[j]
        carry[j] = forgot[rows - 1 :] - coeff * soft_low[rows - 1 :].astype(jnp.float32)
        scores = dot_nt(wide_q[i], key_query[j]) + forgot
        if masked:
            scores = jnp.where(attend, scores, neg_large)
        logit[pair_at(i, j)] = scores
        top = row_top[i]
        for start in range(0, rows, wide):
            top = jnp.maximum(top, scores[:, start : start + wide])
        row_top[i] = top

    def weigh_row(i):
        top = jnp.max(row_top[i], axis=1, keepdims=True)
        row_acc[...] = jnp.zeros_like(row_acc)

        def weigh(j, inner):
            prob = jnp.exp(logit[pair_at(i, j)] - top).astype(low)
            probs[pair_at(i, j)] = prob
            row_acc[...] += dot_nn(prob, vals[j])
            return inner

        lax.fori_loop(0, i + 1, weigh, 0)
        mixed = row_acc[...]
        inverse = 1.0 / mixed[:, HD : HD + 1]
        mixed = mixed * inverse
        mixed_keep[i] = jnp.where(lane < HD, mixed, inverse)
        send_mix[i] = fold_rows(mixed).astype(low)

        @pl.when(i != me)
        def _():
            exchange(send_mix.at[i], recv_mix.at[me], mix_s.at[i], mix_r.at[me], i).start()

    upwards = 1 - z // (depth // 2)
    at_end = (z == 0) | (z == depth - 1)
    pl.when(jnp.logical_not(at_end))(functools.partial(relay, 1))

    def forward_step(step, carried):
        block = upwards * step + (1 - upwards) * (count - 1 - step)
        group = step // 2

        @pl.when(lax.rem(block, 2) != y)
        def _():
            arrived(block)
            for distance in range(1, depth):
                pl.when(at_end & (group + 1 == distance))(functools.partial(relay, distance))
                pl.when(jnp.logical_not(at_end) & (group + 2 == distance))(functools.partial(relay, distance))

        project(block)

        def tiles(k, inner):
            i = upwards * step + (1 - upwards) * (block + k)
            j = upwards * k + (1 - upwards) * block
            pl.when(needs_mask(i, j))(functools.partial(forward_tile, i, j, True))
            pl.when(jnp.logical_not(needs_mask(i, j)))(functools.partial(forward_tile, i, j, False))
            return inner

        lax.fori_loop(0, step + 1, tiles, 0)
        pl.when(upwards == 1)(functools.partial(weigh_row, block))
        return carried

    lax.fori_loop(0, count, forward_step, 0)

    def late_weigh(i, carried):
        weigh_row(i)
        return carried

    lax.fori_loop(0, (1 - upwards) * count, late_weigh, 0)
    recv_mix[me] = send_mix[me]

    for load in loads:
        load.wait()

    def wait_mixed(step, carried):
        source = lax.rem(me + step, count)
        exchange(send_mix.at[source], recv_mix.at[source], mix_s.at[source], mix_r.at[source], source).wait_recv()
        return carried

    lax.fori_loop(1, count, wait_mixed, 0)
    for pair in range(pairs):
        even = recv_mix[2 * pair].astype(jnp.float32)
        odd = recv_mix[2 * pair + 1].astype(jnp.float32)
        columns = pl.ds(pair * wide, wide)
        mixed_ref[pl.ds(0, half), columns] = join_heads(even, swap_halves(odd)).astype(low)
        mixed_ref[pl.ds(half, half), columns] = join_heads(swap_halves(even), odd).astype(low)
    middle = tokens_ref[0].astype(jnp.float32) + dot_nn(mixed_ref[...], w_out_ref[...]) + b_out_ref[...]
    middle_ref[...] = middle
    unit, rstd = normalise(middle)
    unit_two_ref[...] = unit
    rstd_two_ref[...] = rstd
    normed_two_ref[...] = (unit * gain_two_ref[...] + bias_two_ref[...]).astype(low)
    out_acc[...] = jnp.zeros_like(out_acc)
    gn_acc[...] = jnp.zeros_like(gn_acc)
    near_sum = StagedSum(at, near_mine, near_final, [near_core, near_two, near_three, near_four, near_five], near_s, near_r)
    rest_sum = StagedSum(at, rest_mine, rest_final, [rest_core, rest_two, rest_three, rest_four, rest_five], rest_s, rest_r)
    mid_vec = VectorSum(at, vec_mid_mine, vec_mid_seq, vec_mid_sum, vec_mid_dp, vec_s, vec_r, 0)
    in_vec = VectorSum(at, vec_in_mine, vec_in_seq, vec_in_sum, vec_in_dp, vec_s, vec_r, 2)
    chunk = width
    chunks = hidden_width // chunk
    near_rows, rest_rows = near_mine.shape[0] // 2, rest_mine.shape[0] // 2

    def dense(sums, base, c, carried):
        start = pl.multiple_of((base + c) * chunk, chunk)
        cols = pl.ds(start, chunk)
        hidden = dot_nn(normed_two_ref[...], w_up_ref[:, cols]) + b_up_ref[:, cols]
        cdf = exact_cdf(hidden)
        slope = cdf + hidden * jnp.exp(-0.5 * hidden * hidden) * (1.0 / math.sqrt(2.0 * math.pi))
        active = (hidden * cdf).astype(low)
        out_acc[...] += dot_nn(active, w_down_ref[cols, :])
        grad_hidden = (dot_nt(cot_ref[0], w_down_ref[cols, :]) * slope).astype(low)
        here = pl.multiple_of(c * chunk, chunk)
        sums[pl.ds(here, chunk), :] = dot_tn(active, cot_ref[0]).astype(low)
        there = pl.multiple_of(sums.shape[0] // 2 + here, 16)
        sums[pl.ds(there, chunk), :] = dot_tn(normed_two_ref[...], grad_hidden).astype(low)
        vec_mid_mine[pl.ds(base + c, 1), :] = jnp.sum(grad_hidden.astype(jnp.float32), axis=0, keepdims=True)
        gn_acc[...] += dot_nt(grad_hidden, w_up_ref[:, cols])
        return carried

    lax.fori_loop(0, chunks // 2, functools.partial(dense, near_mine, 0), 0)
    near_sum.send(0)
    lax.fori_loop(0, chunks // 2, functools.partial(dense, rest_mine, chunks // 2), 0)
    near_sum.send(1)
    cot = cot_ref[0].astype(jnp.float32)
    grad = gn_acc[...]
    unit = unit_two_ref[...]
    middle = cot + normalise_back(grad, unit, rstd_two_ref[...], gain_two_ref[...])
    output_ref[0] = (middle_ref[...] + out_acc[...] + b_down_ref[...]).astype(low)
    middle_ref[...] = middle
    branch = middle.astype(low)
    for pair in range(pairs):
        back = dot_nt(branch, w_out_ref[pl.ds(pair * wide, wide), :]).astype(low).astype(jnp.float32)
        top, bottom = back[:half], back[half:]
        send_gmix[2 * pair] = join_heads(top, swap_halves(bottom)).astype(low)
        send_gmix[2 * pair + 1] = join_heads(swap_halves(top), bottom).astype(low)

    def send_grads(step, carried):
        to = lax.rem(me + step, count)
        exchange(send_gmix.at[to], recv_gmix.at[me], gmix_s.at[to], gmix_r.at[me], to).start()
        return carried

    lax.fori_loop(1, count, send_grads, 0)
    recv_gmix[me] = send_gmix[me]
    w_out_grad = dot_tn(mixed_ref[...], branch).astype(low)
    quarter = (chunks // 2) * chunk
    rest_mine[pl.ds(quarter, width // 2), :] = w_out_grad[: width // 2]
    rest_mine[pl.ds(rest_rows + quarter, width // 2), :] = w_out_grad[width // 2 :]
    rest_sum.send(0)
    vec_mid_mine[pl.ds(chunks, 1), :] = jnp.sum(cot, axis=0, keepdims=True)
    vec_mid_mine[pl.ds(chunks + 1, 1), :] = jnp.sum(grad * unit, axis=0, keepdims=True)
    vec_mid_mine[pl.ds(chunks + 2, 1), :] = jnp.sum(grad, axis=0, keepdims=True)
    vec_mid_mine[pl.ds(chunks + 3, 1), :] = jnp.sum(branch.astype(jnp.float32), axis=0, keepdims=True)
    mid_vec.start_seq()
    rest_sum.send(1)

    dkv_acc[...] = jnp.zeros_like(dkv_acc)
    dk0_acc[...] = jnp.zeros_like(dk0_acc)
    back_carry[...] = jnp.zeros_like(back_carry)
    wkv_acc[...] = jnp.zeros_like(wkv_acc)
    wqq_acc[...] = jnp.zeros_like(wqq_acc)
    wk0_acc[...] = jnp.zeros_like(wk0_acc)

    def backward_tile(i, j):
        prob = probs[pair_at(i, j)]
        grad_logits = (prob.astype(jnp.float32) * dot_nt(grad_rows[...], vals[j])).astype(low)
        dkv_acc[j, :HD] += dot_nn(grad_rows_t[...], prob)
        dkv_acc[j, HD:] += dot_nn(query_t[i], grad_logits)
        dq_acc[...] += dot_nn(grad_logits, key_query[j])
        later = dot_nn(upper[...], grad_logits) + back_carry[j]
        back_carry[j] = later[:1] - coeff * grad_logits[:1].astype(jnp.float32)
        gated = (later * gates[pair_at(i, j)].astype(jnp.float32)).astype(low)
        dq0_acc[...] += dot_nn(gated, first[j])
        dk0_acc[j] += dot_nn(first_t[i], gated)

    def send_first_sum(i):
        exchange(send_first.at[i], y_first.at[i], fback_y.at[i], fback_yr.at[i], i).wait_recv()
        send_first[i] = (send_first[i].astype(jnp.float32) + y_first[i].astype(jnp.float32)).astype(low)

        @pl.when(i != me)
        def _():
            exchange(send_first.at[i], recv_first.at[z], fback_s.at[i], fback_r.at[z], i).start()

        @pl.when(i == me)
        def _():
            recv_first[z] = send_first[i]

    def backward_row(step, carried):
        i = count - 1 - step

        @pl.when(i != me)
        def _():
            exchange(send_gmix.at[i], recv_gmix.at[i], gmix_s.at[i], gmix_r.at[i], i).wait_recv()

        grad = jnp.where(lane < HD, spread_rows(recv_gmix[i].astype(jnp.float32)), 0.0)
        kept = mixed_keep[i]
        inverse = kept[:, HD : HD + 1]
        delta = -jnp.sum(grad * kept, axis=1, keepdims=True) * inverse
        grad = grad * inverse
        grad_rows_t[...] = grad.T[:HD].astype(low)
        delta_high = delta.astype(low).astype(jnp.float32)
        grad = jnp.where(lane == HD, delta_high, jnp.where(lane == HD + 1, delta - delta_high, grad))
        grad_rows[...] = grad.astype(low)
        dq_acc[...] = jnp.zeros_like(dq_acc)
        dq0_acc[...] = jnp.zeros_like(dq0_acc)

        def tiles(j, inner):
            backward_tile(i, j)
            return inner

        lax.fori_loop(0, i + 1, tiles, 0)
        flat = dkv_acc[i]
        flipped = flat.T
        queries = join_heads(dq_acc[...], swap_halves(dq0_acc[...])) * score_scale
        first_keys = dk0_acc[i]
        first_flipped = jnp.concatenate([first_keys, first_keys], axis=0).T
        send_back[i, :rows] = join_heads(queries, flipped).astype(low)
        send_back[i, rows:] = fold_rows(flipped).astype(low)
        send_first[i] = join_heads(swap_halves(queries), first_flipped).astype(low)

        @pl.when(i != me)
        def _():
            exchange(send_back.at[i], recv_back.at[me], back_s.at[i], back_r.at[me], i).start()

        @pl.when(lax.rem(i, 2) != y)
        def _():
            exchange(send_first.at[i], y_first.at[i], fback_y.at[i], fback_yr.at[i], z * 2 + 1 - y).start()

        normed = normed_all[i]
        wkv_acc[...] += dot_nn(flat.astype(low), normed)
        wqq_acc[...] += dot_nn(queries.T.astype(low), normed)
        wk0_acc[...] += dot_nn(first_keys.astype(low), normed)
        pl.when((step >= 2) & (lax.rem(i, 2) == y))(lambda: send_first_sum(i + 2))
        pl.when(step == 0)(lambda: near_sum.send(2))
        pl.when(step == 1)(lambda: rest_sum.send(2))
        pl.when(step == 2)(mid_vec.start_dp)
        pl.when(step == 3)(lambda: near_sum.send(3))
        pl.when(step == 5)(lambda: rest_sum.send(3))
        return carried

    lax.fori_loop(0, count, backward_row, 0)
    recv_back[me] = send_back[me]

    piece = HD // 4
    for part in range(4):
        for place, (source, start) in enumerate(((wqq_acc, 0), (wkv_acc, HD), (wkv_acc, 0))):
            rows_in = pl.ds(part * 3 * piece + place * piece, piece)
            in_mine[rows_in, :] = source[start + part * piece : start + (part + 1) * piece].astype(low)
    extra_mine[:HD] = wqq_acc[HD:].astype(low)
    extra_mine[HD:] = wk0_acc[...].astype(low)
    core_half, x_half = 6 * piece, 3 * piece
    in_core_copy = remote(rows_of(in_mine, (1 - at.core) * core_half, core_half), in_core, part_s.at[0], part_r.at[0], at.core_peer)
    in_core_copy.start()

    def extra_over_seq(to, slot):
        return exchange(rows_of(extra_mine, to * piece, piece), extra_seq.at[slot], extra_s.at[to], extra_r.at[slot], to)

    def extra_gather(to, owner):
        return exchange(rows_of(extra_all, owner * piece, piece), rows_of(extra_all, owner * piece, piece), gather_s.at[to], gather_r.at[owner], to)

    def extra_over_dp(to, slot):
        return remote(extra_sum, extra_dp.at[slot], edp_s.at[to], edp_r.at[slot], (to, me))

    each_seq = functools.partial(in_vec.each, count, me)
    each_dp = functools.partial(in_vec.each, dp_count, dp)
    each_seq(lambda to: extra_over_seq(to, me).start())
    extra_seq[me] = extra_mine[pl.ds(pl.multiple_of(me * piece, 16), piece), :]
    for i in (1, 0):
        pl.when(y == i)(functools.partial(send_first_sum, i))
    in_core_copy.wait_recv()
    in_start = at.core * core_half
    add_rows(in_mine, in_start, in_core, 0, core_half)
    in_x_copy = remote(rows_of(in_mine, in_start + (1 - at.x) * x_half, x_half), in_x, part_s.at[1], part_r.at[1], at.x_peer)
    in_x_copy.start()
    near_sum.send(4)
    in_start = in_start + at.x * x_half
    in_x_copy.wait_recv()

    shard = x_half
    in_three = ((at.core * 2 + at.two_bit) * 2 + at.three_bit) * depth * shard
    in_own = in_three + z * shard

    def last_add(k, carried):
        here = pl.ds(pl.multiple_of(in_own + k * 16, 16), 16)
        mine = pl.ds(pl.multiple_of(in_start + k * 16, 16), 16)
        there = pl.ds(pl.multiple_of(k * 16, 16), 16)
        in_final[here, :] = (in_mine[mine, :].astype(jnp.float32) + in_x[there, :].astype(jnp.float32)).astype(low)
        return carried

    lax.fori_loop(0, shard // 16, last_add, 0)

    def in_deep(step):
        to_z = lax.rem(z + step, depth)
        block = rows_of(in_final, in_own, shard)
        return remote(block, block, in_s.at[step - 1], in_r.at[step - 1], (dp, to_z * 2 + y))

    def in_gather(start, size, slot, peer):
        block = rows_of(in_final, start, size)
        return remote(block, block, in_s.at[slot], in_r.at[slot], peer)

    in_two = (at.core * 2 + at.two_bit) * 2 * depth * shard
    in_one = at.core * 4 * depth * shard
    in_up = [
        in_gather(in_three, depth * shard, depth - 1, at.three_peer),
        in_gather(in_two, 2 * depth * shard, depth, at.two_peer),
        in_gather(in_one, 4 * depth * shard, depth + 1, at.core_peer),
    ]
    for step in range(1, depth):
        in_deep(step).start()
    each_seq(lambda source: extra_over_seq(source, source).wait_recv())
    summed = extra_seq[0].astype(jnp.float32)
    for k in range(1, count):
        summed = summed + extra_seq[k].astype(jnp.float32)
    extra_sum[...] = summed
    each_dp(lambda to: extra_over_dp(to, dp).start())
    extra_dp[dp] = summed
    rest_sum.send(4)
    near_sum.turn()

    def wait_back(step, carried):
        source = lax.rem(me + step, count)
        exchange(send_back.at[source], recv_back.at[source], back_s.at[source], back_r.at[source], source).wait_recv()
        return carried

    lax.fori_loop(1, count, wait_back, 0)

    def wait_first(step, carried):
        source = lax.rem(z + step, depth)
        exchange(send_first.at[source], recv_first.at[source], fback_s.at[source], fback_r.at[source], source * 2 + y).wait_recv()
        return carried

    lax.fori_loop(1, depth, wait_first, 0)
    first_sum = recv_first[0].astype(jnp.float32)
    for source in range(1, depth):
        first_sum = first_sum + recv_first[source].astype(jnp.float32)
    for pair in range(pairs):
        even = recv_back[2 * pair, :rows].astype(jnp.float32)
        odd = recv_back[2 * pair + 1, :rows].astype(jnp.float32)
        if pair == 0:
            even = even + first_sum
        columns = wide * pair
        joined_ref[:, pl.ds(columns, wide)] = join_heads(even, swap_halves(odd)).astype(low)
        joined_ref[:, pl.ds(width + columns, wide)] = join_heads(swap_halves(even), odd).astype(low)
        even = recv_back[2 * pair, rows:].astype(jnp.float32)
        odd = recv_back[2 * pair + 1, rows:].astype(jnp.float32)
        columns = pl.ds(2 * width + columns, wide)
        joined_ref[pl.ds(0, half), columns] = join_heads(even, swap_halves(odd)).astype(low)
        joined_ref[pl.ds(half, half), columns] = join_heads(swap_halves(even), odd).astype(low)
    grad = dot_nt(joined_ref[...], w_qkv_ref[...])
    unit = unit_one_ref[...]
    vec_in_mine[...] = jnp.zeros_like(vec_in_mine)
    vec_in_mine[pl.ds(0, 1), :] = jnp.sum(grad * unit, axis=0, keepdims=True)
    vec_in_mine[pl.ds(1, 1), :] = jnp.sum(grad, axis=0, keepdims=True)
    vec_in_mine[pl.ds(2, 1), :] = jnp.sum(joined_ref[:, pl.ds(2 * width, width)].astype(jnp.float32), axis=0, keepdims=True)
    in_vec.start_seq()
    tokens_grad_ref[0] = middle_ref[...] + normalise_back(grad, unit, rstd_one_ref[...], gain_one_ref[...])

    for step in range(1, depth):
        in_deep(step).wait_recv()
    in_up[0].start()
    near_sum.gather(3)
    rest_sum.turn()
    each_dp(lambda source: extra_over_dp(source, source).wait_recv())
    summed = extra_dp[0]
    for k in range(1, dp_count):
        summed = summed + extra_dp[k]
    extra_all[pl.ds(pl.multiple_of(me * piece, 16), piece), :] = summed.astype(low)
    each_seq(lambda to: extra_gather(to, me).start())
    in_vec.start_dp()
    in_up[0].wait_recv()
    in_up[1].start()
    near_sum.gather(2)
    rest_sum.gather(3)
    vec_mid_ref[...] = mid_vec.finish()
    near_sum.gather(1)
    rest_sum.gather(2)
    in_up[1].wait_recv()
    in_up[2].start()
    near_sum.gather(0)
    rest_sum.gather(1)
    near_sum.finish()
    half_hidden = hidden_width // 2
    stores = [
        pltpu.make_async_copy(near_final.at[pl.ds(0, half_hidden)], w_down_out.at[pl.ds(0, half_hidden)], store_sem.at[0]),
        pltpu.make_async_copy(near_final.at[pl.ds(near_rows, half_hidden)], w_up_out.at[pl.ds(0, half_hidden)], store_sem.at[1]),
    ]
    for store in stores:
        store.start()
    each_seq(lambda source: extra_gather(source, source).wait_recv())
    in_up[2].wait_recv()
    late = [
        pltpu.make_async_copy(in_final, w_qkv_out, store_sem.at[2]),
        pltpu.make_async_copy(extra_all, first_out, store_sem.at[3]),
    ]
    for store in late:
        store.start()
    stores += late
    rest_sum.gather(0)
    vec_in_ref[...] = in_vec.finish()
    rest_sum.finish()
    late = [
        pltpu.make_async_copy(rest_final.at[pl.ds(0, half_hidden)], w_down_out.at[pl.ds(half_hidden, half_hidden)], store_sem.at[4]),
        pltpu.make_async_copy(rest_final.at[pl.ds(rest_rows, half_hidden)], w_up_out.at[pl.ds(half_hidden, half_hidden)], store_sem.at[5]),
        pltpu.make_async_copy(rest_final.at[pl.ds(quarter, width // 2)], w_out_out.at[pl.ds(0, width // 2)], store_sem.at[6]),
        pltpu.make_async_copy(rest_final.at[pl.ds(rest_rows + quarter, width // 2)], w_out_out.at[pl.ds(width // 2, width // 2)], store_sem.at[7]),
    ]
    for store in late:
        store.start()
    stores += late

    pl.when(has_up(z))(lambda: pass_up(me).wait_send())
    pl.when(z > 0)(lambda: pass_down(me).wait_send())
    pass_y(me).wait_send()
    for distance in range(1, depth):

        def below(distance=distance):
            pl.when(has_up(z))(lambda: pass_up(me - 2 * distance).wait_send())
            pass_y(me - 2 * distance).wait_send()

        def above(distance=distance):
            pl.when(z > 0)(lambda: pass_down(me + 2 * distance).wait_send())
            pass_y(me + 2 * distance).wait_send()

        pl.when(z - distance >= 0)(below)
        pl.when(z + distance < depth)(above)

    def drain(step, carried):
        to = lax.rem(me + step, count)
        exchange(send_mix.at[to], recv_mix.at[me], mix_s.at[to], mix_r.at[me], to).wait_send()
        exchange(send_gmix.at[to], recv_gmix.at[me], gmix_s.at[to], gmix_r.at[me], to).wait_send()
        exchange(send_back.at[to], recv_back.at[me], back_s.at[to], back_r.at[me], to).wait_send()
        extra_over_seq(to, me).wait_send()
        extra_gather(to, me).wait_send()
        return carried

    lax.fori_loop(1, count, drain, 0)

    def drain_first(step, carried):
        to = lax.rem(z + step, depth) * 2 + y
        exchange(send_first.at[to], recv_first.at[z], fback_s.at[to], fback_r.at[z], to).wait_send()
        return carried

    def drain_first_y(step, carried):
        to = step * 2 + 1 - y
        exchange(send_first.at[to], y_first.at[to], fback_y.at[to], fback_yr.at[to], z * 2 + 1 - y).wait_send()
        return carried

    lax.fori_loop(1, depth, drain_first, 0)
    lax.fori_loop(0, depth, drain_first_y, 0)
    each_dp(lambda to: extra_over_dp(to, dp).wait_send())
    in_core_copy.wait_send()
    in_x_copy.wait_send()
    for step in range(1, depth):
        in_deep(step).wait_send()
    for copy in in_up:
        copy.wait_send()
    near_sum.drain()
    rest_sum.drain()
    mid_vec.drain()
    in_vec.drain()
    for store in stores:
        store.wait()


def widen_kernel(
    w_down_in, w_up_in, w_out_in, w_qkv_in, first_in, w_down_out, w_up_out, w_out_out, w_qkv_out,
    down_low, up_low, out_low, qkv_low, first_low, down_wide, up_wide, out_wide, qkv_wide, load_sem, store_sem,
):
    width = out_low.shape[0]
    blocks = down_low.shape[0] // width
    loads = []
    for k, (source, target) in enumerate(
        ((w_qkv_in, qkv_low), (first_in, first_low), (w_out_in, out_low), (w_down_in, down_low), (w_up_in, up_low))
    ):
        loads.append(pltpu.make_async_copy(source, target, load_sem.at[k]))
        loads[-1].start()
    stores = []

    def store(source, target):
        stores.append(pltpu.make_async_copy(source, target, store_sem.at[len(stores)]))
        stores[-1].start()

    def convert(source, target, at, columns):
        def step(k, carried):
            here = pl.ds(pl.multiple_of(at + k * 64, 64), 64)
            there = pl.ds(pl.multiple_of(k * 64, 64), 64)
            if columns is None:
                target[here, :] = source[here, :].astype(jnp.float32)
            else:
                target[there, pl.ds(columns, width)] = source[here, :].astype(jnp.float32)
            return carried

        lax.fori_loop(0, width // 64, step, 0)

    loads[0].wait()
    loads[1].wait()
    piece = HD // 4
    wide = 2 * HD
    for part in range(3):
        for pair in range(width // wide):
            found = []
            for head in (2 * pair, 2 * pair + 1):
                z, y = head // 2, head % 2
                for owner in range(4):
                    core, x = owner // 2, owner % 2
                    two, three = (x, y) if core == 0 else (y, x)
                    depth = width // wide
                    start = ((((core * 2 + two) * 2 + three) * depth + z) * 3 + part) * piece
                    block = qkv_low[start : start + piece].astype(jnp.float32)
                    if head == 0 and part < 2:
                        at = part * HD + owner * piece
                        block = block + first_low[at : at + piece].astype(jnp.float32)
                    found.append(block)
            columns = part * width + pair * wide
            qkv_wide[:, columns : columns + wide] = jnp.concatenate(found, axis=0).T
    store(qkv_wide, w_qkv_out)
    loads[2].wait()
    convert(out_low, out_wide, 0, None)
    store(out_wide, w_out_out)
    loads[3].wait()
    for block in range(blocks):
        convert(down_low, down_wide, block * width, None)
        here = pl.ds(block * width, width)
        store(down_wide.at[here], w_down_out.at[here])
    loads[4].wait()
    for block in range(blocks):
        convert(up_low, up_wide, block * width, block * width)
        here = pl.ds(block * width, width)
        store(up_wide.at[:, here], w_up_out.at[:, here])
    for one in stores:
        one.wait()


def exchange_heads(
    tokens, segment_ids, gain_one, bias_one, w_qkv, b_val, w_out, b_out,
    gain_two, bias_two, w_up, b_up, w_down, b_down, cotangent,
):
    count, dp_count = lax.axis_size("seq"), lax.axis_size("dp")
    rows, width = tokens.shape[1], tokens.shape[2]
    hidden = w_up.shape[1]
    half = rows // 2
    tiles = count * (count + 1) // 2
    wide = 2 * HD
    f32 = jnp.float32
    packed = rows + half
    near, rest = hidden, hidden + width
    depth = count // 2

    def vmem(*shape, dtype=low):
        return pltpu.VMEM(shape, dtype)

    def sems(*shape):
        return pltpu.SemaphoreType.DMA(shape)

    scratch = [
        vmem(width, width), vmem(width, hidden), vmem(hidden, width), sems(3), sems(8),
        vmem(count, rows, width), vmem(width, 2 * wide), vmem(width, wide), vmem(1, wide, dtype=f32),
        vmem(count, rows, wide), vmem(count, rows, wide), vmem(count, rows, wide),
        vmem(count, HD, rows), vmem(count, HD, rows), vmem(count, rows, wide), vmem(count, rows, wide),
        vmem(tiles, rows, rows), vmem(tiles, rows, rows), vmem(tiles, rows, rows, dtype=f32),
        vmem(count, 1, rows, dtype=f32), vmem(count, rows, wide, dtype=f32), vmem(rows, wide, dtype=f32), vmem(count, rows, wide, dtype=f32),
        vmem(count, half, wide), vmem(count, half, wide), vmem(count, half, wide), vmem(count, half, wide), vmem(rows, wide), vmem(HD, rows),
        vmem(rows, wide, dtype=f32), vmem(rows, wide, dtype=f32), vmem(count, wide, rows, dtype=f32), vmem(count, HD, rows, dtype=f32), vmem(count, 1, rows, dtype=f32),
        vmem(count, packed, wide), vmem(count, packed, wide), vmem(count, rows, wide), vmem(count, rows, wide), vmem(depth, rows, wide),
        vmem(rows, rows), vmem(rows, rows),
        vmem(rows, width, dtype=f32), vmem(rows, 1, dtype=f32), vmem(rows, width, dtype=f32), vmem(rows, 1, dtype=f32),
        vmem(rows, width), vmem(rows, width), vmem(rows, width, dtype=f32), vmem(rows, width, dtype=f32), vmem(rows, width, dtype=f32), vmem(rows, 3 * width),
    ]
    for total in (near, rest):
        scratch += [vmem(total, width), vmem(total, width)]
        scratch += [vmem(total >> stage, width) for stage in range(1, 6)]
    scratch += [
        vmem(wide, width, dtype=f32), vmem(wide, width, dtype=f32), vmem(HD, width, dtype=f32),
        vmem(3 * HD, width), vmem(3 * HD // 2, width), vmem(3 * HD // 4, width), vmem(3 * width, width),
        vmem(wide, width), vmem(count, wide // count, width), vmem(wide // count, width, dtype=f32), vmem(dp_count, wide // count, width, dtype=f32), vmem(wide, width),
    ]
    for _ in range(2):
        scratch += [vmem(8, width, dtype=f32), vmem(count, 8, width, dtype=f32), vmem(8, width, dtype=f32), vmem(dp_count, 8, width, dtype=f32)]
    scratch += [sems(count)] * 18
    scratch += [sems(10)] * 4 + [sems(depth + 2), sems(depth + 2), sems(2), sems(2), sems(4, count), sems(4, count), sems(dp_count), sems(dp_count)]
    in_vmem = pl.BlockSpec(memory_space=pltpu.VMEM)
    anywhere = pl.BlockSpec(memory_space=pl.ANY)
    specs = [in_vmem] * 15
    for at in (6, 10, 12):
        specs[at] = anywhere
    shape = jax.ShapeDtypeStruct
    results = pl.pallas_call(
        layer_kernel,
        out_shape=[
            shape((1, rows, width), low), shape((1, rows, width), f32), shape((8, width), f32), shape((8, width), f32),
            shape((hidden, width), low), shape((hidden, width), low), shape((width, width), low), shape((3 * width, width), low), shape((wide, width), low),
        ],
        in_specs=specs,
        out_specs=[in_vmem] * 4 + [anywhere] * 5,
        scratch_shapes=scratch,
        compiler_params=pltpu.CompilerParams(
            collective_id=0, has_side_effects=True, vmem_limit_bytes=vmem_bytes
        ),
    )(
        tokens, segment_ids, gain_one[None], bias_one[None], w_qkv, b_val[None], w_out, b_out[None],
        gain_two[None], bias_two[None], w_up, b_up[None], w_down, b_down[None], cotangent,
    )
    output, tokens_grad, vec_mid, vec_in = results[:4]
    w_down_grad, w_up_grad, w_out_grad, w_qkv_grad = pl.pallas_call(
        widen_kernel,
        out_shape=[shape((hidden, width), f32), shape((width, hidden), f32), shape((width, width), f32), shape((width, 3 * width), f32)],
        in_specs=[anywhere] * 5,
        out_specs=[anywhere] * 4,
        scratch_shapes=[
            vmem(hidden, width), vmem(hidden, width), vmem(width, width), vmem(3 * width, width), vmem(wide, width),
            vmem(hidden, width, dtype=f32), vmem(width, hidden, dtype=f32), vmem(width, width, dtype=f32), vmem(width, 3 * width, dtype=f32),
            sems(5), sems(16),
        ],
        compiler_params=pltpu.CompilerParams(vmem_limit_bytes=vmem_bytes),
    )(*results[4:])
    chunks = hidden // width
    return (
        output,
        tokens_grad,
        vec_in[0],
        vec_in[1],
        w_qkv_grad,
        vec_in[2],
        w_out_grad,
        vec_mid[chunks + 3],
        vec_mid[chunks + 1],
        vec_mid[chunks + 2],
        w_up_grad,
        vec_mid[:chunks].reshape(hidden),
        w_down_grad,
        vec_mid[chunks],
    )


def picks_heads(mesh, length, width, hidden):
    dp_count, count = mesh.shape["dp"], mesh.shape["seq"]
    power = length & (length - 1) == 0
    return dp_count == 4 and count == 8 and width == count * HD and hidden == 4 * width and power


def solution(mesh):
    placed = (
        P("dp", "seq", None),
        P("dp", None),
        P(),
        P(),
        P(),
        P(),
        P(),
        P(),
        P(),
        P(),
        P(),
        P(),
        P(),
        P(),
        P("dp", "seq", None),
    )

    def layer(tokens, *others):
        width, hidden = tokens.shape[-1], others[9].shape[-1]
        length = tokens.shape[1] * mesh.shape["seq"]
        body = exchange_heads if picks_heads(mesh, length, width, hidden) else local
        return body(tokens, *others)

    return jax.shard_map(
        layer,
        mesh=mesh,
        in_specs=placed,
        out_specs=(
            P("dp", "seq", None),
            P("dp", "seq", None),
            P(),
            P(),
            P(),
            P(),
            P(),
            P(),
            P(),
            P(),
            P(),
            P(),
            P(),
            P(),
        ),
        check_vma=False,
    )
```

```python
import functools
import math

import jax
import jax.numpy as jnp
from jax import lax
from jax.experimental import pallas as pl
from jax.experimental.pallas import tpu as pltpu
from jax.sharding import PartitionSpec as P

HD = 64


norm_eps = 1e-05
select_weight = 4.0
neg_large = -1e30
highest = lax.Precision.HIGHEST
vmem_bytes = 63 * 1024 * 1024


def prefix(array, axis, combine, identity, reverse):
    length, here = (lax.axis_size(axis), lax.axis_index(axis))
    everything = lax.all_gather(array.astype(jnp.bfloat16), axis)
    start = jnp.broadcast_to(jnp.asarray(identity, array.dtype), array.shape)

    def hop(k, before):
        at = length - 1 - k if reverse else k
        reached = at > here if reverse else at < here
        new = combine(before, everything[at].astype(array.dtype))
        return jnp.where(reached, new, before)

    return lax.fori_loop(0, length, hop, start)


def layer_norm(values, norm_gain, norm_shift):
    centered = values - jnp.mean(values, axis=-1, keepdims=True)
    variance = jnp.mean(centered * centered, axis=-1, keepdims=True)
    return centered * lax.rsqrt(variance + norm_eps) * norm_gain + norm_shift


def exact_gelu(values):
    return jax.nn.gelu(values, approximate=False)


def add_arrays(earlier, later):
    return earlier + later


def keep_state(state_in):
    return state_in


def pick_block():
    return 512


def local(
    tokens,
    segment_ids,
    gain_one,
    bias_one,
    w_qkv,
    b_val,
    w_out,
    b_out,
    gain_two,
    bias_two,
    w_up,
    b_up,
    w_down,
    b_down,
    cotangent,
):
    seq_count = lax.axis_size("seq")
    seq_rank = lax.axis_index("seq")
    row_tokens = tokens[0].astype(jnp.float32)
    tok_rows = row_tokens.shape[0]
    model_width = row_tokens.shape[1]
    head_count = model_width // HD
    length = tok_rows * seq_count
    score_scale = 1.0 / math.sqrt(HD)
    select_coeff = select_weight / length
    row_segments = segment_ids[0]
    row_base = seq_rank * tok_rows
    query_pos = row_base + jnp.arange(tok_rows, dtype=jnp.int32)
    query_segs = lax.dynamic_slice_in_dim(row_segments, row_base, tok_rows)
    last_query = row_base + tok_rows - 1
    lower_mask = (jnp.arange(tok_rows)[:, None] > jnp.arange(tok_rows)[None, :]).astype(jnp.float32)
    upper_mask = lower_mask.T
    normed_one, norm_one_back = jax.vjp(layer_norm, row_tokens, gain_one, bias_one)
    normed_one_low = normed_one.astype(jnp.bfloat16)
    value_bias = jnp.concatenate([jnp.zeros((2 * model_width,), jnp.float32), b_val])
    joined_low = (
        jnp.dot(normed_one_low, w_qkv, preferred_element_type=jnp.float32) + value_bias
    ).astype(jnp.bfloat16)
    queries = joined_low[:, :model_width]
    keys_mine = joined_low[:, model_width : 2 * model_width]
    values_mine = joined_low[:, 2 * model_width :]
    query_heads = queries.reshape(tok_rows, head_count, HD)
    query_zero = queries[:, :HD]
    query_rest = query_heads[:, 1:]

    def pair_masks(key_start, key_rows):
        key_pos = key_start + jnp.arange(key_rows, dtype=jnp.int32)
        key_segs = lax.dynamic_slice_in_dim(row_segments, key_start, key_rows)
        same_doc = query_segs[:, None] == key_segs[None, :]
        attend_mask = same_doc & (key_pos[None, :] <= query_pos[:, None])
        select_mask = same_doc & (key_pos[None, :] < query_pos[:, None])
        return (attend_mask, select_mask)

    select_init = (
        jnp.zeros((tok_rows, length), jnp.float32),
        jnp.zeros((tok_rows, length), jnp.float32),
        jnp.zeros((length,), jnp.float32),
    )
    running = select_init
    key_piece = lax.all_gather(keys_mine[:, :HD], "seq", axis=0, tiled=True)
    piece_rows = key_piece.shape[0]
    block_rows = pick_block()

    def select_block(state_now, offset):
        zero_scores, local_forgot, column_sums = state_now
        key_block = lax.dynamic_slice_in_dim(key_piece, offset, block_rows)
        attend_mask, select_mask = pair_masks(offset, block_rows)
        scores = (
            jnp.einsum("qd,kd->qk", query_zero, key_block, preferred_element_type=jnp.float32)
            * score_scale
        )
        chosen = jnp.where(select_mask, jax.nn.softplus(scores), 0.0)
        forgot = jnp.dot(lower_mask, chosen, precision=highest)
        zero_scores = lax.dynamic_update_slice_in_dim(zero_scores, scores, offset, 1)
        local_forgot = lax.dynamic_update_slice_in_dim(local_forgot, forgot, offset, 1)
        column_sums = lax.dynamic_update_slice_in_dim(
            column_sums, jnp.sum(chosen, axis=0), offset, 0
        )
        return ((zero_scores, local_forgot, column_sums), None)

    offsets = jnp.arange(piece_rows // block_rows, dtype=jnp.int32) * block_rows
    running, unused = lax.scan(select_block, running, offsets)
    zero_scores, local_forgot, column_sums = running
    column_prefix = prefix(column_sums, "seq", add_arrays, jnp.zeros((length,), jnp.float32), False)
    attend_init = (
        jnp.full((head_count, tok_rows), neg_large, jnp.float32),
        jnp.zeros((head_count, tok_rows), jnp.float32),
        jnp.zeros((tok_rows, head_count, HD), jnp.float32),
    )
    running = attend_init
    attend_key_piece = lax.all_gather(keys_mine, "seq", axis=0, tiled=True)
    value_piece = lax.all_gather(values_mine, "seq", axis=0, tiled=True)
    piece_rows = attend_key_piece.shape[0]
    attend_block_rows = pick_block()

    def attend_block(state_now, offset):
        key_start = offset

        def attend_compute(state_in):
            run_max, run_total, accumulated = state_in
            key_block = lax.dynamic_slice_in_dim(
                attend_key_piece, offset, attend_block_rows
            ).reshape(attend_block_rows, head_count, HD)
            value_block = lax.dynamic_slice_in_dim(value_piece, offset, attend_block_rows).reshape(
                attend_block_rows, head_count, HD
            )
            attend_mask, select_mask = pair_masks(key_start, attend_block_rows)
            rest_scores = (
                jnp.einsum(
                    "qhd,khd->hqk", query_rest, key_block[:, 1:], preferred_element_type=jnp.float32
                )
                * score_scale
            )
            head_zero = lax.dynamic_slice_in_dim(zero_scores, key_start, attend_block_rows, 1)
            scores = jnp.concatenate([head_zero[None], rest_scores], axis=0)
            forgot = lax.dynamic_slice_in_dim(column_prefix, key_start, attend_block_rows)[
                None, :
            ] + lax.dynamic_slice_in_dim(local_forgot, key_start, attend_block_rows, 1)
            logits = jnp.where(attend_mask[None], scores - select_coeff * forgot[None], neg_large)
            new_max = jnp.maximum(run_max, jnp.max(logits, axis=-1))
            weights = jnp.where(attend_mask[None], jnp.exp(logits - new_max[:, :, None]), 0.0)
            decay_factor = jnp.exp(run_max - new_max)
            run_total = run_total * decay_factor + jnp.sum(weights, axis=-1)
            accumulated = accumulated * decay_factor.T[:, :, None] + jnp.einsum(
                "hqk,khd->qhd",
                weights.astype(jnp.bfloat16),
                value_block,
                preferred_element_type=jnp.float32,
            )
            return (new_max, run_total, accumulated)

        state_now = lax.cond(key_start <= last_query, attend_compute, keep_state, state_now)
        return (state_now, None)

    offsets = jnp.arange(piece_rows // attend_block_rows, dtype=jnp.int32) * attend_block_rows
    running, unused = lax.scan(attend_block, running, offsets)
    run_max, run_total, accumulated = running
    log_total = run_max + jnp.log(run_total)
    mixed_float = accumulated / run_total.T[:, :, None]
    mixed_low = mixed_float.reshape(tok_rows, model_width).astype(jnp.bfloat16)
    middle = row_tokens + jnp.dot(mixed_low, w_out, preferred_element_type=jnp.float32) + b_out
    normed_two, norm_two_back = jax.vjp(layer_norm, middle, gain_two, bias_two)
    normed_two_low = normed_two.astype(jnp.bfloat16)
    hidden = jnp.dot(normed_two_low, w_up, preferred_element_type=jnp.float32) + b_up
    active, gelu_back = jax.vjp(exact_gelu, hidden)
    active_low = active.astype(jnp.bfloat16)
    output = middle + jnp.dot(active_low, w_down, preferred_element_type=jnp.float32) + b_down
    grad_out = cotangent[0]
    grad_float = grad_out.astype(jnp.float32)
    w_down_grad = jnp.einsum("tf,td->fd", active_low, grad_out, preferred_element_type=jnp.float32)
    b_down_grad = jnp.sum(grad_float, axis=0)
    grad_active = jnp.einsum("td,fd->tf", grad_out, w_down, preferred_element_type=jnp.float32)
    (grad_hidden,) = gelu_back(grad_active)
    grad_hidden_low = grad_hidden.astype(jnp.bfloat16)
    w_up_grad = jnp.einsum(
        "td,tf->df", normed_two_low, grad_hidden_low, preferred_element_type=jnp.float32
    )
    b_up_grad = jnp.sum(grad_hidden_low.astype(jnp.float32), axis=0)
    grad_normed_two = jnp.einsum(
        "tf,df->td", grad_hidden_low, w_up, preferred_element_type=jnp.float32
    )
    grad_middle_norm, gain_two_grad, bias_two_grad = norm_two_back(grad_normed_two)
    grad_middle = grad_float + grad_middle_norm
    grad_branch_low = grad_middle.astype(jnp.bfloat16)
    w_out_grad = jnp.einsum(
        "td,te->de", mixed_low, grad_branch_low, preferred_element_type=jnp.float32
    )
    b_out_grad = jnp.sum(grad_branch_low.astype(jnp.float32), axis=0)
    grad_mixed_low = jnp.einsum(
        "te,de->td", grad_branch_low, w_out, preferred_element_type=jnp.float32
    ).astype(jnp.bfloat16)
    grad_mixed_heads = grad_mixed_low.reshape(tok_rows, head_count, HD)
    row_delta = jnp.sum(grad_mixed_heads.astype(jnp.float32) * mixed_float, axis=-1).T
    keys_back, values_back = (
        lax.all_gather(keys_mine, "seq", axis=0, tiled=True),
        lax.all_gather(values_mine, "seq", axis=0, tiled=True),
    )
    back_rows = pick_block()
    key_heads = keys_back.reshape(length, head_count, HD)
    value_heads = values_back.reshape(length, head_count, HD)

    def grad_block(state_now, offset):

        def grad_compute(state_in):
            query_grad, key_grad, value_grad, first_part, second_part, grad_cols = state_in
            key_block = lax.dynamic_slice_in_dim(key_heads, offset, back_rows)
            value_block = lax.dynamic_slice_in_dim(value_heads, offset, back_rows)
            attend_mask, select_mask = pair_masks(offset, back_rows)
            scores = (
                jnp.einsum(
                    "qhd,khd->hqk", query_heads, key_block, preferred_element_type=jnp.float32
                )
                * score_scale
            )
            chosen = jnp.where(select_mask, jax.nn.softplus(scores[0]), 0.0)
            forgot = lax.dynamic_slice_in_dim(column_prefix, offset, back_rows)[None, :] + jnp.dot(
                lower_mask, chosen, precision=highest
            )
            logits = scores - select_coeff * forgot[None]
            prob_block = jnp.where(attend_mask[None], jnp.exp(logits - log_total[:, :, None]), 0.0)
            grad_probs = jnp.einsum(
                "qhd,khd->hqk", grad_mixed_heads, value_block, preferred_element_type=jnp.float32
            )
            grad_logits = prob_block * (grad_probs - row_delta[:, :, None])
            value_part = jnp.einsum(
                "hqk,qhd->khd",
                prob_block.astype(jnp.bfloat16),
                grad_mixed_heads,
                preferred_element_type=jnp.float32,
            )
            rest_low = grad_logits[1:].astype(jnp.bfloat16)
            query_grad = (
                query_grad
                + jnp.einsum(
                    "hqk,khd->qhd", rest_low, key_block[:, 1:], preferred_element_type=jnp.float32
                )
                * score_scale
            )
            key_part = (
                jnp.einsum("hqk,qhd->khd", rest_low, query_rest, preferred_element_type=jnp.float32)
                * score_scale
            )
            total_grad = jnp.sum(grad_logits, axis=0)
            suffix_local = jnp.dot(upper_mask, total_grad, precision=highest)
            select_gate = jnp.where(select_mask, select_coeff * jax.nn.sigmoid(scores[0]), 0.0)
            first_part = lax.dynamic_update_slice_in_dim(
                first_part, grad_logits[0] - select_gate * suffix_local, offset, 1
            )
            second_part = lax.dynamic_update_slice_in_dim(second_part, select_gate, offset, 1)
            key_grad = lax.dynamic_update_slice_in_dim(key_grad, key_part, offset, 0)
            value_grad = lax.dynamic_update_slice_in_dim(value_grad, value_part, offset, 0)
            grad_cols = lax.dynamic_update_slice_in_dim(
                grad_cols, jnp.sum(total_grad, axis=0), offset, 0
            )
            return (query_grad, key_grad, value_grad, first_part, second_part, grad_cols)

        state_now = lax.cond(offset <= last_query, grad_compute, keep_state, state_now)
        return (state_now, None)

    grad_init = (
        jnp.zeros((tok_rows, head_count - 1, HD), jnp.float32),
        jnp.zeros((length, head_count - 1, HD), jnp.float32),
        jnp.zeros((length, head_count, HD), jnp.float32),
        jnp.zeros((tok_rows, length), jnp.float32),
        jnp.zeros((tok_rows, length), jnp.float32),
        jnp.zeros((length,), jnp.float32),
    )
    back_offsets = jnp.arange(length // back_rows, dtype=jnp.int32) * back_rows
    grad_state, unused = lax.scan(grad_block, grad_init, back_offsets)
    query_grad, key_grad, value_grad, first_part, second_part, grad_cols = grad_state
    grad_suffix = prefix(grad_cols, "seq", add_arrays, jnp.zeros((length,), jnp.float32), True)
    zero_grad_low = (first_part - second_part * grad_suffix[None, :]).astype(jnp.bfloat16)
    query_zero_grad = (
        jnp.dot(zero_grad_low, keys_back[:, :HD], preferred_element_type=jnp.float32) * score_scale
    )
    key_zero_grad = (
        jnp.einsum("ql,qd->ld", zero_grad_low, query_zero, preferred_element_type=jnp.float32)
        * score_scale
    )
    key_total = jnp.concatenate([key_zero_grad[:, None, :], key_grad], axis=1).reshape(
        length, model_width
    )
    value_total = value_grad.reshape(length, model_width)
    key_mine_grad, value_mine_grad = (
        lax.psum_scatter(
            key_total.astype(jnp.bfloat16), "seq", scatter_dimension=0, tiled=True
        ).astype(jnp.float32),
        lax.psum_scatter(
            value_total.astype(jnp.bfloat16), "seq", scatter_dimension=0, tiled=True
        ).astype(jnp.float32),
    )
    query_total = jnp.concatenate([query_zero_grad[:, None, :], query_grad], axis=1).reshape(
        tok_rows, model_width
    )
    grad_joined_low = jnp.concatenate([query_total, key_mine_grad, value_mine_grad], axis=1).astype(
        jnp.bfloat16
    )
    b_val_grad = jnp.sum(grad_joined_low[:, 2 * model_width :].astype(jnp.float32), axis=0)
    w_qkv_grad = jnp.einsum(
        "td,te->de", normed_one_low, grad_joined_low, preferred_element_type=jnp.float32
    )
    grad_normed_one = jnp.einsum(
        "te,de->td", grad_joined_low, w_qkv, preferred_element_type=jnp.float32
    )
    grad_tokens_norm, gain_one_grad, bias_one_grad = norm_one_back(grad_normed_one)
    tokens_grad = grad_middle + grad_tokens_norm
    summed = lax.psum(
        (
            gain_one_grad,
            bias_one_grad,
            w_qkv_grad,
            b_val_grad,
            w_out_grad,
            b_out_grad,
            gain_two_grad,
            bias_two_grad,
            w_up_grad,
            b_up_grad,
            w_down_grad,
            b_down_grad,
        ),
        ("dp", "seq"),
    )
    return (
        output.astype(jnp.bfloat16)[None],
        tokens_grad[None],
        summed[0],
        summed[1],
        summed[2],
        summed[3],
        summed[4],
        summed[5],
        summed[6],
        summed[7],
        summed[8],
        summed[9],
        summed[10],
        summed[11],
    )


low = jnp.bfloat16
MESH = pl.DeviceIdType.MESH


def dot_nn(left, right):
    return lax.dot_general(left, right, (((1,), (0,)), ((), ())), preferred_element_type=jnp.float32)


def dot_nt(left, right):
    return lax.dot_general(left, right, (((1,), (1,)), ((), ())), preferred_element_type=jnp.float32)


def dot_tn(left, right):
    return lax.dot_general(left, right, (((0,), (0,)), ((), ())), preferred_element_type=jnp.float32)


def swap_halves(wide):
    return pltpu.roll(wide, HD, 1)


def left_lanes(shape):
    return lax.broadcasted_iota(jnp.int32, shape, 1) < HD


def join_heads(left, right):
    return jnp.where(left_lanes(left.shape), left, right)


def fold_rows(wide):
    half = wide.shape[0] // 2
    return join_heads(wide[:half], swap_halves(wide[half:]))


def spread_rows(folded):
    return jnp.concatenate([folded, swap_halves(folded)], axis=0)


def exact_cdf(values):
    return 0.5 * (1.0 + lax.erf(values * (1.0 / math.sqrt(2.0))))


def normalise(values):
    centered = values - jnp.mean(values, axis=-1, keepdims=True)
    rstd = lax.rsqrt(jnp.mean(centered * centered, axis=-1, keepdims=True) + norm_eps)
    return centered * rstd, rstd


def normalise_back(grad, unit, rstd, gain):
    scaled = grad * gain
    mean_one = jnp.mean(scaled, axis=-1, keepdims=True)
    mean_two = jnp.mean(scaled * unit, axis=-1, keepdims=True)
    return rstd * (scaled - mean_one - unit * mean_two)


def rows_of(ref, at, size):
    return ref.at[pl.ds(pl.multiple_of(at, 16), size)]


def add_rows(into, into_at, parts, size):
    def step(k, carried):
        summed = None
        for ref, at in parts:
            block = ref[pl.ds(pl.multiple_of(at + k * 16, 16), 16), :].astype(jnp.float32)
            summed = block if summed is None else summed + block
        into[pl.ds(pl.multiple_of(into_at + k * 16, 16), 16), :] = summed.astype(low)
        return carried

    lax.fori_loop(0, size // 16, step, 0)


class Places:
    def __init__(self):
        self.dp_count, self.count = lax.axis_size("dp"), lax.axis_size("seq")
        self.dp, self.me = lax.axis_index("dp"), lax.axis_index("seq")
        self.core, self.x = lax.rem(self.dp, 2), self.dp // 2
        self.y, self.z = lax.rem(self.me, 2), self.me // 2
        self.depth = self.count // 2
        self.core_peer = (self.dp + 1 - 2 * self.core, self.me)
        self.x_peer = (self.dp + 2 - 4 * self.x, self.me)
        self.y_peer = (self.dp, self.me + 1 - 2 * self.y)
        along_x = 1 - self.core
        self.two_peer = (self.dp + along_x * (2 - 4 * self.x), self.me + (1 - along_x) * (1 - 2 * self.y))
        self.three_peer = (self.dp + (1 - along_x) * (2 - 4 * self.x), self.me + along_x * (1 - 2 * self.y))
        self.two_bit = along_x * self.x + (1 - along_x) * self.y
        self.three_bit = (1 - along_x) * self.x + along_x * self.y
        self.z_low, self.z_high = lax.rem(self.z, 2), self.z // 2
        self.z_near = (self.dp, self.me + 2 * (1 - 2 * self.z_low))
        self.z_far = (self.dp, self.me + 4 * (1 - 2 * self.z_high))


def remote(src, dst, send_sem, recv_sem, target):
    return pltpu.make_async_remote_copy(
        src_ref=src, dst_ref=dst, send_sem=send_sem, recv_sem=recv_sem, device_id=target, device_id_type=MESH
    )


class StagedSum:
    def __init__(self, at, mine, final, got, sems):
        self.mine, self.final, self.got = mine, final, got
        bits = (at.core, at.two_bit, at.three_bit, at.z_low, at.z_high)
        self.peers = (at.core_peer, at.two_peer, at.three_peer, at.z_near, at.z_far)
        self.stages = len(bits)
        self.down_s, self.down_r, self.up_s, self.up_r = sems
        start, size = 0, final.shape[0]
        self.keep, self.give, self.size = [], [], []
        for bit in bits:
            size //= 2
            self.keep.append(start + bit * size)
            self.give.append(start + (1 - bit) * size)
            self.size.append(size)
            start = start + bit * size
        self.give.append(start)
        self.size.append(size)

    def down(self, stage, block):
        if stage == 0:
            source, there, size = self.give[0], 0, self.size[0]
        else:
            there, size = self.give[block] - self.keep[stage], self.size[block]
            source = self.give[stage] + there
        return remote(
            rows_of(self.mine, source, size), rows_of(self.got[stage], there, size),
            self.down_s.at[stage, block], self.down_r.at[stage, block], self.peers[stage],
        )

    def up(self, stage, block):
        here = rows_of(self.final, self.give[block], self.size[block])
        return remote(here, here, self.up_s.at[stage, block], self.up_r.at[stage, block], self.peers[stage])

    def blocks(self, stage):
        return (1,) if stage == 0 else range(stage + 1, self.stages + 1)

    def send(self, stage):
        if stage > 0:
            self.collect(stage, self.mine)
        for block in self.blocks(stage):
            self.down(stage, block).start()

    def collect(self, block, into):
        parts = [(self.mine, self.give[block])]
        for stage in range(block):
            if stage > 0 or block == 1:
                self.down(stage, block).wait_recv()
            parts.append((self.got[stage], self.give[block] - self.keep[stage]))
        add_rows(into, self.give[block], parts, self.size[block])

    def turn(self):
        self.collect(self.stages, self.final)
        self.spread(self.stages)

    def spread(self, block):
        for stage in reversed(range(block)):
            self.up(stage, block).start()

    def arrive(self, stage):
        for block in range(stage + 1, self.stages + 1):
            self.up(stage, block).wait_recv()

    def gather(self, stage):
        self.arrive(stage)
        self.spread(stage)

    def drain(self, summed=True):
        for stage in range(self.stages):
            if summed:
                for block in self.blocks(stage):
                    self.down(stage, block).wait_send()
            for block in range(stage + 1, self.stages + 1):
                self.up(stage, block).wait_send()


class VectorSum:
    def __init__(self, at, mine, seq_got, seq_sum, dp_got, send_sem, recv_sem, base):
        self.at, self.mine, self.seq_got, self.seq_sum, self.dp_got = at, mine, seq_got, seq_sum, dp_got
        self.send_sem, self.recv_sem, self.base = send_sem, recv_sem, base

    def over_seq(self, to, slot):
        return remote(
            self.mine, self.seq_got.at[slot], self.send_sem.at[self.base, to], self.recv_sem.at[self.base, slot],
            (self.at.dp, to),
        )

    def over_dp(self, to, slot):
        return remote(
            self.seq_sum, self.dp_got.at[slot], self.send_sem.at[self.base + 1, to],
            self.recv_sem.at[self.base + 1, slot], (to, self.at.me),
        )

    def each(self, count, mine, act):
        def step(k, carried):
            act(lax.rem(mine + k, count))
            return carried

        lax.fori_loop(1, count, step, 0)

    def start_seq(self):
        at = self.at
        self.each(at.count, at.me, lambda to: self.over_seq(to, at.me).start())
        self.seq_got[at.me] = self.mine[...]

    def start_dp(self):
        at = self.at
        self.each(at.count, at.me, lambda source: self.over_seq(source, source).wait_recv())
        summed = self.seq_got[0]
        for k in range(1, at.count):
            summed = summed + self.seq_got[k]
        self.seq_sum[...] = summed
        self.each(at.dp_count, at.dp, lambda to: self.over_dp(to, at.dp).start())
        self.dp_got[at.dp] = summed

    def finish(self):
        at = self.at
        self.each(at.dp_count, at.dp, lambda source: self.over_dp(source, source).wait_recv())
        summed = self.dp_got[0]
        for k in range(1, at.dp_count):
            summed = summed + self.dp_got[k]
        return summed

    def drain(self):
        at = self.at
        self.each(at.count, at.me, lambda to: self.over_seq(to, at.me).wait_send())
        self.each(at.dp_count, at.dp, lambda to: self.over_dp(to, at.dp).wait_send())


before_backward = ("N2", "R1",)
between_steps = (
    ("N3",),
    ("R2", "O1",),
    ("N4",),
    ("R3", "O2",),
    ("Nt",),
    ("R4", "V1", "O3",),
    ("Ne",),
    ("Rt", "O4",),
)
after_backward = (
    "I0", "E0", "F", "Nd", "I1", "Re", "Ot", "It", "E1", "Nc", "Rd", "T",
    "Oe", "Ie", "Nb", "Rc", "Od", "E2", "Id", "W1", "Rb", "Oc", "Ic", "Ob",
    "Ib", "Vf", "Nf", "Rf", "Of", "If", "Ef", "Wf",
)


def layer_kernel(
    tokens_ref,
    seg_ref,
    gain_one_ref,
    bias_one_ref,
    w_qkv_ref,
    b_val_ref,
    w_out_hbm,
    b_out_ref,
    gain_two_ref,
    bias_two_ref,
    w_up_hbm,
    b_up_ref,
    w_down_hbm,
    b_down_ref,
    cot_ref,
    output_ref,
    tokens_grad_ref,
    vec_mid_ref,
    vec_in_ref,
    w_down_out,
    w_up_out,
    w_out_out,
    w_qkv_out,
    first_out,
    *scratch,
):
    (
        w_out_ref, w_up_ref, w_down_ref, load_sem, store_sem,
        normed_all, w_head, w_value, b_value, queries, keys, keys_zero, vals, queries_t,
        probs, gates, logit, carry, row_wide, row_acc,
        send_mix, recv_mix, send_gmix, recv_gmix, grad_rows, grad_rows_t,
        back_carry,
        send_back, recv_back, send_first, y_first, recv_first,
        lower, upper,
        unit_two_ref, rstd_two_ref,
        mixed_ref, normed_two_ref, middle_ref, out_acc, gn_acc, joined_ref,
        near_mine, near_final, near_core, near_two, near_three, near_four, near_five,
        rest_mine, rest_final, rest_core, rest_two, rest_three, rest_four, rest_five,
        out_mine, out_final, out_core, out_two, out_three, out_four, out_five,
        wkv_acc, wqq_acc, in_mine, in_core, in_x, in_final,
        extra_mine, extra_seq, extra_sum, extra_dp, extra_all,
        vec_mid_mine, vec_mid_seq, vec_mid_sum, vec_mid_dp,
        vec_in_mine, vec_in_seq, vec_in_sum, vec_in_dp,
        norm_y, norm_up, norm_down, norm_r, mix_s, mix_r, gmix_s, gmix_r,
        back_s, back_r, fback_y, fback_yr, fback_s, fback_r, extra_s, extra_r, gather_s, gather_r,
        *sums_sems, in_s, in_r, part_s, part_r, vec_s, vec_r, edp_s, edp_r,
    ) = scratch
    at = Places()
    dp_count, count, dp, me = at.dp_count, at.count, at.dp, at.me
    y, z, depth = at.y, at.z, at.depth
    rows, width = tokens_ref.shape[1], tokens_ref.shape[2]
    half, wide = rows // 2, 2 * HD
    coeff = select_weight / (rows * count)
    hidden_width = w_up_hbm.shape[1]
    pairs = width // wide
    score_scale = 1.0 / math.sqrt(HD)

    barrier = pltpu.get_barrier_semaphore()

    def greet_seq(step, carried):
        to = lax.rem(me + step, count)
        pl.semaphore_signal(barrier, inc=1, device_id=(dp, to), device_id_type=MESH)
        return carried

    def greet_dp(step, carried):
        to = lax.rem(dp + step, dp_count)
        pl.semaphore_signal(barrier, inc=1, device_id=(to, me), device_id_type=MESH)
        return carried

    lax.fori_loop(1, count, greet_seq, 0)
    lax.fori_loop(1, dp_count, greet_dp, 0)
    loads = [
        pltpu.make_async_copy(w_out_hbm, w_out_ref, load_sem.at[0]),
        pltpu.make_async_copy(w_up_hbm, w_up_ref, load_sem.at[1]),
        pltpu.make_async_copy(w_down_hbm, w_down_ref, load_sem.at[2]),
    ]
    for load in loads:
        load.start()

    def exchange(src, dst, send_sem, recv_sem, target):
        return remote(src, dst, send_sem, recv_sem, (dp, target))

    tokens = tokens_ref[0].astype(jnp.float32)
    unit, _ = normalise(tokens)
    normed_all[me] = (unit * gain_one_ref[...] + bias_one_ref[...]).astype(low)
    pl.semaphore_wait(barrier, count + dp_count - 2)

    def pass_y(block):
        return exchange(normed_all.at[block], normed_all.at[block], norm_y.at[block], norm_r.at[block], z * 2 + 1 - y)

    def pass_up(block):
        return exchange(normed_all.at[block], normed_all.at[block], norm_up.at[block], norm_r.at[block], me + 2)

    def pass_down(block):
        return exchange(normed_all.at[block], normed_all.at[block], norm_down.at[block], norm_r.at[block], me - 2)

    def arrived(block):
        exchange(normed_all.at[block], normed_all.at[block], norm_y.at[block], norm_r.at[block], block).wait_recv()

    def has_up(zz):
        return zz < depth - 1

    pl.when(has_up(z))(lambda: pass_up(me).start())
    pl.when(z > 0)(lambda: pass_down(me).start())
    pass_y(me).start()

    def relay(distance):
        def from_below():
            block = me - 2 * distance
            arrived(block)
            pl.when(has_up(z))(lambda: pass_up(block).start())
            pass_y(block).start()

        def from_above():
            block = me + 2 * distance
            arrived(block)
            pl.when(z > 0)(lambda: pass_down(block).start())
            pass_y(block).start()

        pl.when(z - distance >= 0)(from_below)
        pl.when(z + distance < depth)(from_above)

    odd_head = lax.rem(me, 2) == 1
    pair_at_lane = pl.multiple_of((me // 2) * wide, wide)

    def head_columns(part):
        columns = w_qkv_ref[:, pl.ds(part * width + pair_at_lane, wide)].astype(jnp.float32)
        return jnp.where(odd_head, swap_halves(columns), columns)

    def zero_columns(part):
        return swap_halves(w_qkv_ref[:, part * width : part * width + wide].astype(jnp.float32))

    w_head[:, :wide] = (join_heads(head_columns(0), zero_columns(0)) * score_scale).astype(low)
    w_head[:, wide:] = join_heads(head_columns(1), zero_columns(1)).astype(low)
    w_value[...] = head_columns(2).astype(low)
    bias = b_val_ref[:, pl.ds(pair_at_lane, wide)]
    b_value[...] = jnp.where(odd_head, swap_halves(bias), bias)

    ids = seg_ref[...]
    start_one = jnp.sum(jnp.where(ids < 1, 1.0, 0.0), axis=1, keepdims=True)
    start_two = jnp.sum(jnp.where(ids < 2, 1.0, 0.0), axis=1, keepdims=True)
    square = (rows, rows)
    row_at = lax.broadcasted_iota(jnp.int32, square, 0)
    col_at = lax.broadcasted_iota(jnp.int32, square, 1)
    lower[...] = jnp.where(row_at > col_at, -coeff, 0.0).astype(low)
    upper[...] = jnp.where(row_at < col_at, -coeff, 0.0).astype(low)
    lane = lax.broadcasted_iota(jnp.int32, (rows, wide), 1)

    def masks(i, j):
        query_pos = lax.broadcasted_iota(jnp.int32, (rows, 1), 0).astype(jnp.float32) + ((i - j) * rows).astype(jnp.float32)
        key_start = (j * rows).astype(jnp.float32)
        begin_one, begin_two = start_one - key_start, start_two - key_start
        begin = jnp.where(query_pos >= begin_two, begin_two, jnp.where(query_pos >= begin_one, begin_one, -key_start))
        key_pos = col_at.astype(jnp.float32)
        inside = key_pos >= begin
        return inside & (key_pos <= query_pos), inside & (key_pos < query_pos)

    def pair_at(i, j):
        return i * (i + 1) // 2 + j

    carry[...] = jnp.zeros_like(carry)
    row_wide[...] = jnp.full_like(row_wide, neg_large)

    def project(block):
        normed = normed_all[block]
        both = dot_nn(normed, w_head[...])
        query = both[:, :wide]
        queries[block] = query.astype(low)
        queries_t[block] = query.T.astype(low)
        key = both[:, wide:]
        keys[block] = jnp.where(lane < HD, key, 0.0).astype(low)
        keys_zero[block] = jnp.where(lane < HD, 0.0, key).astype(low)
        value = dot_nn(normed, w_value[...]) + b_value[...]
        vals[block] = jnp.where(lane < HD, value, jnp.where(lane < HD + 2, 1.0, 0.0)).astype(low)

    def kept_at(i):
        return pair_at(i, 0) - i // (count - 1) * (count - 2)

    def grads_at(j):
        return pair_at(count - 1, j)

    def forward_group(group, masked):
        spots = [pair_at(i, j) for i, j in group]
        zero_scores = [dot_nt(queries[i], keys_zero[j]) for i, j in group]
        scores = [dot_nt(queries[i], keys[j]) for i, j in group]
        softs, gate_rows, attends = [], [], {}
        for k, (i, j) in enumerate(group):
            score = zero_scores[k]
            soft = jnp.maximum(score, 0.0) + jnp.log(1.0 + jnp.exp(-jnp.abs(score)))
            gate = jnp.exp(score - soft)
            if k in masked:
                attends[k], select = masks(i, j)
                soft = jnp.where(select, soft, 0.0)
                gate = jnp.where(select, gate, 0.0)
            softs.append(soft.astype(low))
            gate_rows.append(gate)
        falls = [dot_nn(lower[...], soft) for soft in softs]
        for k, spot in enumerate(spots):
            gates[spot] = gate_rows[k].astype(low)
        for k, (i, j) in enumerate(group):
            forgot = falls[k] + carry[j]
            carry[j] = forgot[rows - 1 :] - coeff * softs[k][rows - 1 :].astype(jnp.float32)
            scores[k] = scores[k] + forgot
            if k in masked:
                scores[k] = jnp.where(attends[k], scores[k], neg_large)
        for k, spot in enumerate(spots):
            logit[spot] = scores[k]
        for k, (i, _) in enumerate(group):
            top = row_wide[i]
            for start in range(0, rows, wide):
                top = jnp.maximum(top, scores[k][:, start : start + wide])
            row_wide[i] = top

    def in_groups(total, act):
        def four(group, carried):
            act(group * 4, 4)
            return carried

        lax.fori_loop(0, total // 4, four, 0)
        for left in (1, 2, 3):
            pl.when(lax.rem(total, 4) == left)(lambda left=left: act(total - left, left))

    def weigh_row(i):
        top = jnp.max(row_wide[i], axis=1, keepdims=True)
        row_acc[...] = jnp.zeros_like(row_acc)

        def weigh(start, size):
            found = [jnp.exp(logit[pair_at(i, start + k)] - top).astype(low) for k in range(size)]
            added = None
            for k, prob in enumerate(found):
                product = dot_nn(prob, vals[start + k])
                added = product if added is None else added + product
            for k, prob in enumerate(found):
                probs[pair_at(i, start + k)] = prob
            row_acc[...] += added

        in_groups(i + 1, weigh)
        mixed = row_acc[...]
        inverse = 1.0 / mixed[:, HD : HD + 1]
        mixed = mixed * inverse
        logit[kept_at(i), :, :wide] = jnp.where(lane < HD, mixed, inverse)
        send_mix[i] = fold_rows(mixed).astype(low)

        @pl.when(i != me)
        def _():
            exchange(send_mix.at[i], recv_mix.at[me], mix_s.at[i], mix_r.at[me], i).start()

    upwards = 1 - z // (depth // 2)
    at_end = (z == 0) | (z == depth - 1)
    pl.when(jnp.logical_not(at_end))(functools.partial(relay, 1))

    def forward_step(step, carried):
        block = upwards * step + (1 - upwards) * (count - 1 - step)
        group = step // 2

        @pl.when(lax.rem(block, 2) != y)
        def _():
            arrived(block)
            for distance in range(1, depth):
                pl.when(at_end & (group + 1 == distance))(functools.partial(relay, distance))
                pl.when(jnp.logical_not(at_end) & (group + 2 == distance))(functools.partial(relay, distance))

        project(block)

        def group(start, size, all_masked=False):
            members = []
            for k in range(size):
                i = upwards * step + (1 - upwards) * (block + start + k)
                j = upwards * (start + k) + (1 - upwards) * block
                members.append((i, j))
            forward_group(members, range(size) if all_masked else (0, size - 1))

        last = step == count - 1
        pl.when(jnp.logical_not(last))(lambda: in_groups(step + 1, group))

        @pl.when(last)
        def _():
            def four(start, carried):
                group(start * 4, 4, True)
                return carried

            lax.fori_loop(0, count // 4, four, 0)

        pl.when(upwards == 1)(functools.partial(weigh_row, block))
        return carried

    lax.fori_loop(0, count, forward_step, 0)

    def late_weigh(i, carried):
        weigh_row(i)
        return carried

    lax.fori_loop(0, (1 - upwards) * count, late_weigh, 0)
    recv_mix[me] = send_mix[me]

    for load in loads:
        load.wait()

    def wait_mixed(step, carried):
        source = lax.rem(me + step, count)
        exchange(send_mix.at[source], recv_mix.at[source], mix_s.at[source], mix_r.at[source], source).wait_recv()
        return carried

    lax.fori_loop(1, count, wait_mixed, 0)
    for pair in range(pairs):
        even = recv_mix[2 * pair].astype(jnp.float32)
        odd = recv_mix[2 * pair + 1].astype(jnp.float32)
        columns = pl.ds(pair * wide, wide)
        mixed_ref[pl.ds(0, half), columns] = join_heads(even, swap_halves(odd)).astype(low)
        mixed_ref[pl.ds(half, half), columns] = join_heads(swap_halves(even), odd).astype(low)
    middle = tokens_ref[0].astype(jnp.float32) + dot_nn(mixed_ref[...], w_out_ref[...]) + b_out_ref[...]
    middle_ref[...] = middle
    unit, rstd = normalise(middle)
    unit_two_ref[...] = unit
    rstd_two_ref[...] = rstd
    normed_two_ref[...] = (unit * gain_two_ref[...] + bias_two_ref[...]).astype(low)
    out_acc[...] = jnp.zeros_like(out_acc)
    gn_acc[...] = jnp.zeros_like(gn_acc)
    near_sum = StagedSum(at, near_mine, near_final, (near_core, near_two, near_three, near_four, near_five), sums_sems[:4])
    rest_sum = StagedSum(at, rest_mine, rest_final, (rest_core, rest_two, rest_three, rest_four, rest_five), sums_sems[4:8])
    out_sum = StagedSum(at, out_mine, out_final, (out_core, out_two, out_three, out_four, out_five), sums_sems[8:12])
    in_sum = StagedSum(at, None, in_final, None, (None, None, in_s, in_r))
    mid_vec = VectorSum(at, vec_mid_mine, vec_mid_seq, vec_mid_sum, vec_mid_dp, vec_s, vec_r, 0)
    in_vec = VectorSum(at, vec_in_mine, vec_in_seq, vec_in_sum, vec_in_dp, vec_s, vec_r, 2)
    chunk = width
    chunks = hidden_width // chunk
    half_hidden = hidden_width // 2

    def dense(sums, base, c, carried):
        start = pl.multiple_of((base + c) * chunk, chunk)
        cols = pl.ds(start, chunk)
        hidden = dot_nn(normed_two_ref[...], w_up_ref[:, cols]) + b_up_ref[:, cols]
        cdf = exact_cdf(hidden)
        slope = cdf + hidden * jnp.exp(-0.5 * hidden * hidden) * (1.0 / math.sqrt(2.0 * math.pi))
        active = (hidden * cdf).astype(low)
        out_acc[...] += dot_nn(active, w_down_ref[cols, :])
        grad_hidden = (dot_nt(cot_ref[0], w_down_ref[cols, :]) * slope).astype(low)
        here = pl.multiple_of(c * chunk, chunk)
        sums[pl.ds(here, chunk), :] = dot_tn(active, cot_ref[0]).astype(low)
        there = pl.multiple_of(sums.shape[0] // 2 + here, 16)
        sums[pl.ds(there, chunk), :] = dot_tn(normed_two_ref[...], grad_hidden).astype(low)
        vec_mid_mine[pl.ds(base + c, 1), :] = jnp.sum(grad_hidden.astype(jnp.float32), axis=0, keepdims=True)
        gn_acc[...] += dot_nt(grad_hidden, w_up_ref[:, cols])
        return carried

    lax.fori_loop(0, chunks // 2, functools.partial(dense, near_mine, 0), 0)
    near_sum.send(0)
    lax.fori_loop(0, chunks // 2, functools.partial(dense, rest_mine, chunks // 2), 0)
    rest_sum.send(0)
    near_sum.send(1)
    cot = cot_ref[0].astype(jnp.float32)
    grad = gn_acc[...]
    unit = unit_two_ref[...]
    middle = cot + normalise_back(grad, unit, rstd_two_ref[...], gain_two_ref[...])
    output_ref[0] = (middle_ref[...] + out_acc[...] + b_down_ref[...]).astype(low)
    middle_ref[...] = middle
    branch = middle.astype(low)
    for pair in range(pairs):
        back = dot_nt(branch, w_out_ref[pl.ds(pair * wide, wide), :]).astype(low).astype(jnp.float32)
        top, bottom = back[:half], back[half:]
        send_gmix[2 * pair] = join_heads(top, swap_halves(bottom)).astype(low)
        send_gmix[2 * pair + 1] = join_heads(swap_halves(top), bottom).astype(low)

    def send_grads(step, carried):
        to = lax.rem(me + step, count)
        exchange(send_gmix.at[to], recv_gmix.at[me], gmix_s.at[to], gmix_r.at[me], to).start()
        return carried

    lax.fori_loop(1, count, send_grads, 0)
    recv_gmix[me] = send_gmix[me]
    out_mine[...] = dot_tn(mixed_ref[...], branch).astype(low)
    out_sum.send(0)
    vec_mid_mine[pl.ds(chunks, 1), :] = jnp.sum(cot, axis=0, keepdims=True)
    vec_mid_mine[pl.ds(chunks + 1, 1), :] = jnp.sum(grad * unit, axis=0, keepdims=True)
    vec_mid_mine[pl.ds(chunks + 2, 1), :] = jnp.sum(grad, axis=0, keepdims=True)
    vec_mid_mine[pl.ds(chunks + 3, 1), :] = jnp.sum(branch.astype(jnp.float32), axis=0, keepdims=True)
    mid_vec.start_seq()

    def steps_of(sums):
        found = {str(stage): functools.partial(sums.send, stage) for stage in range(1, 5)}
        found["t"] = sums.turn
        found |= {"abcde"[stage]: functools.partial(sums.gather, stage) for stage in range(1, 5)}
        found["f"] = functools.partial(sums.arrive, 0)
        return found

    acts = {}
    for name, sums in (("N", near_sum), ("R", rest_sum), ("O", out_sum), ("I", in_sum)):
        acts |= {name + step: act for step, act in steps_of(sums).items()}
    acts["V1"] = mid_vec.start_dp

    def run(names):
        for name in names:
            acts[name]()

    run(before_backward)

    kv_rows = 3 * HD
    logit[pl.ds(grads_at(0), count), :kv_rows] = jnp.zeros((count, kv_rows, rows), jnp.float32)
    row_wide[...] = jnp.zeros_like(row_wide)
    back_carry[...] = jnp.zeros_like(back_carry)
    wkv_acc[...] = jnp.zeros_like(wkv_acc)
    wqq_acc[...] = jnp.zeros_like(wqq_acc)

    def prepare(i):
        @pl.when(i != me)
        def _():
            exchange(send_gmix.at[i], recv_gmix.at[i], gmix_s.at[i], gmix_r.at[i], i).wait_recv()

        grad = jnp.where(lane < HD, spread_rows(recv_gmix[i].astype(jnp.float32)), 0.0)
        kept = logit[kept_at(i), :, :wide]
        inverse = kept[:, HD : HD + 1]
        delta = -jnp.sum(grad * kept, axis=1, keepdims=True) * inverse
        grad = grad * inverse
        grad_rows_t[i] = grad.T[:HD].astype(low)
        delta_high = delta.astype(low).astype(jnp.float32)
        grad = jnp.where(lane == HD, delta_high, jnp.where(lane == HD + 1, delta - delta_high, grad))
        grad_rows[i] = grad.astype(low)

    def backward_group(group):
        spots = [pair_at(i, j) for i, j in group]
        found = [probs[spot] for spot in spots]
        grads = [dot_nt(grad_rows[i], vals[j]) for i, j in group]
        grads = [(prob.astype(jnp.float32) * grad).astype(low) for prob, grad in zip(found, grads)]
        laters = [dot_nn(upper[...], grad) for grad in grads]
        gated = []
        for k, (i, j) in enumerate(group):
            later = laters[k] + back_carry[j]
            back_carry[j] = later[:1] - coeff * grads[k][:1].astype(jnp.float32)
            gated.append((later * gates[spots[k]].astype(jnp.float32)).astype(low))
        query_parts = [dot_nn(grads[k], keys[j]) + dot_nn(gated[k], keys_zero[j]) for k, (_, j) in enumerate(group)]
        key_parts = [
            (
                dot_nn(grad_rows_t[i], found[k]),
                dot_nn(queries_t[i, :HD], grads[k]),
                dot_nn(queries_t[i, HD:], gated[k]),
            )
            for k, (i, _) in enumerate(group)
        ]
        for k, (i, _) in enumerate(group):
            row_wide[i] += query_parts[k]
        for k, (_, j) in enumerate(group):
            for part in range(3):
                logit[grads_at(j), part * HD : (part + 1) * HD] += key_parts[k][part]

    def send_first_sum(i):
        exchange(send_first.at[i], y_first.at[i], fback_y.at[i], fback_yr.at[i], i).wait_recv()
        send_first[i] = (send_first[i].astype(jnp.float32) + y_first[i].astype(jnp.float32)).astype(low)

        @pl.when(i != me)
        def _():
            exchange(send_first.at[i], recv_first.at[z], fback_s.at[i], fback_r.at[z], i).start()

        @pl.when(i == me)
        def _():
            recv_first[z] = send_first[i]

    def block_of(step):
        return upwards * (count - 1 - step) + (1 - upwards) * step

    def backward_step(step, carried):
        block = block_of(step)
        pl.when(upwards == 1)(functools.partial(prepare, block))

        def group(start, size):
            members = []
            for k in range(size):
                i = upwards * block + (1 - upwards) * (count - 1 - start - k)
                j = upwards * (start + k) + (1 - upwards) * block
                members.append((i, j))
            backward_group(members)

        in_groups(count - step, group)
        flat = logit[grads_at(block), :kv_rows]
        flipped = flat[: 2 * HD].T
        first_flipped = flat[HD:].T
        grad_queries = row_wide[block] * score_scale
        send_back[block, :rows] = join_heads(grad_queries, flipped).astype(low)
        send_back[block, rows:] = fold_rows(flipped).astype(low)
        send_first[block] = join_heads(swap_halves(grad_queries), first_flipped).astype(low)

        @pl.when(block != me)
        def _():
            exchange(send_back.at[block], recv_back.at[me], back_s.at[block], back_r.at[me], block).start()

        @pl.when(lax.rem(block, 2) != y)
        def _():
            exchange(send_first.at[block], y_first.at[block], fback_y.at[block], fback_yr.at[block], z * 2 + 1 - y).start()

        normed = normed_all[block]
        wkv_acc[...] += dot_nn(flat.astype(low), normed)
        wqq_acc[...] += dot_nn(grad_queries.T.astype(low), normed)
        pl.when((step >= 2) & (lax.rem(block, 2) == y))(lambda: send_first_sum(block_of(step - 2)))
        for number, names in enumerate(between_steps):
            if names:
                pl.when(step == number)(functools.partial(run, names))
        return carried

    def prepare_all(i, carried):
        prepare(count - 1 - i)
        return carried

    lax.fori_loop(0, (1 - upwards) * count, prepare_all, 0)
    lax.fori_loop(0, count, backward_step, 0)
    recv_back[me] = send_back[me]

    piece = HD // 4
    core_half, x_half = 6 * piece, 3 * piece
    in_start = at.core * core_half
    in_core_copy = remote(rows_of(in_mine, (1 - at.core) * core_half, core_half), in_core, part_s.at[0], part_r.at[0], at.core_peer)
    in_x_copy = remote(rows_of(in_mine, in_start + (1 - at.x) * x_half, x_half), in_x, part_s.at[1], part_r.at[1], at.x_peer)
    each_seq = functools.partial(in_vec.each, count, me)
    each_dp = functools.partial(in_vec.each, dp_count, dp)

    def extra_over_seq(to, slot):
        return exchange(rows_of(extra_mine, to * piece, piece), extra_seq.at[slot], extra_s.at[to], extra_r.at[slot], to)

    def extra_gather(to, owner):
        block = rows_of(extra_all, owner * piece, piece)
        return exchange(block, block, gather_s.at[to], gather_r.at[owner], to)

    def extra_over_dp(to, slot):
        return remote(extra_sum, extra_dp.at[slot], edp_s.at[to], edp_r.at[slot], (to, me))

    def in_zero():
        for part in range(4):
            for place, (source, start) in enumerate(((wqq_acc, 0), (wkv_acc, HD), (wkv_acc, 0))):
                rows_in = pl.ds(part * 3 * piece + place * piece, piece)
                in_mine[rows_in, :] = source[start + part * piece : start + (part + 1) * piece].astype(low)
        in_core_copy.start()

    def extra_zero():
        extra_mine[:HD] = wqq_acc[HD:].astype(low)
        extra_mine[HD:] = wkv_acc[2 * HD :].astype(low)
        each_seq(lambda to: extra_over_seq(to, me).start())
        extra_seq[me] = extra_mine[pl.ds(pl.multiple_of(me * piece, 16), piece), :]

    def last_first_sums():
        for step in (count - 2, count - 1):
            pl.when(lax.rem(block_of(step), 2) == y)(functools.partial(send_first_sum, block_of(step)))

    def in_one():
        in_core_copy.wait_recv()
        add_rows(in_mine, in_start, [(in_mine, in_start), (in_core, 0)], core_half)
        in_x_copy.start()

    def in_turn():
        in_x_copy.wait_recv()
        add_rows(in_final, in_sum.give[5], [(in_mine, in_start + at.x * x_half), (in_x, 0)], x_half)
        in_sum.spread(5)

    def extra_one():
        each_seq(lambda source: extra_over_seq(source, source).wait_recv())
        summed = extra_seq[0].astype(jnp.float32)
        for k in range(1, count):
            summed = summed + extra_seq[k].astype(jnp.float32)
        extra_sum[...] = summed
        each_dp(lambda to: extra_over_dp(to, dp).start())
        extra_dp[dp] = summed

    def extra_two():
        each_dp(lambda source: extra_over_dp(source, source).wait_recv())
        summed = extra_dp[0]
        for k in range(1, dp_count):
            summed = summed + extra_dp[k]
        extra_all[pl.ds(pl.multiple_of(me * piece, 16), piece), :] = summed.astype(low)
        each_seq(lambda to: extra_gather(to, me).start())

    def wait_back(step, carried):
        source = lax.rem(me + step, count)
        exchange(send_back.at[source], recv_back.at[source], back_s.at[source], back_r.at[source], source).wait_recv()
        return carried

    def wait_first(step, carried):
        source = lax.rem(z + step, depth)
        exchange(send_first.at[source], recv_first.at[source], fback_s.at[source], fback_r.at[source], source * 2 + y).wait_recv()
        return carried

    def first_norm_back():
        lax.fori_loop(1, count, wait_back, 0)
        lax.fori_loop(1, depth, wait_first, 0)
        first_sum = recv_first[0].astype(jnp.float32)
        for source in range(1, depth):
            first_sum = first_sum + recv_first[source].astype(jnp.float32)
        for pair in range(pairs):
            even = recv_back[2 * pair, :rows].astype(jnp.float32)
            odd = recv_back[2 * pair + 1, :rows].astype(jnp.float32)
            if pair == 0:
                even = even + first_sum
            columns = wide * pair
            joined_ref[:, pl.ds(columns, wide)] = join_heads(even, swap_halves(odd)).astype(low)
            joined_ref[:, pl.ds(width + columns, wide)] = join_heads(swap_halves(even), odd).astype(low)
            even = recv_back[2 * pair, rows:].astype(jnp.float32)
            odd = recv_back[2 * pair + 1, rows:].astype(jnp.float32)
            columns = pl.ds(2 * width + columns, wide)
            joined_ref[pl.ds(0, half), columns] = join_heads(even, swap_halves(odd)).astype(low)
            joined_ref[pl.ds(half, half), columns] = join_heads(swap_halves(even), odd).astype(low)
        grad = dot_nt(joined_ref[...], w_qkv_ref[...])
        unit, rstd = normalise(tokens_ref[0].astype(jnp.float32))
        vec_in_mine[...] = jnp.zeros_like(vec_in_mine)
        vec_in_mine[pl.ds(0, 1), :] = jnp.sum(grad * unit, axis=0, keepdims=True)
        vec_in_mine[pl.ds(1, 1), :] = jnp.sum(grad, axis=0, keepdims=True)
        value_grads = joined_ref[:, pl.ds(2 * width, width)].astype(jnp.float32)
        vec_in_mine[pl.ds(2, 1), :] = jnp.sum(value_grads, axis=0, keepdims=True)
        in_vec.start_seq()
        tokens_grad_ref[0] = middle_ref[...] + normalise_back(grad, unit, rstd, gain_one_ref[...])

    stores = []

    def store(source, target):
        stores.append(pltpu.make_async_copy(source, target, store_sem.at[len(stores)]))
        stores[-1].start()

    def finish_near():
        near_sum.arrive(0)
        store(near_final.at[pl.ds(0, half_hidden)], w_down_out.at[pl.ds(0, half_hidden)])
        store(near_final.at[pl.ds(half_hidden, half_hidden)], w_up_out.at[pl.ds(0, half_hidden)])

    def finish_rest():
        rest_sum.arrive(0)
        store(rest_final.at[pl.ds(0, half_hidden)], w_down_out.at[pl.ds(half_hidden, half_hidden)])
        store(rest_final.at[pl.ds(half_hidden, half_hidden)], w_up_out.at[pl.ds(half_hidden, half_hidden)])

    def finish_out():
        out_sum.arrive(0)
        store(out_final, w_out_out)

    def finish_in():
        in_sum.arrive(0)
        store(in_final, w_qkv_out)

    def finish_extra():
        each_seq(lambda source: extra_gather(source, source).wait_recv())
        store(extra_all, first_out)

    def finish_mid_vec():
        vec_mid_ref[...] = mid_vec.finish()

    def finish_in_vec():
        vec_in_ref[...] = in_vec.finish()

    acts |= {
        "I0": in_zero, "I1": in_one, "It": in_turn, "E0": extra_zero, "E1": extra_one, "E2": extra_two,
        "F": last_first_sums, "T": first_norm_back, "W1": in_vec.start_dp, "Vf": finish_mid_vec, "Wf": finish_in_vec,
        "Nf": finish_near, "Rf": finish_rest, "Of": finish_out, "If": finish_in, "Ef": finish_extra,
    }
    run(after_backward)

    pl.when(has_up(z))(lambda: pass_up(me).wait_send())
    pl.when(z > 0)(lambda: pass_down(me).wait_send())
    pass_y(me).wait_send()
    for distance in range(1, depth):

        def below(distance=distance):
            pl.when(has_up(z))(lambda: pass_up(me - 2 * distance).wait_send())
            pass_y(me - 2 * distance).wait_send()

        def above(distance=distance):
            pl.when(z > 0)(lambda: pass_down(me + 2 * distance).wait_send())
            pass_y(me + 2 * distance).wait_send()

        pl.when(z - distance >= 0)(below)
        pl.when(z + distance < depth)(above)

    def drain(step, carried):
        to = lax.rem(me + step, count)
        exchange(send_mix.at[to], recv_mix.at[me], mix_s.at[to], mix_r.at[me], to).wait_send()
        exchange(send_gmix.at[to], recv_gmix.at[me], gmix_s.at[to], gmix_r.at[me], to).wait_send()
        exchange(send_back.at[to], recv_back.at[me], back_s.at[to], back_r.at[me], to).wait_send()
        extra_over_seq(to, me).wait_send()
        extra_gather(to, me).wait_send()
        return carried

    lax.fori_loop(1, count, drain, 0)

    def drain_first(step, carried):
        to = lax.rem(z + step, depth) * 2 + y
        exchange(send_first.at[to], recv_first.at[z], fback_s.at[to], fback_r.at[z], to).wait_send()
        return carried

    def drain_first_y(step, carried):
        to = step * 2 + 1 - y
        exchange(send_first.at[to], y_first.at[to], fback_y.at[to], fback_yr.at[to], z * 2 + 1 - y).wait_send()
        return carried

    lax.fori_loop(1, depth, drain_first, 0)
    lax.fori_loop(0, depth, drain_first_y, 0)
    each_dp(lambda to: extra_over_dp(to, dp).wait_send())
    in_core_copy.wait_send()
    in_x_copy.wait_send()
    near_sum.drain()
    rest_sum.drain()
    out_sum.drain()
    in_sum.drain(False)
    mid_vec.drain()
    in_vec.drain()
    for store in stores:
        store.wait()


def widen_kernel(
    w_down_in, w_up_in, w_out_in, w_qkv_in, first_in, w_down_out, w_up_out, w_out_out, w_qkv_out,
    down_low, up_low, out_low, qkv_low, first_low, down_wide, up_wide, out_wide, qkv_wide, load_sem, store_sem,
):
    width = out_low.shape[0]
    blocks = down_low.shape[0] // width
    loads = []
    for k, (source, target) in enumerate(
        ((w_qkv_in, qkv_low), (first_in, first_low), (w_out_in, out_low), (w_down_in, down_low), (w_up_in, up_low))
    ):
        loads.append(pltpu.make_async_copy(source, target, load_sem.at[k]))
        loads[-1].start()
    stores = []

    def store(source, target):
        stores.append(pltpu.make_async_copy(source, target, store_sem.at[len(stores)]))
        stores[-1].start()

    def convert(source, target, at, columns):
        def step(k, carried):
            here = pl.ds(pl.multiple_of(at + k * 64, 64), 64)
            there = pl.ds(pl.multiple_of(k * 64, 64), 64)
            if columns is None:
                target[here, :] = source[here, :].astype(jnp.float32)
            else:
                target[there, pl.ds(columns, width)] = source[here, :].astype(jnp.float32)
            return carried

        lax.fori_loop(0, width // 64, step, 0)

    loads[0].wait()
    loads[1].wait()
    piece = HD // 4
    wide = 2 * HD
    for part in range(3):
        for pair in range(width // wide):
            found = []
            for head in (2 * pair, 2 * pair + 1):
                z, y = head // 2, head % 2
                for owner in range(4):
                    core, x = owner // 2, owner % 2
                    two, three = (x, y) if core == 0 else (y, x)
                    depth = width // wide
                    start = ((((core * 2 + two) * 2 + three) * depth + z % 2 * 2 + z // 2) * 3 + part) * piece
                    block = qkv_low[start : start + piece].astype(jnp.float32)
                    if head == 0 and part < 2:
                        at = part * HD + owner * piece
                        block = block + first_low[at : at + piece].astype(jnp.float32)
                    found.append(block)
            columns = part * width + pair * wide
            qkv_wide[:, columns : columns + wide] = jnp.concatenate(found, axis=0).T
    store(qkv_wide, w_qkv_out)
    loads[2].wait()
    convert(out_low, out_wide, 0, None)
    store(out_wide, w_out_out)
    loads[3].wait()
    for block in range(blocks):
        convert(down_low, down_wide, block * width, None)
        here = pl.ds(block * width, width)
        store(down_wide.at[here], w_down_out.at[here])
    loads[4].wait()
    for block in range(blocks):
        convert(up_low, up_wide, block * width, block * width)
        here = pl.ds(block * width, width)
        store(up_wide.at[:, here], w_up_out.at[:, here])
    for one in stores:
        one.wait()


def exchange_heads(
    tokens, segment_ids, gain_one, bias_one, w_qkv, b_val, w_out, b_out,
    gain_two, bias_two, w_up, b_up, w_down, b_down, cotangent,
):
    count, dp_count = lax.axis_size("seq"), lax.axis_size("dp")
    rows, width = tokens.shape[1], tokens.shape[2]
    hidden = w_up.shape[1]
    half = rows // 2
    tiles = count * (count + 1) // 2
    wide = 2 * HD
    f32 = jnp.float32
    packed = rows + half
    depth = count // 2

    def vmem(*shape, dtype=low):
        return pltpu.VMEM(shape, dtype)

    def sems(*shape):
        return pltpu.SemaphoreType.DMA(shape)

    scratch = [
        vmem(width, width), vmem(width, hidden), vmem(hidden, width), sems(3), sems(8),
        vmem(count, rows, width), vmem(width, 2 * wide), vmem(width, wide), vmem(1, wide, dtype=f32),
        vmem(count, rows, wide), vmem(count, rows, wide), vmem(count, rows, wide), vmem(count, rows, wide), vmem(count, wide, rows),
        vmem(tiles, rows, rows), vmem(tiles, rows, rows), vmem(tiles, rows, rows, dtype=f32),
        vmem(count, 1, rows, dtype=f32), vmem(count, rows, wide, dtype=f32), vmem(rows, wide, dtype=f32),
        vmem(count, half, wide), vmem(count, half, wide), vmem(count, half, wide), vmem(count, half, wide), vmem(count, rows, wide), vmem(count, HD, rows),
        vmem(count, 1, rows, dtype=f32),
        vmem(count, packed, wide), vmem(count, packed, wide), vmem(count, rows, wide), vmem(count, rows, wide), vmem(depth, rows, wide),
        vmem(rows, rows), vmem(rows, rows),
        vmem(rows, width, dtype=f32), vmem(rows, 1, dtype=f32),
        vmem(rows, width), vmem(rows, width), vmem(rows, width, dtype=f32), vmem(rows, width, dtype=f32), vmem(rows, width, dtype=f32), vmem(rows, 3 * width),
    ]
    for total in (hidden, hidden, width):
        scratch += [vmem(total, width), vmem(total, width)]
        scratch += [vmem(total >> stage, width) for stage in range(1, 6)]
    scratch += [
        vmem(3 * HD, width, dtype=f32), vmem(wide, width, dtype=f32),
        vmem(3 * HD, width), vmem(3 * HD // 2, width), vmem(3 * HD // 4, width), vmem(3 * width, width),
        vmem(wide, width), vmem(count, wide // count, width), vmem(wide // count, width, dtype=f32), vmem(dp_count, wide // count, width, dtype=f32), vmem(wide, width),
    ]
    for _ in range(2):
        scratch += [vmem(8, width, dtype=f32), vmem(count, 8, width, dtype=f32), vmem(8, width, dtype=f32), vmem(dp_count, 8, width, dtype=f32)]
    scratch += [sems(count)] * 18
    scratch += [sems(5, 6)] * 14 + [sems(2), sems(2), sems(4, count), sems(4, count), sems(dp_count), sems(dp_count)]
    in_vmem = pl.BlockSpec(memory_space=pltpu.VMEM)
    anywhere = pl.BlockSpec(memory_space=pl.ANY)
    specs = [in_vmem] * 15
    for at in (6, 10, 12):
        specs[at] = anywhere
    shape = jax.ShapeDtypeStruct
    results = pl.pallas_call(
        layer_kernel,
        out_shape=[
            shape((1, rows, width), low), shape((1, rows, width), f32), shape((8, width), f32), shape((8, width), f32),
            shape((hidden, width), low), shape((hidden, width), low), shape((width, width), low), shape((3 * width, width), low), shape((wide, width), low),
        ],
        in_specs=specs,
        out_specs=[in_vmem] * 4 + [anywhere] * 5,
        scratch_shapes=scratch,
        compiler_params=pltpu.CompilerParams(
            collective_id=0, has_side_effects=True, vmem_limit_bytes=vmem_bytes
        ),
    )(
        tokens, segment_ids, gain_one[None], bias_one[None], w_qkv, b_val[None], w_out, b_out[None],
        gain_two[None], bias_two[None], w_up, b_up[None], w_down, b_down[None], cotangent,
    )
    output, tokens_grad, vec_mid, vec_in = results[:4]
    w_down_grad, w_up_grad, w_out_grad, w_qkv_grad = pl.pallas_call(
        widen_kernel,
        out_shape=[shape((hidden, width), f32), shape((width, hidden), f32), shape((width, width), f32), shape((width, 3 * width), f32)],
        in_specs=[anywhere] * 5,
        out_specs=[anywhere] * 4,
        scratch_shapes=[
            vmem(hidden, width), vmem(hidden, width), vmem(width, width), vmem(3 * width, width), vmem(wide, width),
            vmem(hidden, width, dtype=f32), vmem(width, hidden, dtype=f32), vmem(width, width, dtype=f32), vmem(width, 3 * width, dtype=f32),
            sems(5), sems(16),
        ],
        compiler_params=pltpu.CompilerParams(vmem_limit_bytes=vmem_bytes),
    )(*results[4:])
    chunks = hidden // width
    return (
        output,
        tokens_grad,
        vec_in[0],
        vec_in[1],
        w_qkv_grad,
        vec_in[2],
        w_out_grad,
        vec_mid[chunks + 3],
        vec_mid[chunks + 1],
        vec_mid[chunks + 2],
        w_up_grad,
        vec_mid[:chunks].reshape(hidden),
        w_down_grad,
        vec_mid[chunks],
    )


def picks_heads(mesh, length, width, hidden):
    dp_count, count = mesh.shape["dp"], mesh.shape["seq"]
    power = length & (length - 1) == 0
    return dp_count == 4 and count == 8 and width == count * HD and hidden == 4 * width and power


def solution(mesh):
    placed = (
        P("dp", "seq", None),
        P("dp", None),
        P(),
        P(),
        P(),
        P(),
        P(),
        P(),
        P(),
        P(),
        P(),
        P(),
        P(),
        P(),
        P("dp", "seq", None),
    )

    def layer(tokens, *others):
        width, hidden = tokens.shape[-1], others[9].shape[-1]
        length = tokens.shape[1] * mesh.shape["seq"]
        body = exchange_heads if picks_heads(mesh, length, width, hidden) else local
        return body(tokens, *others)

    return jax.shard_map(
        layer,
        mesh=mesh,
        in_specs=placed,
        out_specs=(
            P("dp", "seq", None),
            P("dp", "seq", None),
            P(),
            P(),
            P(),
            P(),
            P(),
            P(),
            P(),
            P(),
            P(),
            P(),
            P(),
            P(),
        ),
        check_vma=False,
    )
```

```python
import functools
import math

import jax
import jax.numpy as jnp
from jax import lax
from jax.experimental import pallas as pl
from jax.experimental.pallas import tpu as pltpu
from jax.sharding import PartitionSpec as P

HD = 64


norm_eps = 1e-05
select_weight = 4.0
neg_large = -1e30
highest = lax.Precision.HIGHEST
vmem_bytes = 63 * 1024 * 1024


def prefix(array, axis, combine, identity, reverse):
    length, here = (lax.axis_size(axis), lax.axis_index(axis))
    everything = lax.all_gather(array.astype(jnp.bfloat16), axis)
    start = jnp.broadcast_to(jnp.asarray(identity, array.dtype), array.shape)

    def hop(k, before):
        at = length - 1 - k if reverse else k
        reached = at > here if reverse else at < here
        new = combine(before, everything[at].astype(array.dtype))
        return jnp.where(reached, new, before)

    return lax.fori_loop(0, length, hop, start)


def layer_norm(values, norm_gain, norm_shift):
    centered = values - jnp.mean(values, axis=-1, keepdims=True)
    variance = jnp.mean(centered * centered, axis=-1, keepdims=True)
    return centered * lax.rsqrt(variance + norm_eps) * norm_gain + norm_shift


def exact_gelu(values):
    return jax.nn.gelu(values, approximate=False)


def add_arrays(earlier, later):
    return earlier + later


def keep_state(state_in):
    return state_in


def pick_block():
    return 512


def local(
    tokens,
    segment_ids,
    gain_one,
    bias_one,
    w_qkv,
    b_val,
    w_out,
    b_out,
    gain_two,
    bias_two,
    w_up,
    b_up,
    w_down,
    b_down,
    cotangent,
):
    seq_count = lax.axis_size("seq")
    seq_rank = lax.axis_index("seq")
    row_tokens = tokens[0].astype(jnp.float32)
    tok_rows = row_tokens.shape[0]
    model_width = row_tokens.shape[1]
    head_count = model_width // HD
    length = tok_rows * seq_count
    score_scale = 1.0 / math.sqrt(HD)
    select_coeff = select_weight / length
    row_segments = segment_ids[0]
    row_base = seq_rank * tok_rows
    query_pos = row_base + jnp.arange(tok_rows, dtype=jnp.int32)
    query_segs = lax.dynamic_slice_in_dim(row_segments, row_base, tok_rows)
    last_query = row_base + tok_rows - 1
    lower_mask = (jnp.arange(tok_rows)[:, None] > jnp.arange(tok_rows)[None, :]).astype(jnp.float32)
    upper_mask = lower_mask.T
    normed_one, norm_one_back = jax.vjp(layer_norm, row_tokens, gain_one, bias_one)
    normed_one_low = normed_one.astype(jnp.bfloat16)
    value_bias = jnp.concatenate([jnp.zeros((2 * model_width,), jnp.float32), b_val])
    joined_low = (
        jnp.dot(normed_one_low, w_qkv, preferred_element_type=jnp.float32) + value_bias
    ).astype(jnp.bfloat16)
    queries = joined_low[:, :model_width]
    keys_mine = joined_low[:, model_width : 2 * model_width]
    values_mine = joined_low[:, 2 * model_width :]
    query_heads = queries.reshape(tok_rows, head_count, HD)
    query_zero = queries[:, :HD]
    query_rest = query_heads[:, 1:]

    def pair_masks(key_start, key_rows):
        key_pos = key_start + jnp.arange(key_rows, dtype=jnp.int32)
        key_segs = lax.dynamic_slice_in_dim(row_segments, key_start, key_rows)
        same_doc = query_segs[:, None] == key_segs[None, :]
        attend_mask = same_doc & (key_pos[None, :] <= query_pos[:, None])
        select_mask = same_doc & (key_pos[None, :] < query_pos[:, None])
        return (attend_mask, select_mask)

    select_init = (
        jnp.zeros((tok_rows, length), jnp.float32),
        jnp.zeros((tok_rows, length), jnp.float32),
        jnp.zeros((length,), jnp.float32),
    )
    running = select_init
    key_piece = lax.all_gather(keys_mine[:, :HD], "seq", axis=0, tiled=True)
    piece_rows = key_piece.shape[0]
    block_rows = pick_block()

    def select_block(state_now, offset):
        zero_scores, local_forgot, column_sums = state_now
        key_block = lax.dynamic_slice_in_dim(key_piece, offset, block_rows)
        attend_mask, select_mask = pair_masks(offset, block_rows)
        scores = (
            jnp.einsum("qd,kd->qk", query_zero, key_block, preferred_element_type=jnp.float32)
            * score_scale
        )
        chosen = jnp.where(select_mask, jax.nn.softplus(scores), 0.0)
        forgot = jnp.dot(lower_mask, chosen, precision=highest)
        zero_scores = lax.dynamic_update_slice_in_dim(zero_scores, scores, offset, 1)
        local_forgot = lax.dynamic_update_slice_in_dim(local_forgot, forgot, offset, 1)
        column_sums = lax.dynamic_update_slice_in_dim(
            column_sums, jnp.sum(chosen, axis=0), offset, 0
        )
        return ((zero_scores, local_forgot, column_sums), None)

    offsets = jnp.arange(piece_rows // block_rows, dtype=jnp.int32) * block_rows
    running, unused = lax.scan(select_block, running, offsets)
    zero_scores, local_forgot, column_sums = running
    column_prefix = prefix(column_sums, "seq", add_arrays, jnp.zeros((length,), jnp.float32), False)
    attend_init = (
        jnp.full((head_count, tok_rows), neg_large, jnp.float32),
        jnp.zeros((head_count, tok_rows), jnp.float32),
        jnp.zeros((tok_rows, head_count, HD), jnp.float32),
    )
    running = attend_init
    attend_key_piece = lax.all_gather(keys_mine, "seq", axis=0, tiled=True)
    value_piece = lax.all_gather(values_mine, "seq", axis=0, tiled=True)
    piece_rows = attend_key_piece.shape[0]
    attend_block_rows = pick_block()

    def attend_block(state_now, offset):
        key_start = offset

        def attend_compute(state_in):
            run_max, run_total, accumulated = state_in
            key_block = lax.dynamic_slice_in_dim(
                attend_key_piece, offset, attend_block_rows
            ).reshape(attend_block_rows, head_count, HD)
            value_block = lax.dynamic_slice_in_dim(value_piece, offset, attend_block_rows).reshape(
                attend_block_rows, head_count, HD
            )
            attend_mask, select_mask = pair_masks(key_start, attend_block_rows)
            rest_scores = (
                jnp.einsum(
                    "qhd,khd->hqk", query_rest, key_block[:, 1:], preferred_element_type=jnp.float32
                )
                * score_scale
            )
            head_zero = lax.dynamic_slice_in_dim(zero_scores, key_start, attend_block_rows, 1)
            scores = jnp.concatenate([head_zero[None], rest_scores], axis=0)
            forgot = lax.dynamic_slice_in_dim(column_prefix, key_start, attend_block_rows)[
                None, :
            ] + lax.dynamic_slice_in_dim(local_forgot, key_start, attend_block_rows, 1)
            logits = jnp.where(attend_mask[None], scores - select_coeff * forgot[None], neg_large)
            new_max = jnp.maximum(run_max, jnp.max(logits, axis=-1))
            weights = jnp.where(attend_mask[None], jnp.exp(logits - new_max[:, :, None]), 0.0)
            decay_factor = jnp.exp(run_max - new_max)
            run_total = run_total * decay_factor + jnp.sum(weights, axis=-1)
            accumulated = accumulated * decay_factor.T[:, :, None] + jnp.einsum(
                "hqk,khd->qhd",
                weights.astype(jnp.bfloat16),
                value_block,
                preferred_element_type=jnp.float32,
            )
            return (new_max, run_total, accumulated)

        state_now = lax.cond(key_start <= last_query, attend_compute, keep_state, state_now)
        return (state_now, None)

    offsets = jnp.arange(piece_rows // attend_block_rows, dtype=jnp.int32) * attend_block_rows
    running, unused = lax.scan(attend_block, running, offsets)
    run_max, run_total, accumulated = running
    log_total = run_max + jnp.log(run_total)
    mixed_float = accumulated / run_total.T[:, :, None]
    mixed_low = mixed_float.reshape(tok_rows, model_width).astype(jnp.bfloat16)
    middle = row_tokens + jnp.dot(mixed_low, w_out, preferred_element_type=jnp.float32) + b_out
    normed_two, norm_two_back = jax.vjp(layer_norm, middle, gain_two, bias_two)
    normed_two_low = normed_two.astype(jnp.bfloat16)
    hidden = jnp.dot(normed_two_low, w_up, preferred_element_type=jnp.float32) + b_up
    active, gelu_back = jax.vjp(exact_gelu, hidden)
    active_low = active.astype(jnp.bfloat16)
    output = middle + jnp.dot(active_low, w_down, preferred_element_type=jnp.float32) + b_down
    grad_out = cotangent[0]
    grad_float = grad_out.astype(jnp.float32)
    w_down_grad = jnp.einsum("tf,td->fd", active_low, grad_out, preferred_element_type=jnp.float32)
    b_down_grad = jnp.sum(grad_float, axis=0)
    grad_active = jnp.einsum("td,fd->tf", grad_out, w_down, preferred_element_type=jnp.float32)
    (grad_hidden,) = gelu_back(grad_active)
    grad_hidden_low = grad_hidden.astype(jnp.bfloat16)
    w_up_grad = jnp.einsum(
        "td,tf->df", normed_two_low, grad_hidden_low, preferred_element_type=jnp.float32
    )
    b_up_grad = jnp.sum(grad_hidden_low.astype(jnp.float32), axis=0)
    grad_normed_two = jnp.einsum(
        "tf,df->td", grad_hidden_low, w_up, preferred_element_type=jnp.float32
    )
    grad_middle_norm, gain_two_grad, bias_two_grad = norm_two_back(grad_normed_two)
    grad_middle = grad_float + grad_middle_norm
    grad_branch_low = grad_middle.astype(jnp.bfloat16)
    w_out_grad = jnp.einsum(
        "td,te->de", mixed_low, grad_branch_low, preferred_element_type=jnp.float32
    )
    b_out_grad = jnp.sum(grad_branch_low.astype(jnp.float32), axis=0)
    grad_mixed_low = jnp.einsum(
        "te,de->td", grad_branch_low, w_out, preferred_element_type=jnp.float32
    ).astype(jnp.bfloat16)
    grad_mixed_heads = grad_mixed_low.reshape(tok_rows, head_count, HD)
    row_delta = jnp.sum(grad_mixed_heads.astype(jnp.float32) * mixed_float, axis=-1).T
    keys_back, values_back = (
        lax.all_gather(keys_mine, "seq", axis=0, tiled=True),
        lax.all_gather(values_mine, "seq", axis=0, tiled=True),
    )
    back_rows = pick_block()
    key_heads = keys_back.reshape(length, head_count, HD)
    value_heads = values_back.reshape(length, head_count, HD)

    def grad_block(state_now, offset):

        def grad_compute(state_in):
            query_grad, key_grad, value_grad, first_part, second_part, grad_cols = state_in
            key_block = lax.dynamic_slice_in_dim(key_heads, offset, back_rows)
            value_block = lax.dynamic_slice_in_dim(value_heads, offset, back_rows)
            attend_mask, select_mask = pair_masks(offset, back_rows)
            scores = (
                jnp.einsum(
                    "qhd,khd->hqk", query_heads, key_block, preferred_element_type=jnp.float32
                )
                * score_scale
            )
            chosen = jnp.where(select_mask, jax.nn.softplus(scores[0]), 0.0)
            forgot = lax.dynamic_slice_in_dim(column_prefix, offset, back_rows)[None, :] + jnp.dot(
                lower_mask, chosen, precision=highest
            )
            logits = scores - select_coeff * forgot[None]
            prob_block = jnp.where(attend_mask[None], jnp.exp(logits - log_total[:, :, None]), 0.0)
            grad_probs = jnp.einsum(
                "qhd,khd->hqk", grad_mixed_heads, value_block, preferred_element_type=jnp.float32
            )
            grad_logits = prob_block * (grad_probs - row_delta[:, :, None])
            value_part = jnp.einsum(
                "hqk,qhd->khd",
                prob_block.astype(jnp.bfloat16),
                grad_mixed_heads,
                preferred_element_type=jnp.float32,
            )
            rest_low = grad_logits[1:].astype(jnp.bfloat16)
            query_grad = (
                query_grad
                + jnp.einsum(
                    "hqk,khd->qhd", rest_low, key_block[:, 1:], preferred_element_type=jnp.float32
                )
                * score_scale
            )
            key_part = (
                jnp.einsum("hqk,qhd->khd", rest_low, query_rest, preferred_element_type=jnp.float32)
                * score_scale
            )
            total_grad = jnp.sum(grad_logits, axis=0)
            suffix_local = jnp.dot(upper_mask, total_grad, precision=highest)
            select_gate = jnp.where(select_mask, select_coeff * jax.nn.sigmoid(scores[0]), 0.0)
            first_part = lax.dynamic_update_slice_in_dim(
                first_part, grad_logits[0] - select_gate * suffix_local, offset, 1
            )
            second_part = lax.dynamic_update_slice_in_dim(second_part, select_gate, offset, 1)
            key_grad = lax.dynamic_update_slice_in_dim(key_grad, key_part, offset, 0)
            value_grad = lax.dynamic_update_slice_in_dim(value_grad, value_part, offset, 0)
            grad_cols = lax.dynamic_update_slice_in_dim(
                grad_cols, jnp.sum(total_grad, axis=0), offset, 0
            )
            return (query_grad, key_grad, value_grad, first_part, second_part, grad_cols)

        state_now = lax.cond(offset <= last_query, grad_compute, keep_state, state_now)
        return (state_now, None)

    grad_init = (
        jnp.zeros((tok_rows, head_count - 1, HD), jnp.float32),
        jnp.zeros((length, head_count - 1, HD), jnp.float32),
        jnp.zeros((length, head_count, HD), jnp.float32),
        jnp.zeros((tok_rows, length), jnp.float32),
        jnp.zeros((tok_rows, length), jnp.float32),
        jnp.zeros((length,), jnp.float32),
    )
    back_offsets = jnp.arange(length // back_rows, dtype=jnp.int32) * back_rows
    grad_state, unused = lax.scan(grad_block, grad_init, back_offsets)
    query_grad, key_grad, value_grad, first_part, second_part, grad_cols = grad_state
    grad_suffix = prefix(grad_cols, "seq", add_arrays, jnp.zeros((length,), jnp.float32), True)
    zero_grad_low = (first_part - second_part * grad_suffix[None, :]).astype(jnp.bfloat16)
    query_zero_grad = (
        jnp.dot(zero_grad_low, keys_back[:, :HD], preferred_element_type=jnp.float32) * score_scale
    )
    key_zero_grad = (
        jnp.einsum("ql,qd->ld", zero_grad_low, query_zero, preferred_element_type=jnp.float32)
        * score_scale
    )
    key_total = jnp.concatenate([key_zero_grad[:, None, :], key_grad], axis=1).reshape(
        length, model_width
    )
    value_total = value_grad.reshape(length, model_width)
    key_mine_grad, value_mine_grad = (
        lax.psum_scatter(
            key_total.astype(jnp.bfloat16), "seq", scatter_dimension=0, tiled=True
        ).astype(jnp.float32),
        lax.psum_scatter(
            value_total.astype(jnp.bfloat16), "seq", scatter_dimension=0, tiled=True
        ).astype(jnp.float32),
    )
    query_total = jnp.concatenate([query_zero_grad[:, None, :], query_grad], axis=1).reshape(
        tok_rows, model_width
    )
    grad_joined_low = jnp.concatenate([query_total, key_mine_grad, value_mine_grad], axis=1).astype(
        jnp.bfloat16
    )
    b_val_grad = jnp.sum(grad_joined_low[:, 2 * model_width :].astype(jnp.float32), axis=0)
    w_qkv_grad = jnp.einsum(
        "td,te->de", normed_one_low, grad_joined_low, preferred_element_type=jnp.float32
    )
    grad_normed_one = jnp.einsum(
        "te,de->td", grad_joined_low, w_qkv, preferred_element_type=jnp.float32
    )
    grad_tokens_norm, gain_one_grad, bias_one_grad = norm_one_back(grad_normed_one)
    tokens_grad = grad_middle + grad_tokens_norm
    summed = lax.psum(
        (
            gain_one_grad,
            bias_one_grad,
            w_qkv_grad,
            b_val_grad,
            w_out_grad,
            b_out_grad,
            gain_two_grad,
            bias_two_grad,
            w_up_grad,
            b_up_grad,
            w_down_grad,
            b_down_grad,
        ),
        ("dp", "seq"),
    )
    return (
        output.astype(jnp.bfloat16)[None],
        tokens_grad[None],
        summed[0],
        summed[1],
        summed[2],
        summed[3],
        summed[4],
        summed[5],
        summed[6],
        summed[7],
        summed[8],
        summed[9],
        summed[10],
        summed[11],
    )


low = jnp.bfloat16
MESH = pl.DeviceIdType.MESH


def dot_nn(left, right):
    return lax.dot_general(left, right, (((1,), (0,)), ((), ())), preferred_element_type=jnp.float32)


def dot_nt(left, right):
    return lax.dot_general(left, right, (((1,), (1,)), ((), ())), preferred_element_type=jnp.float32)


def dot_tn(left, right):
    return lax.dot_general(left, right, (((0,), (0,)), ((), ())), preferred_element_type=jnp.float32)


def swap_halves(wide):
    return pltpu.roll(wide, HD, 1)


def left_lanes(shape):
    return lax.broadcasted_iota(jnp.int32, shape, 1) < HD


def join_heads(left, right):
    return jnp.where(left_lanes(left.shape), left, right)


def fold_rows(wide):
    half = wide.shape[0] // 2
    return join_heads(wide[:half], swap_halves(wide[half:]))


def spread_rows(folded):
    return jnp.concatenate([folded, swap_halves(folded)], axis=0)


def exact_cdf(values):
    return 0.5 * (1.0 + lax.erf(values * (1.0 / math.sqrt(2.0))))


def normalise(values):
    centered = values - jnp.mean(values, axis=-1, keepdims=True)
    rstd = lax.rsqrt(jnp.mean(centered * centered, axis=-1, keepdims=True) + norm_eps)
    return centered * rstd, rstd


def normalise_back(grad, unit, rstd, gain):
    scaled = grad * gain
    mean_one = jnp.mean(scaled, axis=-1, keepdims=True)
    mean_two = jnp.mean(scaled * unit, axis=-1, keepdims=True)
    return rstd * (scaled - mean_one - unit * mean_two)


def rows_of(ref, at, size):
    return ref.at[pl.ds(pl.multiple_of(at, 16), size)]


def wait_all(like, sem):
    pltpu.make_async_copy(like, like, sem).wait()


def add_rows(into, into_at, parts, size):
    piece = next(rows for rows in (64, 48, 32, 16) if size % rows == 0)

    def step(k, carried):
        summed = None
        for ref, at in parts:
            block = ref[pl.ds(pl.multiple_of(at + k * piece, 16), piece), :].astype(jnp.float32)
            summed = block if summed is None else summed + block
        into[pl.ds(pl.multiple_of(into_at + k * piece, 16), piece), :] = summed.astype(low)
        return carried

    lax.fori_loop(0, size // piece, step, 0)


class Places:
    def __init__(self):
        self.dp_count, self.count = lax.axis_size("dp"), lax.axis_size("seq")
        self.dp, self.me = lax.axis_index("dp"), lax.axis_index("seq")
        self.core, self.x = lax.rem(self.dp, 2), self.dp // 2
        self.y, self.z = lax.rem(self.me, 2), self.me // 2
        self.depth = self.count // 2
        self.core_peer = (self.dp + 1 - 2 * self.core, self.me)
        self.x_peer = (self.dp + 2 - 4 * self.x, self.me)
        self.y_peer = (self.dp, self.me + 1 - 2 * self.y)
        along_x = 1 - self.core
        self.two_peer = (self.dp + along_x * (2 - 4 * self.x), self.me + (1 - along_x) * (1 - 2 * self.y))
        self.three_peer = (self.dp + (1 - along_x) * (2 - 4 * self.x), self.me + along_x * (1 - 2 * self.y))
        self.two_bit = along_x * self.x + (1 - along_x) * self.y
        self.three_bit = (1 - along_x) * self.x + along_x * self.y
        self.z_low, self.z_high = lax.rem(self.z, 2), self.z // 2
        self.z_near = (self.dp, self.me + 2 * (1 - 2 * self.z_low))
        self.z_far = (self.dp, self.me + 4 * (1 - 2 * self.z_high))


def remote(src, dst, send_sem, recv_sem, target):
    return pltpu.make_async_remote_copy(
        src_ref=src, dst_ref=dst, send_sem=send_sem, recv_sem=recv_sem, device_id=target, device_id_type=MESH
    )


class StagedSum:
    def __init__(self, at, x_first, mine, final, got, sems):
        self.mine, self.final, self.got = mine, final, got
        if x_first:
            bits = (at.core, at.x, at.y, at.z_low, at.z_high)
            self.peers = (at.core_peer, at.x_peer, at.y_peer, at.z_near, at.z_far)
        else:
            bits = (at.core, at.two_bit, at.three_bit, at.z_low, at.z_high)
            self.peers = (at.core_peer, at.two_peer, at.three_peer, at.z_near, at.z_far)
        self.stages = len(bits)
        self.down_s, self.down_r, self.up_s, self.up_r = sems
        self.total = final.shape[0]
        start, size = 0, self.total
        self.keep, self.give, self.size = [], [], []
        for bit in bits:
            size //= 2
            self.keep.append(start + bit * size)
            self.give.append(start + (1 - bit) * size)
            self.size.append(size)
            start = start + bit * size
        self.give.append(start)
        self.size.append(size)

    def down(self, stage, block):
        if stage == 0:
            source, there, size = self.give[0], 0, self.size[0]
        else:
            there, size = self.give[block] - self.keep[stage], self.size[block]
            source = self.give[stage] + there
        return remote(
            rows_of(self.mine, source, size), rows_of(self.got[stage], there, size),
            self.down_s.at[0], self.down_r.at[block - 1], self.peers[stage],
        )

    def up(self, stage, block):
        here = rows_of(self.final, self.give[block], self.size[block])
        return remote(here, here, self.up_s.at[0], self.up_r.at[stage], self.peers[stage])

    def blocks(self, stage):
        return (1,) if stage == 0 else range(stage + 1, self.stages + 1)

    def send(self, stage):
        if stage > 0:
            self.collect(stage, self.mine)
        for block in self.blocks(stage):
            self.down(stage, block).start()

    def collect(self, block, into):
        parts = [(self.mine, self.give[block])]
        for stage in range(block):
            parts.append((self.got[stage], self.give[block] - self.keep[stage]))
        came = self.size[0] if block == 1 else (block - 1) * self.size[block]
        wait_all(self.final.at[pl.ds(0, came)], self.down_r.at[block - 1])
        add_rows(into, self.give[block], parts, self.size[block])

    def turn(self):
        self.collect(self.stages, self.final)
        self.spread(self.stages)

    def spread(self, block):
        for stage in reversed(range(block)):
            self.up(stage, block).start()

    def arrive(self, stage):
        wait_all(rows_of(self.final, self.give[stage], self.size[stage]), self.up_r.at[stage])

    def gather(self, stage):
        self.arrive(stage)
        self.spread(stage)

    def drain(self):
        left = self.final.at[pl.ds(0, self.total - self.size[-1])]
        if self.mine is not None:
            wait_all(left, self.down_s.at[0])
        wait_all(left, self.up_s.at[0])


class VectorSum:
    def __init__(self, at, mine, seq_got, seq_sum, dp_got, send_sem, recv_sem, base):
        self.at, self.mine, self.seq_got, self.seq_sum, self.dp_got = at, mine, seq_got, seq_sum, dp_got
        self.send_sem, self.recv_sem, self.base = send_sem, recv_sem, base

    def over_seq(self, to):
        at = self.at
        return remote(
            self.mine, self.seq_got.at[at.me], self.send_sem.at[self.base], self.recv_sem.at[self.base], (at.dp, to)
        )

    def over_dp(self, to):
        at = self.at
        return remote(
            self.seq_sum, self.dp_got.at[at.dp], self.send_sem.at[self.base + 1], self.recv_sem.at[self.base + 1],
            (to, at.me),
        )

    def each(self, count, mine, act):
        def step(k, carried):
            act(lax.rem(mine + k, count))
            return carried

        lax.fori_loop(1, count, step, 0)

    def start_seq(self):
        at = self.at
        self.each(at.count, at.me, lambda to: self.over_seq(to).start())
        self.seq_got[at.me] = self.mine[...]

    def start_dp(self):
        at = self.at
        wait_all(self.seq_got.at[pl.ds(0, at.count - 1)], self.recv_sem.at[self.base])
        summed = self.seq_got[0]
        for k in range(1, at.count):
            summed = summed + self.seq_got[k]
        self.seq_sum[...] = summed
        self.each(at.dp_count, at.dp, lambda to: self.over_dp(to).start())
        self.dp_got[at.dp] = summed

    def finish(self):
        at = self.at
        wait_all(self.dp_got.at[pl.ds(0, at.dp_count - 1)], self.recv_sem.at[self.base + 1])
        summed = self.dp_got[0]
        for k in range(1, at.dp_count):
            summed = summed + self.dp_got[k]
        return summed

    def drain(self):
        wait_all(self.seq_got.at[pl.ds(0, self.at.count - 1)], self.send_sem.at[self.base])
        wait_all(self.dp_got.at[pl.ds(0, self.at.dp_count - 1)], self.send_sem.at[self.base + 1])


before_backward = ("N2", "R1")
within_steps = (
    (),
    (),
    (),
    (),
)
between_steps = (
    ("B0", "N3"),
    ("B1", "R2", "O1"),
    ("B2", "F0", "N4"),
    ("B3", "F1", "R3", "O2"),
    ("B4", "F2", "Nt"),
    ("B5", "F3", "R4", "V1", "O3"),
    ("B6", "F4", "Ne"),
    ("B7", "F5", "Rt", "O4"),
)
after_backward = (
    "I0", "E0", "F6", "F7", "Nd", "I1", "Re", "Ot", "It", "E1", "Nc", "Rd",
    "T", "Oe", "Ie", "Nb", "Rc", "Od", "E2", "Id", "W1", "Rb", "Oc", "Ic",
    "Ob", "Ib", "Vf", "Nf", "Rf", "Of", "If", "Ef", "Wf",
)

near_x, rest_x, out_x = False, False, False


def layer_kernel(
    tokens_ref,
    seg_ref,
    gain_one_ref,
    bias_one_ref,
    w_qkv_ref,
    b_val_ref,
    w_out_hbm,
    b_out_ref,
    gain_two_ref,
    bias_two_ref,
    w_up_hbm,
    b_up_ref,
    w_down_hbm,
    b_down_ref,
    cot_ref,
    output_ref,
    tokens_grad_ref,
    vec_mid_ref,
    vec_in_ref,
    w_down_out,
    w_up_out,
    w_out_out,
    w_qkv_out,
    first_out,
    *scratch,
):
    (
        w_out_ref, w_up_ref, w_down_ref, load_sem, store_sem,
        normed_all, w_head, w_value, b_value, queries, keys, keys_zero, vals, queries_t,
        probs, gates, logit, carry, row_wide, row_acc,
        send_mix, recv_mix, send_gmix, recv_gmix, grad_rows, grad_rows_t,
        back_carry,
        send_back, recv_back, send_first, y_first, recv_first,
        lower, upper,
        unit_two_ref, rstd_two_ref,
        mixed_ref, normed_two_ref, middle_ref, out_acc, gn_acc, joined_ref,
        near_mine, near_final, near_core, near_two, near_three, near_four, near_five,
        rest_mine, rest_final, rest_core, rest_two, rest_three, rest_four, rest_five,
        out_mine, out_final, out_core, out_two, out_three, out_four, out_five,
        wkv_acc, wqq_acc, in_mine, in_core, in_x, in_final,
        extra_mine, extra_seq, extra_sum, extra_dp, extra_all,
        vec_mid_mine, vec_mid_seq, vec_mid_sum, vec_mid_dp,
        vec_in_mine, vec_in_seq, vec_in_sum, vec_in_dp,
        norm_s, norm_r, mix_s, mix_r, gmix_s, gmix_r,
        back_s, back_r, fback_y, fback_yr, fback_s, fback_r, extra_s, extra_r,
        *sums_sems, in_s, in_r, part_s, part_r, vec_s, vec_r,
    ) = scratch
    at = Places()
    dp_count, count, dp, me = at.dp_count, at.count, at.dp, at.me
    y, z, depth = at.y, at.z, at.depth
    rows, width = tokens_ref.shape[1], tokens_ref.shape[2]
    half, wide = rows // 2, 2 * HD
    coeff = select_weight / (rows * count)
    hidden_width = w_up_hbm.shape[1]
    pairs = width // wide
    score_scale = 1.0 / math.sqrt(HD)

    barrier = pltpu.get_barrier_semaphore()

    def greet_seq(step, carried):
        to = lax.rem(me + step, count)
        pl.semaphore_signal(barrier, inc=1, device_id=(dp, to), device_id_type=MESH)
        return carried

    def greet_dp(step, carried):
        to = lax.rem(dp + step, dp_count)
        pl.semaphore_signal(barrier, inc=1, device_id=(to, me), device_id_type=MESH)
        return carried

    lax.fori_loop(1, count, greet_seq, 0)
    lax.fori_loop(1, dp_count, greet_dp, 0)
    loads = [
        pltpu.make_async_copy(w_out_hbm, w_out_ref, load_sem.at[0]),
        pltpu.make_async_copy(w_up_hbm, w_up_ref, load_sem.at[1]),
        pltpu.make_async_copy(w_down_hbm, w_down_ref, load_sem.at[2]),
    ]
    for load in loads:
        load.start()

    def exchange(src, dst, send_sem, recv_sem, target):
        return remote(src, dst, send_sem, recv_sem, (dp, target))

    tokens = tokens_ref[0].astype(jnp.float32)
    unit, _ = normalise(tokens)
    normed_all[me] = (unit * gain_one_ref[...] + bias_one_ref[...]).astype(low)
    pl.semaphore_wait(barrier, count + dp_count - 2)

    def pass_y(block):
        return exchange(normed_all.at[block], normed_all.at[block], norm_s.at[0], norm_r.at[block], z * 2 + 1 - y)

    def pass_up(block):
        return exchange(normed_all.at[block], normed_all.at[block], norm_s.at[1], norm_r.at[block], me + 2)

    def pass_down(block):
        return exchange(normed_all.at[block], normed_all.at[block], norm_s.at[2], norm_r.at[block], me - 2)

    def arrived(block):
        wait_all(normed_all.at[block], norm_r.at[block])

    def has_up(zz):
        return zz < depth - 1

    pl.when(has_up(z))(lambda: pass_up(me).start())
    pl.when(z > 0)(lambda: pass_down(me).start())
    pass_y(me).start()

    def relay(distance):
        def from_below():
            block = me - 2 * distance
            arrived(block)
            pl.when(has_up(z))(lambda: pass_up(block).start())
            pass_y(block).start()

        def from_above():
            block = me + 2 * distance
            arrived(block)
            pl.when(z > 0)(lambda: pass_down(block).start())
            pass_y(block).start()

        pl.when(z - distance >= 0)(from_below)
        pl.when(z + distance < depth)(from_above)

    odd_head = lax.rem(me, 2) == 1
    pair_at_lane = pl.multiple_of((me // 2) * wide, wide)

    def head_columns(part):
        columns = w_qkv_ref[:, pl.ds(part * width + pair_at_lane, wide)].astype(jnp.float32)
        return jnp.where(odd_head, swap_halves(columns), columns)

    def zero_columns(part):
        return swap_halves(w_qkv_ref[:, part * width : part * width + wide].astype(jnp.float32))

    w_head[:, :wide] = (join_heads(head_columns(0), zero_columns(0)) * score_scale).astype(low)
    w_head[:, wide:] = join_heads(head_columns(1), zero_columns(1)).astype(low)
    w_value[...] = head_columns(2).astype(low)
    bias = b_val_ref[:, pl.ds(pair_at_lane, wide)]
    b_value[...] = jnp.where(odd_head, swap_halves(bias), bias)

    ids = seg_ref[...]
    start_one = jnp.sum(jnp.where(ids < 1, 1.0, 0.0), axis=1, keepdims=True)
    start_two = jnp.sum(jnp.where(ids < 2, 1.0, 0.0), axis=1, keepdims=True)
    square = (rows, rows)
    row_at = lax.broadcasted_iota(jnp.int32, square, 0)
    col_at = lax.broadcasted_iota(jnp.int32, square, 1)
    lower[...] = jnp.where(row_at > col_at, -coeff, 0.0).astype(low)
    upper[...] = jnp.where(row_at < col_at, -coeff, 0.0).astype(low)
    lane = lax.broadcasted_iota(jnp.int32, (rows, wide), 1)

    def masks(i, j):
        query_pos = lax.broadcasted_iota(jnp.int32, (rows, 1), 0).astype(jnp.float32) + ((i - j) * rows).astype(jnp.float32)
        key_start = (j * rows).astype(jnp.float32)
        begin_one, begin_two = start_one - key_start, start_two - key_start
        begin = jnp.where(query_pos >= begin_two, begin_two, jnp.where(query_pos >= begin_one, begin_one, -key_start))
        key_pos = col_at.astype(jnp.float32)
        inside = key_pos >= begin
        return inside & (key_pos <= query_pos), inside & (key_pos < query_pos)

    def pair_at(i, j):
        return i * (i + 1) // 2 + j

    carry[...] = jnp.zeros_like(carry)
    row_wide[...] = jnp.full_like(row_wide, neg_large)

    def project(block):
        normed = normed_all[block]
        both = dot_nn(normed, w_head[...])
        query = both[:, :wide]
        queries[block] = query.astype(low)
        queries_t[block] = query.T.astype(low)
        key = both[:, wide:]
        keys[block] = jnp.where(lane < HD, key, 0.0).astype(low)
        keys_zero[block] = jnp.where(lane < HD, 0.0, key).astype(low)
        value = dot_nn(normed, w_value[...]) + b_value[...]
        vals[block] = jnp.where(lane < HD, value, jnp.where(lane < HD + 2, 1.0, 0.0)).astype(low)

    def kept_at(i):
        return pair_at(i, 0) - i // (count - 1) * (count - 2)

    def grads_at(j):
        return pair_at(count - 1, j)

    def forward_group(group, masked):
        spots = [pair_at(i, j) for i, j in group]
        zero_scores = [dot_nt(queries[i], keys_zero[j]) for i, j in group]
        scores = [dot_nt(queries[i], keys[j]) for i, j in group]
        softs, gate_rows, attends = [], [], {}
        for k, (i, j) in enumerate(group):
            score = zero_scores[k]
            soft = jnp.maximum(score, 0.0) + jnp.log(1.0 + jnp.exp(-jnp.abs(score)))
            gate = jnp.exp(score - soft)
            if k in masked:
                attends[k], select = masks(i, j)
                soft = jnp.where(select, soft, 0.0)
                gate = jnp.where(select, gate, 0.0)
            softs.append(soft.astype(low))
            gate_rows.append(gate)
        falls = [dot_nn(lower[...], soft) for soft in softs]
        for k, spot in enumerate(spots):
            gates[spot] = gate_rows[k].astype(low)
        for k, (i, j) in enumerate(group):
            forgot = falls[k] + carry[j]
            carry[j] = forgot[rows - 1 :] - coeff * softs[k][rows - 1 :].astype(jnp.float32)
            scores[k] = scores[k] + forgot
            if k in masked:
                scores[k] = jnp.where(attends[k], scores[k], neg_large)
        for k, spot in enumerate(spots):
            logit[spot] = scores[k]
        for k, (i, _) in enumerate(group):
            top = row_wide[i]
            for start in range(0, rows, wide):
                top = jnp.maximum(top, scores[k][:, start : start + wide])
            row_wide[i] = top

    def in_groups(total, act, after_four=None):
        def four(group, carried):
            act(group * 4, 4)
            if after_four is not None:
                pl.when((group == 0) & (total > 4))(after_four)
            return carried

        lax.fori_loop(0, total // 4, four, 0)
        for left in (1, 2, 3):
            pl.when(lax.rem(total, 4) == left)(lambda left=left: act(total - left, left))

    def weigh_row(i):
        top = jnp.max(row_wide[i], axis=1, keepdims=True)
        row_acc[...] = jnp.zeros_like(row_acc)

        def weigh(start, size):
            found = [jnp.exp(logit[pair_at(i, start + k)] - top).astype(low) for k in range(size)]
            added = None
            for k, prob in enumerate(found):
                product = dot_nn(prob, vals[start + k])
                added = product if added is None else added + product
            for k, prob in enumerate(found):
                probs[pair_at(i, start + k)] = prob
            row_acc[...] += added

        in_groups(i + 1, weigh)
        mixed = row_acc[...]
        inverse = 1.0 / mixed[:, HD : HD + 1]
        mixed = mixed * inverse
        logit[kept_at(i), :, :wide] = jnp.where(lane < HD, mixed, inverse)
        send_mix[i] = fold_rows(mixed).astype(low)

        @pl.when(i != me)
        def _():
            exchange(send_mix.at[i], recv_mix.at[me], mix_s.at[0], mix_r.at[0], i).start()

    upwards = 1 - z // (depth // 2)
    at_end = (z == 0) | (z == depth - 1)
    pl.when(jnp.logical_not(at_end))(functools.partial(relay, 1))

    def forward_step(step, carried):
        block = upwards * step + (1 - upwards) * (count - 1 - step)
        group = step // 2

        @pl.when(lax.rem(block, 2) != y)
        def _():
            arrived(block)
            for distance in range(1, depth):
                pl.when(at_end & (group + 1 == distance))(functools.partial(relay, distance))
                pl.when(jnp.logical_not(at_end) & (group + 2 == distance))(functools.partial(relay, distance))

        project(block)

        def group(start, size, all_masked=False):
            members = []
            for k in range(size):
                i = upwards * step + (1 - upwards) * (block + start + k)
                j = upwards * (start + k) + (1 - upwards) * block
                members.append((i, j))
            forward_group(members, range(size) if all_masked else (0, size - 1))

        last = step == count - 1
        pl.when(jnp.logical_not(last))(lambda: in_groups(step + 1, group))

        @pl.when(last)
        def _():
            def four(start, carried):
                group(start * 4, 4, True)
                return carried

            lax.fori_loop(0, count // 4, four, 0)

        pl.when(upwards == 1)(functools.partial(weigh_row, block))
        return carried

    lax.fori_loop(0, count, forward_step, 0)

    def late_weigh(i, carried):
        weigh_row(i)
        return carried

    lax.fori_loop(0, (1 - upwards) * count, late_weigh, 0)
    recv_mix[me] = send_mix[me]

    for load in loads:
        load.wait()

    wait_all(recv_mix.at[pl.ds(0, count - 1)], mix_r.at[0])
    for pair in range(pairs):
        even = recv_mix[2 * pair].astype(jnp.float32)
        odd = recv_mix[2 * pair + 1].astype(jnp.float32)
        columns = pl.ds(pair * wide, wide)
        mixed_ref[pl.ds(0, half), columns] = join_heads(even, swap_halves(odd)).astype(low)
        mixed_ref[pl.ds(half, half), columns] = join_heads(swap_halves(even), odd).astype(low)
    middle = tokens_ref[0].astype(jnp.float32) + dot_nn(mixed_ref[...], w_out_ref[...]) + b_out_ref[...]
    middle_ref[...] = middle
    unit, rstd = normalise(middle)
    unit_two_ref[...] = unit
    rstd_two_ref[...] = rstd
    normed_two_ref[...] = (unit * gain_two_ref[...] + bias_two_ref[...]).astype(low)
    out_acc[...] = jnp.zeros_like(out_acc)
    gn_acc[...] = jnp.zeros_like(gn_acc)
    near_sum = StagedSum(at, near_x, near_mine, near_final, (near_core, near_two, near_three, near_four, near_five), sums_sems[:4])
    rest_sum = StagedSum(at, rest_x, rest_mine, rest_final, (rest_core, rest_two, rest_three, rest_four, rest_five), sums_sems[4:8])
    out_sum = StagedSum(at, out_x, out_mine, out_final, (out_core, out_two, out_three, out_four, out_five), sums_sems[8:12])
    in_sum = StagedSum(at, False, None, in_final, None, (None, None, in_s, in_r))
    mid_vec = VectorSum(at, vec_mid_mine, vec_mid_seq, vec_mid_sum, vec_mid_dp, vec_s, vec_r, 0)
    in_vec = VectorSum(at, vec_in_mine, vec_in_seq, vec_in_sum, vec_in_dp, vec_s, vec_r, 2)
    chunk = width
    chunks = hidden_width // chunk
    half_hidden = hidden_width // 2

    def dense(sums, base, c, carried):
        start = pl.multiple_of((base + c) * chunk, chunk)
        cols = pl.ds(start, chunk)
        hidden = dot_nn(normed_two_ref[...], w_up_ref[:, cols]) + b_up_ref[:, cols]
        cdf = exact_cdf(hidden)
        slope = cdf + hidden * jnp.exp(-0.5 * hidden * hidden) * (1.0 / math.sqrt(2.0 * math.pi))
        active = (hidden * cdf).astype(low)
        out_acc[...] += dot_nn(active, w_down_ref[cols, :])
        grad_hidden = (dot_nt(cot_ref[0], w_down_ref[cols, :]) * slope).astype(low)
        here = pl.multiple_of(c * chunk, chunk)
        sums[pl.ds(here, chunk), :] = dot_tn(active, cot_ref[0]).astype(low)
        there = pl.multiple_of(sums.shape[0] // 2 + here, 16)
        sums[pl.ds(there, chunk), :] = dot_tn(normed_two_ref[...], grad_hidden).astype(low)
        vec_mid_mine[pl.ds(base + c, 1), :] = jnp.sum(grad_hidden.astype(jnp.float32), axis=0, keepdims=True)
        gn_acc[...] += dot_nt(grad_hidden, w_up_ref[:, cols])
        return carried

    lax.fori_loop(0, chunks // 2, functools.partial(dense, near_mine, 0), 0)
    near_sum.send(0)
    lax.fori_loop(0, chunks // 2, functools.partial(dense, rest_mine, chunks // 2), 0)
    rest_sum.send(0)
    near_sum.send(1)
    cot = cot_ref[0].astype(jnp.float32)
    grad = gn_acc[...]
    unit = unit_two_ref[...]
    middle = cot + normalise_back(grad, unit, rstd_two_ref[...], gain_two_ref[...])
    output_ref[0] = (middle_ref[...] + out_acc[...] + b_down_ref[...]).astype(low)
    middle_ref[...] = middle
    branch = middle.astype(low)
    for pair in range(pairs):
        back = dot_nt(branch, w_out_ref[pl.ds(pair * wide, wide), :]).astype(low).astype(jnp.float32)
        top, bottom = back[:half], back[half:]
        send_gmix[2 * pair] = join_heads(top, swap_halves(bottom)).astype(low)
        send_gmix[2 * pair + 1] = join_heads(swap_halves(top), bottom).astype(low)

    def send_grads(step, carried):
        to = lax.rem(me + step, count)
        exchange(send_gmix.at[to], recv_gmix.at[me], gmix_s.at[0], gmix_r.at[me], to).start()
        return carried

    lax.fori_loop(1, count, send_grads, 0)
    recv_gmix[me] = send_gmix[me]
    out_mine[...] = dot_tn(mixed_ref[...], branch).astype(low)
    out_sum.send(0)
    vec_mid_mine[pl.ds(chunks, 1), :] = jnp.sum(cot, axis=0, keepdims=True)
    vec_mid_mine[pl.ds(chunks + 1, 1), :] = jnp.sum(grad * unit, axis=0, keepdims=True)
    vec_mid_mine[pl.ds(chunks + 2, 1), :] = jnp.sum(grad, axis=0, keepdims=True)
    vec_mid_mine[pl.ds(chunks + 3, 1), :] = jnp.sum(branch.astype(jnp.float32), axis=0, keepdims=True)
    mid_vec.start_seq()

    def steps_of(sums):
        found = {str(stage): functools.partial(sums.send, stage) for stage in range(1, 5)}
        found["t"] = sums.turn
        found |= {"abcde"[stage]: functools.partial(sums.gather, stage) for stage in range(1, 5)}
        found["f"] = functools.partial(sums.arrive, 0)
        return found

    acts = {}
    for name, sums in (("N", near_sum), ("R", rest_sum), ("O", out_sum), ("I", in_sum)):
        acts |= {name + step: act for step, act in steps_of(sums).items()}
    acts["V1"] = mid_vec.start_dp

    def run(names):
        for name in names:
            acts[name]()

    run(before_backward)

    kv_rows = 3 * HD
    logit[pl.ds(grads_at(0), count), :kv_rows] = jnp.zeros((count, kv_rows, rows), jnp.float32)
    row_wide[...] = jnp.zeros_like(row_wide)
    back_carry[...] = jnp.zeros_like(back_carry)
    wkv_acc[...] = jnp.zeros_like(wkv_acc)
    wqq_acc[...] = jnp.zeros_like(wqq_acc)

    def prepare(i):
        @pl.when(i != me)
        def _():
            wait_all(recv_gmix.at[i], gmix_r.at[i])

        grad = jnp.where(lane < HD, spread_rows(recv_gmix[i].astype(jnp.float32)), 0.0)
        kept = logit[kept_at(i), :, :wide]
        inverse = kept[:, HD : HD + 1]
        delta = -jnp.sum(grad * kept, axis=1, keepdims=True) * inverse
        grad = grad * inverse
        grad_rows_t[i] = grad.T[:HD].astype(low)
        delta_high = delta.astype(low).astype(jnp.float32)
        grad = jnp.where(lane == HD, delta_high, jnp.where(lane == HD + 1, delta - delta_high, grad))
        grad_rows[i] = grad.astype(low)

    def backward_group(group):
        spots = [pair_at(i, j) for i, j in group]
        found = [probs[spot] for spot in spots]
        grads = [dot_nt(grad_rows[i], vals[j]) for i, j in group]
        grads = [(prob.astype(jnp.float32) * grad).astype(low) for prob, grad in zip(found, grads)]
        laters = [dot_nn(upper[...], grad) for grad in grads]
        gated = []
        for k, (i, j) in enumerate(group):
            later = laters[k] + back_carry[j]
            back_carry[j] = later[:1] - coeff * grads[k][:1].astype(jnp.float32)
            gated.append((later * gates[spots[k]].astype(jnp.float32)).astype(low))
        query_parts = [dot_nn(grads[k], keys[j]) + dot_nn(gated[k], keys_zero[j]) for k, (_, j) in enumerate(group)]
        key_parts = [
            (
                dot_nn(grad_rows_t[i], found[k]),
                dot_nn(queries_t[i, :HD], grads[k]),
                dot_nn(queries_t[i, HD:], gated[k]),
            )
            for k, (i, _) in enumerate(group)
        ]
        for k, (i, _) in enumerate(group):
            row_wide[i] += query_parts[k]
        for k, (_, j) in enumerate(group):
            for part in range(3):
                logit[grads_at(j), part * HD : (part + 1) * HD] += key_parts[k][part]

    def send_first_sum(i):
        wait_all(y_first.at[i], fback_yr.at[i])
        send_first[i] = (send_first[i].astype(jnp.float32) + y_first[i].astype(jnp.float32)).astype(low)

        @pl.when(i != me)
        def _():
            exchange(send_first.at[i], recv_first.at[z], fback_s.at[0], fback_r.at[0], i).start()

        @pl.when(i == me)
        def _():
            recv_first[z] = send_first[i]

    def block_of(step):
        return upwards * (count - 1 - step) + (1 - upwards) * step

    def send_home(step):
        block = block_of(step)

        @pl.when(block != me)
        def _():
            exchange(send_back.at[block], recv_back.at[me], back_s.at[0], back_r.at[0], block).start()

        @pl.when(lax.rem(block, 2) != y)
        def _():
            exchange(send_first.at[block], y_first.at[block], fback_y.at[0], fback_yr.at[block], z * 2 + 1 - y).start()

    def send_first_home(step):
        block = block_of(step)
        pl.when(lax.rem(block, 2) == y)(functools.partial(send_first_sum, block))

    for step in range(count):
        acts[f"B{step}"] = functools.partial(send_home, step)
        acts[f"F{step}"] = functools.partial(send_first_home, step)

    def between(step, number, names):
        if names:
            pl.when(step == number)(functools.partial(run, names))

    def backward_step(step, carried):
        block = block_of(step)
        pl.when(upwards == 1)(functools.partial(prepare, block))

        def group(start, size):
            members = []
            for k in range(size):
                i = upwards * block + (1 - upwards) * (count - 1 - start - k)
                j = upwards * (start + k) + (1 - upwards) * block
                members.append((i, j))
            backward_group(members)

        def half_way():
            for number, names in enumerate(within_steps):
                between(step, number, names)

        in_groups(count - step, group, half_way)
        flat = logit[grads_at(block), :kv_rows]
        flipped = flat[: 2 * HD].T
        first_flipped = flat[HD:].T
        grad_queries = row_wide[block] * score_scale
        send_back[block, :rows] = join_heads(grad_queries, flipped).astype(low)
        send_back[block, rows:] = fold_rows(flipped).astype(low)
        send_first[block] = join_heads(swap_halves(grad_queries), first_flipped).astype(low)

        normed = normed_all[block]
        wkv_acc[...] += dot_nn(flat.astype(low), normed)
        wqq_acc[...] += dot_nn(grad_queries.T.astype(low), normed)
        for number, names in enumerate(between_steps):
            between(step, number, names)
        return carried

    def prepare_all(i, carried):
        prepare(count - 1 - i)
        return carried

    lax.fori_loop(0, (1 - upwards) * count, prepare_all, 0)
    lax.fori_loop(0, count, backward_step, 0)
    recv_back[me] = send_back[me]

    piece = HD // 4
    core_half, x_half = 6 * piece, 3 * piece
    in_start = at.core * core_half
    in_core_copy = remote(rows_of(in_mine, (1 - at.core) * core_half, core_half), in_core, part_s.at[0], part_r.at[0], at.core_peer)
    in_x_copy = remote(rows_of(in_mine, in_start + (1 - at.x) * x_half, x_half), in_x, part_s.at[1], part_r.at[1], at.x_peer)
    each_seq = functools.partial(in_vec.each, count, me)
    each_dp = functools.partial(in_vec.each, dp_count, dp)

    def extra_over_seq(to):
        return exchange(rows_of(extra_mine, to * piece, piece), extra_seq.at[me], extra_s.at[0], extra_r.at[0], to)

    def extra_over_dp(to):
        return remote(extra_sum, extra_dp.at[dp], extra_s.at[1], extra_r.at[1], (to, me))

    def extra_gather(to):
        block = rows_of(extra_all, me * piece, piece)
        return exchange(block, block, extra_s.at[2], extra_r.at[2], to)

    def in_zero():
        for part in range(4):
            for place, (source, start) in enumerate(((wqq_acc, 0), (wkv_acc, HD), (wkv_acc, 0))):
                rows_in = pl.ds(part * 3 * piece + place * piece, piece)
                in_mine[rows_in, :] = source[start + part * piece : start + (part + 1) * piece].astype(low)
        in_core_copy.start()

    def extra_zero():
        extra_mine[:HD] = wqq_acc[HD:].astype(low)
        extra_mine[HD:] = wkv_acc[2 * HD :].astype(low)
        each_seq(lambda to: extra_over_seq(to).start())
        extra_seq[me] = extra_mine[pl.ds(pl.multiple_of(me * piece, 16), piece), :]

    def in_one():
        in_core_copy.wait_recv()
        add_rows(in_mine, in_start, [(in_mine, in_start), (in_core, 0)], core_half)
        in_x_copy.start()

    def in_turn():
        in_x_copy.wait_recv()
        add_rows(in_final, in_sum.give[5], [(in_mine, in_start + at.x * x_half), (in_x, 0)], x_half)
        in_sum.spread(5)

    def extra_one():
        wait_all(extra_seq.at[pl.ds(0, count - 1)], extra_r.at[0])
        summed = extra_seq[0].astype(jnp.float32)
        for k in range(1, count):
            summed = summed + extra_seq[k].astype(jnp.float32)
        extra_sum[...] = summed
        each_dp(lambda to: extra_over_dp(to).start())
        extra_dp[dp] = summed

    def extra_two():
        wait_all(extra_dp.at[pl.ds(0, dp_count - 1)], extra_r.at[1])
        summed = extra_dp[0]
        for k in range(1, dp_count):
            summed = summed + extra_dp[k]
        extra_all[pl.ds(pl.multiple_of(me * piece, 16), piece), :] = summed.astype(low)
        each_seq(lambda to: extra_gather(to).start())

    def first_norm_back():
        wait_all(recv_back.at[pl.ds(0, count - 1)], back_r.at[0])
        wait_all(recv_first.at[pl.ds(0, depth - 1)], fback_r.at[0])
        first_sum = recv_first[0].astype(jnp.float32)
        for source in range(1, depth):
            first_sum = first_sum + recv_first[source].astype(jnp.float32)
        for pair in range(pairs):
            even = recv_back[2 * pair, :rows].astype(jnp.float32)
            odd = recv_back[2 * pair + 1, :rows].astype(jnp.float32)
            if pair == 0:
                even = even + first_sum
            columns = wide * pair
            joined_ref[:, pl.ds(columns, wide)] = join_heads(even, swap_halves(odd)).astype(low)
            joined_ref[:, pl.ds(width + columns, wide)] = join_heads(swap_halves(even), odd).astype(low)
            even = recv_back[2 * pair, rows:].astype(jnp.float32)
            odd = recv_back[2 * pair + 1, rows:].astype(jnp.float32)
            columns = pl.ds(2 * width + columns, wide)
            joined_ref[pl.ds(0, half), columns] = join_heads(even, swap_halves(odd)).astype(low)
            joined_ref[pl.ds(half, half), columns] = join_heads(swap_halves(even), odd).astype(low)
        grad = dot_nt(joined_ref[...], w_qkv_ref[...])
        unit, rstd = normalise(tokens_ref[0].astype(jnp.float32))
        vec_in_mine[...] = jnp.zeros_like(vec_in_mine)
        vec_in_mine[pl.ds(0, 1), :] = jnp.sum(grad * unit, axis=0, keepdims=True)
        vec_in_mine[pl.ds(1, 1), :] = jnp.sum(grad, axis=0, keepdims=True)
        value_grads = joined_ref[:, pl.ds(2 * width, width)].astype(jnp.float32)
        vec_in_mine[pl.ds(2, 1), :] = jnp.sum(value_grads, axis=0, keepdims=True)
        in_vec.start_seq()
        tokens_grad_ref[0] = middle_ref[...] + normalise_back(grad, unit, rstd, gain_one_ref[...])

    stores = []

    def store(source, target):
        stores.append(pltpu.make_async_copy(source, target, store_sem.at[len(stores)]))
        stores[-1].start()

    def finish_near():
        near_sum.arrive(0)
        store(near_final.at[pl.ds(0, half_hidden)], w_down_out.at[pl.ds(0, half_hidden)])
        store(near_final.at[pl.ds(half_hidden, half_hidden)], w_up_out.at[pl.ds(0, half_hidden)])

    def finish_rest():
        rest_sum.arrive(0)
        store(rest_final.at[pl.ds(0, half_hidden)], w_down_out.at[pl.ds(half_hidden, half_hidden)])
        store(rest_final.at[pl.ds(half_hidden, half_hidden)], w_up_out.at[pl.ds(half_hidden, half_hidden)])

    def finish_out():
        out_sum.arrive(0)
        store(out_final, w_out_out)

    def finish_in():
        in_sum.arrive(0)
        store(in_final, w_qkv_out)

    def finish_extra():
        wait_all(extra_all.at[pl.ds(0, (count - 1) * piece)], extra_r.at[2])
        store(extra_all, first_out)

    def finish_mid_vec():
        vec_mid_ref[...] = mid_vec.finish()

    def finish_in_vec():
        vec_in_ref[...] = in_vec.finish()

    acts |= {
        "I0": in_zero, "I1": in_one, "It": in_turn, "E0": extra_zero, "E1": extra_one, "E2": extra_two,
        "T": first_norm_back, "W1": in_vec.start_dp, "Vf": finish_mid_vec, "Wf": finish_in_vec,
        "Nf": finish_near, "Rf": finish_rest, "Of": finish_out, "If": finish_in, "Ef": finish_extra,
    }
    run(after_backward)

    wait_all(normed_all.at[pl.ds(0, depth)], norm_s.at[0])
    for at_z in range(depth - 1):
        went = normed_all.at[pl.ds(0, at_z + 1)]
        pl.when(z == at_z)(functools.partial(wait_all, went, norm_s.at[1]))
        pl.when(z == depth - 1 - at_z)(functools.partial(wait_all, went, norm_s.at[2]))
    wait_all(send_mix.at[pl.ds(0, count - 1)], mix_s.at[0])
    wait_all(send_gmix.at[pl.ds(0, count - 1)], gmix_s.at[0])
    wait_all(send_back.at[pl.ds(0, count - 1)], back_s.at[0])
    wait_all(send_first.at[pl.ds(0, depth)], fback_y.at[0])
    wait_all(send_first.at[pl.ds(0, depth - 1)], fback_s.at[0])
    wait_all(extra_seq.at[pl.ds(0, count - 1)], extra_s.at[0])
    wait_all(extra_dp.at[pl.ds(0, dp_count - 1)], extra_s.at[1])
    wait_all(extra_all.at[pl.ds(0, (count - 1) * piece)], extra_s.at[2])
    in_core_copy.wait_send()
    in_x_copy.wait_send()
    near_sum.drain()
    rest_sum.drain()
    out_sum.drain()
    in_sum.drain()
    mid_vec.drain()
    in_vec.drain()
    for store in stores:
        store.wait()


def widen_kernel(
    w_down_in, w_up_in, w_out_in, w_qkv_in, first_in, w_down_out, w_up_out, w_out_out, w_qkv_out,
    down_low, up_low, out_low, qkv_low, first_low, down_wide, up_wide, out_wide, qkv_wide, load_sem, store_sem,
):
    width = out_low.shape[0]
    blocks = down_low.shape[0] // width
    loads = []
    for k, (source, target) in enumerate(
        ((w_qkv_in, qkv_low), (first_in, first_low), (w_out_in, out_low), (w_down_in, down_low), (w_up_in, up_low))
    ):
        loads.append(pltpu.make_async_copy(source, target, load_sem.at[k]))
        loads[-1].start()
    stores = []

    def store(source, target):
        stores.append(pltpu.make_async_copy(source, target, store_sem.at[len(stores)]))
        stores[-1].start()

    def convert(source, target, at, columns):
        def step(k, carried):
            here = pl.ds(pl.multiple_of(at + k * 64, 64), 64)
            there = pl.ds(pl.multiple_of(k * 64, 64), 64)
            if columns is None:
                target[here, :] = source[here, :].astype(jnp.float32)
            else:
                target[there, pl.ds(columns, width)] = source[here, :].astype(jnp.float32)
            return carried

        lax.fori_loop(0, width // 64, step, 0)

    loads[0].wait()
    loads[1].wait()
    piece = HD // 4
    wide = 2 * HD
    for part in range(3):
        for pair in range(width // wide):
            found = []
            for head in (2 * pair, 2 * pair + 1):
                z, y = head // 2, head % 2
                for owner in range(4):
                    core, x = owner // 2, owner % 2
                    two, three = (x, y) if core == 0 else (y, x)
                    depth = width // wide
                    start = ((((core * 2 + two) * 2 + three) * depth + z % 2 * 2 + z // 2) * 3 + part) * piece
                    block = qkv_low[start : start + piece].astype(jnp.float32)
                    if head == 0 and part < 2:
                        at = part * HD + owner * piece
                        block = block + first_low[at : at + piece].astype(jnp.float32)
                    found.append(block)
            columns = part * width + pair * wide
            qkv_wide[:, columns : columns + wide] = jnp.concatenate(found, axis=0).T
    store(qkv_wide, w_qkv_out)
    loads[2].wait()
    convert(out_low, out_wide, 0, None)
    store(out_wide, w_out_out)
    loads[3].wait()
    for block in range(blocks):
        convert(down_low, down_wide, block * width, None)
        here = pl.ds(block * width, width)
        store(down_wide.at[here], w_down_out.at[here])
    loads[4].wait()
    for block in range(blocks):
        convert(up_low, up_wide, block * width, block * width)
        here = pl.ds(block * width, width)
        store(up_wide.at[:, here], w_up_out.at[:, here])
    for one in stores:
        one.wait()


def exchange_heads(
    tokens, segment_ids, gain_one, bias_one, w_qkv, b_val, w_out, b_out,
    gain_two, bias_two, w_up, b_up, w_down, b_down, cotangent,
):
    count, dp_count = lax.axis_size("seq"), lax.axis_size("dp")
    rows, width = tokens.shape[1], tokens.shape[2]
    hidden = w_up.shape[1]
    half = rows // 2
    tiles = count * (count + 1) // 2
    wide = 2 * HD
    f32 = jnp.float32
    packed = rows + half
    depth = count // 2

    def vmem(*shape, dtype=low):
        return pltpu.VMEM(shape, dtype)

    def sems(*shape):
        return pltpu.SemaphoreType.DMA(shape)

    scratch = [
        vmem(width, width), vmem(width, hidden), vmem(hidden, width), sems(3), sems(8),
        vmem(count, rows, width), vmem(width, 2 * wide), vmem(width, wide), vmem(1, wide, dtype=f32),
        vmem(count, rows, wide), vmem(count, rows, wide), vmem(count, rows, wide), vmem(count, rows, wide), vmem(count, wide, rows),
        vmem(tiles, rows, rows), vmem(tiles, rows, rows), vmem(tiles, rows, rows, dtype=f32),
        vmem(count, 1, rows, dtype=f32), vmem(count, rows, wide, dtype=f32), vmem(rows, wide, dtype=f32),
        vmem(count, half, wide), vmem(count, half, wide), vmem(count, half, wide), vmem(count, half, wide), vmem(count, rows, wide), vmem(count, HD, rows),
        vmem(count, 1, rows, dtype=f32),
        vmem(count, packed, wide), vmem(count, packed, wide), vmem(count, rows, wide), vmem(count, rows, wide), vmem(depth, rows, wide),
        vmem(rows, rows), vmem(rows, rows),
        vmem(rows, width, dtype=f32), vmem(rows, 1, dtype=f32),
        vmem(rows, width), vmem(rows, width), vmem(rows, width, dtype=f32), vmem(rows, width, dtype=f32), vmem(rows, width, dtype=f32), vmem(rows, 3 * width),
    ]
    for total in (hidden, hidden, width):
        scratch += [vmem(total, width), vmem(total, width)]
        scratch += [vmem(total >> stage, width) for stage in range(1, 6)]
    scratch += [
        vmem(3 * HD, width, dtype=f32), vmem(wide, width, dtype=f32),
        vmem(3 * HD, width), vmem(3 * HD // 2, width), vmem(3 * HD // 4, width), vmem(3 * width, width),
        vmem(wide, width), vmem(count, wide // count, width), vmem(wide // count, width, dtype=f32), vmem(dp_count, wide // count, width, dtype=f32), vmem(wide, width),
    ]
    for _ in range(2):
        scratch += [vmem(8, width, dtype=f32), vmem(count, 8, width, dtype=f32), vmem(8, width, dtype=f32), vmem(dp_count, 8, width, dtype=f32)]
    scratch += [sems(3), sems(count), sems(1), sems(1), sems(1), sems(count)]
    scratch += [sems(1), sems(1), sems(1), sems(count), sems(1), sems(1), sems(3), sems(3)]
    scratch += [sems(1), sems(5)] * 6
    scratch += [sems(1), sems(5), sems(2), sems(2), sems(4), sems(4)]
    in_vmem = pl.BlockSpec(memory_space=pltpu.VMEM)
    anywhere = pl.BlockSpec(memory_space=pl.ANY)
    specs = [in_vmem] * 15
    for at in (6, 10, 12):
        specs[at] = anywhere
    shape = jax.ShapeDtypeStruct
    results = pl.pallas_call(
        layer_kernel,
        out_shape=[
            shape((1, rows, width), low), shape((1, rows, width), f32), shape((8, width), f32), shape((8, width), f32),
            shape((hidden, width), low), shape((hidden, width), low), shape((width, width), low), shape((3 * width, width), low), shape((wide, width), low),
        ],
        in_specs=specs,
        out_specs=[in_vmem] * 4 + [anywhere] * 5,
        scratch_shapes=scratch,
        compiler_params=pltpu.CompilerParams(
            collective_id=0, has_side_effects=True, vmem_limit_bytes=vmem_bytes
        ),
    )(
        tokens, segment_ids, gain_one[None], bias_one[None], w_qkv, b_val[None], w_out, b_out[None],
        gain_two[None], bias_two[None], w_up, b_up[None], w_down, b_down[None], cotangent,
    )
    output, tokens_grad, vec_mid, vec_in = results[:4]
    w_down_grad, w_up_grad, w_out_grad, w_qkv_grad = pl.pallas_call(
        widen_kernel,
        out_shape=[shape((hidden, width), f32), shape((width, hidden), f32), shape((width, width), f32), shape((width, 3 * width), f32)],
        in_specs=[anywhere] * 5,
        out_specs=[anywhere] * 4,
        scratch_shapes=[
            vmem(hidden, width), vmem(hidden, width), vmem(width, width), vmem(3 * width, width), vmem(wide, width),
            vmem(hidden, width, dtype=f32), vmem(width, hidden, dtype=f32), vmem(width, width, dtype=f32), vmem(width, 3 * width, dtype=f32),
            sems(5), sems(16),
        ],
        compiler_params=pltpu.CompilerParams(vmem_limit_bytes=vmem_bytes),
    )(*results[4:])
    chunks = hidden // width
    return (
        output,
        tokens_grad,
        vec_in[0],
        vec_in[1],
        w_qkv_grad,
        vec_in[2],
        w_out_grad,
        vec_mid[chunks + 3],
        vec_mid[chunks + 1],
        vec_mid[chunks + 2],
        w_up_grad,
        vec_mid[:chunks].reshape(hidden),
        w_down_grad,
        vec_mid[chunks],
    )


def picks_heads(mesh, length, width, hidden):
    dp_count, count = mesh.shape["dp"], mesh.shape["seq"]
    power = length & (length - 1) == 0
    return dp_count == 4 and count == 8 and width == count * HD and hidden == 4 * width and power


def solution(mesh):
    placed = (
        P("dp", "seq", None),
        P("dp", None),
        P(),
        P(),
        P(),
        P(),
        P(),
        P(),
        P(),
        P(),
        P(),
        P(),
        P(),
        P(),
        P("dp", "seq", None),
    )

    def layer(tokens, *others):
        width, hidden = tokens.shape[-1], others[9].shape[-1]
        length = tokens.shape[1] * mesh.shape["seq"]
        body = exchange_heads if picks_heads(mesh, length, width, hidden) else local
        return body(tokens, *others)

    return jax.shard_map(
        layer,
        mesh=mesh,
        in_specs=placed,
        out_specs=(
            P("dp", "seq", None),
            P("dp", "seq", None),
            P(),
            P(),
            P(),
            P(),
            P(),
            P(),
            P(),
            P(),
            P(),
            P(),
            P(),
            P(),
        ),
        check_vma=False,
    )
```

```python
import functools
import math

import jax
import jax.numpy as jnp
from jax import lax
from jax.experimental import pallas as pl
from jax.experimental.pallas import tpu as pltpu
from jax.sharding import PartitionSpec as P

HD = 64


norm_eps = 1e-05
select_weight = 4.0
neg_large = -1e30
highest = lax.Precision.HIGHEST
vmem_bytes = 63 * 1024 * 1024


def prefix(array, axis, combine, identity, reverse):
    length, here = (lax.axis_size(axis), lax.axis_index(axis))
    everything = lax.all_gather(array.astype(jnp.bfloat16), axis)
    start = jnp.broadcast_to(jnp.asarray(identity, array.dtype), array.shape)

    def hop(k, before):
        at = length - 1 - k if reverse else k
        reached = at > here if reverse else at < here
        new = combine(before, everything[at].astype(array.dtype))
        return jnp.where(reached, new, before)

    return lax.fori_loop(0, length, hop, start)


def layer_norm(values, norm_gain, norm_shift):
    centered = values - jnp.mean(values, axis=-1, keepdims=True)
    variance = jnp.mean(centered * centered, axis=-1, keepdims=True)
    return centered * lax.rsqrt(variance + norm_eps) * norm_gain + norm_shift


def exact_gelu(values):
    return jax.nn.gelu(values, approximate=False)


def add_arrays(earlier, later):
    return earlier + later


def keep_state(state_in):
    return state_in


def pick_block():
    return 512


def local(
    tokens,
    segment_ids,
    gain_one,
    bias_one,
    w_qkv,
    b_val,
    w_out,
    b_out,
    gain_two,
    bias_two,
    w_up,
    b_up,
    w_down,
    b_down,
    cotangent,
):
    seq_count = lax.axis_size("seq")
    seq_rank = lax.axis_index("seq")
    row_tokens = tokens[0].astype(jnp.float32)
    tok_rows = row_tokens.shape[0]
    model_width = row_tokens.shape[1]
    head_count = model_width // HD
    length = tok_rows * seq_count
    score_scale = 1.0 / math.sqrt(HD)
    select_coeff = select_weight / length
    row_segments = segment_ids[0]
    row_base = seq_rank * tok_rows
    query_pos = row_base + jnp.arange(tok_rows, dtype=jnp.int32)
    query_segs = lax.dynamic_slice_in_dim(row_segments, row_base, tok_rows)
    last_query = row_base + tok_rows - 1
    lower_mask = (jnp.arange(tok_rows)[:, None] > jnp.arange(tok_rows)[None, :]).astype(jnp.float32)
    upper_mask = lower_mask.T
    normed_one, norm_one_back = jax.vjp(layer_norm, row_tokens, gain_one, bias_one)
    normed_one_low = normed_one.astype(jnp.bfloat16)
    value_bias = jnp.concatenate([jnp.zeros((2 * model_width,), jnp.float32), b_val])
    joined_low = (
        jnp.dot(normed_one_low, w_qkv, preferred_element_type=jnp.float32) + value_bias
    ).astype(jnp.bfloat16)
    queries = joined_low[:, :model_width]
    keys_mine = joined_low[:, model_width : 2 * model_width]
    values_mine = joined_low[:, 2 * model_width :]
    query_heads = queries.reshape(tok_rows, head_count, HD)
    query_zero = queries[:, :HD]
    query_rest = query_heads[:, 1:]

    def pair_masks(key_start, key_rows):
        key_pos = key_start + jnp.arange(key_rows, dtype=jnp.int32)
        key_segs = lax.dynamic_slice_in_dim(row_segments, key_start, key_rows)
        same_doc = query_segs[:, None] == key_segs[None, :]
        attend_mask = same_doc & (key_pos[None, :] <= query_pos[:, None])
        select_mask = same_doc & (key_pos[None, :] < query_pos[:, None])
        return (attend_mask, select_mask)

    select_init = (
        jnp.zeros((tok_rows, length), jnp.float32),
        jnp.zeros((tok_rows, length), jnp.float32),
        jnp.zeros((length,), jnp.float32),
    )
    running = select_init
    key_piece = lax.all_gather(keys_mine[:, :HD], "seq", axis=0, tiled=True)
    piece_rows = key_piece.shape[0]
    block_rows = pick_block()

    def select_block(state_now, offset):
        zero_scores, local_forgot, column_sums = state_now
        key_block = lax.dynamic_slice_in_dim(key_piece, offset, block_rows)
        attend_mask, select_mask = pair_masks(offset, block_rows)
        scores = (
            jnp.einsum("qd,kd->qk", query_zero, key_block, preferred_element_type=jnp.float32)
            * score_scale
        )
        chosen = jnp.where(select_mask, jax.nn.softplus(scores), 0.0)
        forgot = jnp.dot(lower_mask, chosen, precision=highest)
        zero_scores = lax.dynamic_update_slice_in_dim(zero_scores, scores, offset, 1)
        local_forgot = lax.dynamic_update_slice_in_dim(local_forgot, forgot, offset, 1)
        column_sums = lax.dynamic_update_slice_in_dim(
            column_sums, jnp.sum(chosen, axis=0), offset, 0
        )
        return ((zero_scores, local_forgot, column_sums), None)

    offsets = jnp.arange(piece_rows // block_rows, dtype=jnp.int32) * block_rows
    running, unused = lax.scan(select_block, running, offsets)
    zero_scores, local_forgot, column_sums = running
    column_prefix = prefix(column_sums, "seq", add_arrays, jnp.zeros((length,), jnp.float32), False)
    attend_init = (
        jnp.full((head_count, tok_rows), neg_large, jnp.float32),
        jnp.zeros((head_count, tok_rows), jnp.float32),
        jnp.zeros((tok_rows, head_count, HD), jnp.float32),
    )
    running = attend_init
    attend_key_piece = lax.all_gather(keys_mine, "seq", axis=0, tiled=True)
    value_piece = lax.all_gather(values_mine, "seq", axis=0, tiled=True)
    piece_rows = attend_key_piece.shape[0]
    attend_block_rows = pick_block()

    def attend_block(state_now, offset):
        key_start = offset

        def attend_compute(state_in):
            run_max, run_total, accumulated = state_in
            key_block = lax.dynamic_slice_in_dim(
                attend_key_piece, offset, attend_block_rows
            ).reshape(attend_block_rows, head_count, HD)
            value_block = lax.dynamic_slice_in_dim(value_piece, offset, attend_block_rows).reshape(
                attend_block_rows, head_count, HD
            )
            attend_mask, select_mask = pair_masks(key_start, attend_block_rows)
            rest_scores = (
                jnp.einsum(
                    "qhd,khd->hqk", query_rest, key_block[:, 1:], preferred_element_type=jnp.float32
                )
                * score_scale
            )
            head_zero = lax.dynamic_slice_in_dim(zero_scores, key_start, attend_block_rows, 1)
            scores = jnp.concatenate([head_zero[None], rest_scores], axis=0)
            forgot = lax.dynamic_slice_in_dim(column_prefix, key_start, attend_block_rows)[
                None, :
            ] + lax.dynamic_slice_in_dim(local_forgot, key_start, attend_block_rows, 1)
            logits = jnp.where(attend_mask[None], scores - select_coeff * forgot[None], neg_large)
            new_max = jnp.maximum(run_max, jnp.max(logits, axis=-1))
            weights = jnp.where(attend_mask[None], jnp.exp(logits - new_max[:, :, None]), 0.0)
            decay_factor = jnp.exp(run_max - new_max)
            run_total = run_total * decay_factor + jnp.sum(weights, axis=-1)
            accumulated = accumulated * decay_factor.T[:, :, None] + jnp.einsum(
                "hqk,khd->qhd",
                weights.astype(jnp.bfloat16),
                value_block,
                preferred_element_type=jnp.float32,
            )
            return (new_max, run_total, accumulated)

        state_now = lax.cond(key_start <= last_query, attend_compute, keep_state, state_now)
        return (state_now, None)

    offsets = jnp.arange(piece_rows // attend_block_rows, dtype=jnp.int32) * attend_block_rows
    running, unused = lax.scan(attend_block, running, offsets)
    run_max, run_total, accumulated = running
    log_total = run_max + jnp.log(run_total)
    mixed_float = accumulated / run_total.T[:, :, None]
    mixed_low = mixed_float.reshape(tok_rows, model_width).astype(jnp.bfloat16)
    middle = row_tokens + jnp.dot(mixed_low, w_out, preferred_element_type=jnp.float32) + b_out
    normed_two, norm_two_back = jax.vjp(layer_norm, middle, gain_two, bias_two)
    normed_two_low = normed_two.astype(jnp.bfloat16)
    hidden = jnp.dot(normed_two_low, w_up, preferred_element_type=jnp.float32) + b_up
    active, gelu_back = jax.vjp(exact_gelu, hidden)
    active_low = active.astype(jnp.bfloat16)
    output = middle + jnp.dot(active_low, w_down, preferred_element_type=jnp.float32) + b_down
    grad_out = cotangent[0]
    grad_float = grad_out.astype(jnp.float32)
    w_down_grad = jnp.einsum("tf,td->fd", active_low, grad_out, preferred_element_type=jnp.float32)
    b_down_grad = jnp.sum(grad_float, axis=0)
    grad_active = jnp.einsum("td,fd->tf", grad_out, w_down, preferred_element_type=jnp.float32)
    (grad_hidden,) = gelu_back(grad_active)
    grad_hidden_low = grad_hidden.astype(jnp.bfloat16)
    w_up_grad = jnp.einsum(
        "td,tf->df", normed_two_low, grad_hidden_low, preferred_element_type=jnp.float32
    )
    b_up_grad = jnp.sum(grad_hidden_low.astype(jnp.float32), axis=0)
    grad_normed_two = jnp.einsum(
        "tf,df->td", grad_hidden_low, w_up, preferred_element_type=jnp.float32
    )
    grad_middle_norm, gain_two_grad, bias_two_grad = norm_two_back(grad_normed_two)
    grad_middle = grad_float + grad_middle_norm
    grad_branch_low = grad_middle.astype(jnp.bfloat16)
    w_out_grad = jnp.einsum(
        "td,te->de", mixed_low, grad_branch_low, preferred_element_type=jnp.float32
    )
    b_out_grad = jnp.sum(grad_branch_low.astype(jnp.float32), axis=0)
    grad_mixed_low = jnp.einsum(
        "te,de->td", grad_branch_low, w_out, preferred_element_type=jnp.float32
    ).astype(jnp.bfloat16)
    grad_mixed_heads = grad_mixed_low.reshape(tok_rows, head_count, HD)
    row_delta = jnp.sum(grad_mixed_heads.astype(jnp.float32) * mixed_float, axis=-1).T
    keys_back, values_back = (
        lax.all_gather(keys_mine, "seq", axis=0, tiled=True),
        lax.all_gather(values_mine, "seq", axis=0, tiled=True),
    )
    back_rows = pick_block()
    key_heads = keys_back.reshape(length, head_count, HD)
    value_heads = values_back.reshape(length, head_count, HD)

    def grad_block(state_now, offset):

        def grad_compute(state_in):
            query_grad, key_grad, value_grad, first_part, second_part, grad_cols = state_in
            key_block = lax.dynamic_slice_in_dim(key_heads, offset, back_rows)
            value_block = lax.dynamic_slice_in_dim(value_heads, offset, back_rows)
            attend_mask, select_mask = pair_masks(offset, back_rows)
            scores = (
                jnp.einsum(
                    "qhd,khd->hqk", query_heads, key_block, preferred_element_type=jnp.float32
                )
                * score_scale
            )
            chosen = jnp.where(select_mask, jax.nn.softplus(scores[0]), 0.0)
            forgot = lax.dynamic_slice_in_dim(column_prefix, offset, back_rows)[None, :] + jnp.dot(
                lower_mask, chosen, precision=highest
            )
            logits = scores - select_coeff * forgot[None]
            prob_block = jnp.where(attend_mask[None], jnp.exp(logits - log_total[:, :, None]), 0.0)
            grad_probs = jnp.einsum(
                "qhd,khd->hqk", grad_mixed_heads, value_block, preferred_element_type=jnp.float32
            )
            grad_logits = prob_block * (grad_probs - row_delta[:, :, None])
            value_part = jnp.einsum(
                "hqk,qhd->khd",
                prob_block.astype(jnp.bfloat16),
                grad_mixed_heads,
                preferred_element_type=jnp.float32,
            )
            rest_low = grad_logits[1:].astype(jnp.bfloat16)
            query_grad = (
                query_grad
                + jnp.einsum(
                    "hqk,khd->qhd", rest_low, key_block[:, 1:], preferred_element_type=jnp.float32
                )
                * score_scale
            )
            key_part = (
                jnp.einsum("hqk,qhd->khd", rest_low, query_rest, preferred_element_type=jnp.float32)
                * score_scale
            )
            total_grad = jnp.sum(grad_logits, axis=0)
            suffix_local = jnp.dot(upper_mask, total_grad, precision=highest)
            select_gate = jnp.where(select_mask, select_coeff * jax.nn.sigmoid(scores[0]), 0.0)
            first_part = lax.dynamic_update_slice_in_dim(
                first_part, grad_logits[0] - select_gate * suffix_local, offset, 1
            )
            second_part = lax.dynamic_update_slice_in_dim(second_part, select_gate, offset, 1)
            key_grad = lax.dynamic_update_slice_in_dim(key_grad, key_part, offset, 0)
            value_grad = lax.dynamic_update_slice_in_dim(value_grad, value_part, offset, 0)
            grad_cols = lax.dynamic_update_slice_in_dim(
                grad_cols, jnp.sum(total_grad, axis=0), offset, 0
            )
            return (query_grad, key_grad, value_grad, first_part, second_part, grad_cols)

        state_now = lax.cond(offset <= last_query, grad_compute, keep_state, state_now)
        return (state_now, None)

    grad_init = (
        jnp.zeros((tok_rows, head_count - 1, HD), jnp.float32),
        jnp.zeros((length, head_count - 1, HD), jnp.float32),
        jnp.zeros((length, head_count, HD), jnp.float32),
        jnp.zeros((tok_rows, length), jnp.float32),
        jnp.zeros((tok_rows, length), jnp.float32),
        jnp.zeros((length,), jnp.float32),
    )
    back_offsets = jnp.arange(length // back_rows, dtype=jnp.int32) * back_rows
    grad_state, unused = lax.scan(grad_block, grad_init, back_offsets)
    query_grad, key_grad, value_grad, first_part, second_part, grad_cols = grad_state
    grad_suffix = prefix(grad_cols, "seq", add_arrays, jnp.zeros((length,), jnp.float32), True)
    zero_grad_low = (first_part - second_part * grad_suffix[None, :]).astype(jnp.bfloat16)
    query_zero_grad = (
        jnp.dot(zero_grad_low, keys_back[:, :HD], preferred_element_type=jnp.float32) * score_scale
    )
    key_zero_grad = (
        jnp.einsum("ql,qd->ld", zero_grad_low, query_zero, preferred_element_type=jnp.float32)
        * score_scale
    )
    key_total = jnp.concatenate([key_zero_grad[:, None, :], key_grad], axis=1).reshape(
        length, model_width
    )
    value_total = value_grad.reshape(length, model_width)
    key_mine_grad, value_mine_grad = (
        lax.psum_scatter(
            key_total.astype(jnp.bfloat16), "seq", scatter_dimension=0, tiled=True
        ).astype(jnp.float32),
        lax.psum_scatter(
            value_total.astype(jnp.bfloat16), "seq", scatter_dimension=0, tiled=True
        ).astype(jnp.float32),
    )
    query_total = jnp.concatenate([query_zero_grad[:, None, :], query_grad], axis=1).reshape(
        tok_rows, model_width
    )
    grad_joined_low = jnp.concatenate([query_total, key_mine_grad, value_mine_grad], axis=1).astype(
        jnp.bfloat16
    )
    b_val_grad = jnp.sum(grad_joined_low[:, 2 * model_width :].astype(jnp.float32), axis=0)
    w_qkv_grad = jnp.einsum(
        "td,te->de", normed_one_low, grad_joined_low, preferred_element_type=jnp.float32
    )
    grad_normed_one = jnp.einsum(
        "te,de->td", grad_joined_low, w_qkv, preferred_element_type=jnp.float32
    )
    grad_tokens_norm, gain_one_grad, bias_one_grad = norm_one_back(grad_normed_one)
    tokens_grad = grad_middle + grad_tokens_norm
    summed = lax.psum(
        (
            gain_one_grad,
            bias_one_grad,
            w_qkv_grad,
            b_val_grad,
            w_out_grad,
            b_out_grad,
            gain_two_grad,
            bias_two_grad,
            w_up_grad,
            b_up_grad,
            w_down_grad,
            b_down_grad,
        ),
        ("dp", "seq"),
    )
    return (
        output.astype(jnp.bfloat16)[None],
        tokens_grad[None],
        summed[0],
        summed[1],
        summed[2],
        summed[3],
        summed[4],
        summed[5],
        summed[6],
        summed[7],
        summed[8],
        summed[9],
        summed[10],
        summed[11],
    )


low = jnp.bfloat16
MESH = pl.DeviceIdType.MESH


def dot_nn(left, right):
    return lax.dot_general(left, right, (((1,), (0,)), ((), ())), preferred_element_type=jnp.float32)


def dot_nt(left, right):
    return lax.dot_general(left, right, (((1,), (1,)), ((), ())), preferred_element_type=jnp.float32)


def dot_tn(left, right):
    return lax.dot_general(left, right, (((0,), (0,)), ((), ())), preferred_element_type=jnp.float32)


def swap_halves(wide):
    return pltpu.roll(wide, HD, 1)


def left_lanes(shape):
    return lax.broadcasted_iota(jnp.int32, shape, 1) < HD


def join_heads(left, right):
    return jnp.where(left_lanes(left.shape), left, right)


def fold_rows(wide):
    half = wide.shape[0] // 2
    return join_heads(wide[:half], swap_halves(wide[half:]))


def spread_rows(folded):
    return jnp.concatenate([folded, swap_halves(folded)], axis=0)


def exact_cdf(values):
    return 0.5 * (1.0 + lax.erf(values * (1.0 / math.sqrt(2.0))))


def normalise(values):
    centered = values - jnp.mean(values, axis=-1, keepdims=True)
    rstd = lax.rsqrt(jnp.mean(centered * centered, axis=-1, keepdims=True) + norm_eps)
    return centered * rstd, rstd


def normalise_back(grad, unit, rstd, gain):
    scaled = grad * gain
    mean_one = jnp.mean(scaled, axis=-1, keepdims=True)
    mean_two = jnp.mean(scaled * unit, axis=-1, keepdims=True)
    return rstd * (scaled - mean_one - unit * mean_two)


def rows_of(ref, at, size):
    return ref.at[pl.ds(pl.multiple_of(at, 16), size)]


def wait_all(like, sem):
    pltpu.make_async_copy(like, like, sem).wait()


def add_rows(into, into_at, parts, size):
    piece = next(rows for rows in (64, 48, 32, 16) if size % rows == 0)

    def step(k, carried):
        summed = None
        for ref, at in parts:
            block = ref[pl.ds(pl.multiple_of(at + k * piece, 16), piece), :].astype(jnp.float32)
            summed = block if summed is None else summed + block
        into[pl.ds(pl.multiple_of(into_at + k * piece, 16), piece), :] = summed.astype(low)
        return carried

    lax.fori_loop(0, size // piece, step, 0)


class Places:
    def __init__(self):
        self.dp_count, self.count = lax.axis_size("dp"), lax.axis_size("seq")
        self.dp, self.me = lax.axis_index("dp"), lax.axis_index("seq")
        self.core, self.x = lax.rem(self.dp, 2), self.dp // 2
        self.y, self.z = lax.rem(self.me, 2), self.me // 2
        self.depth = self.count // 2
        self.core_peer = (self.dp + 1 - 2 * self.core, self.me)
        self.x_peer = (self.dp + 2 - 4 * self.x, self.me)
        self.y_peer = (self.dp, self.me + 1 - 2 * self.y)
        along_x = 1 - self.core
        self.two_peer = (self.dp + along_x * (2 - 4 * self.x), self.me + (1 - along_x) * (1 - 2 * self.y))
        self.three_peer = (self.dp + (1 - along_x) * (2 - 4 * self.x), self.me + along_x * (1 - 2 * self.y))
        self.two_bit = along_x * self.x + (1 - along_x) * self.y
        self.three_bit = (1 - along_x) * self.x + along_x * self.y
        self.z_low, self.z_high = lax.rem(self.z, 2), self.z // 2
        self.z_near = (self.dp, self.me + 2 * (1 - 2 * self.z_low))
        self.z_far = (self.dp, self.me + 4 * (1 - 2 * self.z_high))


def remote(src, dst, send_sem, recv_sem, target):
    return pltpu.make_async_remote_copy(
        src_ref=src, dst_ref=dst, send_sem=send_sem, recv_sem=recv_sem, device_id=target, device_id_type=MESH
    )


class StagedSum:
    def __init__(self, at, x_first, mine, final, got, sems):
        self.mine, self.final, self.got = mine, final, got
        if x_first:
            bits = (at.core, at.x, at.y, at.z_low, at.z_high)
            self.peers = (at.core_peer, at.x_peer, at.y_peer, at.z_near, at.z_far)
        else:
            bits = (at.core, at.two_bit, at.three_bit, at.z_low, at.z_high)
            self.peers = (at.core_peer, at.two_peer, at.three_peer, at.z_near, at.z_far)
        self.stages = len(bits)
        self.down_s, self.down_r, self.up_s, self.up_r = sems
        self.total = final.shape[0]
        start, size = 0, self.total
        self.keep, self.give, self.size = [], [], []
        for bit in bits:
            size //= 2
            self.keep.append(start + bit * size)
            self.give.append(start + (1 - bit) * size)
            self.size.append(size)
            start = start + bit * size
        self.give.append(start)
        self.size.append(size)

    def down(self, stage, block):
        if stage == 0:
            source, there, size = self.give[0], 0, self.size[0]
        else:
            there, size = self.give[block] - self.keep[stage], self.size[block]
            source = self.give[stage] + there
        return remote(
            rows_of(self.mine, source, size), rows_of(self.got[stage], there, size),
            self.down_s.at[0], self.down_r.at[block - 1], self.peers[stage],
        )

    def up(self, stage, block):
        here = rows_of(self.final, self.give[block], self.size[block])
        return remote(here, here, self.up_s.at[0], self.up_r.at[stage], self.peers[stage])

    def blocks(self, stage):
        return (1,) if stage == 0 else range(stage + 1, self.stages + 1)

    def send(self, stage):
        if stage > 0:
            self.collect(stage, self.mine)
        for block in self.blocks(stage):
            self.down(stage, block).start()

    def collect(self, block, into):
        parts = [(self.mine, self.give[block])]
        for stage in range(block):
            parts.append((self.got[stage], self.give[block] - self.keep[stage]))
        came = self.size[0] if block == 1 else (block - 1) * self.size[block]
        wait_all(self.final.at[pl.ds(0, came)], self.down_r.at[block - 1])
        add_rows(into, self.give[block], parts, self.size[block])

    def turn(self):
        self.collect(self.stages, self.final)
        self.spread(self.stages)

    def spread(self, block):
        for stage in reversed(range(block)):
            self.up(stage, block).start()

    def arrive(self, stage):
        wait_all(rows_of(self.final, self.give[stage], self.size[stage]), self.up_r.at[stage])

    def gather(self, stage):
        self.arrive(stage)
        self.spread(stage)

    def drain(self):
        left = self.final.at[pl.ds(0, self.total - self.size[-1])]
        if self.mine is not None:
            wait_all(left, self.down_s.at[0])
        wait_all(left, self.up_s.at[0])


class VectorSum:
    def __init__(self, at, mine, seq_got, seq_sum, dp_got, send_sem, recv_sem, base):
        self.at, self.mine, self.seq_got, self.seq_sum, self.dp_got = at, mine, seq_got, seq_sum, dp_got
        self.send_sem, self.recv_sem, self.base = send_sem, recv_sem, base

    def over_seq(self, to):
        at = self.at
        return remote(
            self.mine, self.seq_got.at[at.me], self.send_sem.at[self.base], self.recv_sem.at[self.base], (at.dp, to)
        )

    def over_dp(self, to):
        at = self.at
        return remote(
            self.seq_sum, self.dp_got.at[at.dp], self.send_sem.at[self.base + 1], self.recv_sem.at[self.base + 1],
            (to, at.me),
        )

    def each(self, count, mine, act):
        def step(k, carried):
            act(lax.rem(mine + k, count))
            return carried

        lax.fori_loop(1, count, step, 0)

    def start_seq(self):
        at = self.at
        self.each(at.count, at.me, lambda to: self.over_seq(to).start())
        self.seq_got[at.me] = self.mine[...]

    def start_dp(self):
        at = self.at
        wait_all(self.seq_got.at[pl.ds(0, at.count - 1)], self.recv_sem.at[self.base])
        summed = self.seq_got[0]
        for k in range(1, at.count):
            summed = summed + self.seq_got[k]
        self.seq_sum[...] = summed
        self.each(at.dp_count, at.dp, lambda to: self.over_dp(to).start())
        self.dp_got[at.dp] = summed

    def finish(self):
        at = self.at
        wait_all(self.dp_got.at[pl.ds(0, at.dp_count - 1)], self.recv_sem.at[self.base + 1])
        summed = self.dp_got[0]
        for k in range(1, at.dp_count):
            summed = summed + self.dp_got[k]
        return summed

    def drain(self):
        wait_all(self.seq_got.at[pl.ds(0, self.at.count - 1)], self.send_sem.at[self.base])
        wait_all(self.dp_got.at[pl.ds(0, self.at.dp_count - 1)], self.send_sem.at[self.base + 1])


before_backward = ("N2", "R1")
within_steps = (
    (),
    (),
    (),
    (),
)
between_steps = (
    ("B0", "N3"),
    ("B1", "R2", "O1"),
    ("B2", "F0", "N4"),
    ("B3", "F1", "R3", "O2"),
    ("B4", "F2"),
    ("B5", "F3", "Nt", "V1"),
    ("B6", "F4", "R4", "O3"),
    ("B7", "F5"),
)
after_backward = (
    "I0", "E0", "F6", "F7", "Ne", "Rt", "O4", "I1", "Nd", "Re", "Ot", "It",
    "E1", "Nc", "Rd", "Oe", "Rc", "T", "Ie", "Nb", "Od", "E2", "Id", "W1",
    "Rb", "Oc", "Ic", "Ob", "Ib", "Vf", "Nf", "Rf", "Of", "If", "Ef", "Wf",
)

near_x, rest_x, out_x = False, False, False


def layer_kernel(
    tokens_ref,
    seg_ref,
    gain_one_ref,
    bias_one_ref,
    w_qkv_hbm,
    b_val_ref,
    w_out_hbm,
    b_out_ref,
    gain_two_ref,
    bias_two_ref,
    w_up_hbm,
    b_up_ref,
    w_down_hbm,
    b_down_ref,
    cot_hbm,
    output_ref,
    tokens_grad_ref,
    vec_mid_ref,
    vec_in_ref,
    w_down_out,
    w_up_out,
    w_out_out,
    w_qkv_out,
    first_out,
    *scratch,
):
    (
        w_out_ref, w_up_ref, w_down_ref, w_qkv_ref, cot_ref, load_sem, store_sem,
        normed_all, w_head, w_value, b_value, queries, keys, keys_zero, vals, queries_t,
        probs, gates, logit, carry, row_wide, row_acc,
        send_mix, recv_mix, send_gmix, recv_gmix, grad_rows, grad_rows_t,
        back_carry,
        send_back, recv_back, send_first, y_first, recv_first,
        lower, upper,
        unit_two_ref, rstd_two_ref,
        mixed_ref, normed_two_ref, middle_ref, out_acc, gn_acc, joined_ref,
        near_mine, near_final, near_core, near_two, near_three, near_four, near_five,
        rest_mine, rest_final, rest_core, rest_two, rest_three, rest_four, rest_five,
        out_mine, out_final, out_core, out_two, out_three, out_four, out_five,
        wkv_acc, wqq_acc, in_mine, in_core, in_x, in_final,
        extra_mine, extra_seq, extra_sum, extra_dp, extra_all,
        vec_mid_mine, vec_mid_seq, vec_mid_sum, vec_mid_dp,
        vec_in_mine, vec_in_seq, vec_in_sum, vec_in_dp,
        norm_s, norm_r, mix_s, mix_r, gmix_s, gmix_r,
        back_s, back_r, fback_y, fback_yr, fback_s, fback_r, extra_s, extra_r,
        *sums_sems, in_s, in_r, part_s, part_r, vec_s, vec_r,
    ) = scratch
    at = Places()
    dp_count, count, dp, me = at.dp_count, at.count, at.dp, at.me
    y, z, depth = at.y, at.z, at.depth
    rows, width = tokens_ref.shape[1], tokens_ref.shape[2]
    half, wide = rows // 2, 2 * HD
    coeff = select_weight / (rows * count)
    hidden_width = w_up_hbm.shape[1]
    pairs = width // wide
    score_scale = 1.0 / math.sqrt(HD)

    barrier = pltpu.get_barrier_semaphore()

    def greet_seq(step, carried):
        to = lax.rem(me + step, count)
        pl.semaphore_signal(barrier, inc=1, device_id=(dp, to), device_id_type=MESH)
        return carried

    def greet_dp(step, carried):
        to = lax.rem(dp + step, dp_count)
        pl.semaphore_signal(barrier, inc=1, device_id=(to, me), device_id_type=MESH)
        return carried

    lax.fori_loop(1, count, greet_seq, 0)
    lax.fori_loop(1, dp_count, greet_dp, 0)
    projection_load = pltpu.make_async_copy(w_qkv_hbm, w_qkv_ref, load_sem.at[3])
    projection_load.start()
    loads = [
        pltpu.make_async_copy(cot_hbm, cot_ref, load_sem.at[4]),
        pltpu.make_async_copy(w_out_hbm, w_out_ref, load_sem.at[0]),
        pltpu.make_async_copy(w_up_hbm, w_up_ref, load_sem.at[1]),
        pltpu.make_async_copy(w_down_hbm, w_down_ref, load_sem.at[2]),
    ]
    for load in loads:
        load.start()

    def exchange(src, dst, send_sem, recv_sem, target):
        return remote(src, dst, send_sem, recv_sem, (dp, target))

    tokens = tokens_ref[0].astype(jnp.float32)
    unit, _ = normalise(tokens)
    normed_all[me] = (unit * gain_one_ref[...] + bias_one_ref[...]).astype(low)
    pl.semaphore_wait(barrier, count + dp_count - 2)

    def pass_y(block):
        return exchange(normed_all.at[block], normed_all.at[block], norm_s.at[0], norm_r.at[block], z * 2 + 1 - y)

    def pass_up(block):
        return exchange(normed_all.at[block], normed_all.at[block], norm_s.at[1], norm_r.at[block], me + 2)

    def pass_down(block):
        return exchange(normed_all.at[block], normed_all.at[block], norm_s.at[2], norm_r.at[block], me - 2)

    def arrived(block):
        wait_all(normed_all.at[block], norm_r.at[block])

    def has_up(zz):
        return zz < depth - 1

    pl.when(has_up(z))(lambda: pass_up(me).start())
    pl.when(z > 0)(lambda: pass_down(me).start())
    pass_y(me).start()

    def relay(distance):
        def from_below():
            block = me - 2 * distance
            arrived(block)
            pl.when(has_up(z))(lambda: pass_up(block).start())
            pass_y(block).start()

        def from_above():
            block = me + 2 * distance
            arrived(block)
            pl.when(z > 0)(lambda: pass_down(block).start())
            pass_y(block).start()

        pl.when(z - distance >= 0)(from_below)
        pl.when(z + distance < depth)(from_above)

    projection_load.wait()

    odd_head = lax.rem(me, 2) == 1
    pair_at_lane = pl.multiple_of((me // 2) * wide, wide)

    def head_columns(part):
        columns = w_qkv_ref[:, pl.ds(part * width + pair_at_lane, wide)].astype(jnp.float32)
        return jnp.where(odd_head, swap_halves(columns), columns)

    def zero_columns(part):
        return swap_halves(w_qkv_ref[:, part * width : part * width + wide].astype(jnp.float32))

    w_head[:, :wide] = (join_heads(head_columns(0), zero_columns(0)) * score_scale).astype(low)
    w_head[:, wide:] = join_heads(head_columns(1), zero_columns(1)).astype(low)
    w_value[...] = head_columns(2).astype(low)
    bias = b_val_ref[:, pl.ds(pair_at_lane, wide)]
    b_value[...] = jnp.where(odd_head, swap_halves(bias), bias)

    ids = seg_ref[...]
    start_one = jnp.sum(jnp.where(ids < 1, 1.0, 0.0), axis=1, keepdims=True)
    start_two = jnp.sum(jnp.where(ids < 2, 1.0, 0.0), axis=1, keepdims=True)
    square = (rows, rows)
    row_at = lax.broadcasted_iota(jnp.int32, square, 0)
    col_at = lax.broadcasted_iota(jnp.int32, square, 1)
    lower[...] = jnp.where(row_at > col_at, -coeff, 0.0).astype(low)
    upper[...] = jnp.where(row_at < col_at, -coeff, 0.0).astype(low)
    lane = lax.broadcasted_iota(jnp.int32, (rows, wide), 1)

    def masks(i, j):
        query_pos = lax.broadcasted_iota(jnp.int32, (rows, 1), 0).astype(jnp.float32) + ((i - j) * rows).astype(jnp.float32)
        key_start = (j * rows).astype(jnp.float32)
        begin_one, begin_two = start_one - key_start, start_two - key_start
        begin = jnp.where(query_pos >= begin_two, begin_two, jnp.where(query_pos >= begin_one, begin_one, -key_start))
        key_pos = col_at.astype(jnp.float32)
        inside = key_pos >= begin
        return inside & (key_pos <= query_pos), inside & (key_pos < query_pos)

    def pair_at(i, j):
        return i * (i + 1) // 2 + j

    carry[...] = jnp.zeros_like(carry)
    row_wide[...] = jnp.full_like(row_wide, neg_large)

    def project(block):
        normed = normed_all[block]
        both = dot_nn(normed, w_head[...])
        query = both[:, :wide]
        queries[block] = query.astype(low)
        queries_t[block] = query.T.astype(low)
        key = both[:, wide:]
        keys[block] = jnp.where(lane < HD, key, 0.0).astype(low)
        keys_zero[block] = jnp.where(lane < HD, 0.0, key).astype(low)
        value = dot_nn(normed, w_value[...]) + b_value[...]
        vals[block] = jnp.where(lane < HD, value, jnp.where(lane < HD + 2, 1.0, 0.0)).astype(low)

    def kept_at(i):
        return pair_at(i, 0) - i // (count - 1) * (count - 2)

    def grads_at(j):
        return pair_at(count - 1, j)

    def forward_group(group, masked):
        spots = [pair_at(i, j) for i, j in group]
        zero_scores = [dot_nt(queries[i], keys_zero[j]) for i, j in group]
        scores = [dot_nt(queries[i], keys[j]) for i, j in group]
        softs, gate_rows, attends = [], [], {}
        for k, (i, j) in enumerate(group):
            score = zero_scores[k]
            soft = jnp.maximum(score, 0.0) + jnp.log(1.0 + jnp.exp(-jnp.abs(score)))
            gate = jnp.exp(score - soft)
            if k in masked:
                attends[k], select = masks(i, j)
                soft = jnp.where(select, soft, 0.0)
                gate = jnp.where(select, gate, 0.0)
            softs.append(soft.astype(low))
            gate_rows.append(gate)
        falls = [dot_nn(lower[...], soft) for soft in softs]
        for k, spot in enumerate(spots):
            gates[spot] = gate_rows[k].astype(low)
        for k, (i, j) in enumerate(group):
            forgot = falls[k] + carry[j]
            carry[j] = forgot[rows - 1 :] - coeff * softs[k][rows - 1 :].astype(jnp.float32)
            scores[k] = scores[k] + forgot
            if k in masked:
                scores[k] = jnp.where(attends[k], scores[k], neg_large)
        for k, spot in enumerate(spots):
            logit[spot] = scores[k]
        for k, (i, _) in enumerate(group):
            top = row_wide[i]
            for start in range(0, rows, wide):
                top = jnp.maximum(top, scores[k][:, start : start + wide])
            row_wide[i] = top

    def in_groups(total, act, after_four=None):
        def four(group, carried):
            act(group * 4, 4)
            if after_four is not None:
                pl.when((group == 0) & (total > 4))(after_four)
            return carried

        lax.fori_loop(0, total // 4, four, 0)
        for left in (1, 2, 3):
            pl.when(lax.rem(total, 4) == left)(lambda left=left: act(total - left, left))

    def weigh_row(i):
        top = jnp.max(row_wide[i], axis=1, keepdims=True)
        row_acc[...] = jnp.zeros_like(row_acc)

        def weigh(start, size):
            found = [jnp.exp(logit[pair_at(i, start + k)] - top).astype(low) for k in range(size)]
            added = None
            for k, prob in enumerate(found):
                product = dot_nn(prob, vals[start + k])
                added = product if added is None else added + product
            for k, prob in enumerate(found):
                probs[pair_at(i, start + k)] = prob
            row_acc[...] += added

        in_groups(i + 1, weigh)
        mixed = row_acc[...]
        inverse = 1.0 / mixed[:, HD : HD + 1]
        mixed = mixed * inverse
        logit[kept_at(i), :, :wide] = jnp.where(lane < HD, mixed, inverse)
        send_mix[i] = fold_rows(mixed).astype(low)

        @pl.when(i != me)
        def _():
            exchange(send_mix.at[i], recv_mix.at[me], mix_s.at[0], mix_r.at[0], i).start()

    upwards = 1 - z // (depth // 2)
    at_end = (z == 0) | (z == depth - 1)
    pl.when(jnp.logical_not(at_end))(functools.partial(relay, 1))

    def forward_step(step, carried):
        block = upwards * step + (1 - upwards) * (count - 1 - step)
        group = step // 2

        @pl.when(lax.rem(block, 2) != y)
        def _():
            arrived(block)
            for distance in range(1, depth):
                pl.when(at_end & (group + 1 == distance))(functools.partial(relay, distance))
                pl.when(jnp.logical_not(at_end) & (group + 2 == distance))(functools.partial(relay, distance))

        project(block)

        def group(start, size, all_masked=False):
            members = []
            for k in range(size):
                i = upwards * step + (1 - upwards) * (block + start + k)
                j = upwards * (start + k) + (1 - upwards) * block
                members.append((i, j))
            forward_group(members, range(size) if all_masked else (0, size - 1))

        last = step == count - 1
        pl.when(jnp.logical_not(last))(lambda: in_groups(step + 1, group))

        @pl.when(last)
        def _():
            def four(start, carried):
                group(start * 4, 4, True)
                return carried

            lax.fori_loop(0, count // 4, four, 0)

        pl.when(upwards == 1)(functools.partial(weigh_row, block))
        return carried

    lax.fori_loop(0, count, forward_step, 0)

    def late_weigh(i, carried):
        weigh_row(i)
        return carried

    lax.fori_loop(0, (1 - upwards) * count, late_weigh, 0)
    recv_mix[me] = send_mix[me]

    for load in loads:
        load.wait()

    wait_all(recv_mix.at[pl.ds(0, count - 1)], mix_r.at[0])
    for pair in range(pairs):
        even = recv_mix[2 * pair].astype(jnp.float32)
        odd = recv_mix[2 * pair + 1].astype(jnp.float32)
        columns = pl.ds(pair * wide, wide)
        mixed_ref[pl.ds(0, half), columns] = join_heads(even, swap_halves(odd)).astype(low)
        mixed_ref[pl.ds(half, half), columns] = join_heads(swap_halves(even), odd).astype(low)
    middle = tokens_ref[0].astype(jnp.float32) + dot_nn(mixed_ref[...], w_out_ref[...]) + b_out_ref[...]
    middle_ref[...] = middle
    unit, rstd = normalise(middle)
    unit_two_ref[...] = unit
    rstd_two_ref[...] = rstd
    normed_two_ref[...] = (unit * gain_two_ref[...] + bias_two_ref[...]).astype(low)
    out_acc[...] = jnp.zeros_like(out_acc)
    gn_acc[...] = jnp.zeros_like(gn_acc)
    near_sum = StagedSum(at, near_x, near_mine, near_final, (near_core, near_two, near_three, near_four, near_five), sums_sems[:4])
    rest_sum = StagedSum(at, rest_x, rest_mine, rest_final, (rest_core, rest_two, rest_three, rest_four, rest_five), sums_sems[4:8])
    out_sum = StagedSum(at, out_x, out_mine, out_final, (out_core, out_two, out_three, out_four, out_five), sums_sems[8:12])
    in_sum = StagedSum(at, False, None, in_final, None, (None, None, in_s, in_r))
    mid_vec = VectorSum(at, vec_mid_mine, vec_mid_seq, vec_mid_sum, vec_mid_dp, vec_s, vec_r, 0)
    in_vec = VectorSum(at, vec_in_mine, vec_in_seq, vec_in_sum, vec_in_dp, vec_s, vec_r, 2)
    chunk = width
    chunks = hidden_width // chunk
    half_hidden = hidden_width // 2

    def dense(sums, base, c, carried):
        start = pl.multiple_of((base + c) * chunk, chunk)
        cols = pl.ds(start, chunk)
        hidden = dot_nn(normed_two_ref[...], w_up_ref[:, cols]) + b_up_ref[:, cols]
        cdf = exact_cdf(hidden)
        slope = cdf + hidden * jnp.exp(-0.5 * hidden * hidden) * (1.0 / math.sqrt(2.0 * math.pi))
        active = (hidden * cdf).astype(low)
        out_acc[...] += dot_nn(active, w_down_ref[cols, :])
        grad_hidden = (dot_nt(cot_ref[0], w_down_ref[cols, :]) * slope).astype(low)
        here = pl.multiple_of(c * chunk, chunk)
        sums[pl.ds(here, chunk), :] = dot_tn(active, cot_ref[0]).astype(low)
        there = pl.multiple_of(sums.shape[0] // 2 + here, 16)
        sums[pl.ds(there, chunk), :] = dot_tn(normed_two_ref[...], grad_hidden).astype(low)
        vec_mid_mine[pl.ds(base + c, 1), :] = jnp.sum(grad_hidden.astype(jnp.float32), axis=0, keepdims=True)
        gn_acc[...] += dot_nt(grad_hidden, w_up_ref[:, cols])
        return carried

    lax.fori_loop(0, chunks // 2, functools.partial(dense, near_mine, 0), 0)
    near_sum.send(0)
    lax.fori_loop(0, chunks // 2, functools.partial(dense, rest_mine, chunks // 2), 0)
    rest_sum.send(0)
    near_sum.send(1)
    cot = cot_ref[0].astype(jnp.float32)
    grad = gn_acc[...]
    unit = unit_two_ref[...]
    middle = cot + normalise_back(grad, unit, rstd_two_ref[...], gain_two_ref[...])
    output_ref[0] = (middle_ref[...] + out_acc[...] + b_down_ref[...]).astype(low)
    middle_ref[...] = middle
    branch = middle.astype(low)
    for pair in range(pairs):
        back = dot_nt(branch, w_out_ref[pl.ds(pair * wide, wide), :]).astype(low).astype(jnp.float32)
        top, bottom = back[:half], back[half:]
        send_gmix[2 * pair] = join_heads(top, swap_halves(bottom)).astype(low)
        send_gmix[2 * pair + 1] = join_heads(swap_halves(top), bottom).astype(low)

    def send_grads(step, carried):
        to = lax.rem(me + step, count)
        exchange(send_gmix.at[to], recv_gmix.at[me], gmix_s.at[0], gmix_r.at[me], to).start()
        return carried

    lax.fori_loop(1, count, send_grads, 0)
    recv_gmix[me] = send_gmix[me]
    out_mine[...] = dot_tn(mixed_ref[...], branch).astype(low)
    out_sum.send(0)
    vec_mid_mine[pl.ds(chunks, 1), :] = jnp.sum(cot, axis=0, keepdims=True)
    vec_mid_mine[pl.ds(chunks + 1, 1), :] = jnp.sum(grad * unit, axis=0, keepdims=True)
    vec_mid_mine[pl.ds(chunks + 2, 1), :] = jnp.sum(grad, axis=0, keepdims=True)
    vec_mid_mine[pl.ds(chunks + 3, 1), :] = jnp.sum(branch.astype(jnp.float32), axis=0, keepdims=True)
    mid_vec.start_seq()

    def steps_of(sums):
        found = {str(stage): functools.partial(sums.send, stage) for stage in range(1, 5)}
        found["t"] = sums.turn
        found |= {"abcde"[stage]: functools.partial(sums.gather, stage) for stage in range(1, 5)}
        found["f"] = functools.partial(sums.arrive, 0)
        return found

    acts = {}
    for name, sums in (("N", near_sum), ("R", rest_sum), ("O", out_sum), ("I", in_sum)):
        acts |= {name + step: act for step, act in steps_of(sums).items()}
    acts["V1"] = mid_vec.start_dp

    def run(names):
        for name in names:
            acts[name]()

    run(before_backward)

    kv_rows = 3 * HD
    logit[pl.ds(grads_at(0), count), :kv_rows] = jnp.zeros((count, kv_rows, rows), jnp.float32)
    row_wide[...] = jnp.zeros_like(row_wide)
    back_carry[...] = jnp.zeros_like(back_carry)
    wkv_acc[...] = jnp.zeros_like(wkv_acc)
    wqq_acc[...] = jnp.zeros_like(wqq_acc)

    def prepare(i):
        @pl.when(i != me)
        def _():
            wait_all(recv_gmix.at[i], gmix_r.at[i])

        grad = jnp.where(lane < HD, spread_rows(recv_gmix[i].astype(jnp.float32)), 0.0)
        kept = logit[kept_at(i), :, :wide]
        inverse = kept[:, HD : HD + 1]
        delta = -jnp.sum(grad * kept, axis=1, keepdims=True) * inverse
        grad = grad * inverse
        grad_rows_t[i] = grad.T[:HD].astype(low)
        delta_high = delta.astype(low).astype(jnp.float32)
        grad = jnp.where(lane == HD, delta_high, jnp.where(lane == HD + 1, delta - delta_high, grad))
        grad_rows[i] = grad.astype(low)

    def backward_group(group):
        spots = [pair_at(i, j) for i, j in group]
        found = [probs[spot] for spot in spots]
        grads = [dot_nt(grad_rows[i], vals[j]) for i, j in group]
        grads = [(prob.astype(jnp.float32) * grad).astype(low) for prob, grad in zip(found, grads)]
        laters = [dot_nn(upper[...], grad) for grad in grads]
        gated = []
        for k, (i, j) in enumerate(group):
            later = laters[k] + back_carry[j]
            back_carry[j] = later[:1] - coeff * grads[k][:1].astype(jnp.float32)
            gated.append((later * gates[spots[k]].astype(jnp.float32)).astype(low))
        query_parts = [dot_nn(grads[k], keys[j]) + dot_nn(gated[k], keys_zero[j]) for k, (_, j) in enumerate(group)]
        key_parts = [
            (
                dot_nn(grad_rows_t[i], found[k]),
                dot_nn(queries_t[i, :HD], grads[k]),
                dot_nn(queries_t[i, HD:], gated[k]),
            )
            for k, (i, _) in enumerate(group)
        ]
        for k, (i, _) in enumerate(group):
            row_wide[i] += query_parts[k]
        for k, (_, j) in enumerate(group):
            for part in range(3):
                logit[grads_at(j), part * HD : (part + 1) * HD] += key_parts[k][part]

    def send_first_sum(i):
        wait_all(y_first.at[i], fback_yr.at[i])
        send_first[i] = (send_first[i].astype(jnp.float32) + y_first[i].astype(jnp.float32)).astype(low)

        @pl.when(i != me)
        def _():
            exchange(send_first.at[i], recv_first.at[z], fback_s.at[0], fback_r.at[0], i).start()

        @pl.when(i == me)
        def _():
            recv_first[z] = send_first[i]

    def block_of(step):
        return upwards * (count - 1 - step) + (1 - upwards) * step

    def send_home(step):
        block = block_of(step)

        @pl.when(block != me)
        def _():
            exchange(send_back.at[block], recv_back.at[me], back_s.at[0], back_r.at[0], block).start()

        @pl.when(lax.rem(block, 2) != y)
        def _():
            exchange(send_first.at[block], y_first.at[block], fback_y.at[0], fback_yr.at[block], z * 2 + 1 - y).start()

    def send_first_home(step):
        block = block_of(step)
        pl.when(lax.rem(block, 2) == y)(functools.partial(send_first_sum, block))

    for step in range(count):
        acts[f"B{step}"] = functools.partial(send_home, step)
        acts[f"F{step}"] = functools.partial(send_first_home, step)

    def between(step, number, names):
        if names:
            pl.when(step == number)(functools.partial(run, names))

    def backward_step(step, carried):
        block = block_of(step)
        pl.when(upwards == 1)(functools.partial(prepare, block))

        def group(start, size):
            members = []
            for k in range(size):
                i = upwards * block + (1 - upwards) * (count - 1 - start - k)
                j = upwards * (start + k) + (1 - upwards) * block
                members.append((i, j))
            backward_group(members)

        def half_way():
            for number, names in enumerate(within_steps):
                between(step, number, names)

        in_groups(count - step, group, half_way)
        flat = logit[grads_at(block), :kv_rows]
        flipped = flat[: 2 * HD].T
        first_flipped = flat[HD:].T
        grad_queries = row_wide[block] * score_scale
        send_back[block, :rows] = join_heads(grad_queries, flipped).astype(low)
        send_back[block, rows:] = fold_rows(flipped).astype(low)
        send_first[block] = join_heads(swap_halves(grad_queries), first_flipped).astype(low)

        normed = normed_all[block]
        wkv_acc[...] += dot_nn(flat.astype(low), normed)
        wqq_acc[...] += dot_nn(grad_queries.T.astype(low), normed)
        for number, names in enumerate(between_steps):
            between(step, number, names)
        return carried

    def prepare_all(i, carried):
        prepare(count - 1 - i)
        return carried

    lax.fori_loop(0, (1 - upwards) * count, prepare_all, 0)
    lax.fori_loop(0, count, backward_step, 0)
    recv_back[me] = send_back[me]

    piece = HD // 4
    core_half, x_half = 6 * piece, 3 * piece
    in_start = at.core * core_half
    in_core_copy = remote(rows_of(in_mine, (1 - at.core) * core_half, core_half), in_core, part_s.at[0], part_r.at[0], at.core_peer)
    in_x_copy = remote(rows_of(in_mine, in_start + (1 - at.x) * x_half, x_half), in_x, part_s.at[1], part_r.at[1], at.x_peer)
    each_seq = functools.partial(in_vec.each, count, me)
    each_dp = functools.partial(in_vec.each, dp_count, dp)

    def extra_over_seq(to):
        return exchange(rows_of(extra_mine, to * piece, piece), extra_seq.at[me], extra_s.at[0], extra_r.at[0], to)

    def extra_over_dp(to):
        return remote(extra_sum, extra_dp.at[dp], extra_s.at[1], extra_r.at[1], (to, me))

    def extra_gather(to):
        block = rows_of(extra_all, me * piece, piece)
        return exchange(block, block, extra_s.at[2], extra_r.at[2], to)

    def in_zero():
        for part in range(4):
            for place, (source, start) in enumerate(((wqq_acc, 0), (wkv_acc, HD), (wkv_acc, 0))):
                rows_in = pl.ds(part * 3 * piece + place * piece, piece)
                in_mine[rows_in, :] = source[start + part * piece : start + (part + 1) * piece].astype(low)
        in_core_copy.start()

    def extra_zero():
        extra_mine[:HD] = wqq_acc[HD:].astype(low)
        extra_mine[HD:] = wkv_acc[2 * HD :].astype(low)
        each_seq(lambda to: extra_over_seq(to).start())
        extra_seq[me] = extra_mine[pl.ds(pl.multiple_of(me * piece, 16), piece), :]

    def in_one():
        in_core_copy.wait_recv()
        add_rows(in_mine, in_start, [(in_mine, in_start), (in_core, 0)], core_half)
        in_x_copy.start()

    def in_turn():
        in_x_copy.wait_recv()
        add_rows(in_final, in_sum.give[5], [(in_mine, in_start + at.x * x_half), (in_x, 0)], x_half)
        in_sum.spread(5)

    def extra_one():
        wait_all(extra_seq.at[pl.ds(0, count - 1)], extra_r.at[0])
        summed = extra_seq[0].astype(jnp.float32)
        for k in range(1, count):
            summed = summed + extra_seq[k].astype(jnp.float32)
        extra_sum[...] = summed
        each_dp(lambda to: extra_over_dp(to).start())
        extra_dp[dp] = summed

    def extra_two():
        wait_all(extra_dp.at[pl.ds(0, dp_count - 1)], extra_r.at[1])
        summed = extra_dp[0]
        for k in range(1, dp_count):
            summed = summed + extra_dp[k]
        extra_all[pl.ds(pl.multiple_of(me * piece, 16), piece), :] = summed.astype(low)
        each_seq(lambda to: extra_gather(to).start())

    def first_norm_back():
        wait_all(recv_back.at[pl.ds(0, count - 1)], back_r.at[0])
        wait_all(recv_first.at[pl.ds(0, depth - 1)], fback_r.at[0])
        first_sum = recv_first[0].astype(jnp.float32)
        for source in range(1, depth):
            first_sum = first_sum + recv_first[source].astype(jnp.float32)
        for pair in range(pairs):
            even = recv_back[2 * pair, :rows].astype(jnp.float32)
            odd = recv_back[2 * pair + 1, :rows].astype(jnp.float32)
            if pair == 0:
                even = even + first_sum
            columns = wide * pair
            joined_ref[:, pl.ds(columns, wide)] = join_heads(even, swap_halves(odd)).astype(low)
            joined_ref[:, pl.ds(width + columns, wide)] = join_heads(swap_halves(even), odd).astype(low)
            even = recv_back[2 * pair, rows:].astype(jnp.float32)
            odd = recv_back[2 * pair + 1, rows:].astype(jnp.float32)
            columns = pl.ds(2 * width + columns, wide)
            joined_ref[pl.ds(0, half), columns] = join_heads(even, swap_halves(odd)).astype(low)
            joined_ref[pl.ds(half, half), columns] = join_heads(swap_halves(even), odd).astype(low)
        grad = dot_nt(joined_ref[...], w_qkv_ref[...])
        unit, rstd = normalise(tokens_ref[0].astype(jnp.float32))
        vec_in_mine[...] = jnp.zeros_like(vec_in_mine)
        vec_in_mine[pl.ds(0, 1), :] = jnp.sum(grad * unit, axis=0, keepdims=True)
        vec_in_mine[pl.ds(1, 1), :] = jnp.sum(grad, axis=0, keepdims=True)
        value_grads = joined_ref[:, pl.ds(2 * width, width)].astype(jnp.float32)
        vec_in_mine[pl.ds(2, 1), :] = jnp.sum(value_grads, axis=0, keepdims=True)
        in_vec.start_seq()
        tokens_grad_ref[0] = middle_ref[...] + normalise_back(grad, unit, rstd, gain_one_ref[...])

    stores = []

    def store(source, target):
        stores.append(pltpu.make_async_copy(source, target, store_sem.at[len(stores)]))
        stores[-1].start()

    def finish_near():
        near_sum.arrive(0)
        store(near_final.at[pl.ds(0, half_hidden)], w_down_out.at[pl.ds(0, half_hidden)])
        store(near_final.at[pl.ds(half_hidden, half_hidden)], w_up_out.at[pl.ds(0, half_hidden)])

    def finish_rest():
        rest_sum.arrive(0)
        store(rest_final.at[pl.ds(0, half_hidden)], w_down_out.at[pl.ds(half_hidden, half_hidden)])
        store(rest_final.at[pl.ds(half_hidden, half_hidden)], w_up_out.at[pl.ds(half_hidden, half_hidden)])

    def finish_out():
        out_sum.arrive(0)
        store(out_final, w_out_out)

    def finish_in():
        in_sum.arrive(0)
        store(in_final, w_qkv_out)

    def finish_extra():
        wait_all(extra_all.at[pl.ds(0, (count - 1) * piece)], extra_r.at[2])
        store(extra_all, first_out)

    def finish_mid_vec():
        vec_mid_ref[...] = mid_vec.finish()

    def finish_in_vec():
        vec_in_ref[...] = in_vec.finish()

    acts |= {
        "I0": in_zero, "I1": in_one, "It": in_turn, "E0": extra_zero, "E1": extra_one, "E2": extra_two,
        "T": first_norm_back, "W1": in_vec.start_dp, "Vf": finish_mid_vec, "Wf": finish_in_vec,
        "Nf": finish_near, "Rf": finish_rest, "Of": finish_out, "If": finish_in, "Ef": finish_extra,
    }
    run(after_backward)

    wait_all(normed_all.at[pl.ds(0, depth)], norm_s.at[0])
    for at_z in range(depth - 1):
        went = normed_all.at[pl.ds(0, at_z + 1)]
        pl.when(z == at_z)(functools.partial(wait_all, went, norm_s.at[1]))
        pl.when(z == depth - 1 - at_z)(functools.partial(wait_all, went, norm_s.at[2]))
    wait_all(send_mix.at[pl.ds(0, count - 1)], mix_s.at[0])
    wait_all(send_gmix.at[pl.ds(0, count - 1)], gmix_s.at[0])
    wait_all(send_back.at[pl.ds(0, count - 1)], back_s.at[0])
    wait_all(send_first.at[pl.ds(0, depth)], fback_y.at[0])
    wait_all(send_first.at[pl.ds(0, depth - 1)], fback_s.at[0])
    wait_all(extra_seq.at[pl.ds(0, count - 1)], extra_s.at[0])
    wait_all(extra_dp.at[pl.ds(0, dp_count - 1)], extra_s.at[1])
    wait_all(extra_all.at[pl.ds(0, (count - 1) * piece)], extra_s.at[2])
    in_core_copy.wait_send()
    in_x_copy.wait_send()
    near_sum.drain()
    rest_sum.drain()
    out_sum.drain()
    in_sum.drain()
    mid_vec.drain()
    in_vec.drain()
    for store in stores:
        store.wait()


def widen_kernel(
    output_in, tokens_grad_in, vec_mid_ref, vec_in_ref, w_down_in, w_up_in, w_out_in, w_qkv_in, first_in,
    output_out, tokens_grad_out, gain_one_out, bias_one_out, b_val_out, b_out_out, gain_two_out, bias_two_out, b_up_out, b_down_out,
    w_down_out, w_up_out, w_out_out, w_qkv_out,
    down_low, up_low, out_low, qkv_low, first_low, tokens_grad_held, output_held, down_wide, up_wide, out_wide, qkv_wide, load_sem, store_sem,
):
    width = out_low.shape[0]
    blocks = down_low.shape[0] // width
    loads = []
    for k, (source, target) in enumerate(
        (
            (w_down_in, down_low), (w_up_in, up_low), (w_qkv_in, qkv_low), (first_in, first_low), (w_out_in, out_low),
            (tokens_grad_in, tokens_grad_held), (output_in, output_held),
        )
    ):
        loads.append(pltpu.make_async_copy(source, target, load_sem.at[k]))
        loads[-1].start()
    stores = []

    def store(source, target):
        stores.append(pltpu.make_async_copy(source, target, store_sem.at[len(stores)]))
        stores[-1].start()

    for row, target in enumerate((gain_one_out, bias_one_out, b_val_out)):
        target[...] = vec_in_ref[row : row + 1, :]
    for row in range(blocks):
        b_up_out[:, row * width : (row + 1) * width] = vec_mid_ref[row : row + 1, :]
    for row, target in enumerate((b_down_out, gain_two_out, bias_two_out, b_out_out)):
        target[...] = vec_mid_ref[blocks + row : blocks + row + 1, :]

    def convert(source, target, at, columns):
        def step(k, carried):
            here = pl.ds(pl.multiple_of(at + k * 64, 64), 64)
            there = pl.ds(pl.multiple_of(k * 64, 64), 64)
            if columns is None:
                target[here, :] = source[here, :].astype(jnp.float32)
            else:
                target[there, pl.ds(columns, width)] = source[here, :].astype(jnp.float32)
            return carried

        lax.fori_loop(0, width // 64, step, 0)

    loads[0].wait()
    for block in range(blocks):
        convert(down_low, down_wide, block * width, None)
        here = pl.ds(block * width, width)
        store(down_wide.at[here], w_down_out.at[here])
    loads[1].wait()
    for block in range(blocks):
        convert(up_low, up_wide, block * width, block * width)
        here = pl.ds(block * width, width)
        store(up_wide.at[:, here], w_up_out.at[:, here])
    loads[4].wait()
    convert(out_low, out_wide, 0, None)
    store(out_wide, w_out_out)
    loads[5].wait()
    store(tokens_grad_held, tokens_grad_out)
    loads[6].wait()
    store(output_held, output_out)
    loads[2].wait()
    loads[3].wait()
    piece = HD // 4
    wide = 2 * HD
    for part in range(3):
        for pair in range(width // wide):
            found = []
            for head in (2 * pair, 2 * pair + 1):
                z, y = head // 2, head % 2
                for owner in range(4):
                    core, x = owner // 2, owner % 2
                    two, three = (x, y) if core == 0 else (y, x)
                    depth = width // wide
                    start = ((((core * 2 + two) * 2 + three) * depth + z % 2 * 2 + z // 2) * 3 + part) * piece
                    block = qkv_low[start : start + piece].astype(jnp.float32)
                    if head == 0 and part < 2:
                        at = part * HD + owner * piece
                        block = block + first_low[at : at + piece].astype(jnp.float32)
                    found.append(block)
            columns = part * width + pair * wide
            qkv_wide[:, columns : columns + wide] = jnp.concatenate(found, axis=0).T
    store(qkv_wide, w_qkv_out)
    for one in stores:
        one.wait()


def exchange_heads(
    tokens, segment_ids, gain_one, bias_one, w_qkv, b_val, w_out, b_out,
    gain_two, bias_two, w_up, b_up, w_down, b_down, cotangent,
):
    count, dp_count = lax.axis_size("seq"), lax.axis_size("dp")
    rows, width = tokens.shape[1], tokens.shape[2]
    hidden = w_up.shape[1]
    half = rows // 2
    tiles = count * (count + 1) // 2
    wide = 2 * HD
    f32 = jnp.float32
    packed = rows + half
    depth = count // 2

    def vmem(*shape, dtype=low):
        return pltpu.VMEM(shape, dtype)

    def sems(*shape):
        return pltpu.SemaphoreType.DMA(shape)

    scratch = [
        vmem(width, width), vmem(width, hidden), vmem(hidden, width), vmem(width, 3 * width), vmem(1, rows, width), sems(5), sems(8),
        vmem(count, rows, width), vmem(width, 2 * wide), vmem(width, wide), vmem(1, wide, dtype=f32),
        vmem(count, rows, wide), vmem(count, rows, wide), vmem(count, rows, wide), vmem(count, rows, wide), vmem(count, wide, rows),
        vmem(tiles, rows, rows), vmem(tiles, rows, rows), vmem(tiles, rows, rows, dtype=f32),
        vmem(count, 1, rows, dtype=f32), vmem(count, rows, wide, dtype=f32), vmem(rows, wide, dtype=f32),
        vmem(count, half, wide), vmem(count, half, wide), vmem(count, half, wide), vmem(count, half, wide), vmem(count, rows, wide), vmem(count, HD, rows),
        vmem(count, 1, rows, dtype=f32),
        vmem(count, packed, wide), vmem(count, packed, wide), vmem(count, rows, wide), vmem(count, rows, wide), vmem(depth, rows, wide),
        vmem(rows, rows), vmem(rows, rows),
        vmem(rows, width, dtype=f32), vmem(rows, 1, dtype=f32),
        vmem(rows, width), vmem(rows, width), vmem(rows, width, dtype=f32), vmem(rows, width, dtype=f32), vmem(rows, width, dtype=f32), vmem(rows, 3 * width),
    ]
    for total in (hidden, hidden, width):
        scratch += [vmem(total, width), vmem(total, width)]
        scratch += [vmem(total >> stage, width) for stage in range(1, 6)]
    scratch += [
        vmem(3 * HD, width, dtype=f32), vmem(wide, width, dtype=f32),
        vmem(3 * HD, width), vmem(3 * HD // 2, width), vmem(3 * HD // 4, width), vmem(3 * width, width),
        vmem(wide, width), vmem(count, wide // count, width), vmem(wide // count, width, dtype=f32), vmem(dp_count, wide // count, width, dtype=f32), vmem(wide, width),
    ]
    for _ in range(2):
        scratch += [vmem(8, width, dtype=f32), vmem(count, 8, width, dtype=f32), vmem(8, width, dtype=f32), vmem(dp_count, 8, width, dtype=f32)]
    scratch += [sems(3), sems(count), sems(1), sems(1), sems(1), sems(count)]
    scratch += [sems(1), sems(1), sems(1), sems(count), sems(1), sems(1), sems(3), sems(3)]
    scratch += [sems(1), sems(5)] * 6
    scratch += [sems(1), sems(5), sems(2), sems(2), sems(4), sems(4)]
    in_vmem = pl.BlockSpec(memory_space=pltpu.VMEM)
    anywhere = pl.BlockSpec(memory_space=pl.ANY)
    specs = [in_vmem] * 15
    for at in (4, 6, 10, 12, 14):
        specs[at] = anywhere
    shape = jax.ShapeDtypeStruct
    results = pl.pallas_call(
        layer_kernel,
        out_shape=[
            shape((1, rows, width), low), shape((1, rows, width), f32), shape((8, width), f32), shape((8, width), f32),
            shape((hidden, width), low), shape((hidden, width), low), shape((width, width), low), shape((3 * width, width), low), shape((wide, width), low),
        ],
        in_specs=specs,
        out_specs=[in_vmem] * 4 + [anywhere] * 5,
        scratch_shapes=scratch,
        compiler_params=pltpu.CompilerParams(
            collective_id=0, has_side_effects=True, vmem_limit_bytes=vmem_bytes
        ),
    )(
        tokens, segment_ids, gain_one[None], bias_one[None], w_qkv, b_val[None], w_out, b_out[None],
        gain_two[None], bias_two[None], w_up, b_up[None], w_down, b_down[None], cotangent,
    )
    vector = shape((1, width), f32)
    widened = pl.pallas_call(
        widen_kernel,
        out_shape=[
            shape((1, rows, width), low), shape((1, rows, width), f32), vector, vector, vector, vector, vector, vector, shape((1, hidden), f32), vector,
            shape((hidden, width), f32), shape((width, hidden), f32), shape((width, width), f32), shape((width, 3 * width), f32),
        ],
        in_specs=[anywhere] * 2 + [in_vmem] * 2 + [anywhere] * 5,
        out_specs=[anywhere] * 2 + [in_vmem] * 8 + [anywhere] * 4,
        scratch_shapes=[
            vmem(hidden, width), vmem(hidden, width), vmem(width, width), vmem(3 * width, width), vmem(wide, width), vmem(1, rows, width, dtype=f32), vmem(1, rows, width),
            vmem(hidden, width, dtype=f32), vmem(width, hidden, dtype=f32), vmem(width, width, dtype=f32), vmem(width, 3 * width, dtype=f32),
            sems(7), sems(12),
        ],
        compiler_params=pltpu.CompilerParams(vmem_limit_bytes=vmem_bytes),
    )(*results)
    output, tokens_grad = widened[:2]
    gain_one_grad, bias_one_grad, b_val_grad, b_out_grad, gain_two_grad, bias_two_grad, b_up_grad, b_down_grad = (
        row.reshape(row.shape[1]) for row in widened[2:10]
    )
    w_down_grad, w_up_grad, w_out_grad, w_qkv_grad = widened[10:]
    return (
        output, tokens_grad, gain_one_grad, bias_one_grad, w_qkv_grad, b_val_grad, w_out_grad, b_out_grad,
        gain_two_grad, bias_two_grad, w_up_grad, b_up_grad, w_down_grad, b_down_grad,
    )


def picks_heads(mesh, length, width, hidden):
    dp_count, count = mesh.shape["dp"], mesh.shape["seq"]
    power = length & (length - 1) == 0
    return dp_count == 4 and count == 8 and width == count * HD and hidden == 4 * width and power


def solution(mesh):
    placed = (
        P("dp", "seq", None),
        P("dp", None),
        P(),
        P(),
        P(),
        P(),
        P(),
        P(),
        P(),
        P(),
        P(),
        P(),
        P(),
        P(),
        P("dp", "seq", None),
    )

    def layer(tokens, *others):
        width, hidden = tokens.shape[-1], others[9].shape[-1]
        length = tokens.shape[1] * mesh.shape["seq"]
        body = exchange_heads if picks_heads(mesh, length, width, hidden) else local
        return body(tokens, *others)

    return jax.shard_map(
        layer,
        mesh=mesh,
        in_specs=placed,
        out_specs=(
            P("dp", "seq", None),
            P("dp", "seq", None),
            P(),
            P(),
            P(),
            P(),
            P(),
            P(),
            P(),
            P(),
            P(),
            P(),
            P(),
            P(),
        ),
        check_vma=False,
    )
```

```python
import functools
import math

import jax
import jax.numpy as jnp
from jax import lax
from jax.experimental import pallas as pl
from jax.experimental.pallas import tpu as pltpu
from jax.sharding import PartitionSpec as P

HD = 64


norm_eps = 1e-05
select_weight = 4.0
neg_large = -1e30
highest = lax.Precision.HIGHEST
vmem_bytes = 63 * 1024 * 1024


def prefix(array, axis, combine, identity, reverse):
    length, here = (lax.axis_size(axis), lax.axis_index(axis))
    everything = lax.all_gather(array.astype(jnp.bfloat16), axis)
    start = jnp.broadcast_to(jnp.asarray(identity, array.dtype), array.shape)

    def hop(k, before):
        at = length - 1 - k if reverse else k
        reached = at > here if reverse else at < here
        new = combine(before, everything[at].astype(array.dtype))
        return jnp.where(reached, new, before)

    return lax.fori_loop(0, length, hop, start)


def layer_norm(values, norm_gain, norm_shift):
    centered = values - jnp.mean(values, axis=-1, keepdims=True)
    variance = jnp.mean(centered * centered, axis=-1, keepdims=True)
    return centered * lax.rsqrt(variance + norm_eps) * norm_gain + norm_shift


def exact_gelu(values):
    return jax.nn.gelu(values, approximate=False)


def add_arrays(earlier, later):
    return earlier + later


def keep_state(state_in):
    return state_in


def pick_block():
    return 512


def local(
    tokens,
    segment_ids,
    gain_one,
    bias_one,
    w_qkv,
    b_val,
    w_out,
    b_out,
    gain_two,
    bias_two,
    w_up,
    b_up,
    w_down,
    b_down,
    cotangent,
):
    seq_count = lax.axis_size("seq")
    seq_rank = lax.axis_index("seq")
    row_tokens = tokens[0].astype(jnp.float32)
    tok_rows = row_tokens.shape[0]
    model_width = row_tokens.shape[1]
    head_count = model_width // HD
    length = tok_rows * seq_count
    score_scale = 1.0 / math.sqrt(HD)
    select_coeff = select_weight / length
    row_segments = segment_ids[0]
    row_base = seq_rank * tok_rows
    query_pos = row_base + jnp.arange(tok_rows, dtype=jnp.int32)
    query_segs = lax.dynamic_slice_in_dim(row_segments, row_base, tok_rows)
    last_query = row_base + tok_rows - 1
    lower_mask = (jnp.arange(tok_rows)[:, None] > jnp.arange(tok_rows)[None, :]).astype(jnp.float32)
    upper_mask = lower_mask.T
    normed_one, norm_one_back = jax.vjp(layer_norm, row_tokens, gain_one, bias_one)
    normed_one_low = normed_one.astype(jnp.bfloat16)
    value_bias = jnp.concatenate([jnp.zeros((2 * model_width,), jnp.float32), b_val])
    joined_low = (
        jnp.dot(normed_one_low, w_qkv, preferred_element_type=jnp.float32) + value_bias
    ).astype(jnp.bfloat16)
    queries = joined_low[:, :model_width]
    keys_mine = joined_low[:, model_width : 2 * model_width]
    values_mine = joined_low[:, 2 * model_width :]
    query_heads = queries.reshape(tok_rows, head_count, HD)
    query_zero = queries[:, :HD]
    query_rest = query_heads[:, 1:]

    def pair_masks(key_start, key_rows):
        key_pos = key_start + jnp.arange(key_rows, dtype=jnp.int32)
        key_segs = lax.dynamic_slice_in_dim(row_segments, key_start, key_rows)
        same_doc = query_segs[:, None] == key_segs[None, :]
        attend_mask = same_doc & (key_pos[None, :] <= query_pos[:, None])
        select_mask = same_doc & (key_pos[None, :] < query_pos[:, None])
        return (attend_mask, select_mask)

    select_init = (
        jnp.zeros((tok_rows, length), jnp.float32),
        jnp.zeros((tok_rows, length), jnp.float32),
        jnp.zeros((length,), jnp.float32),
    )
    running = select_init
    key_piece = lax.all_gather(keys_mine[:, :HD], "seq", axis=0, tiled=True)
    piece_rows = key_piece.shape[0]
    block_rows = pick_block()

    def select_block(state_now, offset):
        zero_scores, local_forgot, column_sums = state_now
        key_block = lax.dynamic_slice_in_dim(key_piece, offset, block_rows)
        attend_mask, select_mask = pair_masks(offset, block_rows)
        scores = (
            jnp.einsum("qd,kd->qk", query_zero, key_block, preferred_element_type=jnp.float32)
            * score_scale
        )
        chosen = jnp.where(select_mask, jax.nn.softplus(scores), 0.0)
        forgot = jnp.dot(lower_mask, chosen, precision=highest)
        zero_scores = lax.dynamic_update_slice_in_dim(zero_scores, scores, offset, 1)
        local_forgot = lax.dynamic_update_slice_in_dim(local_forgot, forgot, offset, 1)
        column_sums = lax.dynamic_update_slice_in_dim(
            column_sums, jnp.sum(chosen, axis=0), offset, 0
        )
        return ((zero_scores, local_forgot, column_sums), None)

    offsets = jnp.arange(piece_rows // block_rows, dtype=jnp.int32) * block_rows
    running, unused = lax.scan(select_block, running, offsets)
    zero_scores, local_forgot, column_sums = running
    column_prefix = prefix(column_sums, "seq", add_arrays, jnp.zeros((length,), jnp.float32), False)
    attend_init = (
        jnp.full((head_count, tok_rows), neg_large, jnp.float32),
        jnp.zeros((head_count, tok_rows), jnp.float32),
        jnp.zeros((tok_rows, head_count, HD), jnp.float32),
    )
    running = attend_init
    attend_key_piece = lax.all_gather(keys_mine, "seq", axis=0, tiled=True)
    value_piece = lax.all_gather(values_mine, "seq", axis=0, tiled=True)
    piece_rows = attend_key_piece.shape[0]
    attend_block_rows = pick_block()

    def attend_block(state_now, offset):
        key_start = offset

        def attend_compute(state_in):
            run_max, run_total, accumulated = state_in
            key_block = lax.dynamic_slice_in_dim(
                attend_key_piece, offset, attend_block_rows
            ).reshape(attend_block_rows, head_count, HD)
            value_block = lax.dynamic_slice_in_dim(value_piece, offset, attend_block_rows).reshape(
                attend_block_rows, head_count, HD
            )
            attend_mask, select_mask = pair_masks(key_start, attend_block_rows)
            rest_scores = (
                jnp.einsum(
                    "qhd,khd->hqk", query_rest, key_block[:, 1:], preferred_element_type=jnp.float32
                )
                * score_scale
            )
            head_zero = lax.dynamic_slice_in_dim(zero_scores, key_start, attend_block_rows, 1)
            scores = jnp.concatenate([head_zero[None], rest_scores], axis=0)
            forgot = lax.dynamic_slice_in_dim(column_prefix, key_start, attend_block_rows)[
                None, :
            ] + lax.dynamic_slice_in_dim(local_forgot, key_start, attend_block_rows, 1)
            logits = jnp.where(attend_mask[None], scores - select_coeff * forgot[None], neg_large)
            new_max = jnp.maximum(run_max, jnp.max(logits, axis=-1))
            weights = jnp.where(attend_mask[None], jnp.exp(logits - new_max[:, :, None]), 0.0)
            decay_factor = jnp.exp(run_max - new_max)
            run_total = run_total * decay_factor + jnp.sum(weights, axis=-1)
            accumulated = accumulated * decay_factor.T[:, :, None] + jnp.einsum(
                "hqk,khd->qhd",
                weights.astype(jnp.bfloat16),
                value_block,
                preferred_element_type=jnp.float32,
            )
            return (new_max, run_total, accumulated)

        state_now = lax.cond(key_start <= last_query, attend_compute, keep_state, state_now)
        return (state_now, None)

    offsets = jnp.arange(piece_rows // attend_block_rows, dtype=jnp.int32) * attend_block_rows
    running, unused = lax.scan(attend_block, running, offsets)
    run_max, run_total, accumulated = running
    log_total = run_max + jnp.log(run_total)
    mixed_float = accumulated / run_total.T[:, :, None]
    mixed_low = mixed_float.reshape(tok_rows, model_width).astype(jnp.bfloat16)
    middle = row_tokens + jnp.dot(mixed_low, w_out, preferred_element_type=jnp.float32) + b_out
    normed_two, norm_two_back = jax.vjp(layer_norm, middle, gain_two, bias_two)
    normed_two_low = normed_two.astype(jnp.bfloat16)
    hidden = jnp.dot(normed_two_low, w_up, preferred_element_type=jnp.float32) + b_up
    active, gelu_back = jax.vjp(exact_gelu, hidden)
    active_low = active.astype(jnp.bfloat16)
    output = middle + jnp.dot(active_low, w_down, preferred_element_type=jnp.float32) + b_down
    grad_out = cotangent[0]
    grad_float = grad_out.astype(jnp.float32)
    w_down_grad = jnp.einsum("tf,td->fd", active_low, grad_out, preferred_element_type=jnp.float32)
    b_down_grad = jnp.sum(grad_float, axis=0)
    grad_active = jnp.einsum("td,fd->tf", grad_out, w_down, preferred_element_type=jnp.float32)
    (grad_hidden,) = gelu_back(grad_active)
    grad_hidden_low = grad_hidden.astype(jnp.bfloat16)
    w_up_grad = jnp.einsum(
        "td,tf->df", normed_two_low, grad_hidden_low, preferred_element_type=jnp.float32
    )
    b_up_grad = jnp.sum(grad_hidden_low.astype(jnp.float32), axis=0)
    grad_normed_two = jnp.einsum(
        "tf,df->td", grad_hidden_low, w_up, preferred_element_type=jnp.float32
    )
    grad_middle_norm, gain_two_grad, bias_two_grad = norm_two_back(grad_normed_two)
    grad_middle = grad_float + grad_middle_norm
    grad_branch_low = grad_middle.astype(jnp.bfloat16)
    w_out_grad = jnp.einsum(
        "td,te->de", mixed_low, grad_branch_low, preferred_element_type=jnp.float32
    )
    b_out_grad = jnp.sum(grad_branch_low.astype(jnp.float32), axis=0)
    grad_mixed_low = jnp.einsum(
        "te,de->td", grad_branch_low, w_out, preferred_element_type=jnp.float32
    ).astype(jnp.bfloat16)
    grad_mixed_heads = grad_mixed_low.reshape(tok_rows, head_count, HD)
    row_delta = jnp.sum(grad_mixed_heads.astype(jnp.float32) * mixed_float, axis=-1).T
    keys_back, values_back = (
        lax.all_gather(keys_mine, "seq", axis=0, tiled=True),
        lax.all_gather(values_mine, "seq", axis=0, tiled=True),
    )
    back_rows = pick_block()
    key_heads = keys_back.reshape(length, head_count, HD)
    value_heads = values_back.reshape(length, head_count, HD)

    def grad_block(state_now, offset):

        def grad_compute(state_in):
            query_grad, key_grad, value_grad, first_part, second_part, grad_cols = state_in
            key_block = lax.dynamic_slice_in_dim(key_heads, offset, back_rows)
            value_block = lax.dynamic_slice_in_dim(value_heads, offset, back_rows)
            attend_mask, select_mask = pair_masks(offset, back_rows)
            scores = (
                jnp.einsum(
                    "qhd,khd->hqk", query_heads, key_block, preferred_element_type=jnp.float32
                )
                * score_scale
            )
            chosen = jnp.where(select_mask, jax.nn.softplus(scores[0]), 0.0)
            forgot = lax.dynamic_slice_in_dim(column_prefix, offset, back_rows)[None, :] + jnp.dot(
                lower_mask, chosen, precision=highest
            )
            logits = scores - select_coeff * forgot[None]
            prob_block = jnp.where(attend_mask[None], jnp.exp(logits - log_total[:, :, None]), 0.0)
            grad_probs = jnp.einsum(
                "qhd,khd->hqk", grad_mixed_heads, value_block, preferred_element_type=jnp.float32
            )
            grad_logits = prob_block * (grad_probs - row_delta[:, :, None])
            value_part = jnp.einsum(
                "hqk,qhd->khd",
                prob_block.astype(jnp.bfloat16),
                grad_mixed_heads,
                preferred_element_type=jnp.float32,
            )
            rest_low = grad_logits[1:].astype(jnp.bfloat16)
            query_grad = (
                query_grad
                + jnp.einsum(
                    "hqk,khd->qhd", rest_low, key_block[:, 1:], preferred_element_type=jnp.float32
                )
                * score_scale
            )
            key_part = (
                jnp.einsum("hqk,qhd->khd", rest_low, query_rest, preferred_element_type=jnp.float32)
                * score_scale
            )
            total_grad = jnp.sum(grad_logits, axis=0)
            suffix_local = jnp.dot(upper_mask, total_grad, precision=highest)
            select_gate = jnp.where(select_mask, select_coeff * jax.nn.sigmoid(scores[0]), 0.0)
            first_part = lax.dynamic_update_slice_in_dim(
                first_part, grad_logits[0] - select_gate * suffix_local, offset, 1
            )
            second_part = lax.dynamic_update_slice_in_dim(second_part, select_gate, offset, 1)
            key_grad = lax.dynamic_update_slice_in_dim(key_grad, key_part, offset, 0)
            value_grad = lax.dynamic_update_slice_in_dim(value_grad, value_part, offset, 0)
            grad_cols = lax.dynamic_update_slice_in_dim(
                grad_cols, jnp.sum(total_grad, axis=0), offset, 0
            )
            return (query_grad, key_grad, value_grad, first_part, second_part, grad_cols)

        state_now = lax.cond(offset <= last_query, grad_compute, keep_state, state_now)
        return (state_now, None)

    grad_init = (
        jnp.zeros((tok_rows, head_count - 1, HD), jnp.float32),
        jnp.zeros((length, head_count - 1, HD), jnp.float32),
        jnp.zeros((length, head_count, HD), jnp.float32),
        jnp.zeros((tok_rows, length), jnp.float32),
        jnp.zeros((tok_rows, length), jnp.float32),
        jnp.zeros((length,), jnp.float32),
    )
    back_offsets = jnp.arange(length // back_rows, dtype=jnp.int32) * back_rows
    grad_state, unused = lax.scan(grad_block, grad_init, back_offsets)
    query_grad, key_grad, value_grad, first_part, second_part, grad_cols = grad_state
    grad_suffix = prefix(grad_cols, "seq", add_arrays, jnp.zeros((length,), jnp.float32), True)
    zero_grad_low = (first_part - second_part * grad_suffix[None, :]).astype(jnp.bfloat16)
    query_zero_grad = (
        jnp.dot(zero_grad_low, keys_back[:, :HD], preferred_element_type=jnp.float32) * score_scale
    )
    key_zero_grad = (
        jnp.einsum("ql,qd->ld", zero_grad_low, query_zero, preferred_element_type=jnp.float32)
        * score_scale
    )
    key_total = jnp.concatenate([key_zero_grad[:, None, :], key_grad], axis=1).reshape(
        length, model_width
    )
    value_total = value_grad.reshape(length, model_width)
    key_mine_grad, value_mine_grad = (
        lax.psum_scatter(
            key_total.astype(jnp.bfloat16), "seq", scatter_dimension=0, tiled=True
        ).astype(jnp.float32),
        lax.psum_scatter(
            value_total.astype(jnp.bfloat16), "seq", scatter_dimension=0, tiled=True
        ).astype(jnp.float32),
    )
    query_total = jnp.concatenate([query_zero_grad[:, None, :], query_grad], axis=1).reshape(
        tok_rows, model_width
    )
    grad_joined_low = jnp.concatenate([query_total, key_mine_grad, value_mine_grad], axis=1).astype(
        jnp.bfloat16
    )
    b_val_grad = jnp.sum(grad_joined_low[:, 2 * model_width :].astype(jnp.float32), axis=0)
    w_qkv_grad = jnp.einsum(
        "td,te->de", normed_one_low, grad_joined_low, preferred_element_type=jnp.float32
    )
    grad_normed_one = jnp.einsum(
        "te,de->td", grad_joined_low, w_qkv, preferred_element_type=jnp.float32
    )
    grad_tokens_norm, gain_one_grad, bias_one_grad = norm_one_back(grad_normed_one)
    tokens_grad = grad_middle + grad_tokens_norm
    summed = lax.psum(
        (
            gain_one_grad,
            bias_one_grad,
            w_qkv_grad,
            b_val_grad,
            w_out_grad,
            b_out_grad,
            gain_two_grad,
            bias_two_grad,
            w_up_grad,
            b_up_grad,
            w_down_grad,
            b_down_grad,
        ),
        ("dp", "seq"),
    )
    return (
        output.astype(jnp.bfloat16)[None],
        tokens_grad[None],
        summed[0],
        summed[1],
        summed[2],
        summed[3],
        summed[4],
        summed[5],
        summed[6],
        summed[7],
        summed[8],
        summed[9],
        summed[10],
        summed[11],
    )


low = jnp.bfloat16
MESH = pl.DeviceIdType.MESH


def dot_nn(left, right):
    return lax.dot_general(left, right, (((1,), (0,)), ((), ())), preferred_element_type=jnp.float32)


def dot_nt(left, right):
    return lax.dot_general(left, right, (((1,), (1,)), ((), ())), preferred_element_type=jnp.float32)


def dot_tn(left, right):
    return lax.dot_general(left, right, (((0,), (0,)), ((), ())), preferred_element_type=jnp.float32)


def swap_halves(wide):
    return pltpu.roll(wide, HD, 1)


def left_lanes(shape):
    return lax.broadcasted_iota(jnp.int32, shape, 1) < HD


def join_heads(left, right):
    return jnp.where(left_lanes(left.shape), left, right)


def fold_rows(wide):
    half = wide.shape[0] // 2
    return join_heads(wide[:half], swap_halves(wide[half:]))


def spread_rows(folded):
    return jnp.concatenate([folded, swap_halves(folded)], axis=0)


def exact_cdf(values):
    return 0.5 * (1.0 + lax.erf(values * (1.0 / math.sqrt(2.0))))


def normalise(values):
    centered = values - jnp.mean(values, axis=-1, keepdims=True)
    rstd = lax.rsqrt(jnp.mean(centered * centered, axis=-1, keepdims=True) + norm_eps)
    return centered * rstd, rstd


def normalise_back(grad, unit, rstd, gain):
    scaled = grad * gain
    mean_one = jnp.mean(scaled, axis=-1, keepdims=True)
    mean_two = jnp.mean(scaled * unit, axis=-1, keepdims=True)
    return rstd * (scaled - mean_one - unit * mean_two)


def rows_of(ref, at, size):
    return ref.at[pl.ds(pl.multiple_of(at, 16), size)]


def wait_all(like, sem):
    pltpu.make_async_copy(like, like, sem).wait()


def add_rows(into, into_at, parts, size):
    piece = next(rows for rows in (64, 48, 32, 16) if size % rows == 0)

    def step(k, carried):
        summed = None
        for ref, at in parts:
            block = ref[pl.ds(pl.multiple_of(at + k * piece, 16), piece), :].astype(jnp.float32)
            summed = block if summed is None else summed + block
        into[pl.ds(pl.multiple_of(into_at + k * piece, 16), piece), :] = summed.astype(low)
        return carried

    lax.fori_loop(0, size // piece, step, 0)


class Places:
    def __init__(self):
        self.dp_count, self.count = lax.axis_size("dp"), lax.axis_size("seq")
        self.dp, self.me = lax.axis_index("dp"), lax.axis_index("seq")
        self.core, self.x = lax.rem(self.dp, 2), self.dp // 2
        self.y, self.z = lax.rem(self.me, 2), self.me // 2
        self.depth = self.count // 2
        self.core_peer = (self.dp + 1 - 2 * self.core, self.me)
        self.x_peer = (self.dp + 2 - 4 * self.x, self.me)
        self.y_peer = (self.dp, self.me + 1 - 2 * self.y)
        along_x = 1 - self.core
        self.two_peer = (self.dp + along_x * (2 - 4 * self.x), self.me + (1 - along_x) * (1 - 2 * self.y))
        self.three_peer = (self.dp + (1 - along_x) * (2 - 4 * self.x), self.me + along_x * (1 - 2 * self.y))
        self.two_bit = along_x * self.x + (1 - along_x) * self.y
        self.three_bit = (1 - along_x) * self.x + along_x * self.y
        self.z_low, self.z_high = lax.rem(self.z, 2), self.z // 2
        self.z_near = (self.dp, self.me + 2 * (1 - 2 * self.z_low))
        self.z_far = (self.dp, self.me + 4 * (1 - 2 * self.z_high))


def remote(src, dst, send_sem, recv_sem, target):
    return pltpu.make_async_remote_copy(
        src_ref=src, dst_ref=dst, send_sem=send_sem, recv_sem=recv_sem, device_id=target, device_id_type=MESH
    )


class StagedSum:
    def __init__(self, at, x_first, mine, final, got, sems):
        self.mine, self.final, self.got = mine, final, got
        if x_first:
            bits = (at.core, at.x, at.y, at.z_low, at.z_high)
            self.peers = (at.core_peer, at.x_peer, at.y_peer, at.z_near, at.z_far)
        else:
            bits = (at.core, at.two_bit, at.three_bit, at.z_low, at.z_high)
            self.peers = (at.core_peer, at.two_peer, at.three_peer, at.z_near, at.z_far)
        self.stages = len(bits)
        self.down_s, self.down_r, self.up_s, self.up_r = sems
        self.total = final.shape[0]
        start, size = 0, self.total
        self.keep, self.give, self.size = [], [], []
        for bit in bits:
            size //= 2
            self.keep.append(start + bit * size)
            self.give.append(start + (1 - bit) * size)
            self.size.append(size)
            start = start + bit * size
        self.give.append(start)
        self.size.append(size)

    def down(self, stage, block):
        if stage == 0:
            source, there, size = self.give[0], 0, self.size[0]
        else:
            there, size = self.give[block] - self.keep[stage], self.size[block]
            source = self.give[stage] + there
        return remote(
            rows_of(self.mine, source, size), rows_of(self.got[stage], there, size),
            self.down_s.at[0], self.down_r.at[block - 1], self.peers[stage],
        )

    def up(self, stage, block):
        here = rows_of(self.final, self.give[block], self.size[block])
        return remote(here, here, self.up_s.at[0], self.up_r.at[stage], self.peers[stage])

    def blocks(self, stage):
        return (1,) if stage == 0 else range(stage + 1, self.stages + 1)

    def send(self, stage):
        if stage > 0:
            self.collect(stage, self.mine)
        for block in self.blocks(stage):
            self.down(stage, block).start()

    def collect(self, block, into):
        parts = [(self.mine, self.give[block])]
        for stage in range(block):
            parts.append((self.got[stage], self.give[block] - self.keep[stage]))
        came = self.size[0] if block == 1 else (block - 1) * self.size[block]
        wait_all(self.final.at[pl.ds(0, came)], self.down_r.at[block - 1])
        add_rows(into, self.give[block], parts, self.size[block])

    def turn(self):
        self.collect(self.stages, self.final)
        self.spread(self.stages)

    def spread(self, block):
        for stage in reversed(range(block)):
            self.up(stage, block).start()

    def arrive(self, stage):
        wait_all(rows_of(self.final, self.give[stage], self.size[stage]), self.up_r.at[stage])

    def gather(self, stage):
        self.arrive(stage)
        self.spread(stage)

    def drain(self):
        left = self.final.at[pl.ds(0, self.total - self.size[-1])]
        if self.mine is not None:
            wait_all(left, self.down_s.at[0])
        wait_all(left, self.up_s.at[0])


class VectorSum:
    def __init__(self, at, mine, seq_got, seq_sum, dp_got, send_sem, recv_sem, base):
        self.at, self.mine, self.seq_got, self.seq_sum, self.dp_got = at, mine, seq_got, seq_sum, dp_got
        self.send_sem, self.recv_sem, self.base = send_sem, recv_sem, base

    def over_seq(self, to):
        at = self.at
        return remote(
            self.mine, self.seq_got.at[at.me], self.send_sem.at[self.base], self.recv_sem.at[self.base], (at.dp, to)
        )

    def over_dp(self, to):
        at = self.at
        return remote(
            self.seq_sum, self.dp_got.at[at.dp], self.send_sem.at[self.base + 1], self.recv_sem.at[self.base + 1],
            (to, at.me),
        )

    def each(self, count, mine, act):
        def step(k, carried):
            act(lax.rem(mine + k, count))
            return carried

        lax.fori_loop(1, count, step, 0)

    def start_seq(self):
        at = self.at
        self.each(at.count, at.me, lambda to: self.over_seq(to).start())
        self.seq_got[at.me] = self.mine[...]

    def start_dp(self):
        at = self.at
        wait_all(self.seq_got.at[pl.ds(0, at.count - 1)], self.recv_sem.at[self.base])
        summed = self.seq_got[0]
        for k in range(1, at.count):
            summed = summed + self.seq_got[k]
        self.seq_sum[...] = summed
        self.each(at.dp_count, at.dp, lambda to: self.over_dp(to).start())
        self.dp_got[at.dp] = summed

    def finish(self):
        at = self.at
        wait_all(self.dp_got.at[pl.ds(0, at.dp_count - 1)], self.recv_sem.at[self.base + 1])
        summed = self.dp_got[0]
        for k in range(1, at.dp_count):
            summed = summed + self.dp_got[k]
        return summed

    def drain(self):
        wait_all(self.seq_got.at[pl.ds(0, self.at.count - 1)], self.send_sem.at[self.base])
        wait_all(self.dp_got.at[pl.ds(0, self.at.dp_count - 1)], self.send_sem.at[self.base + 1])


before_backward = ("N2", "R1")
within_steps = (
    (),
    (),
    (),
    (),
)
between_steps = (
    ("B0", "N3"),
    ("B1", "R2", "O1"),
    ("B2", "F0", "N4"),
    ("B3", "F1", "R3", "O2"),
    ("B4", "F2"),
    ("B5", "F3", "Nt", "V1"),
    ("B6", "F4", "R4", "O3"),
    ("B7", "F5"),
)
after_backward = (
    "I0", "E0", "F6", "F7", "Ne", "Rt", "O4", "I1", "Nd", "Re", "Ot", "It",
    "E1", "Nc", "Rd", "Oe", "Rc", "T", "Ie", "Nb", "Od", "E2", "Id", "W1",
    "Rb", "Oc", "Ic", "Ob", "Ib", "Vf", "Nf", "Rf", "Of", "If", "Ef", "Wf",
)

near_x, rest_x, out_x = False, False, False


def layer_kernel(
    tokens_ref,
    seg_ref,
    gain_one_ref,
    bias_one_ref,
    w_qkv_hbm,
    b_val_ref,
    w_out_hbm,
    b_out_ref,
    gain_two_ref,
    bias_two_ref,
    w_up_hbm,
    b_up_ref,
    w_down_hbm,
    b_down_ref,
    cot_hbm,
    output_ref,
    tokens_grad_ref,
    vec_mid_ref,
    vec_in_ref,
    w_down_out,
    w_up_out,
    w_out_out,
    w_qkv_out,
    first_out,
    *scratch,
):
    (
        w_out_ref, w_up_ref, w_down_ref, w_qkv_ref, cot_ref, load_sem, store_sem,
        normed_all, w_head, w_value, b_value, queries, keys, keys_zero, vals, queries_t,
        probs, gates, logit, carry, row_wide, row_acc,
        send_mix, recv_mix, send_gmix, recv_gmix, grad_rows, grad_rows_t,
        back_carry,
        send_back, recv_back, send_first, y_first, recv_first,
        lower, upper,
        unit_two_ref, rstd_two_ref,
        mixed_ref, normed_two_ref, middle_ref, out_acc, gn_acc, joined_ref,
        near_mine, near_final, near_core, near_two, near_three, near_four, near_five,
        rest_mine, rest_final, rest_core, rest_two, rest_three, rest_four, rest_five,
        out_mine, out_final, out_core, out_two, out_three, out_four, out_five,
        wkv_acc, wqq_acc, in_mine, in_core, in_x, in_final,
        extra_mine, extra_seq, extra_sum, extra_dp, extra_all,
        vec_mid_mine, vec_mid_seq, vec_mid_sum, vec_mid_dp,
        vec_in_mine, vec_in_seq, vec_in_sum, vec_in_dp,
        norm_s, norm_r, mix_s, mix_r, gmix_s, gmix_r,
        back_s, back_r, fback_y, fback_yr, fback_s, fback_r, extra_s, extra_r,
        *sums_sems, in_s, in_r, part_s, part_r, vec_s, vec_r,
    ) = scratch
    at = Places()
    dp_count, count, dp, me = at.dp_count, at.count, at.dp, at.me
    y, z, depth = at.y, at.z, at.depth
    rows, width = tokens_ref.shape[1], tokens_ref.shape[2]
    half, wide = rows // 2, 2 * HD
    coeff = select_weight / (rows * count)
    hidden_width = w_up_hbm.shape[1]
    pairs = width // wide
    score_scale = 1.0 / math.sqrt(HD)

    barrier = pltpu.get_barrier_semaphore()

    def greet_seq(step, carried):
        to = lax.rem(me + step, count)
        pl.semaphore_signal(barrier, inc=1, device_id=(dp, to), device_id_type=MESH)
        return carried

    def greet_dp(step, carried):
        to = lax.rem(dp + step, dp_count)
        pl.semaphore_signal(barrier, inc=1, device_id=(to, me), device_id_type=MESH)
        return carried

    lax.fori_loop(1, count, greet_seq, 0)
    lax.fori_loop(1, dp_count, greet_dp, 0)
    projection_load = pltpu.make_async_copy(w_qkv_hbm, w_qkv_ref, load_sem.at[3])
    projection_load.start()
    loads = [
        pltpu.make_async_copy(cot_hbm, cot_ref, load_sem.at[4]),
        pltpu.make_async_copy(w_out_hbm, w_out_ref, load_sem.at[0]),
        pltpu.make_async_copy(w_up_hbm, w_up_ref, load_sem.at[1]),
        pltpu.make_async_copy(w_down_hbm, w_down_ref, load_sem.at[2]),
    ]
    for load in loads:
        load.start()

    def exchange(src, dst, send_sem, recv_sem, target):
        return remote(src, dst, send_sem, recv_sem, (dp, target))

    tokens = tokens_ref[0].astype(jnp.float32)
    unit, _ = normalise(tokens)
    normed_all[me] = (unit * gain_one_ref[...] + bias_one_ref[...]).astype(low)
    pl.semaphore_wait(barrier, count + dp_count - 2)

    def part_of(block, part):
        return normed_all.at[block, pl.ds(part * half, half)]

    def pass_on(block, part, way, target):
        here = part_of(block, part)
        return exchange(here, here, norm_s.at[way], norm_r.at[block * 2 + part], target)

    def pass_y(block, part):
        pass_on(block, part, 0, z * 2 + 1 - y).start()

    def pass_up(block, part):
        pass_on(block, part, 1, me + 2).start()

    def pass_down(block, part):
        pass_on(block, part, 2, me - 2).start()

    def arrived(block, part):
        wait_all(part_of(block, part), norm_r.at[block * 2 + part])

    def has_up(zz):
        return zz < depth - 1

    for part in range(2):
        pl.when(has_up(z))(functools.partial(pass_up, me, part))
        pl.when(z > 0)(functools.partial(pass_down, me, part))
        pass_y(me, part)

    def relay(distance):
        def from_below():
            block = me - 2 * distance
            for part in range(2):
                arrived(block, part)
                pl.when(has_up(z))(functools.partial(pass_up, block, part))
                pass_y(block, part)

        def from_above():
            block = me + 2 * distance
            for part in range(2):
                arrived(block, part)
                pl.when(z > 0)(functools.partial(pass_down, block, part))
                pass_y(block, part)

        pl.when(z - distance >= 0)(from_below)
        pl.when(z + distance < depth)(from_above)

    projection_load.wait()

    odd_head = lax.rem(me, 2) == 1
    pair_at_lane = pl.multiple_of((me // 2) * wide, wide)

    def head_columns(part):
        columns = w_qkv_ref[:, pl.ds(part * width + pair_at_lane, wide)].astype(jnp.float32)
        return jnp.where(odd_head, swap_halves(columns), columns)

    def zero_columns(part):
        return swap_halves(w_qkv_ref[:, part * width : part * width + wide].astype(jnp.float32))

    w_head[:, :wide] = (join_heads(head_columns(0), zero_columns(0)) * score_scale).astype(low)
    w_head[:, wide:] = join_heads(head_columns(1), zero_columns(1)).astype(low)
    w_value[...] = head_columns(2).astype(low)
    bias = b_val_ref[:, pl.ds(pair_at_lane, wide)]
    b_value[...] = jnp.where(odd_head, swap_halves(bias), bias)

    ids = seg_ref[...]
    start_one = jnp.sum(jnp.where(ids < 1, 1.0, 0.0), axis=1, keepdims=True)
    start_two = jnp.sum(jnp.where(ids < 2, 1.0, 0.0), axis=1, keepdims=True)
    square = (rows, rows)
    row_at = lax.broadcasted_iota(jnp.int32, square, 0)
    col_at = lax.broadcasted_iota(jnp.int32, square, 1)
    lower[...] = jnp.where(row_at > col_at, -coeff, 0.0).astype(low)
    upper[...] = jnp.where(row_at < col_at, -coeff, 0.0).astype(low)
    lane = lax.broadcasted_iota(jnp.int32, (rows, wide), 1)

    def masks(i, j):
        query_pos = lax.broadcasted_iota(jnp.int32, (rows, 1), 0).astype(jnp.float32) + ((i - j) * rows).astype(jnp.float32)
        key_start = (j * rows).astype(jnp.float32)
        begin_one, begin_two = start_one - key_start, start_two - key_start
        begin = jnp.where(query_pos >= begin_two, begin_two, jnp.where(query_pos >= begin_one, begin_one, -key_start))
        key_pos = col_at.astype(jnp.float32)
        inside = key_pos >= begin
        return inside & (key_pos <= query_pos), inside & (key_pos < query_pos)

    def pair_at(i, j):
        return i * (i + 1) // 2 + j

    carry[...] = jnp.zeros_like(carry)
    row_wide[...] = jnp.full_like(row_wide, neg_large)

    def project(block):
        normed = normed_all[block]
        both = dot_nn(normed, w_head[...])
        query = both[:, :wide]
        queries[block] = query.astype(low)
        queries_t[block] = query.T.astype(low)
        key = both[:, wide:]
        keys[block] = jnp.where(lane < HD, key, 0.0).astype(low)
        keys_zero[block] = jnp.where(lane < HD, 0.0, key).astype(low)
        value = dot_nn(normed, w_value[...]) + b_value[...]
        vals[block] = jnp.where(lane < HD, value, jnp.where(lane < HD + 2, 1.0, 0.0)).astype(low)

    def kept_at(i):
        return pair_at(i, 0) - i // (count - 1) * (count - 2)

    def grads_at(j):
        return pair_at(count - 1, j)

    def forward_group(group, masked):
        spots = [pair_at(i, j) for i, j in group]
        zero_scores = [dot_nt(queries[i], keys_zero[j]) for i, j in group]
        scores = [dot_nt(queries[i], keys[j]) for i, j in group]
        softs, gate_rows, attends = [], [], {}
        for k, (i, j) in enumerate(group):
            score = zero_scores[k]
            soft = jnp.maximum(score, 0.0) + jnp.log(1.0 + jnp.exp(-jnp.abs(score)))
            gate = jnp.exp(score - soft)
            if k in masked:
                attends[k], select = masks(i, j)
                soft = jnp.where(select, soft, 0.0)
                gate = jnp.where(select, gate, 0.0)
            softs.append(soft.astype(low))
            gate_rows.append(gate)
        falls = [dot_nn(lower[...], soft) for soft in softs]
        for k, spot in enumerate(spots):
            gates[spot] = gate_rows[k].astype(low)
        for k, (i, j) in enumerate(group):
            forgot = falls[k] + carry[j]
            carry[j] = forgot[rows - 1 :] - coeff * softs[k][rows - 1 :].astype(jnp.float32)
            scores[k] = scores[k] + forgot
            if k in masked:
                scores[k] = jnp.where(attends[k], scores[k], neg_large)
        for k, spot in enumerate(spots):
            logit[spot] = scores[k]
        for k, (i, _) in enumerate(group):
            top = row_wide[i]
            for start in range(0, rows, wide):
                top = jnp.maximum(top, scores[k][:, start : start + wide])
            row_wide[i] = top

    def in_groups(total, act, after_four=None):
        def four(group, carried):
            act(group * 4, 4)
            if after_four is not None:
                pl.when((group == 0) & (total > 4))(after_four)
            return carried

        lax.fori_loop(0, total // 4, four, 0)
        for left in (1, 2, 3):
            pl.when(lax.rem(total, 4) == left)(lambda left=left: act(total - left, left))

    def weigh_row(i):
        top = jnp.max(row_wide[i], axis=1, keepdims=True)
        row_acc[...] = jnp.zeros_like(row_acc)

        def weigh(start, size):
            found = [jnp.exp(logit[pair_at(i, start + k)] - top).astype(low) for k in range(size)]
            added = None
            for k, prob in enumerate(found):
                product = dot_nn(prob, vals[start + k])
                added = product if added is None else added + product
            for k, prob in enumerate(found):
                probs[pair_at(i, start + k)] = prob
            row_acc[...] += added

        in_groups(i + 1, weigh)
        mixed = row_acc[...]
        inverse = 1.0 / mixed[:, HD : HD + 1]
        mixed = mixed * inverse
        logit[kept_at(i), :, :wide] = jnp.where(lane < HD, mixed, inverse)
        send_mix[i] = fold_rows(mixed).astype(low)

        @pl.when(i != me)
        def _():
            exchange(send_mix.at[i], recv_mix.at[me], mix_s.at[0], mix_r.at[0], i).start()

    upwards = 1 - z // (depth // 2)
    at_end = (z == 0) | (z == depth - 1)
    pl.when(jnp.logical_not(at_end))(functools.partial(relay, 1))

    def forward_step(step, carried):
        block = upwards * step + (1 - upwards) * (count - 1 - step)
        group = step // 2

        @pl.when(lax.rem(block, 2) != y)
        def _():
            arrived(block, 0)
            arrived(block, 1)
            for distance in range(1, depth):
                pl.when(at_end & (group + 1 == distance))(functools.partial(relay, distance))
                pl.when(jnp.logical_not(at_end) & (group + 2 == distance))(functools.partial(relay, distance))

        project(block)

        def group(start, size, all_masked=False):
            members = []
            for k in range(size):
                i = upwards * step + (1 - upwards) * (block + start + k)
                j = upwards * (start + k) + (1 - upwards) * block
                members.append((i, j))
            forward_group(members, range(size) if all_masked else (0, size - 1))

        last = step == count - 1
        pl.when(jnp.logical_not(last))(lambda: in_groups(step + 1, group))

        @pl.when(last)
        def _():
            def four(start, carried):
                group(start * 4, 4, True)
                return carried

            lax.fori_loop(0, count // 4, four, 0)

        pl.when(upwards == 1)(functools.partial(weigh_row, block))
        return carried

    lax.fori_loop(0, count, forward_step, 0)

    def late_weigh(i, carried):
        weigh_row(i)
        return carried

    lax.fori_loop(0, (1 - upwards) * count, late_weigh, 0)
    recv_mix[me] = send_mix[me]

    for load in loads:
        load.wait()

    wait_all(recv_mix.at[pl.ds(0, count - 1)], mix_r.at[0])
    for pair in range(pairs):
        even = recv_mix[2 * pair].astype(jnp.float32)
        odd = recv_mix[2 * pair + 1].astype(jnp.float32)
        columns = pl.ds(pair * wide, wide)
        mixed_ref[pl.ds(0, half), columns] = join_heads(even, swap_halves(odd)).astype(low)
        mixed_ref[pl.ds(half, half), columns] = join_heads(swap_halves(even), odd).astype(low)
    middle = tokens_ref[0].astype(jnp.float32) + dot_nn(mixed_ref[...], w_out_ref[...]) + b_out_ref[...]
    middle_ref[...] = middle
    unit, rstd = normalise(middle)
    unit_two_ref[...] = unit
    rstd_two_ref[...] = rstd
    normed_two_ref[...] = (unit * gain_two_ref[...] + bias_two_ref[...]).astype(low)
    out_acc[...] = jnp.zeros_like(out_acc)
    gn_acc[...] = jnp.zeros_like(gn_acc)
    near_sum = StagedSum(at, near_x, near_mine, near_final, (near_core, near_two, near_three, near_four, near_five), sums_sems[:4])
    rest_sum = StagedSum(at, rest_x, rest_mine, rest_final, (rest_core, rest_two, rest_three, rest_four, rest_five), sums_sems[4:8])
    out_sum = StagedSum(at, out_x, out_mine, out_final, (out_core, out_two, out_three, out_four, out_five), sums_sems[8:12])
    in_sum = StagedSum(at, False, None, in_final, None, (None, None, in_s, in_r))
    mid_vec = VectorSum(at, vec_mid_mine, vec_mid_seq, vec_mid_sum, vec_mid_dp, vec_s, vec_r, 0)
    in_vec = VectorSum(at, vec_in_mine, vec_in_seq, vec_in_sum, vec_in_dp, vec_s, vec_r, 2)
    chunk = width
    chunks = hidden_width // chunk
    half_hidden = hidden_width // 2

    def dense(sums, base, c, carried):
        start = pl.multiple_of((base + c) * chunk, chunk)
        cols = pl.ds(start, chunk)
        hidden = dot_nn(normed_two_ref[...], w_up_ref[:, cols]) + b_up_ref[:, cols]
        cdf = exact_cdf(hidden)
        slope = cdf + hidden * jnp.exp(-0.5 * hidden * hidden) * (1.0 / math.sqrt(2.0 * math.pi))
        active = (hidden * cdf).astype(low)
        out_acc[...] += dot_nn(active, w_down_ref[cols, :])
        grad_hidden = (dot_nt(cot_ref[0], w_down_ref[cols, :]) * slope).astype(low)
        here = pl.multiple_of(c * chunk, chunk)
        sums[pl.ds(here, chunk), :] = dot_tn(active, cot_ref[0]).astype(low)
        there = pl.multiple_of(sums.shape[0] // 2 + here, 16)
        sums[pl.ds(there, chunk), :] = dot_tn(normed_two_ref[...], grad_hidden).astype(low)
        vec_mid_mine[pl.ds(base + c, 1), :] = jnp.sum(grad_hidden.astype(jnp.float32), axis=0, keepdims=True)
        gn_acc[...] += dot_nt(grad_hidden, w_up_ref[:, cols])
        return carried

    lax.fori_loop(0, chunks // 2, functools.partial(dense, near_mine, 0), 0)
    near_sum.send(0)
    lax.fori_loop(0, chunks // 2, functools.partial(dense, rest_mine, chunks // 2), 0)
    rest_sum.send(0)
    near_sum.send(1)
    cot = cot_ref[0].astype(jnp.float32)
    grad = gn_acc[...]
    unit = unit_two_ref[...]
    middle = cot + normalise_back(grad, unit, rstd_two_ref[...], gain_two_ref[...])
    output_ref[0] = (middle_ref[...] + out_acc[...] + b_down_ref[...]).astype(low)
    middle_ref[...] = middle
    branch = middle.astype(low)
    for pair in range(pairs):
        back = dot_nt(branch, w_out_ref[pl.ds(pair * wide, wide), :]).astype(low).astype(jnp.float32)
        top, bottom = back[:half], back[half:]
        send_gmix[2 * pair] = join_heads(top, swap_halves(bottom)).astype(low)
        send_gmix[2 * pair + 1] = join_heads(swap_halves(top), bottom).astype(low)

    def send_grads(step, carried):
        to = lax.rem(me + step, count)
        exchange(send_gmix.at[to], recv_gmix.at[me], gmix_s.at[0], gmix_r.at[me], to).start()
        return carried

    lax.fori_loop(1, count, send_grads, 0)
    recv_gmix[me] = send_gmix[me]
    out_mine[...] = dot_tn(mixed_ref[...], branch).astype(low)
    out_sum.send(0)
    vec_mid_mine[pl.ds(chunks, 1), :] = jnp.sum(cot, axis=0, keepdims=True)
    vec_mid_mine[pl.ds(chunks + 1, 1), :] = jnp.sum(grad * unit, axis=0, keepdims=True)
    vec_mid_mine[pl.ds(chunks + 2, 1), :] = jnp.sum(grad, axis=0, keepdims=True)
    vec_mid_mine[pl.ds(chunks + 3, 1), :] = jnp.sum(branch.astype(jnp.float32), axis=0, keepdims=True)
    mid_vec.start_seq()

    def steps_of(sums):
        found = {str(stage): functools.partial(sums.send, stage) for stage in range(1, 5)}
        found["t"] = sums.turn
        found |= {"abcde"[stage]: functools.partial(sums.gather, stage) for stage in range(1, 5)}
        found["f"] = functools.partial(sums.arrive, 0)
        return found

    acts = {}
    for name, sums in (("N", near_sum), ("R", rest_sum), ("O", out_sum), ("I", in_sum)):
        acts |= {name + step: act for step, act in steps_of(sums).items()}
    acts["V1"] = mid_vec.start_dp

    def run(names):
        for name in names:
            acts[name]()

    run(before_backward)

    kv_rows = 3 * HD
    logit[pl.ds(grads_at(0), count), :kv_rows] = jnp.zeros((count, kv_rows, rows), jnp.float32)
    row_wide[...] = jnp.zeros_like(row_wide)
    back_carry[...] = jnp.zeros_like(back_carry)
    wkv_acc[...] = jnp.zeros_like(wkv_acc)
    wqq_acc[...] = jnp.zeros_like(wqq_acc)

    def prepare(i):
        @pl.when(i != me)
        def _():
            wait_all(recv_gmix.at[i], gmix_r.at[i])

        grad = jnp.where(lane < HD, spread_rows(recv_gmix[i].astype(jnp.float32)), 0.0)
        kept = logit[kept_at(i), :, :wide]
        inverse = kept[:, HD : HD + 1]
        delta = -jnp.sum(grad * kept, axis=1, keepdims=True) * inverse
        grad = grad * inverse
        grad_rows_t[i] = grad.T[:HD].astype(low)
        delta_high = delta.astype(low).astype(jnp.float32)
        grad = jnp.where(lane == HD, delta_high, jnp.where(lane == HD + 1, delta - delta_high, grad))
        grad_rows[i] = grad.astype(low)

    def backward_group(group):
        spots = [pair_at(i, j) for i, j in group]
        found = [probs[spot] for spot in spots]
        grads = [dot_nt(grad_rows[i], vals[j]) for i, j in group]
        grads = [(prob.astype(jnp.float32) * grad).astype(low) for prob, grad in zip(found, grads)]
        laters = [dot_nn(upper[...], grad) for grad in grads]
        gated = []
        for k, (i, j) in enumerate(group):
            later = laters[k] + back_carry[j]
            back_carry[j] = later[:1] - coeff * grads[k][:1].astype(jnp.float32)
            gated.append((later * gates[spots[k]].astype(jnp.float32)).astype(low))
        query_parts = [dot_nn(grads[k], keys[j]) + dot_nn(gated[k], keys_zero[j]) for k, (_, j) in enumerate(group)]
        key_parts = [
            (
                dot_nn(grad_rows_t[i], found[k]),
                dot_nn(queries_t[i, :HD], grads[k]),
                dot_nn(queries_t[i, HD:], gated[k]),
            )
            for k, (i, _) in enumerate(group)
        ]
        for k, (i, _) in enumerate(group):
            row_wide[i] += query_parts[k]
        for k, (_, j) in enumerate(group):
            for part in range(3):
                logit[grads_at(j), part * HD : (part + 1) * HD] += key_parts[k][part]

    def send_first_sum(i):
        wait_all(y_first.at[i], fback_yr.at[i])
        send_first[i] = (send_first[i].astype(jnp.float32) + y_first[i].astype(jnp.float32)).astype(low)

        @pl.when(i != me)
        def _():
            exchange(send_first.at[i], recv_first.at[z], fback_s.at[0], fback_r.at[0], i).start()

        @pl.when(i == me)
        def _():
            recv_first[z] = send_first[i]

    def block_of(step):
        return upwards * (count - 1 - step) + (1 - upwards) * step

    def send_home(step):
        block = block_of(step)

        @pl.when(block != me)
        def _():
            exchange(send_back.at[block], recv_back.at[me], back_s.at[0], back_r.at[0], block).start()

        @pl.when(lax.rem(block, 2) != y)
        def _():
            exchange(send_first.at[block], y_first.at[block], fback_y.at[0], fback_yr.at[block], z * 2 + 1 - y).start()

    def send_first_home(step):
        block = block_of(step)
        pl.when(lax.rem(block, 2) == y)(functools.partial(send_first_sum, block))

    for step in range(count):
        acts[f"B{step}"] = functools.partial(send_home, step)
        acts[f"F{step}"] = functools.partial(send_first_home, step)

    def between(step, number, names):
        if names:
            pl.when(step == number)(functools.partial(run, names))

    def backward_step(step, carried):
        block = block_of(step)
        pl.when(upwards == 1)(functools.partial(prepare, block))

        def group(start, size):
            members = []
            for k in range(size):
                i = upwards * block + (1 - upwards) * (count - 1 - start - k)
                j = upwards * (start + k) + (1 - upwards) * block
                members.append((i, j))
            backward_group(members)

        def half_way():
            for number, names in enumerate(within_steps):
                between(step, number, names)

        in_groups(count - step, group, half_way)
        flat = logit[grads_at(block), :kv_rows]
        flipped = flat[: 2 * HD].T
        first_flipped = flat[HD:].T
        grad_queries = row_wide[block] * score_scale
        send_back[block, :rows] = join_heads(grad_queries, flipped).astype(low)
        send_back[block, rows:] = fold_rows(flipped).astype(low)
        send_first[block] = join_heads(swap_halves(grad_queries), first_flipped).astype(low)

        normed = normed_all[block]
        wkv_acc[...] += dot_nn(flat.astype(low), normed)
        wqq_acc[...] += dot_nn(grad_queries.T.astype(low), normed)
        for number, names in enumerate(between_steps):
            between(step, number, names)
        return carried

    def prepare_all(i, carried):
        prepare(count - 1 - i)
        return carried

    lax.fori_loop(0, (1 - upwards) * count, prepare_all, 0)
    lax.fori_loop(0, count, backward_step, 0)
    recv_back[me] = send_back[me]

    piece = HD // 4
    core_half, x_half = 6 * piece, 3 * piece
    in_start = at.core * core_half
    in_core_copy = remote(rows_of(in_mine, (1 - at.core) * core_half, core_half), in_core, part_s.at[0], part_r.at[0], at.core_peer)
    in_x_copy = remote(rows_of(in_mine, in_start + (1 - at.x) * x_half, x_half), in_x, part_s.at[1], part_r.at[1], at.x_peer)
    each_seq = functools.partial(in_vec.each, count, me)
    each_dp = functools.partial(in_vec.each, dp_count, dp)

    def extra_over_seq(to):
        return exchange(rows_of(extra_mine, to * piece, piece), extra_seq.at[me], extra_s.at[0], extra_r.at[0], to)

    def extra_over_dp(to):
        return remote(extra_sum, extra_dp.at[dp], extra_s.at[1], extra_r.at[1], (to, me))

    def extra_gather(to):
        block = rows_of(extra_all, me * piece, piece)
        return exchange(block, block, extra_s.at[2], extra_r.at[2], to)

    def in_zero():
        for part in range(4):
            for place, (source, start) in enumerate(((wqq_acc, 0), (wkv_acc, HD), (wkv_acc, 0))):
                rows_in = pl.ds(part * 3 * piece + place * piece, piece)
                in_mine[rows_in, :] = source[start + part * piece : start + (part + 1) * piece].astype(low)
        in_core_copy.start()

    def extra_zero():
        extra_mine[:HD] = wqq_acc[HD:].astype(low)
        extra_mine[HD:] = wkv_acc[2 * HD :].astype(low)
        each_seq(lambda to: extra_over_seq(to).start())
        extra_seq[me] = extra_mine[pl.ds(pl.multiple_of(me * piece, 16), piece), :]

    def in_one():
        in_core_copy.wait_recv()
        add_rows(in_mine, in_start, [(in_mine, in_start), (in_core, 0)], core_half)
        in_x_copy.start()

    def in_turn():
        in_x_copy.wait_recv()
        add_rows(in_final, in_sum.give[5], [(in_mine, in_start + at.x * x_half), (in_x, 0)], x_half)
        in_sum.spread(5)

    def extra_one():
        wait_all(extra_seq.at[pl.ds(0, count - 1)], extra_r.at[0])
        summed = extra_seq[0].astype(jnp.float32)
        for k in range(1, count):
            summed = summed + extra_seq[k].astype(jnp.float32)
        extra_sum[...] = summed
        each_dp(lambda to: extra_over_dp(to).start())
        extra_dp[dp] = summed

    def extra_two():
        wait_all(extra_dp.at[pl.ds(0, dp_count - 1)], extra_r.at[1])
        summed = extra_dp[0]
        for k in range(1, dp_count):
            summed = summed + extra_dp[k]
        extra_all[pl.ds(pl.multiple_of(me * piece, 16), piece), :] = summed.astype(low)
        each_seq(lambda to: extra_gather(to).start())

    def first_norm_back():
        unit, rstd = normalise(tokens_ref[0].astype(jnp.float32))
        wait_all(recv_back.at[pl.ds(0, count - 1)], back_r.at[0])
        wait_all(recv_first.at[pl.ds(0, depth - 1)], fback_r.at[0])
        first_sum = recv_first[0].astype(jnp.float32)
        for source in range(1, depth):
            first_sum = first_sum + recv_first[source].astype(jnp.float32)
        for pair in range(pairs):
            even = recv_back[2 * pair, :rows].astype(jnp.float32)
            odd = recv_back[2 * pair + 1, :rows].astype(jnp.float32)
            if pair == 0:
                even = even + first_sum
            columns = wide * pair
            joined_ref[:, pl.ds(columns, wide)] = join_heads(even, swap_halves(odd)).astype(low)
            joined_ref[:, pl.ds(width + columns, wide)] = join_heads(swap_halves(even), odd).astype(low)
            even = recv_back[2 * pair, rows:].astype(jnp.float32)
            odd = recv_back[2 * pair + 1, rows:].astype(jnp.float32)
            columns = pl.ds(2 * width + columns, wide)
            joined_ref[pl.ds(0, half), columns] = join_heads(even, swap_halves(odd)).astype(low)
            joined_ref[pl.ds(half, half), columns] = join_heads(swap_halves(even), odd).astype(low)
        grad = dot_nt(joined_ref[...], w_qkv_ref[...])
        vec_in_mine[...] = jnp.zeros_like(vec_in_mine)
        vec_in_mine[pl.ds(0, 1), :] = jnp.sum(grad * unit, axis=0, keepdims=True)
        vec_in_mine[pl.ds(1, 1), :] = jnp.sum(grad, axis=0, keepdims=True)
        value_grads = joined_ref[:, pl.ds(2 * width, width)].astype(jnp.float32)
        vec_in_mine[pl.ds(2, 1), :] = jnp.sum(value_grads, axis=0, keepdims=True)
        in_vec.start_seq()
        tokens_grad_ref[0] = middle_ref[...] + normalise_back(grad, unit, rstd, gain_one_ref[...])

    stores = []

    def store(source, target):
        stores.append(pltpu.make_async_copy(source, target, store_sem.at[len(stores)]))
        stores[-1].start()

    def finish_near():
        near_sum.arrive(0)
        store(near_final.at[pl.ds(0, half_hidden)], w_down_out.at[pl.ds(0, half_hidden)])
        store(near_final.at[pl.ds(half_hidden, half_hidden)], w_up_out.at[pl.ds(0, half_hidden)])

    def finish_rest():
        rest_sum.arrive(0)
        store(rest_final.at[pl.ds(0, half_hidden)], w_down_out.at[pl.ds(half_hidden, half_hidden)])
        store(rest_final.at[pl.ds(half_hidden, half_hidden)], w_up_out.at[pl.ds(half_hidden, half_hidden)])

    def finish_out():
        out_sum.arrive(0)
        store(out_final, w_out_out)

    def finish_in():
        in_sum.arrive(0)
        store(in_final, w_qkv_out)

    def finish_extra():
        wait_all(extra_all.at[pl.ds(0, (count - 1) * piece)], extra_r.at[2])
        store(extra_all, first_out)

    def finish_mid_vec():
        vec_mid_ref[...] = mid_vec.finish()

    def finish_in_vec():
        vec_in_ref[...] = in_vec.finish()

    acts |= {
        "I0": in_zero, "I1": in_one, "It": in_turn, "E0": extra_zero, "E1": extra_one, "E2": extra_two,
        "T": first_norm_back, "W1": in_vec.start_dp, "Vf": finish_mid_vec, "Wf": finish_in_vec,
        "Nf": finish_near, "Rf": finish_rest, "Of": finish_out, "If": finish_in, "Ef": finish_extra,
    }
    run(after_backward)

    wait_all(normed_all.at[pl.ds(0, depth)], norm_s.at[0])
    for at_z in range(depth - 1):
        went = normed_all.at[pl.ds(0, at_z + 1)]
        pl.when(z == at_z)(functools.partial(wait_all, went, norm_s.at[1]))
        pl.when(z == depth - 1 - at_z)(functools.partial(wait_all, went, norm_s.at[2]))
    wait_all(send_mix.at[pl.ds(0, count - 1)], mix_s.at[0])
    wait_all(send_gmix.at[pl.ds(0, count - 1)], gmix_s.at[0])
    wait_all(send_back.at[pl.ds(0, count - 1)], back_s.at[0])
    wait_all(send_first.at[pl.ds(0, depth)], fback_y.at[0])
    wait_all(send_first.at[pl.ds(0, depth - 1)], fback_s.at[0])
    wait_all(extra_seq.at[pl.ds(0, count - 1)], extra_s.at[0])
    wait_all(extra_dp.at[pl.ds(0, dp_count - 1)], extra_s.at[1])
    wait_all(extra_all.at[pl.ds(0, (count - 1) * piece)], extra_s.at[2])
    in_core_copy.wait_send()
    in_x_copy.wait_send()
    near_sum.drain()
    rest_sum.drain()
    out_sum.drain()
    in_sum.drain()
    mid_vec.drain()
    in_vec.drain()
    for store in stores:
        store.wait()


def widen_kernel(
    output_in, tokens_grad_in, vec_mid_ref, vec_in_ref, w_down_in, w_up_in, w_out_in, w_qkv_in, first_in,
    output_out, tokens_grad_out, gain_one_out, bias_one_out, b_val_out, b_out_out, gain_two_out, bias_two_out, b_up_out, b_down_out,
    w_down_out, w_up_out, w_out_out, w_qkv_out,
    down_low, up_low, out_low, qkv_low, first_low, tokens_grad_held, output_held, down_wide, up_wide, out_wide, qkv_wide, load_sem, store_sem,
):
    width = out_low.shape[0]
    blocks = down_low.shape[0] // width
    loads = []
    for k, (source, target) in enumerate(
        (
            (w_down_in, down_low), (w_up_in, up_low), (w_qkv_in, qkv_low), (first_in, first_low), (w_out_in, out_low),
            (tokens_grad_in, tokens_grad_held), (output_in, output_held),
        )
    ):
        loads.append(pltpu.make_async_copy(source, target, load_sem.at[k]))
        loads[-1].start()
    stores = []

    def store(source, target):
        stores.append(pltpu.make_async_copy(source, target, store_sem.at[len(stores)]))
        stores[-1].start()

    for row, target in enumerate((gain_one_out, bias_one_out, b_val_out)):
        target[...] = vec_in_ref[row : row + 1, :]
    for row in range(blocks):
        b_up_out[:, row * width : (row + 1) * width] = vec_mid_ref[row : row + 1, :]
    for row, target in enumerate((b_down_out, gain_two_out, bias_two_out, b_out_out)):
        target[...] = vec_mid_ref[blocks + row : blocks + row + 1, :]

    def convert(source, target, at, columns):
        def step(k, carried):
            here = pl.ds(pl.multiple_of(at + k * 64, 64), 64)
            there = pl.ds(pl.multiple_of(k * 64, 64), 64)
            if columns is None:
                target[here, :] = source[here, :].astype(jnp.float32)
            else:
                target[there, pl.ds(columns, width)] = source[here, :].astype(jnp.float32)
            return carried

        lax.fori_loop(0, width // 64, step, 0)

    loads[0].wait()
    for block in range(blocks):
        convert(down_low, down_wide, block * width, None)
        here = pl.ds(block * width, width)
        store(down_wide.at[here], w_down_out.at[here])
    loads[1].wait()
    for block in range(blocks):
        convert(up_low, up_wide, block * width, block * width)
        here = pl.ds(block * width, width)
        store(up_wide.at[:, here], w_up_out.at[:, here])
    loads[4].wait()
    convert(out_low, out_wide, 0, None)
    store(out_wide, w_out_out)
    loads[5].wait()
    store(tokens_grad_held, tokens_grad_out)
    loads[6].wait()
    store(output_held, output_out)
    loads[2].wait()
    loads[3].wait()
    piece = HD // 4
    wide = 2 * HD
    for part in range(3):
        for pair in range(width // wide):
            found = []
            for head in (2 * pair, 2 * pair + 1):
                z, y = head // 2, head % 2
                for owner in range(4):
                    core, x = owner // 2, owner % 2
                    two, three = (x, y) if core == 0 else (y, x)
                    depth = width // wide
                    start = ((((core * 2 + two) * 2 + three) * depth + z % 2 * 2 + z // 2) * 3 + part) * piece
                    block = qkv_low[start : start + piece].astype(jnp.float32)
                    if head == 0 and part < 2:
                        at = part * HD + owner * piece
                        block = block + first_low[at : at + piece].astype(jnp.float32)
                    found.append(block)
            columns = part * width + pair * wide
            qkv_wide[:, columns : columns + wide] = jnp.concatenate(found, axis=0).T
    store(qkv_wide, w_qkv_out)
    for one in stores:
        one.wait()


def exchange_heads(
    tokens, segment_ids, gain_one, bias_one, w_qkv, b_val, w_out, b_out,
    gain_two, bias_two, w_up, b_up, w_down, b_down, cotangent,
):
    count, dp_count = lax.axis_size("seq"), lax.axis_size("dp")
    rows, width = tokens.shape[1], tokens.shape[2]
    hidden = w_up.shape[1]
    half = rows // 2
    tiles = count * (count + 1) // 2
    wide = 2 * HD
    f32 = jnp.float32
    packed = rows + half
    depth = count // 2

    def vmem(*shape, dtype=low):
        return pltpu.VMEM(shape, dtype)

    def sems(*shape):
        return pltpu.SemaphoreType.DMA(shape)

    scratch = [
        vmem(width, width), vmem(width, hidden), vmem(hidden, width), vmem(width, 3 * width), vmem(1, rows, width), sems(5), sems(8),
        vmem(count, rows, width), vmem(width, 2 * wide), vmem(width, wide), vmem(1, wide, dtype=f32),
        vmem(count, rows, wide), vmem(count, rows, wide), vmem(count, rows, wide), vmem(count, rows, wide), vmem(count, wide, rows),
        vmem(tiles, rows, rows), vmem(tiles, rows, rows), vmem(tiles, rows, rows, dtype=f32),
        vmem(count, 1, rows, dtype=f32), vmem(count, rows, wide, dtype=f32), vmem(rows, wide, dtype=f32),
        vmem(count, half, wide), vmem(count, half, wide), vmem(count, half, wide), vmem(count, half, wide), vmem(count, rows, wide), vmem(count, HD, rows),
        vmem(count, 1, rows, dtype=f32),
        vmem(count, packed, wide), vmem(count, packed, wide), vmem(count, rows, wide), vmem(count, rows, wide), vmem(depth, rows, wide),
        vmem(rows, rows), vmem(rows, rows),
        vmem(rows, width, dtype=f32), vmem(rows, 1, dtype=f32),
        vmem(rows, width), vmem(rows, width), vmem(rows, width, dtype=f32), vmem(rows, width, dtype=f32), vmem(rows, width, dtype=f32), vmem(rows, 3 * width),
    ]
    for total in (hidden, hidden, width):
        scratch += [vmem(total, width), vmem(total, width)]
        scratch += [vmem(total >> stage, width) for stage in range(1, 6)]
    scratch += [
        vmem(3 * HD, width, dtype=f32), vmem(wide, width, dtype=f32),
        vmem(3 * HD, width), vmem(3 * HD // 2, width), vmem(3 * HD // 4, width), vmem(3 * width, width),
        vmem(wide, width), vmem(count, wide // count, width), vmem(wide // count, width, dtype=f32), vmem(dp_count, wide // count, width, dtype=f32), vmem(wide, width),
    ]
    for _ in range(2):
        scratch += [vmem(8, width, dtype=f32), vmem(count, 8, width, dtype=f32), vmem(8, width, dtype=f32), vmem(dp_count, 8, width, dtype=f32)]
    scratch += [sems(3), sems(2 * count), sems(1), sems(1), sems(1), sems(count)]
    scratch += [sems(1), sems(1), sems(1), sems(count), sems(1), sems(1), sems(3), sems(3)]
    scratch += [sems(1), sems(5)] * 6
    scratch += [sems(1), sems(5), sems(2), sems(2), sems(4), sems(4)]
    in_vmem = pl.BlockSpec(memory_space=pltpu.VMEM)
    anywhere = pl.BlockSpec(memory_space=pl.ANY)
    specs = [in_vmem] * 15
    for at in (4, 6, 10, 12, 14):
        specs[at] = anywhere
    shape = jax.ShapeDtypeStruct
    results = pl.pallas_call(
        layer_kernel,
        out_shape=[
            shape((1, rows, width), low), shape((1, rows, width), f32), shape((8, width), f32), shape((8, width), f32),
            shape((hidden, width), low), shape((hidden, width), low), shape((width, width), low), shape((3 * width, width), low), shape((wide, width), low),
        ],
        in_specs=specs,
        out_specs=[in_vmem] * 4 + [anywhere] * 5,
        scratch_shapes=scratch,
        compiler_params=pltpu.CompilerParams(
            collective_id=0, has_side_effects=True, vmem_limit_bytes=vmem_bytes
        ),
    )(
        tokens, segment_ids, gain_one[None], bias_one[None], w_qkv, b_val[None], w_out, b_out[None],
        gain_two[None], bias_two[None], w_up, b_up[None], w_down, b_down[None], cotangent,
    )
    vector = shape((1, width), f32)
    widened = pl.pallas_call(
        widen_kernel,
        out_shape=[
            shape((1, rows, width), low), shape((1, rows, width), f32), vector, vector, vector, vector, vector, vector, shape((1, hidden), f32), vector,
            shape((hidden, width), f32), shape((width, hidden), f32), shape((width, width), f32), shape((width, 3 * width), f32),
        ],
        in_specs=[anywhere] * 2 + [in_vmem] * 2 + [anywhere] * 5,
        out_specs=[anywhere] * 2 + [in_vmem] * 8 + [anywhere] * 4,
        scratch_shapes=[
            vmem(hidden, width), vmem(hidden, width), vmem(width, width), vmem(3 * width, width), vmem(wide, width), vmem(1, rows, width, dtype=f32), vmem(1, rows, width),
            vmem(hidden, width, dtype=f32), vmem(width, hidden, dtype=f32), vmem(width, width, dtype=f32), vmem(width, 3 * width, dtype=f32),
            sems(7), sems(12),
        ],
        compiler_params=pltpu.CompilerParams(vmem_limit_bytes=vmem_bytes),
    )(*results)
    output, tokens_grad = widened[:2]
    gain_one_grad, bias_one_grad, b_val_grad, b_out_grad, gain_two_grad, bias_two_grad, b_up_grad, b_down_grad = (
        row.reshape(row.shape[1]) for row in widened[2:10]
    )
    w_down_grad, w_up_grad, w_out_grad, w_qkv_grad = widened[10:]
    return (
        output, tokens_grad, gain_one_grad, bias_one_grad, w_qkv_grad, b_val_grad, w_out_grad, b_out_grad,
        gain_two_grad, bias_two_grad, w_up_grad, b_up_grad, w_down_grad, b_down_grad,
    )


def picks_heads(mesh, length, width, hidden):
    dp_count, count = mesh.shape["dp"], mesh.shape["seq"]
    power = length & (length - 1) == 0
    return dp_count == 4 and count == 8 and width == count * HD and hidden == 4 * width and power


def solution(mesh):
    placed = (
        P("dp", "seq", None),
        P("dp", None),
        P(),
        P(),
        P(),
        P(),
        P(),
        P(),
        P(),
        P(),
        P(),
        P(),
        P(),
        P(),
        P("dp", "seq", None),
    )

    def layer(tokens, *others):
        width, hidden = tokens.shape[-1], others[9].shape[-1]
        length = tokens.shape[1] * mesh.shape["seq"]
        body = exchange_heads if picks_heads(mesh, length, width, hidden) else local
        return body(tokens, *others)

    return jax.shard_map(
        layer,
        mesh=mesh,
        in_specs=placed,
        out_specs=(
            P("dp", "seq", None),
            P("dp", "seq", None),
            P(),
            P(),
            P(),
            P(),
            P(),
            P(),
            P(),
            P(),
            P(),
            P(),
            P(),
            P(),
        ),
        check_vma=False,
    )
```

```python
import functools
import math

import jax
import jax.numpy as jnp
from jax import lax
from jax.experimental import pallas as pl
from jax.experimental.pallas import tpu as pltpu
from jax.sharding import PartitionSpec as P

HD = 64


norm_eps = 1e-05
select_weight = 4.0
neg_large = -1e30
highest = lax.Precision.HIGHEST
vmem_bytes = 63 * 1024 * 1024


def prefix(array, axis, combine, identity, reverse):
    length, here = (lax.axis_size(axis), lax.axis_index(axis))
    everything = lax.all_gather(array.astype(jnp.bfloat16), axis)
    start = jnp.broadcast_to(jnp.asarray(identity, array.dtype), array.shape)

    def hop(k, before):
        at = length - 1 - k if reverse else k
        reached = at > here if reverse else at < here
        new = combine(before, everything[at].astype(array.dtype))
        return jnp.where(reached, new, before)

    return lax.fori_loop(0, length, hop, start)


def layer_norm(values, norm_gain, norm_shift):
    centered = values - jnp.mean(values, axis=-1, keepdims=True)
    variance = jnp.mean(centered * centered, axis=-1, keepdims=True)
    return centered * lax.rsqrt(variance + norm_eps) * norm_gain + norm_shift


def exact_gelu(values):
    return jax.nn.gelu(values, approximate=False)


def add_arrays(earlier, later):
    return earlier + later


def keep_state(state_in):
    return state_in


def pick_block():
    return 512


def local(
    tokens,
    segment_ids,
    gain_one,
    bias_one,
    w_qkv,
    b_val,
    w_out,
    b_out,
    gain_two,
    bias_two,
    w_up,
    b_up,
    w_down,
    b_down,
    cotangent,
):
    seq_count = lax.axis_size("seq")
    seq_rank = lax.axis_index("seq")
    row_tokens = tokens[0].astype(jnp.float32)
    tok_rows = row_tokens.shape[0]
    model_width = row_tokens.shape[1]
    head_count = model_width // HD
    length = tok_rows * seq_count
    score_scale = 1.0 / math.sqrt(HD)
    select_coeff = select_weight / length
    row_segments = segment_ids[0]
    row_base = seq_rank * tok_rows
    query_pos = row_base + jnp.arange(tok_rows, dtype=jnp.int32)
    query_segs = lax.dynamic_slice_in_dim(row_segments, row_base, tok_rows)
    last_query = row_base + tok_rows - 1
    lower_mask = (jnp.arange(tok_rows)[:, None] > jnp.arange(tok_rows)[None, :]).astype(jnp.float32)
    upper_mask = lower_mask.T
    normed_one, norm_one_back = jax.vjp(layer_norm, row_tokens, gain_one, bias_one)
    normed_one_low = normed_one.astype(jnp.bfloat16)
    value_bias = jnp.concatenate([jnp.zeros((2 * model_width,), jnp.float32), b_val])
    joined_low = (
        jnp.dot(normed_one_low, w_qkv, preferred_element_type=jnp.float32) + value_bias
    ).astype(jnp.bfloat16)
    queries = joined_low[:, :model_width]
    keys_mine = joined_low[:, model_width : 2 * model_width]
    values_mine = joined_low[:, 2 * model_width :]
    query_heads = queries.reshape(tok_rows, head_count, HD)
    query_zero = queries[:, :HD]
    query_rest = query_heads[:, 1:]

    def pair_masks(key_start, key_rows):
        key_pos = key_start + jnp.arange(key_rows, dtype=jnp.int32)
        key_segs = lax.dynamic_slice_in_dim(row_segments, key_start, key_rows)
        same_doc = query_segs[:, None] == key_segs[None, :]
        attend_mask = same_doc & (key_pos[None, :] <= query_pos[:, None])
        select_mask = same_doc & (key_pos[None, :] < query_pos[:, None])
        return (attend_mask, select_mask)

    select_init = (
        jnp.zeros((tok_rows, length), jnp.float32),
        jnp.zeros((tok_rows, length), jnp.float32),
        jnp.zeros((length,), jnp.float32),
    )
    running = select_init
    key_piece = lax.all_gather(keys_mine[:, :HD], "seq", axis=0, tiled=True)
    piece_rows = key_piece.shape[0]
    block_rows = pick_block()

    def select_block(state_now, offset):
        zero_scores, local_forgot, column_sums = state_now
        key_block = lax.dynamic_slice_in_dim(key_piece, offset, block_rows)
        attend_mask, select_mask = pair_masks(offset, block_rows)
        scores = (
            jnp.einsum("qd,kd->qk", query_zero, key_block, preferred_element_type=jnp.float32)
            * score_scale
        )
        chosen = jnp.where(select_mask, jax.nn.softplus(scores), 0.0)
        forgot = jnp.dot(lower_mask, chosen, precision=highest)
        zero_scores = lax.dynamic_update_slice_in_dim(zero_scores, scores, offset, 1)
        local_forgot = lax.dynamic_update_slice_in_dim(local_forgot, forgot, offset, 1)
        column_sums = lax.dynamic_update_slice_in_dim(
            column_sums, jnp.sum(chosen, axis=0), offset, 0
        )
        return ((zero_scores, local_forgot, column_sums), None)

    offsets = jnp.arange(piece_rows // block_rows, dtype=jnp.int32) * block_rows
    running, unused = lax.scan(select_block, running, offsets)
    zero_scores, local_forgot, column_sums = running
    column_prefix = prefix(column_sums, "seq", add_arrays, jnp.zeros((length,), jnp.float32), False)
    attend_init = (
        jnp.full((head_count, tok_rows), neg_large, jnp.float32),
        jnp.zeros((head_count, tok_rows), jnp.float32),
        jnp.zeros((tok_rows, head_count, HD), jnp.float32),
    )
    running = attend_init
    attend_key_piece = lax.all_gather(keys_mine, "seq", axis=0, tiled=True)
    value_piece = lax.all_gather(values_mine, "seq", axis=0, tiled=True)
    piece_rows = attend_key_piece.shape[0]
    attend_block_rows = pick_block()

    def attend_block(state_now, offset):
        key_start = offset

        def attend_compute(state_in):
            run_max, run_total, accumulated = state_in
            key_block = lax.dynamic_slice_in_dim(
                attend_key_piece, offset, attend_block_rows
            ).reshape(attend_block_rows, head_count, HD)
            value_block = lax.dynamic_slice_in_dim(value_piece, offset, attend_block_rows).reshape(
                attend_block_rows, head_count, HD
            )
            attend_mask, select_mask = pair_masks(key_start, attend_block_rows)
            rest_scores = (
                jnp.einsum(
                    "qhd,khd->hqk", query_rest, key_block[:, 1:], preferred_element_type=jnp.float32
                )
                * score_scale
            )
            head_zero = lax.dynamic_slice_in_dim(zero_scores, key_start, attend_block_rows, 1)
            scores = jnp.concatenate([head_zero[None], rest_scores], axis=0)
            forgot = lax.dynamic_slice_in_dim(column_prefix, key_start, attend_block_rows)[
                None, :
            ] + lax.dynamic_slice_in_dim(local_forgot, key_start, attend_block_rows, 1)
            logits = jnp.where(attend_mask[None], scores - select_coeff * forgot[None], neg_large)
            new_max = jnp.maximum(run_max, jnp.max(logits, axis=-1))
            weights = jnp.where(attend_mask[None], jnp.exp(logits - new_max[:, :, None]), 0.0)
            decay_factor = jnp.exp(run_max - new_max)
            run_total = run_total * decay_factor + jnp.sum(weights, axis=-1)
            accumulated = accumulated * decay_factor.T[:, :, None] + jnp.einsum(
                "hqk,khd->qhd",
                weights.astype(jnp.bfloat16),
                value_block,
                preferred_element_type=jnp.float32,
            )
            return (new_max, run_total, accumulated)

        state_now = lax.cond(key_start <= last_query, attend_compute, keep_state, state_now)
        return (state_now, None)

    offsets = jnp.arange(piece_rows // attend_block_rows, dtype=jnp.int32) * attend_block_rows
    running, unused = lax.scan(attend_block, running, offsets)
    run_max, run_total, accumulated = running
    log_total = run_max + jnp.log(run_total)
    mixed_float = accumulated / run_total.T[:, :, None]
    mixed_low = mixed_float.reshape(tok_rows, model_width).astype(jnp.bfloat16)
    middle = row_tokens + jnp.dot(mixed_low, w_out, preferred_element_type=jnp.float32) + b_out
    normed_two, norm_two_back = jax.vjp(layer_norm, middle, gain_two, bias_two)
    normed_two_low = normed_two.astype(jnp.bfloat16)
    hidden = jnp.dot(normed_two_low, w_up, preferred_element_type=jnp.float32) + b_up
    active, gelu_back = jax.vjp(exact_gelu, hidden)
    active_low = active.astype(jnp.bfloat16)
    output = middle + jnp.dot(active_low, w_down, preferred_element_type=jnp.float32) + b_down
    grad_out = cotangent[0]
    grad_float = grad_out.astype(jnp.float32)
    w_down_grad = jnp.einsum("tf,td->fd", active_low, grad_out, preferred_element_type=jnp.float32)
    b_down_grad = jnp.sum(grad_float, axis=0)
    grad_active = jnp.einsum("td,fd->tf", grad_out, w_down, preferred_element_type=jnp.float32)
    (grad_hidden,) = gelu_back(grad_active)
    grad_hidden_low = grad_hidden.astype(jnp.bfloat16)
    w_up_grad = jnp.einsum(
        "td,tf->df", normed_two_low, grad_hidden_low, preferred_element_type=jnp.float32
    )
    b_up_grad = jnp.sum(grad_hidden_low.astype(jnp.float32), axis=0)
    grad_normed_two = jnp.einsum(
        "tf,df->td", grad_hidden_low, w_up, preferred_element_type=jnp.float32
    )
    grad_middle_norm, gain_two_grad, bias_two_grad = norm_two_back(grad_normed_two)
    grad_middle = grad_float + grad_middle_norm
    grad_branch_low = grad_middle.astype(jnp.bfloat16)
    w_out_grad = jnp.einsum(
        "td,te->de", mixed_low, grad_branch_low, preferred_element_type=jnp.float32
    )
    b_out_grad = jnp.sum(grad_branch_low.astype(jnp.float32), axis=0)
    grad_mixed_low = jnp.einsum(
        "te,de->td", grad_branch_low, w_out, preferred_element_type=jnp.float32
    ).astype(jnp.bfloat16)
    grad_mixed_heads = grad_mixed_low.reshape(tok_rows, head_count, HD)
    row_delta = jnp.sum(grad_mixed_heads.astype(jnp.float32) * mixed_float, axis=-1).T
    keys_back, values_back = (
        lax.all_gather(keys_mine, "seq", axis=0, tiled=True),
        lax.all_gather(values_mine, "seq", axis=0, tiled=True),
    )
    back_rows = pick_block()
    key_heads = keys_back.reshape(length, head_count, HD)
    value_heads = values_back.reshape(length, head_count, HD)

    def grad_block(state_now, offset):

        def grad_compute(state_in):
            query_grad, key_grad, value_grad, first_part, second_part, grad_cols = state_in
            key_block = lax.dynamic_slice_in_dim(key_heads, offset, back_rows)
            value_block = lax.dynamic_slice_in_dim(value_heads, offset, back_rows)
            attend_mask, select_mask = pair_masks(offset, back_rows)
            scores = (
                jnp.einsum(
                    "qhd,khd->hqk", query_heads, key_block, preferred_element_type=jnp.float32
                )
                * score_scale
            )
            chosen = jnp.where(select_mask, jax.nn.softplus(scores[0]), 0.0)
            forgot = lax.dynamic_slice_in_dim(column_prefix, offset, back_rows)[None, :] + jnp.dot(
                lower_mask, chosen, precision=highest
            )
            logits = scores - select_coeff * forgot[None]
            prob_block = jnp.where(attend_mask[None], jnp.exp(logits - log_total[:, :, None]), 0.0)
            grad_probs = jnp.einsum(
                "qhd,khd->hqk", grad_mixed_heads, value_block, preferred_element_type=jnp.float32
            )
            grad_logits = prob_block * (grad_probs - row_delta[:, :, None])
            value_part = jnp.einsum(
                "hqk,qhd->khd",
                prob_block.astype(jnp.bfloat16),
                grad_mixed_heads,
                preferred_element_type=jnp.float32,
            )
            rest_low = grad_logits[1:].astype(jnp.bfloat16)
            query_grad = (
                query_grad
                + jnp.einsum(
                    "hqk,khd->qhd", rest_low, key_block[:, 1:], preferred_element_type=jnp.float32
                )
                * score_scale
            )
            key_part = (
                jnp.einsum("hqk,qhd->khd", rest_low, query_rest, preferred_element_type=jnp.float32)
                * score_scale
            )
            total_grad = jnp.sum(grad_logits, axis=0)
            suffix_local = jnp.dot(upper_mask, total_grad, precision=highest)
            select_gate = jnp.where(select_mask, select_coeff * jax.nn.sigmoid(scores[0]), 0.0)
            first_part = lax.dynamic_update_slice_in_dim(
                first_part, grad_logits[0] - select_gate * suffix_local, offset, 1
            )
            second_part = lax.dynamic_update_slice_in_dim(second_part, select_gate, offset, 1)
            key_grad = lax.dynamic_update_slice_in_dim(key_grad, key_part, offset, 0)
            value_grad = lax.dynamic_update_slice_in_dim(value_grad, value_part, offset, 0)
            grad_cols = lax.dynamic_update_slice_in_dim(
                grad_cols, jnp.sum(total_grad, axis=0), offset, 0
            )
            return (query_grad, key_grad, value_grad, first_part, second_part, grad_cols)

        state_now = lax.cond(offset <= last_query, grad_compute, keep_state, state_now)
        return (state_now, None)

    grad_init = (
        jnp.zeros((tok_rows, head_count - 1, HD), jnp.float32),
        jnp.zeros((length, head_count - 1, HD), jnp.float32),
        jnp.zeros((length, head_count, HD), jnp.float32),
        jnp.zeros((tok_rows, length), jnp.float32),
        jnp.zeros((tok_rows, length), jnp.float32),
        jnp.zeros((length,), jnp.float32),
    )
    back_offsets = jnp.arange(length // back_rows, dtype=jnp.int32) * back_rows
    grad_state, unused = lax.scan(grad_block, grad_init, back_offsets)
    query_grad, key_grad, value_grad, first_part, second_part, grad_cols = grad_state
    grad_suffix = prefix(grad_cols, "seq", add_arrays, jnp.zeros((length,), jnp.float32), True)
    zero_grad_low = (first_part - second_part * grad_suffix[None, :]).astype(jnp.bfloat16)
    query_zero_grad = (
        jnp.dot(zero_grad_low, keys_back[:, :HD], preferred_element_type=jnp.float32) * score_scale
    )
    key_zero_grad = (
        jnp.einsum("ql,qd->ld", zero_grad_low, query_zero, preferred_element_type=jnp.float32)
        * score_scale
    )
    key_total = jnp.concatenate([key_zero_grad[:, None, :], key_grad], axis=1).reshape(
        length, model_width
    )
    value_total = value_grad.reshape(length, model_width)
    key_mine_grad, value_mine_grad = (
        lax.psum_scatter(
            key_total.astype(jnp.bfloat16), "seq", scatter_dimension=0, tiled=True
        ).astype(jnp.float32),
        lax.psum_scatter(
            value_total.astype(jnp.bfloat16), "seq", scatter_dimension=0, tiled=True
        ).astype(jnp.float32),
    )
    query_total = jnp.concatenate([query_zero_grad[:, None, :], query_grad], axis=1).reshape(
        tok_rows, model_width
    )
    grad_joined_low = jnp.concatenate([query_total, key_mine_grad, value_mine_grad], axis=1).astype(
        jnp.bfloat16
    )
    b_val_grad = jnp.sum(grad_joined_low[:, 2 * model_width :].astype(jnp.float32), axis=0)
    w_qkv_grad = jnp.einsum(
        "td,te->de", normed_one_low, grad_joined_low, preferred_element_type=jnp.float32
    )
    grad_normed_one = jnp.einsum(
        "te,de->td", grad_joined_low, w_qkv, preferred_element_type=jnp.float32
    )
    grad_tokens_norm, gain_one_grad, bias_one_grad = norm_one_back(grad_normed_one)
    tokens_grad = grad_middle + grad_tokens_norm
    summed = lax.psum(
        (
            gain_one_grad,
            bias_one_grad,
            w_qkv_grad,
            b_val_grad,
            w_out_grad,
            b_out_grad,
            gain_two_grad,
            bias_two_grad,
            w_up_grad,
            b_up_grad,
            w_down_grad,
            b_down_grad,
        ),
        ("dp", "seq"),
    )
    return (
        output.astype(jnp.bfloat16)[None],
        tokens_grad[None],
        summed[0],
        summed[1],
        summed[2],
        summed[3],
        summed[4],
        summed[5],
        summed[6],
        summed[7],
        summed[8],
        summed[9],
        summed[10],
        summed[11],
    )


low = jnp.bfloat16
MESH = pl.DeviceIdType.MESH


def dot_nn(left, right):
    return lax.dot_general(left, right, (((1,), (0,)), ((), ())), preferred_element_type=jnp.float32)


def dot_nt(left, right):
    return lax.dot_general(left, right, (((1,), (1,)), ((), ())), preferred_element_type=jnp.float32)


def dot_tn(left, right):
    return lax.dot_general(left, right, (((0,), (0,)), ((), ())), preferred_element_type=jnp.float32)


def swap_halves(wide):
    return pltpu.roll(wide, HD, 1)


def left_lanes(shape):
    return lax.broadcasted_iota(jnp.int32, shape, 1) < HD


def join_heads(left, right):
    return jnp.where(left_lanes(left.shape), left, right)


def fold_rows(wide):
    half = wide.shape[0] // 2
    return join_heads(wide[:half], swap_halves(wide[half:]))


def spread_rows(folded):
    return jnp.concatenate([folded, swap_halves(folded)], axis=0)


def exact_cdf(values):
    return 0.5 * (1.0 + lax.erf(values * (1.0 / math.sqrt(2.0))))


def normalise(values):
    centered = values - jnp.mean(values, axis=-1, keepdims=True)
    rstd = lax.rsqrt(jnp.mean(centered * centered, axis=-1, keepdims=True) + norm_eps)
    return centered * rstd, rstd


def normalise_back(grad, unit, rstd, gain):
    scaled = grad * gain
    mean_one = jnp.mean(scaled, axis=-1, keepdims=True)
    mean_two = jnp.mean(scaled * unit, axis=-1, keepdims=True)
    return rstd * (scaled - mean_one - unit * mean_two)


def rows_of(ref, at, size):
    return ref.at[pl.ds(pl.multiple_of(at, 16), size)]


def wait_all(like, sem):
    pltpu.make_async_copy(like, like, sem).wait()


def add_rows(into, into_at, parts, size):
    piece = next(rows for rows in (64, 48, 32, 16) if size % rows == 0)

    def step(k, carried):
        summed = None
        for ref, at in parts:
            block = ref[pl.ds(pl.multiple_of(at + k * piece, 16), piece), :].astype(jnp.float32)
            summed = block if summed is None else summed + block
        into[pl.ds(pl.multiple_of(into_at + k * piece, 16), piece), :] = summed.astype(low)
        return carried

    lax.fori_loop(0, size // piece, step, 0)


class Places:
    def __init__(self):
        self.dp_count, self.count = lax.axis_size("dp"), lax.axis_size("seq")
        self.dp, self.me = lax.axis_index("dp"), lax.axis_index("seq")
        self.core, self.x = lax.rem(self.dp, 2), self.dp // 2
        self.y, self.z = lax.rem(self.me, 2), self.me // 2
        self.depth = self.count // 2
        self.core_peer = (self.dp + 1 - 2 * self.core, self.me)
        self.x_peer = (self.dp + 2 - 4 * self.x, self.me)
        self.y_peer = (self.dp, self.me + 1 - 2 * self.y)
        along_x = 1 - self.core
        self.two_peer = (self.dp + along_x * (2 - 4 * self.x), self.me + (1 - along_x) * (1 - 2 * self.y))
        self.three_peer = (self.dp + (1 - along_x) * (2 - 4 * self.x), self.me + along_x * (1 - 2 * self.y))
        self.two_bit = along_x * self.x + (1 - along_x) * self.y
        self.three_bit = (1 - along_x) * self.x + along_x * self.y
        self.z_low, self.z_high = lax.rem(self.z, 2), self.z // 2
        self.z_near = (self.dp, self.me + 2 * (1 - 2 * self.z_low))
        self.z_far = (self.dp, self.me + 4 * (1 - 2 * self.z_high))


def remote(src, dst, send_sem, recv_sem, target):
    return pltpu.make_async_remote_copy(
        src_ref=src, dst_ref=dst, send_sem=send_sem, recv_sem=recv_sem, device_id=target, device_id_type=MESH
    )


class StagedSum:
    def __init__(self, at, x_first, mine, final, got, sems):
        self.mine, self.final, self.got = mine, final, got
        if x_first:
            bits = (at.core, at.x, at.y, at.z_low, at.z_high)
            self.peers = (at.core_peer, at.x_peer, at.y_peer, at.z_near, at.z_far)
        else:
            bits = (at.core, at.two_bit, at.three_bit, at.z_low, at.z_high)
            self.peers = (at.core_peer, at.two_peer, at.three_peer, at.z_near, at.z_far)
        self.stages = len(bits)
        self.down_s, self.down_r, self.up_s, self.up_r = sems
        self.total = final.shape[0]
        start, size = 0, self.total
        self.keep, self.give, self.size = [], [], []
        for bit in bits:
            size //= 2
            self.keep.append(start + bit * size)
            self.give.append(start + (1 - bit) * size)
            self.size.append(size)
            start = start + bit * size
        self.give.append(start)
        self.size.append(size)

    def down(self, stage, block):
        if stage == 0:
            source, there, size = self.give[0], 0, self.size[0]
        else:
            there, size = self.give[block] - self.keep[stage], self.size[block]
            source = self.give[stage] + there
        return remote(
            rows_of(self.mine, source, size), rows_of(self.got[stage], there, size),
            self.down_s.at[0], self.down_r.at[block - 1], self.peers[stage],
        )

    def up(self, stage, block):
        here = rows_of(self.final, self.give[block], self.size[block])
        return remote(here, here, self.up_s.at[0], self.up_r.at[stage], self.peers[stage])

    def blocks(self, stage):
        return (1,) if stage == 0 else range(stage + 1, self.stages + 1)

    def send(self, stage):
        if stage > 0:
            self.collect(stage, self.mine)
        for block in self.blocks(stage):
            self.down(stage, block).start()

    def collect(self, block, into):
        parts = [(self.mine, self.give[block])]
        for stage in range(block):
            parts.append((self.got[stage], self.give[block] - self.keep[stage]))
        came = self.size[0] if block == 1 else (block - 1) * self.size[block]
        wait_all(self.final.at[pl.ds(0, came)], self.down_r.at[block - 1])
        add_rows(into, self.give[block], parts, self.size[block])

    def turn(self):
        self.collect(self.stages, self.final)
        self.spread(self.stages)

    def spread(self, block):
        for stage in reversed(range(block)):
            self.up(stage, block).start()

    def arrive(self, stage):
        wait_all(rows_of(self.final, self.give[stage], self.size[stage]), self.up_r.at[stage])

    def gather(self, stage):
        self.arrive(stage)
        self.spread(stage)

    def drain(self):
        left = self.final.at[pl.ds(0, self.total - self.size[-1])]
        if self.mine is not None:
            wait_all(left, self.down_s.at[0])
        wait_all(left, self.up_s.at[0])


class VectorSum:
    def __init__(self, at, mine, seq_got, seq_sum, dp_got, send_sem, recv_sem, base):
        self.at, self.mine, self.seq_got, self.seq_sum, self.dp_got = at, mine, seq_got, seq_sum, dp_got
        self.send_sem, self.recv_sem, self.base = send_sem, recv_sem, base

    def over_seq(self, to):
        at = self.at
        return remote(
            self.mine, self.seq_got.at[at.me], self.send_sem.at[self.base], self.recv_sem.at[self.base], (at.dp, to)
        )

    def over_dp(self, to):
        at = self.at
        return remote(
            self.seq_sum, self.dp_got.at[at.dp], self.send_sem.at[self.base + 1], self.recv_sem.at[self.base + 1],
            (to, at.me),
        )

    def each(self, count, mine, act):
        def step(k, carried):
            act(lax.rem(mine + k, count))
            return carried

        lax.fori_loop(1, count, step, 0)

    def start_seq(self):
        at = self.at
        self.each(at.count, at.me, lambda to: self.over_seq(to).start())
        self.seq_got[at.me] = self.mine[...]

    def start_dp(self):
        at = self.at
        wait_all(self.seq_got.at[pl.ds(0, at.count - 1)], self.recv_sem.at[self.base])
        summed = self.seq_got[0]
        for k in range(1, at.count):
            summed = summed + self.seq_got[k]
        self.seq_sum[...] = summed
        self.each(at.dp_count, at.dp, lambda to: self.over_dp(to).start())
        self.dp_got[at.dp] = summed

    def finish(self):
        at = self.at
        wait_all(self.dp_got.at[pl.ds(0, at.dp_count - 1)], self.recv_sem.at[self.base + 1])
        summed = self.dp_got[0]
        for k in range(1, at.dp_count):
            summed = summed + self.dp_got[k]
        return summed

    def drain(self):
        wait_all(self.seq_got.at[pl.ds(0, self.at.count - 1)], self.send_sem.at[self.base])
        wait_all(self.dp_got.at[pl.ds(0, self.at.dp_count - 1)], self.send_sem.at[self.base + 1])


before_backward = ("N2", "R1")
within_steps = (
    (),
    (),
    (),
    (),
)
between_steps = (
    ("B0", "N3"),
    ("B1", "R2", "O1"),
    ("B2", "F0", "N4"),
    ("B3", "F1", "R3", "O2"),
    ("B4", "F2"),
    ("B5", "F3", "Nt", "V1"),
    ("B6", "F4", "R4", "O3"),
    ("B7", "F5"),
)
after_backward = (
    "I0", "E0", "F6", "F7", "Ne", "Rt", "O4", "I1", "Nd", "Re", "Ot", "It",
    "E1", "Nc", "Rd", "Oe", "Rc", "T", "Ie", "Nb", "Od", "E2", "Id", "W1",
    "Rb", "Oc", "Ic", "Ob", "Ib", "Vf", "Nf", "Rf", "Of", "If", "Ef", "Wf",
)

near_x, rest_x, out_x = False, False, False


def layer_kernel(
    tokens_ref,
    seg_ref,
    gain_one_ref,
    bias_one_ref,
    w_qkv_hbm,
    b_val_ref,
    w_out_hbm,
    b_out_ref,
    gain_two_ref,
    bias_two_ref,
    w_up_hbm,
    b_up_ref,
    w_down_hbm,
    b_down_ref,
    cot_hbm,
    output_ref,
    tokens_grad_ref,
    vec_mid_ref,
    vec_in_ref,
    w_down_out,
    w_up_out,
    w_out_out,
    w_qkv_out,
    first_out,
    *scratch,
):
    (
        w_out_ref, w_up_ref, w_down_ref, w_qkv_ref, cot_ref, load_sem, store_sem,
        normed_all, w_head, w_value, b_value, queries, keys, keys_zero, vals, queries_t,
        probs, gates, logit, carry, row_wide, row_acc,
        send_mix, recv_mix, send_gmix, recv_gmix, grad_rows, grad_rows_t,
        back_carry,
        send_back, recv_back, send_first, y_first, recv_first,
        lower, upper,
        unit_two_ref, rstd_two_ref,
        mixed_ref, normed_two_ref, middle_ref, out_acc, gn_acc, joined_ref,
        near_mine, near_final, near_core, near_two, near_three, near_four, near_five,
        rest_mine, rest_final, rest_core, rest_two, rest_three, rest_four, rest_five,
        out_mine, out_final, out_core, out_two, out_three, out_four, out_five,
        wkv_acc, wqq_acc, in_mine, in_core, in_x, in_final,
        extra_mine, extra_seq, extra_sum, extra_dp, extra_all,
        vec_mid_mine, vec_mid_seq, vec_mid_sum, vec_mid_dp,
        vec_in_mine, vec_in_seq, vec_in_sum, vec_in_dp,
        norm_s, norm_r, mix_s, mix_r, gmix_s, gmix_r,
        back_s, back_r, fback_y, fback_yr, fback_s, fback_r, extra_s, extra_r,
        *sums_sems, in_s, in_r, part_s, part_r, vec_s, vec_r,
    ) = scratch
    at = Places()
    dp_count, count, dp, me = at.dp_count, at.count, at.dp, at.me
    y, z, depth = at.y, at.z, at.depth
    rows, width = tokens_ref.shape[1], tokens_ref.shape[2]
    half, wide = rows // 2, 2 * HD
    coeff = select_weight / (rows * count)
    hidden_width = w_up_hbm.shape[1]
    pairs = width // wide
    score_scale = 1.0 / math.sqrt(HD)

    barrier = pltpu.get_barrier_semaphore()

    def greet_seq(step, carried):
        to = lax.rem(me + step, count)
        pl.semaphore_signal(barrier, inc=1, device_id=(dp, to), device_id_type=MESH)
        return carried

    def greet_dp(step, carried):
        to = lax.rem(dp + step, dp_count)
        pl.semaphore_signal(barrier, inc=1, device_id=(to, me), device_id_type=MESH)
        return carried

    lax.fori_loop(1, count, greet_seq, 0)
    lax.fori_loop(1, dp_count, greet_dp, 0)
    projection_load = pltpu.make_async_copy(w_qkv_hbm, w_qkv_ref, load_sem.at[3])
    projection_load.start()
    loads = [
        pltpu.make_async_copy(cot_hbm, cot_ref, load_sem.at[4]),
        pltpu.make_async_copy(w_out_hbm, w_out_ref, load_sem.at[0]),
        pltpu.make_async_copy(w_up_hbm, w_up_ref, load_sem.at[1]),
        pltpu.make_async_copy(w_down_hbm, w_down_ref, load_sem.at[2]),
    ]
    for load in loads:
        load.start()

    def exchange(src, dst, send_sem, recv_sem, target):
        return remote(src, dst, send_sem, recv_sem, (dp, target))

    tokens = tokens_ref[0].astype(jnp.float32)
    unit, _ = normalise(tokens)
    normed_all[me] = (unit * gain_one_ref[...] + bias_one_ref[...]).astype(low)
    pl.semaphore_wait(barrier, count + dp_count - 2)

    def part_of(block, part):
        return normed_all.at[block, pl.ds(part * half, half)]

    def pass_on(block, part, way, target):
        here = part_of(block, part)
        return exchange(here, here, norm_s.at[way], norm_r.at[block * 2 + part], target)

    def pass_y(block, part):
        pass_on(block, part, 0, z * 2 + 1 - y).start()

    def pass_up(block, part):
        pass_on(block, part, 1, me + 2).start()

    def pass_down(block, part):
        pass_on(block, part, 2, me - 2).start()

    def arrived(block, part):
        wait_all(part_of(block, part), norm_r.at[block * 2 + part])

    def has_up(zz):
        return zz < depth - 1

    for part in range(2):
        pl.when(has_up(z))(functools.partial(pass_up, me, part))
        pl.when(z > 0)(functools.partial(pass_down, me, part))
        pass_y(me, part)

    def relay(distance):
        def from_below():
            block = me - 2 * distance
            for part in range(2):
                arrived(block, part)
                pl.when(has_up(z))(functools.partial(pass_up, block, part))
                pass_y(block, part)

        def from_above():
            block = me + 2 * distance
            for part in range(2):
                arrived(block, part)
                pl.when(z > 0)(functools.partial(pass_down, block, part))
                pass_y(block, part)

        pl.when(z - distance >= 0)(from_below)
        pl.when(z + distance < depth)(from_above)

    projection_load.wait()

    odd_head = lax.rem(me, 2) == 1
    pair_at_lane = pl.multiple_of((me // 2) * wide, wide)

    def head_columns(part):
        columns = w_qkv_ref[:, pl.ds(part * width + pair_at_lane, wide)].astype(jnp.float32)
        return jnp.where(odd_head, swap_halves(columns), columns)

    def zero_columns(part):
        return swap_halves(w_qkv_ref[:, part * width : part * width + wide].astype(jnp.float32))

    w_head[:, :wide] = (join_heads(head_columns(0), zero_columns(0)) * score_scale).astype(low)
    w_head[:, wide:] = join_heads(head_columns(1), zero_columns(1)).astype(low)
    w_value[...] = head_columns(2).astype(low)
    bias = b_val_ref[:, pl.ds(pair_at_lane, wide)]
    b_value[...] = jnp.where(odd_head, swap_halves(bias), bias)

    ids = seg_ref[...]
    start_one = jnp.sum(jnp.where(ids < 1, 1.0, 0.0), axis=1, keepdims=True)
    start_two = jnp.sum(jnp.where(ids < 2, 1.0, 0.0), axis=1, keepdims=True)
    square = (rows, rows)
    row_at = lax.broadcasted_iota(jnp.int32, square, 0)
    col_at = lax.broadcasted_iota(jnp.int32, square, 1)
    lower[...] = jnp.where(row_at > col_at, -coeff, 0.0).astype(low)
    upper[...] = jnp.where(row_at < col_at, -coeff, 0.0).astype(low)
    lane = lax.broadcasted_iota(jnp.int32, (rows, wide), 1)

    def masks(i, j):
        query_pos = lax.broadcasted_iota(jnp.int32, (rows, 1), 0).astype(jnp.float32) + ((i - j) * rows).astype(jnp.float32)
        key_start = (j * rows).astype(jnp.float32)
        begin_one, begin_two = start_one - key_start, start_two - key_start
        begin = jnp.where(query_pos >= begin_two, begin_two, jnp.where(query_pos >= begin_one, begin_one, -key_start))
        key_pos = col_at.astype(jnp.float32)
        inside = key_pos >= begin
        return inside & (key_pos <= query_pos), inside & (key_pos < query_pos)

    def pair_at(i, j):
        return i * (i + 1) // 2 + j

    carry[...] = jnp.zeros_like(carry)
    row_wide[...] = jnp.full_like(row_wide, neg_large)

    def project(block):
        normed = normed_all[block]
        both = dot_nn(normed, w_head[...])
        query = both[:, :wide]
        queries[block] = query.astype(low)
        queries_t[block] = query.T.astype(low)
        key = both[:, wide:]
        keys[block] = jnp.where(lane < HD, key, 0.0).astype(low)
        keys_zero[block] = jnp.where(lane < HD, 0.0, key).astype(low)
        value = dot_nn(normed, w_value[...]) + b_value[...]
        vals[block] = jnp.where(lane < HD, value, jnp.where(lane < HD + 2, 1.0, 0.0)).astype(low)

    def kept_at(i):
        return pair_at(i, 0) - i // (count - 1) * (count - 2)

    def grads_at(j):
        return pair_at(count - 1, j)

    def forward_group(group, masked):
        spots = [pair_at(i, j) for i, j in group]
        zero_scores = [dot_nt(queries[i], keys_zero[j]) for i, j in group]
        scores = [dot_nt(queries[i], keys[j]) for i, j in group]
        softs, gate_rows, attends = [], [], {}
        for k, (i, j) in enumerate(group):
            score = zero_scores[k]
            soft = jnp.maximum(score, 0.0) + jnp.log(1.0 + jnp.exp(-jnp.abs(score)))
            gate = jnp.exp(score - soft)
            if k in masked:
                attends[k], select = masks(i, j)
                soft = jnp.where(select, soft, 0.0)
                gate = jnp.where(select, gate, 0.0)
            softs.append(soft.astype(low))
            gate_rows.append(gate)
        falls = [dot_nn(lower[...], soft) for soft in softs]
        for k, spot in enumerate(spots):
            gates[spot] = gate_rows[k].astype(low)
        for k, (i, j) in enumerate(group):
            forgot = falls[k] + carry[j]
            carry[j] = forgot[rows - 1 :] - coeff * softs[k][rows - 1 :].astype(jnp.float32)
            scores[k] = scores[k] + forgot
            if k in masked:
                scores[k] = jnp.where(attends[k], scores[k], neg_large)
        for k, spot in enumerate(spots):
            logit[spot] = scores[k]
        for k, (i, _) in enumerate(group):
            top = row_wide[i]
            for start in range(0, rows, wide):
                top = jnp.maximum(top, scores[k][:, start : start + wide])
            row_wide[i] = top

    def in_groups(total, act, after_four=None):
        def four(group, carried):
            act(group * 4, 4)
            if after_four is not None:
                pl.when((group == 0) & (total > 4))(after_four)
            return carried

        lax.fori_loop(0, total // 4, four, 0)
        for left in (1, 2, 3):
            pl.when(lax.rem(total, 4) == left)(lambda left=left: act(total - left, left))

    def weigh_row(i):
        top = jnp.max(row_wide[i], axis=1, keepdims=True)
        row_acc[...] = jnp.zeros_like(row_acc)

        def weigh(start, size):
            found = [jnp.exp(logit[pair_at(i, start + k)] - top).astype(low) for k in range(size)]
            added = None
            for k, prob in enumerate(found):
                product = dot_nn(prob, vals[start + k])
                added = product if added is None else added + product
            for k, prob in enumerate(found):
                probs[pair_at(i, start + k)] = prob
            row_acc[...] += added

        in_groups(i + 1, weigh)
        mixed = row_acc[...]
        inverse = 1.0 / mixed[:, HD : HD + 1]
        mixed = mixed * inverse
        logit[kept_at(i), :, :wide] = jnp.where(lane < HD, mixed, inverse)
        send_mix[i] = fold_rows(mixed).astype(low)

        @pl.when(i != me)
        def _():
            exchange(send_mix.at[i], recv_mix.at[me], mix_s.at[0], mix_r.at[0], i).start()

    upwards = 1 - z // (depth // 2)
    at_end = (z == 0) | (z == depth - 1)
    pl.when(jnp.logical_not(at_end))(functools.partial(relay, 1))

    def forward_step(step, carried):
        block = upwards * step + (1 - upwards) * (count - 1 - step)
        group = step // 2

        @pl.when(lax.rem(block, 2) != y)
        def _():
            arrived(block, 0)
            arrived(block, 1)
            for distance in range(1, depth):
                pl.when(at_end & (group + 1 == distance))(functools.partial(relay, distance))
                pl.when(jnp.logical_not(at_end) & (group + 2 == distance))(functools.partial(relay, distance))

        project(block)

        def group(start, size, all_masked=False):
            members = []
            for k in range(size):
                i = upwards * step + (1 - upwards) * (block + start + k)
                j = upwards * (start + k) + (1 - upwards) * block
                members.append((i, j))
            forward_group(members, range(size) if all_masked else (0, size - 1))

        last = step == count - 1
        pl.when(jnp.logical_not(last))(lambda: in_groups(step + 1, group))

        @pl.when(last)
        def _():
            def four(start, carried):
                group(start * 4, 4, True)
                return carried

            lax.fori_loop(0, count // 4, four, 0)

        pl.when(upwards == 1)(functools.partial(weigh_row, block))
        return carried

    lax.fori_loop(0, count, forward_step, 0)

    def late_weigh(i, carried):
        weigh_row(i)
        return carried

    lax.fori_loop(0, (1 - upwards) * count, late_weigh, 0)
    recv_mix[me] = send_mix[me]

    for load in loads:
        load.wait()

    wait_all(recv_mix.at[pl.ds(0, count - 1)], mix_r.at[0])
    for pair in range(pairs):
        even = recv_mix[2 * pair].astype(jnp.float32)
        odd = recv_mix[2 * pair + 1].astype(jnp.float32)
        columns = pl.ds(pair * wide, wide)
        mixed_ref[pl.ds(0, half), columns] = join_heads(even, swap_halves(odd)).astype(low)
        mixed_ref[pl.ds(half, half), columns] = join_heads(swap_halves(even), odd).astype(low)
    middle = tokens_ref[0].astype(jnp.float32) + dot_nn(mixed_ref[...], w_out_ref[...]) + b_out_ref[...]
    middle_ref[...] = middle
    unit, rstd = normalise(middle)
    unit_two_ref[...] = unit
    rstd_two_ref[...] = rstd
    normed_two_ref[...] = (unit * gain_two_ref[...] + bias_two_ref[...]).astype(low)
    out_acc[...] = jnp.zeros_like(out_acc)
    gn_acc[...] = jnp.zeros_like(gn_acc)
    near_sum = StagedSum(at, near_x, near_mine, near_final, (near_core, near_two, near_three, near_four, near_five), sums_sems[:4])
    rest_sum = StagedSum(at, rest_x, rest_mine, rest_final, (rest_core, rest_two, rest_three, rest_four, rest_five), sums_sems[4:8])
    out_sum = StagedSum(at, out_x, out_mine, out_final, (out_core, out_two, out_three, out_four, out_five), sums_sems[8:12])
    in_sum = StagedSum(at, False, None, in_final, None, (None, None, in_s, in_r))
    mid_vec = VectorSum(at, vec_mid_mine, vec_mid_seq, vec_mid_sum, vec_mid_dp, vec_s, vec_r, 0)
    in_vec = VectorSum(at, vec_in_mine, vec_in_seq, vec_in_sum, vec_in_dp, vec_s, vec_r, 2)
    chunk = width
    chunks = hidden_width // chunk
    half_hidden = hidden_width // 2

    def dense(sums, base, c, carried):
        start = pl.multiple_of((base + c) * chunk, chunk)
        cols = pl.ds(start, chunk)
        hidden = dot_nn(normed_two_ref[...], w_up_ref[:, cols]) + b_up_ref[:, cols]
        cdf = exact_cdf(hidden)
        slope = cdf + hidden * jnp.exp(-0.5 * hidden * hidden) * (1.0 / math.sqrt(2.0 * math.pi))
        active = (hidden * cdf).astype(low)
        out_acc[...] += dot_nn(active, w_down_ref[cols, :])
        grad_hidden = (dot_nt(cot_ref[0], w_down_ref[cols, :]) * slope).astype(low)
        here = pl.multiple_of(c * chunk, chunk)
        sums[pl.ds(here, chunk), :] = dot_tn(active, cot_ref[0]).astype(low)
        there = pl.multiple_of(sums.shape[0] // 2 + here, 16)
        sums[pl.ds(there, chunk), :] = dot_tn(normed_two_ref[...], grad_hidden).astype(low)
        vec_mid_mine[pl.ds(base + c, 1), :] = jnp.sum(grad_hidden.astype(jnp.float32), axis=0, keepdims=True)
        gn_acc[...] += dot_nt(grad_hidden, w_up_ref[:, cols])
        return carried

    lax.fori_loop(0, chunks // 2, functools.partial(dense, near_mine, 0), 0)
    near_sum.send(0)
    lax.fori_loop(0, chunks // 2, functools.partial(dense, rest_mine, chunks // 2), 0)
    rest_sum.send(0)
    cot = cot_ref[0].astype(jnp.float32)
    grad = gn_acc[...]
    unit = unit_two_ref[...]
    middle = cot + normalise_back(grad, unit, rstd_two_ref[...], gain_two_ref[...])
    output_ref[0] = (middle_ref[...] + out_acc[...] + b_down_ref[...]).astype(low)
    middle_ref[...] = middle
    branch = middle.astype(low)
    for pair in range(pairs):
        back = dot_nt(branch, w_out_ref[pl.ds(pair * wide, wide), :]).astype(low).astype(jnp.float32)
        top, bottom = back[:half], back[half:]
        send_gmix[2 * pair] = join_heads(top, swap_halves(bottom)).astype(low)
        send_gmix[2 * pair + 1] = join_heads(swap_halves(top), bottom).astype(low)

    def send_grads(step, carried):
        to = lax.rem(me + step, count)
        exchange(send_gmix.at[to], recv_gmix.at[me], gmix_s.at[0], gmix_r.at[me], to).start()
        return carried

    lax.fori_loop(1, count, send_grads, 0)
    near_sum.send(1)
    recv_gmix[me] = send_gmix[me]
    out_mine[...] = dot_tn(mixed_ref[...], branch).astype(low)
    out_sum.send(0)
    vec_mid_mine[pl.ds(chunks, 1), :] = jnp.sum(cot, axis=0, keepdims=True)
    vec_mid_mine[pl.ds(chunks + 1, 1), :] = jnp.sum(grad * unit, axis=0, keepdims=True)
    vec_mid_mine[pl.ds(chunks + 2, 1), :] = jnp.sum(grad, axis=0, keepdims=True)
    vec_mid_mine[pl.ds(chunks + 3, 1), :] = jnp.sum(branch.astype(jnp.float32), axis=0, keepdims=True)
    mid_vec.start_seq()

    def steps_of(sums):
        found = {str(stage): functools.partial(sums.send, stage) for stage in range(1, 5)}
        found["t"] = sums.turn
        found |= {"abcde"[stage]: functools.partial(sums.gather, stage) for stage in range(1, 5)}
        found["f"] = functools.partial(sums.arrive, 0)
        return found

    acts = {}
    for name, sums in (("N", near_sum), ("R", rest_sum), ("O", out_sum), ("I", in_sum)):
        acts |= {name + step: act for step, act in steps_of(sums).items()}
    acts["V1"] = mid_vec.start_dp

    def run(names):
        for name in names:
            acts[name]()

    run(before_backward)

    kv_rows = 3 * HD
    logit[pl.ds(grads_at(0), count), :kv_rows] = jnp.zeros((count, kv_rows, rows), jnp.float32)
    row_wide[...] = jnp.zeros_like(row_wide)
    back_carry[...] = jnp.zeros_like(back_carry)
    wkv_acc[...] = jnp.zeros_like(wkv_acc)
    wqq_acc[...] = jnp.zeros_like(wqq_acc)

    def prepare(i):
        @pl.when(i != me)
        def _():
            wait_all(recv_gmix.at[i], gmix_r.at[i])

        grad = jnp.where(lane < HD, spread_rows(recv_gmix[i].astype(jnp.float32)), 0.0)
        kept = logit[kept_at(i), :, :wide]
        inverse = kept[:, HD : HD + 1]
        delta = -jnp.sum(grad * kept, axis=1, keepdims=True) * inverse
        grad = grad * inverse
        grad_rows_t[i] = grad.T[:HD].astype(low)
        delta_high = delta.astype(low).astype(jnp.float32)
        grad = jnp.where(lane == HD, delta_high, jnp.where(lane == HD + 1, delta - delta_high, grad))
        grad_rows[i] = grad.astype(low)

    def backward_group(group):
        spots = [pair_at(i, j) for i, j in group]
        found = [probs[spot] for spot in spots]
        grads = [dot_nt(grad_rows[i], vals[j]) for i, j in group]
        grads = [(prob.astype(jnp.float32) * grad).astype(low) for prob, grad in zip(found, grads)]
        laters = [dot_nn(upper[...], grad) for grad in grads]
        gated = []
        for k, (i, j) in enumerate(group):
            later = laters[k] + back_carry[j]
            back_carry[j] = later[:1] - coeff * grads[k][:1].astype(jnp.float32)
            gated.append((later * gates[spots[k]].astype(jnp.float32)).astype(low))
        query_parts = [dot_nn(grads[k], keys[j]) + dot_nn(gated[k], keys_zero[j]) for k, (_, j) in enumerate(group)]
        key_parts = [
            (
                dot_nn(grad_rows_t[i], found[k]),
                dot_nn(queries_t[i, :HD], grads[k]),
                dot_nn(queries_t[i, HD:], gated[k]),
            )
            for k, (i, _) in enumerate(group)
        ]
        for k, (i, _) in enumerate(group):
            row_wide[i] += query_parts[k]
        for k, (_, j) in enumerate(group):
            for part in range(3):
                logit[grads_at(j), part * HD : (part + 1) * HD] += key_parts[k][part]

    def send_first_sum(i):
        wait_all(y_first.at[i], fback_yr.at[i])
        send_first[i] = (send_first[i].astype(jnp.float32) + y_first[i].astype(jnp.float32)).astype(low)

        @pl.when(i != me)
        def _():
            exchange(send_first.at[i], recv_first.at[z], fback_s.at[0], fback_r.at[0], i).start()

        @pl.when(i == me)
        def _():
            recv_first[z] = send_first[i]

    def block_of(step):
        return upwards * (count - 1 - step) + (1 - upwards) * step

    def send_home(step):
        block = block_of(step)

        @pl.when(block != me)
        def _():
            exchange(send_back.at[block], recv_back.at[me], back_s.at[0], back_r.at[0], block).start()

        @pl.when(lax.rem(block, 2) != y)
        def _():
            exchange(send_first.at[block], y_first.at[block], fback_y.at[0], fback_yr.at[block], z * 2 + 1 - y).start()

    def send_first_home(step):
        block = block_of(step)
        pl.when(lax.rem(block, 2) == y)(functools.partial(send_first_sum, block))

    for step in range(count):
        acts[f"B{step}"] = functools.partial(send_home, step)
        acts[f"F{step}"] = functools.partial(send_first_home, step)

    def between(step, number, names):
        if names:
            pl.when(step == number)(functools.partial(run, names))

    def backward_step(step, carried):
        block = block_of(step)
        pl.when(upwards == 1)(functools.partial(prepare, block))

        def group(start, size):
            members = []
            for k in range(size):
                i = upwards * block + (1 - upwards) * (count - 1 - start - k)
                j = upwards * (start + k) + (1 - upwards) * block
                members.append((i, j))
            backward_group(members)

        def half_way():
            for number, names in enumerate(within_steps):
                between(step, number, names)

        in_groups(count - step, group, half_way)
        flat = logit[grads_at(block), :kv_rows]
        flipped = flat[: 2 * HD].T
        first_flipped = flat[HD:].T
        grad_queries = row_wide[block] * score_scale
        send_back[block, :rows] = join_heads(grad_queries, flipped).astype(low)
        send_back[block, rows:] = fold_rows(flipped).astype(low)
        send_first[block] = join_heads(swap_halves(grad_queries), first_flipped).astype(low)

        normed = normed_all[block]
        wkv_acc[...] += dot_nn(flat.astype(low), normed)
        wqq_acc[...] += dot_nn(grad_queries.T.astype(low), normed)
        for number, names in enumerate(between_steps):
            between(step, number, names)
        return carried

    def prepare_all(i, carried):
        prepare(count - 1 - i)
        return carried

    lax.fori_loop(0, (1 - upwards) * count, prepare_all, 0)
    lax.fori_loop(0, count, backward_step, 0)
    recv_back[me] = send_back[me]

    piece = HD // 4
    core_half, x_half = 6 * piece, 3 * piece
    in_start = at.core * core_half
    in_core_copy = remote(rows_of(in_mine, (1 - at.core) * core_half, core_half), in_core, part_s.at[0], part_r.at[0], at.core_peer)
    in_x_copy = remote(rows_of(in_mine, in_start + (1 - at.x) * x_half, x_half), in_x, part_s.at[1], part_r.at[1], at.x_peer)
    each_seq = functools.partial(in_vec.each, count, me)
    each_dp = functools.partial(in_vec.each, dp_count, dp)

    def extra_over_seq(to):
        return exchange(rows_of(extra_mine, to * piece, piece), extra_seq.at[me], extra_s.at[0], extra_r.at[0], to)

    def extra_over_dp(to):
        return remote(extra_sum, extra_dp.at[dp], extra_s.at[1], extra_r.at[1], (to, me))

    def extra_gather(to):
        block = rows_of(extra_all, me * piece, piece)
        return exchange(block, block, extra_s.at[2], extra_r.at[2], to)

    def in_zero():
        for part in range(4):
            for place, (source, start) in enumerate(((wqq_acc, 0), (wkv_acc, HD), (wkv_acc, 0))):
                rows_in = pl.ds(part * 3 * piece + place * piece, piece)
                in_mine[rows_in, :] = source[start + part * piece : start + (part + 1) * piece].astype(low)
        in_core_copy.start()

    def extra_zero():
        extra_mine[:HD] = wqq_acc[HD:].astype(low)
        extra_mine[HD:] = wkv_acc[2 * HD :].astype(low)
        each_seq(lambda to: extra_over_seq(to).start())
        extra_seq[me] = extra_mine[pl.ds(pl.multiple_of(me * piece, 16), piece), :]

    def in_one():
        in_core_copy.wait_recv()
        add_rows(in_mine, in_start, [(in_mine, in_start), (in_core, 0)], core_half)
        in_x_copy.start()

    def in_turn():
        in_x_copy.wait_recv()
        add_rows(in_final, in_sum.give[5], [(in_mine, in_start + at.x * x_half), (in_x, 0)], x_half)
        in_sum.spread(5)

    def extra_one():
        wait_all(extra_seq.at[pl.ds(0, count - 1)], extra_r.at[0])
        summed = extra_seq[0].astype(jnp.float32)
        for k in range(1, count):
            summed = summed + extra_seq[k].astype(jnp.float32)
        extra_sum[...] = summed
        each_dp(lambda to: extra_over_dp(to).start())
        extra_dp[dp] = summed

    def extra_two():
        wait_all(extra_dp.at[pl.ds(0, dp_count - 1)], extra_r.at[1])
        summed = extra_dp[0]
        for k in range(1, dp_count):
            summed = summed + extra_dp[k]
        extra_all[pl.ds(pl.multiple_of(me * piece, 16), piece), :] = summed.astype(low)
        each_seq(lambda to: extra_gather(to).start())

    def first_norm_back():
        unit, rstd = normalise(tokens_ref[0].astype(jnp.float32))
        wait_all(recv_back.at[pl.ds(0, count - 1)], back_r.at[0])
        wait_all(recv_first.at[pl.ds(0, depth - 1)], fback_r.at[0])
        first_sum = recv_first[0].astype(jnp.float32)
        for source in range(1, depth):
            first_sum = first_sum + recv_first[source].astype(jnp.float32)
        for pair in range(pairs):
            even = recv_back[2 * pair, :rows].astype(jnp.float32)
            odd = recv_back[2 * pair + 1, :rows].astype(jnp.float32)
            if pair == 0:
                even = even + first_sum
            columns = wide * pair
            joined_ref[:, pl.ds(columns, wide)] = join_heads(even, swap_halves(odd)).astype(low)
            joined_ref[:, pl.ds(width + columns, wide)] = join_heads(swap_halves(even), odd).astype(low)
            even = recv_back[2 * pair, rows:].astype(jnp.float32)
            odd = recv_back[2 * pair + 1, rows:].astype(jnp.float32)
            columns = pl.ds(2 * width + columns, wide)
            joined_ref[pl.ds(0, half), columns] = join_heads(even, swap_halves(odd)).astype(low)
            joined_ref[pl.ds(half, half), columns] = join_heads(swap_halves(even), odd).astype(low)
        grad = dot_nt(joined_ref[...], w_qkv_ref[...])
        vec_in_mine[...] = jnp.zeros_like(vec_in_mine)
        vec_in_mine[pl.ds(0, 1), :] = jnp.sum(grad * unit, axis=0, keepdims=True)
        vec_in_mine[pl.ds(1, 1), :] = jnp.sum(grad, axis=0, keepdims=True)
        value_grads = joined_ref[:, pl.ds(2 * width, width)].astype(jnp.float32)
        vec_in_mine[pl.ds(2, 1), :] = jnp.sum(value_grads, axis=0, keepdims=True)
        in_vec.start_seq()
        tokens_grad_ref[0] = middle_ref[...] + normalise_back(grad, unit, rstd, gain_one_ref[...])

    stores = []

    def store(source, target):
        stores.append(pltpu.make_async_copy(source, target, store_sem.at[len(stores)]))
        stores[-1].start()

    def finish_near():
        near_sum.arrive(0)
        store(near_final.at[pl.ds(0, half_hidden)], w_down_out.at[pl.ds(0, half_hidden)])
        store(near_final.at[pl.ds(half_hidden, half_hidden)], w_up_out.at[pl.ds(0, half_hidden)])

    def finish_rest():
        rest_sum.arrive(0)
        store(rest_final.at[pl.ds(0, half_hidden)], w_down_out.at[pl.ds(half_hidden, half_hidden)])
        store(rest_final.at[pl.ds(half_hidden, half_hidden)], w_up_out.at[pl.ds(half_hidden, half_hidden)])

    def finish_out():
        out_sum.arrive(0)
        store(out_final, w_out_out)

    def finish_in():
        in_sum.arrive(0)
        store(in_final, w_qkv_out)

    def finish_extra():
        wait_all(extra_all.at[pl.ds(0, (count - 1) * piece)], extra_r.at[2])
        store(extra_all, first_out)

    def finish_mid_vec():
        vec_mid_ref[...] = mid_vec.finish()

    def finish_in_vec():
        vec_in_ref[...] = in_vec.finish()

    acts |= {
        "I0": in_zero, "I1": in_one, "It": in_turn, "E0": extra_zero, "E1": extra_one, "E2": extra_two,
        "T": first_norm_back, "W1": in_vec.start_dp, "Vf": finish_mid_vec, "Wf": finish_in_vec,
        "Nf": finish_near, "Rf": finish_rest, "Of": finish_out, "If": finish_in, "Ef": finish_extra,
    }
    run(after_backward)

    wait_all(normed_all.at[pl.ds(0, depth)], norm_s.at[0])
    for at_z in range(depth - 1):
        went = normed_all.at[pl.ds(0, at_z + 1)]
        pl.when(z == at_z)(functools.partial(wait_all, went, norm_s.at[1]))
        pl.when(z == depth - 1 - at_z)(functools.partial(wait_all, went, norm_s.at[2]))
    wait_all(send_mix.at[pl.ds(0, count - 1)], mix_s.at[0])
    wait_all(send_gmix.at[pl.ds(0, count - 1)], gmix_s.at[0])
    wait_all(send_back.at[pl.ds(0, count - 1)], back_s.at[0])
    wait_all(send_first.at[pl.ds(0, depth)], fback_y.at[0])
    wait_all(send_first.at[pl.ds(0, depth - 1)], fback_s.at[0])
    wait_all(extra_seq.at[pl.ds(0, count - 1)], extra_s.at[0])
    wait_all(extra_dp.at[pl.ds(0, dp_count - 1)], extra_s.at[1])
    wait_all(extra_all.at[pl.ds(0, (count - 1) * piece)], extra_s.at[2])
    in_core_copy.wait_send()
    in_x_copy.wait_send()
    near_sum.drain()
    rest_sum.drain()
    out_sum.drain()
    in_sum.drain()
    mid_vec.drain()
    in_vec.drain()
    for store in stores:
        store.wait()


def widen_kernel(
    output_in, tokens_grad_in, vec_mid_ref, vec_in_ref, w_down_in, w_up_in, w_out_in, w_qkv_in, first_in,
    output_out, tokens_grad_out, gain_one_out, bias_one_out, b_val_out, b_out_out, gain_two_out, bias_two_out, b_up_out, b_down_out,
    w_down_out, w_up_out, w_out_out, w_qkv_out,
    down_low, up_low, out_low, qkv_low, first_low, tokens_grad_held, output_held, down_wide, up_wide, out_wide, qkv_wide, load_sem, store_sem,
):
    width = out_low.shape[0]
    blocks = down_low.shape[0] // width
    loads = []
    for k, (source, target) in enumerate(
        (
            (w_down_in, down_low), (w_up_in, up_low), (w_qkv_in, qkv_low), (first_in, first_low), (w_out_in, out_low),
            (tokens_grad_in, tokens_grad_held), (output_in, output_held),
        )
    ):
        loads.append(pltpu.make_async_copy(source, target, load_sem.at[k]))
        loads[-1].start()
    stores = []

    def store(source, target):
        stores.append(pltpu.make_async_copy(source, target, store_sem.at[len(stores)]))
        stores[-1].start()

    for row, target in enumerate((gain_one_out, bias_one_out, b_val_out)):
        target[...] = vec_in_ref[row : row + 1, :]
    for row in range(blocks):
        b_up_out[:, row * width : (row + 1) * width] = vec_mid_ref[row : row + 1, :]
    for row, target in enumerate((b_down_out, gain_two_out, bias_two_out, b_out_out)):
        target[...] = vec_mid_ref[blocks + row : blocks + row + 1, :]

    def convert(source, target, at, columns):
        def step(k, carried):
            here = pl.ds(pl.multiple_of(at + k * 64, 64), 64)
            there = pl.ds(pl.multiple_of(k * 64, 64), 64)
            if columns is None:
                target[here, :] = source[here, :].astype(jnp.float32)
            else:
                target[there, pl.ds(columns, width)] = source[here, :].astype(jnp.float32)
            return carried

        lax.fori_loop(0, width // 64, step, 0)

    loads[0].wait()
    for block in range(blocks):
        convert(down_low, down_wide, block * width, None)
        here = pl.ds(block * width, width)
        store(down_wide.at[here], w_down_out.at[here])
    loads[1].wait()
    for block in range(blocks):
        convert(up_low, up_wide, block * width, block * width)
        here = pl.ds(block * width, width)
        store(up_wide.at[:, here], w_up_out.at[:, here])
    loads[4].wait()
    convert(out_low, out_wide, 0, None)
    store(out_wide, w_out_out)
    loads[5].wait()
    store(tokens_grad_held, tokens_grad_out)
    loads[6].wait()
    store(output_held, output_out)
    loads[2].wait()
    loads[3].wait()
    piece = HD // 4
    wide = 2 * HD
    for part in range(3):
        for pair in range(width // wide):
            found = []
            for head in (2 * pair, 2 * pair + 1):
                z, y = head // 2, head % 2
                for owner in range(4):
                    core, x = owner // 2, owner % 2
                    two, three = (x, y) if core == 0 else (y, x)
                    depth = width // wide
                    start = ((((core * 2 + two) * 2 + three) * depth + z % 2 * 2 + z // 2) * 3 + part) * piece
                    block = qkv_low[start : start + piece].astype(jnp.float32)
                    if head == 0 and part < 2:
                        at = part * HD + owner * piece
                        block = block + first_low[at : at + piece].astype(jnp.float32)
                    found.append(block)
            columns = part * width + pair * wide
            qkv_wide[:, columns : columns + wide] = jnp.concatenate(found, axis=0).T
    store(qkv_wide, w_qkv_out)
    for one in stores:
        one.wait()


def exchange_heads(
    tokens, segment_ids, gain_one, bias_one, w_qkv, b_val, w_out, b_out,
    gain_two, bias_two, w_up, b_up, w_down, b_down, cotangent,
):
    count, dp_count = lax.axis_size("seq"), lax.axis_size("dp")
    rows, width = tokens.shape[1], tokens.shape[2]
    hidden = w_up.shape[1]
    half = rows // 2
    tiles = count * (count + 1) // 2
    wide = 2 * HD
    f32 = jnp.float32
    packed = rows + half
    depth = count // 2

    def vmem(*shape, dtype=low):
        return pltpu.VMEM(shape, dtype)

    def sems(*shape):
        return pltpu.SemaphoreType.DMA(shape)

    scratch = [
        vmem(width, width), vmem(width, hidden), vmem(hidden, width), vmem(width, 3 * width), vmem(1, rows, width), sems(5), sems(8),
        vmem(count, rows, width), vmem(width, 2 * wide), vmem(width, wide), vmem(1, wide, dtype=f32),
        vmem(count, rows, wide), vmem(count, rows, wide), vmem(count, rows, wide), vmem(count, rows, wide), vmem(count, wide, rows),
        vmem(tiles, rows, rows), vmem(tiles, rows, rows), vmem(tiles, rows, rows, dtype=f32),
        vmem(count, 1, rows, dtype=f32), vmem(count, rows, wide, dtype=f32), vmem(rows, wide, dtype=f32),
        vmem(count, half, wide), vmem(count, half, wide), vmem(count, half, wide), vmem(count, half, wide), vmem(count, rows, wide), vmem(count, HD, rows),
        vmem(count, 1, rows, dtype=f32),
        vmem(count, packed, wide), vmem(count, packed, wide), vmem(count, rows, wide), vmem(count, rows, wide), vmem(depth, rows, wide),
        vmem(rows, rows), vmem(rows, rows),
        vmem(rows, width, dtype=f32), vmem(rows, 1, dtype=f32),
        vmem(rows, width), vmem(rows, width), vmem(rows, width, dtype=f32), vmem(rows, width, dtype=f32), vmem(rows, width, dtype=f32), vmem(rows, 3 * width),
    ]
    for total in (hidden, hidden, width):
        scratch += [vmem(total, width), vmem(total, width)]
        scratch += [vmem(total >> stage, width) for stage in range(1, 6)]
    scratch += [
        vmem(3 * HD, width, dtype=f32), vmem(wide, width, dtype=f32),
        vmem(3 * HD, width), vmem(3 * HD // 2, width), vmem(3 * HD // 4, width), vmem(3 * width, width),
        vmem(wide, width), vmem(count, wide // count, width), vmem(wide // count, width, dtype=f32), vmem(dp_count, wide // count, width, dtype=f32), vmem(wide, width),
    ]
    for _ in range(2):
        scratch += [vmem(8, width, dtype=f32), vmem(count, 8, width, dtype=f32), vmem(8, width, dtype=f32), vmem(dp_count, 8, width, dtype=f32)]
    scratch += [sems(3), sems(2 * count), sems(1), sems(1), sems(1), sems(count)]
    scratch += [sems(1), sems(1), sems(1), sems(count), sems(1), sems(1), sems(3), sems(3)]
    scratch += [sems(1), sems(5)] * 6
    scratch += [sems(1), sems(5), sems(2), sems(2), sems(4), sems(4)]
    in_vmem = pl.BlockSpec(memory_space=pltpu.VMEM)
    anywhere = pl.BlockSpec(memory_space=pl.ANY)
    specs = [in_vmem] * 15
    for at in (4, 6, 10, 12, 14):
        specs[at] = anywhere
    shape = jax.ShapeDtypeStruct
    results = pl.pallas_call(
        layer_kernel,
        out_shape=[
            shape((1, rows, width), low), shape((1, rows, width), f32), shape((8, width), f32), shape((8, width), f32),
            shape((hidden, width), low), shape((hidden, width), low), shape((width, width), low), shape((3 * width, width), low), shape((wide, width), low),
        ],
        in_specs=specs,
        out_specs=[in_vmem] * 4 + [anywhere] * 5,
        scratch_shapes=scratch,
        compiler_params=pltpu.CompilerParams(
            collective_id=0, has_side_effects=True, vmem_limit_bytes=vmem_bytes
        ),
    )(
        tokens, segment_ids, gain_one[None], bias_one[None], w_qkv, b_val[None], w_out, b_out[None],
        gain_two[None], bias_two[None], w_up, b_up[None], w_down, b_down[None], cotangent,
    )
    vector = shape((1, width), f32)
    widened = pl.pallas_call(
        widen_kernel,
        out_shape=[
            shape((1, rows, width), low), shape((1, rows, width), f32), vector, vector, vector, vector, vector, vector, shape((1, hidden), f32), vector,
            shape((hidden, width), f32), shape((width, hidden), f32), shape((width, width), f32), shape((width, 3 * width), f32),
        ],
        in_specs=[anywhere] * 2 + [in_vmem] * 2 + [anywhere] * 5,
        out_specs=[anywhere] * 2 + [in_vmem] * 8 + [anywhere] * 4,
        scratch_shapes=[
            vmem(hidden, width), vmem(hidden, width), vmem(width, width), vmem(3 * width, width), vmem(wide, width), vmem(1, rows, width, dtype=f32), vmem(1, rows, width),
            vmem(hidden, width, dtype=f32), vmem(width, hidden, dtype=f32), vmem(width, width, dtype=f32), vmem(width, 3 * width, dtype=f32),
            sems(7), sems(12),
        ],
        compiler_params=pltpu.CompilerParams(vmem_limit_bytes=vmem_bytes),
    )(*results)
    output, tokens_grad = widened[:2]
    gain_one_grad, bias_one_grad, b_val_grad, b_out_grad, gain_two_grad, bias_two_grad, b_up_grad, b_down_grad = (
        row.reshape(row.shape[1]) for row in widened[2:10]
    )
    w_down_grad, w_up_grad, w_out_grad, w_qkv_grad = widened[10:]
    return (
        output, tokens_grad, gain_one_grad, bias_one_grad, w_qkv_grad, b_val_grad, w_out_grad, b_out_grad,
        gain_two_grad, bias_two_grad, w_up_grad, b_up_grad, w_down_grad, b_down_grad,
    )


def picks_heads(mesh, length, width, hidden):
    dp_count, count = mesh.shape["dp"], mesh.shape["seq"]
    power = length & (length - 1) == 0
    return dp_count == 4 and count == 8 and width == count * HD and hidden == 4 * width and power


def solution(mesh):
    placed = (
        P("dp", "seq", None),
        P("dp", None),
        P(),
        P(),
        P(),
        P(),
        P(),
        P(),
        P(),
        P(),
        P(),
        P(),
        P(),
        P(),
        P("dp", "seq", None),
    )

    def layer(tokens, *others):
        width, hidden = tokens.shape[-1], others[9].shape[-1]
        length = tokens.shape[1] * mesh.shape["seq"]
        body = exchange_heads if picks_heads(mesh, length, width, hidden) else local
        return body(tokens, *others)

    return jax.shard_map(
        layer,
        mesh=mesh,
        in_specs=placed,
        out_specs=(
            P("dp", "seq", None),
            P("dp", "seq", None),
            P(),
            P(),
            P(),
            P(),
            P(),
            P(),
            P(),
            P(),
            P(),
            P(),
            P(),
            P(),
        ),
        check_vma=False,
    )
```
